32 devices in a mesh: row: 8 (over y, x, core), col: 4 (over z).
Axes of the slice: x: 2, y: 2, z: 4, core: 2. Of those that a mesh axis runs over, the one named last changes fastest.
Arguments:
- tokens: bfloat16 [8192, 1536], P(('row', 'col')), may hold values from -6 to 6
- attn_gain: bfloat16 [1536], P(('row', 'col')), may hold values from 0.5 to 1.5
- w_query: bfloat16 [1536, 1536], P('row', 'col'), may hold values from -0.15625 to 0.15625
- w_key: bfloat16 [1536, 512], P('row', 'col'), may hold values from -0.15625 to 0.15625
- w_value: bfloat16 [1536, 512], P('row', 'col'), may hold values from -0.15625 to 0.15625
- w_out: bfloat16 [1536, 1536], P('row', 'col'), may hold values from -0.875 to 0.875
- expert_gain: bfloat16 [1536], P(('row', 'col')), may hold values from 0.5 to 1.5
- router: bfloat16 [1536, 8], P('row', 'col'), may hold values from -0.109375 to 0.109375
- w_gate: bfloat16 [8, 1536, 1024], P('row', 'col'), may hold values from -0.15625 to 0.15625
- w_up: bfloat16 [8, 1536, 1024], P('row', 'col'), may hold values from -0.15625 to 0.15625
- w_down: bfloat16 [8, 1024, 1536], P('row', 'col'), may hold values from -0.375 to 0.375
- segment_ids: int32 [32, 256], P(('row', 'col')), may hold values from 0 to 7, never falling along the last dimension, each value on 1 to 128 neighbouring positions
- expert_ids: int32 [8192, 2], P(('row', 'col')), may hold values from 0 to 7, all different within a row; in each aligned block of 256 rows (0 to 255, 256 to 511, ...) at most 128 rows name the same one
- cotangent: bfloat16 [8192, 1536], P(('row', 'col')), may hold values from -6 to 6
Outputs:
- output: bfloat16 [8192, 1536], P(('row', 'col'))
- d_tokens: float32 [8192, 1536], P(('row', 'col'))
- grad_attn_gain: float32 [1536], P(('row', 'col'))
- grad_w_query: float32 [1536, 1536], P('row', 'col')
- grad_w_key: float32 [1536, 512], P('row', 'col')
- grad_w_value: float32 [1536, 512], P('row', 'col')
- grad_w_out: float32 [1536, 1536], P('row', 'col')
- grad_expert_gain: float32 [1536], P(('row', 'col'))
- grad_router: float32 [1536, 8], P('row', 'col')
- grad_w_gate: float32 [8, 1536, 1024], P('row', 'col')
- grad_w_up: float32 [8, 1536, 1024], P('row', 'col')
- grad_w_down: float32 [8, 1024, 1536], P('row', 'col')
The draws below stay inside these ranges and needn't reach their ends.
Inputs may be any that keep to these rules, and one draw needn't show every extreme that they name: `expert_ids`: each row names 2 different experts. Among the 256 rows of one device no expert is named more than 128 times, and in every draw some device names some expert exactly 128 times. `segment_ids`: within each row the ids never fall and mark 8 documents of 1 to 128 tokens, one of exactly 128 tokens.
All inputs are finite; a program needn't handle non-finite values.
Results may differ from the reference program's by a relative error of at most 0.018.
Values may be sent and summed in bfloat16 or wider, within the bound.
A program may use at most 192 MiB of HBM per device.

```python
import math
import jax
import jax.numpy as jnp
import numpy as np
from jax import lax

D = 1536
HQ = 24
KEY_VALUE_HEADS = 8
HEAD_SIZE = 64
H = 1024
TOP = 2
DOCS = 8
TOK_DEV = 256
QD = 1536
KD = 512
QUERY_PER_KEY = 3
EXPERTS = 8
CAP = 128
DOC_MOST = 128
SEQS = 32
TOKENS = 8192


def steps_of(key, extent, cuts, low, high):
    level = 1.0
    for axis_at, shards_of in cuts:
        draws = jax.random.uniform(jax.random.fold_in(jax.random.fold_in(key, 6), axis_at), (shards_of,), jnp.float32, low / len(cuts), high / len(cuts))
        level = level * jnp.repeat(jnp.exp(draws), extent[axis_at] // shards_of).reshape((-1,) + (1,) * (len(extent) - 1 - axis_at))
    return level


def profile(amount, total, most, lean):
    weights = [(1 << 20) // math.isqrt(grade ** lean) + 1 for grade in range(2, amount + 1)]
    spare, given = total - most - (amount - 1), [1] * (amount - 1)
    while spare > 0:
        free = [i for i in range(amount - 1) if given[i] < most]
        whole, left = sum([weights[i] for i in free]), spare
        for i in free:
            extra = min(most - given[i], max(1, left * weights[i] // whole), spare)
            given[i] = given[i] + extra
            spare = spare - extra
    return np.array([most] + given)


def uneven_parts(stream_key, count, total, limit, lean):
    if count == 2:
        one = jax.random.randint(stream_key, (), max(1, total - limit), min(limit, total - 1) + 1)
        return jnp.stack([one, total - one])
    tallies = jnp.asarray(profile(count, total, limit, lean), jnp.int32)
    twos = (count - 1) // 2
    source_of, sink = tallies[1:1 + 2 * twos:2], tallies[2:2 + 2 * twos:2]
    slack = jnp.minimum(source_of - 1, limit - sink)
    moved = jax.random.randint(jax.random.fold_in(stream_key, 1), (twos,), 0, 1 << 20) % (slack + 1)
    tallies = tallies.at[1:1 + 2 * twos:2].set(source_of - moved).at[2:2 + 2 * twos:2].set(sink + moved)
    return tallies[jax.random.permutation(jax.random.fold_in(stream_key, 2), count)]


def routed_block(stream_key, own, number, rows, number_of, top, bound, slope):
    ranking = jax.random.permutation(stream_key, number_of)
    crowded, ordinary = load_shares(number_of, rows * top, bound, slope, True), load_shares(number_of, rows * top, bound, slope, False)
    places = jnp.arange(number_of)

    def named(sizes, turn):
        used = int((sizes > 0).sum())
        fixed = max(1, used // 4)
        passed = fixed + (places - fixed + turn * (used - fixed)) % max(1, number_of - fixed)
        return jnp.zeros((number_of,), jnp.int32).at[ranking[jnp.where(places < fixed, places, passed)]].set(jnp.asarray(sizes, jnp.int32))

    sizes = jnp.where(number % 4 == 0, named(crowded, number // 4), named(ordinary, number - number // 4 - 1))
    mixed = jax.random.permutation(jax.random.fold_in(own, 3), number_of)
    source_of, receiver = mixed[0:number_of // 2 * 2:2], mixed[1:number_of // 2 * 2:2]
    slack = jnp.minimum(sizes[source_of] - 1, bound - sizes[receiver]) // 2
    slack = jnp.where((source_of == ranking[0]) | (receiver == ranking[0]) | (sizes[receiver] == 0), 0, jnp.maximum(slack, 0))
    passed = jax.random.randint(jax.random.fold_in(own, 4), (number_of // 2,), 0, 1 << 20) % (slack + 1)
    sizes = sizes.at[source_of].add(-passed).at[receiver].add(passed)
    items = jnp.searchsorted(jnp.cumsum(sizes), jnp.arange(rows * top), side="right").astype(jnp.int32)
    table = items.reshape(top, rows).T
    table = table[jax.random.permutation(jax.random.fold_in(own, 1), rows)]
    turn = jax.random.randint(jax.random.fold_in(own, 2), (rows, 1), 0, top)
    return jnp.take_along_axis(table, (jnp.arange(top)[None, :] + turn) % top, axis=1)


def load_shares(amount, total, most, lean, full):
    weights = [(1 << 20) // math.isqrt(standing ** lean) + 1 for standing in range(1, amount + 1)]
    largest = most if full else min(most, max(-(-total // amount), total * weights[0] // sum(weights)))
    least = 1 if total - largest >= amount - 1 else 0
    given, rest = [largest] + [least] * (amount - 1), total - largest - least * (amount - 1)
    while rest > 0:
        free = [i for i in range(1, amount) if given[i] < largest] or [i for i in range(1, amount) if given[i] < most]
        whole, left = sum([weights[i] for i in free]), rest
        for i in free:
            extra = min(most - given[i], max(1, left * weights[i] // whole), rest)
            given[i] = given[i] + extra
            rest = rest - extra
    return np.array(given)


def normal_values(own_key, dims, deviation, bound, shards=(), kind=jnp.bfloat16):
    gain = steps_of(own_key, dims, shards, -0.22, 0.18) if shards else 1.0
    drawn = jax.random.normal(own_key, dims, jnp.float32) * deviation * gain
    return jnp.minimum(jnp.maximum(drawn, -bound), bound).astype(kind)


def setup_inputs(seed: int = 0) -> dict:
    splits = jax.random.split(jax.random.key(seed), 15)
    tokens = normal_values(splits[0], (TOKENS, D), 1.0, 6.0, ((0, 32),))
    attn_gain = jnp.clip(1.0 + 0.1 * jax.random.normal(splits[1], (D,), jnp.float32), 0.5, 1.5).astype(jnp.bfloat16)
    w_query = normal_values(splits[2], (D, QD), D ** -0.5, 0.15625, ((0, 8), (1, 4)))
    w_key = normal_values(splits[3], (D, KD), D ** -0.5, 0.15625, ((0, 8), (1, 4)))
    w_value = normal_values(splits[4], (D, KD), D ** -0.5, 0.15625, ((0, 8), (1, 4)))
    w_out = normal_values(splits[5], (QD, D), (QD // 32) ** -0.5, 0.875, ((0, 8), (1, 4)))
    expert_gain = jnp.clip(1.0 + 0.1 * jax.random.normal(splits[6], (D,), jnp.float32), 0.5, 1.5).astype(jnp.bfloat16)
    router = normal_values(splits[7], (D, EXPERTS), (2 * D) ** -0.5, 0.109375, ((0, 8), (1, 4)))
    w_gate = normal_values(splits[8], (EXPERTS, D, H), D ** -0.5, 0.15625, ((0, 8), (1, 4)))
    w_up = normal_values(splits[9], (EXPERTS, D, H), D ** -0.5, 0.15625, ((0, 8), (1, 4)))
    w_down = normal_values(splits[10], (EXPERTS, H, D), (H // 4) ** -0.5, 0.375, ((0, 8), (1, 4)))
    segment_ids = jax.vmap(lambda own: jnp.searchsorted(jnp.cumsum(uneven_parts(own, DOCS, TOK_DEV, DOC_MOST, 2)), jnp.arange(TOK_DEV), side="right"))(jax.random.split(splits[11], SEQS)).reshape((SEQS, TOK_DEV)).astype(jnp.int32)
    expert_ids_keys = jax.random.split(jax.random.fold_in(splits[12], 1), TOKENS // TOK_DEV)
    expert_ids_turns = jax.random.permutation(jax.random.fold_in(splits[12], 3), TOKENS // TOK_DEV)
    expert_ids = jax.vmap(lambda own, number: routed_block(jax.random.fold_in(splits[12], 2), own, number, TOK_DEV, EXPERTS, TOP, CAP, 1))(expert_ids_keys, expert_ids_turns).reshape((TOKENS, TOP))
    cotangent = normal_values(splits[13], (TOKENS, D), 1.0, 6.0, ((0, 32),))
    return dict(tokens=tokens, attn_gain=attn_gain, w_query=w_query, w_key=w_key, w_value=w_value, w_out=w_out, expert_gain=expert_gain, router=router, w_gate=w_gate, w_up=w_up, w_down=w_down, segment_ids=segment_ids, expert_ids=expert_ids, cotangent=cotangent)


@jax.custom_vjp
def low(v):
    return lax.optimization_barrier(v.astype(jnp.bfloat16)).astype(jnp.float32)

@jax.custom_vjp
def low_back(v):
    return v

def low_keep(v):
    return (low(v), None)

def low_pass(kept, grad):
    return (grad,)

def back_keep(v):
    return (v, None)

def back_low(kept, grad):
    return (low(grad),)
low.defvjp(low_keep, low_pass)
low_back.defvjp(back_keep, back_low)
EPSILON = 1e-05
NEGATIVE = -1e+30
HIGHEST = lax.Precision.HIGHEST

def rounded(value):
    return low(low_back(value))

def rms_factor(rows_in):
    return lax.rsqrt(lax.optimization_barrier(jnp.mean(rows_in * rows_in, axis=1, keepdims=True)) + EPSILON)

def slot_tables(routes):
    pair_count = routes.shape[0] * routes.shape[1]
    pair_ids = routes.reshape(-1).astype(jnp.int32)
    one_hot = (pair_ids[:, None] == jnp.arange(EXPERTS, dtype=jnp.int32)[None, :]).astype(jnp.int32)
    before = lax.optimization_barrier(jnp.sum((jnp.cumsum(one_hot, axis=0) - one_hot) * one_hot, axis=1)).astype(jnp.int32)
    slot_place = (pair_ids * CAP + before).astype(jnp.int32)
    pair_index = jnp.arange(pair_count, dtype=jnp.int32)
    slot_owner = jnp.full((EXPERTS * CAP,), pair_count, jnp.int32).at[slot_place].set(pair_index)
    return (slot_place, slot_owner)

def attention_rows(query_rows, rows_of_key, rows_of_value, segments):
    length_total = query_rows.shape[0]
    heads_of_query = query_rows.reshape(length_total, KEY_VALUE_HEADS, QUERY_PER_KEY, HEAD_SIZE)
    heads_of_key = rows_of_key.reshape(length_total, KEY_VALUE_HEADS, HEAD_SIZE)
    heads_of_value = rows_of_value.reshape(length_total, KEY_VALUE_HEADS, HEAD_SIZE)
    scores = jnp.einsum('qkgd,skd->kgqs', heads_of_query, heads_of_key, precision=HIGHEST) * HEAD_SIZE ** (-0.5)
    scores = low_back(scores)
    positions = jnp.arange(length_total, dtype=jnp.int32)
    allowed = (positions[None, :] <= positions[:, None]) & (segments[None, :] == segments[:, None])
    scores = jnp.where(allowed, scores, NEGATIVE)
    soft_probs = low(jax.nn.softmax(scores, axis=-1))
    head_mix = jnp.einsum('kgqs,skd->qkgd', soft_probs, heads_of_value, precision=HIGHEST)
    return head_mix.reshape(length_total, HQ * HEAD_SIZE)

def layer_rows(rows_in, segments, routes, params):
    attn_gain, w_query, w_key, w_value, w_out, expert_gain, router, w_gate, w_up, w_down = params
    length_total = rows_in.shape[0]
    normed = low(rows_in * rms_factor(rows_in) * attn_gain)
    query_rows = rounded(jnp.dot(normed, w_query, precision=HIGHEST))
    rows_of_key = rounded(jnp.dot(normed, w_key, precision=HIGHEST))
    rows_of_value = rounded(jnp.dot(normed, w_value, precision=HIGHEST))
    attended = rounded(attention_rows(query_rows, rows_of_key, rows_of_value, segments))
    hidden = rows_in + low_back(jnp.dot(attended, w_out, precision=HIGHEST))
    normed_two = low(hidden * rms_factor(hidden) * expert_gain)
    logits = low_back(jnp.dot(normed_two, router, precision=HIGHEST))
    gate_probs = jax.nn.softmax(jnp.take_along_axis(logits, routes, axis=1), axis=1)
    slot_place, slot_owner = slot_tables(routes)
    sent_rows = jnp.take(normed_two, slot_owner // TOP, axis=0, mode='fill', fill_value=0.0)
    sent_rows = low_back(sent_rows).reshape(EXPERTS, CAP, D)
    gate_pre = low_back(jnp.einsum('ecd,edh->ech', sent_rows, w_gate, precision=HIGHEST))
    up_pre = low_back(jnp.einsum('ecd,edh->ech', sent_rows, w_up, precision=HIGHEST))
    activation = low(jax.nn.silu(gate_pre) * up_pre)
    produced = rounded(jnp.einsum('ech,ehd->ecd', activation, w_down, precision=HIGHEST))
    returned = jnp.take(produced.reshape(EXPERTS * CAP, D), slot_place, axis=0).reshape(length_total, TOP, D)
    return hidden + lax.optimization_barrier(jnp.sum(returned * gate_probs[:, :, None], axis=1))

def reference(tokens, attn_gain, w_query, w_key, w_value, w_out, expert_gain, router, w_gate, w_up, w_down, segment_ids, expert_ids, cotangent):
    params = tuple((weight.astype(jnp.float32) for weight in (attn_gain, w_query, w_key, w_value, w_out, expert_gain, router, w_gate, w_up, w_down)))
    group_size = math.gcd(SEQS, max(1, 4096 // TOK_DEV))
    blocks = SEQS // group_size
    rows_all = tokens.astype(jnp.float32).reshape(blocks, group_size, TOK_DEV, D)
    segments_all = segment_ids.astype(jnp.int32).reshape(blocks, group_size, TOK_DEV)
    routes_all = expert_ids.astype(jnp.int32).reshape(blocks, group_size, TOK_DEV, TOP)

    def forward(rows_given, weights):

        def one_block(block_in):
            rows_blk, segments_blk, routes_blk = block_in

            def single(rows_one, segments_one, routes_one):
                return layer_rows(rows_one, segments_one, routes_one, weights)
            return jax.vmap(single)(rows_blk, segments_blk, routes_blk)
        return lax.map(jax.checkpoint(one_block), (rows_given, segments_all, routes_all))
    result, pullback = jax.vjp(forward, rows_all, params)
    grad_rows, grads = pullback(cotangent.astype(jnp.float32).reshape(blocks, group_size, TOK_DEV, D))
    return (result.reshape(TOKENS, D).astype(jnp.bfloat16), grad_rows.reshape(TOKENS, D), grads[0], grads[1], grads[2], grads[3], grads[4], grads[5], grads[6], grads[7], grads[8], grads[9])
```

```python
import functools

import jax
import jax.numpy as jnp
from jax import lax
from jax.experimental import pallas as pl
from jax.experimental.pallas import tpu as pltpu
from jax.sharding import PartitionSpec as P

KEY_VALUE_HEADS = 8
HEAD_SIZE = 64
TOP = 2
QUERY_PER_KEY = 3


EPSILON = 1e-05
NEGATIVE = -1e30


MESH = pl.DeviceIdType.MESH
ANY = pl.BlockSpec(memory_space=pl.ANY)


def row_at(row, flip):
    y, x, core = row // 4, (row // 2) % 2, row % 2
    return (
        (y + flip // 4) % 2 * 4 + (x + (flip // 2) % 2) % 2 * 2 + (core + flip % 2) % 2
    )


def remote(source, target, send, receive, device):
    return pltpu.make_async_remote_copy(
        source, target, send, receive, device_id=device, device_id_type=MESH
    )


def greet(row_flips, col_steps):
    row, col = lax.axis_index("row"), lax.axis_index("col")
    sem = pltpu.get_barrier_semaphore()
    for flip in row_flips:
        pl.semaphore_signal(
            sem, inc=1, device_id={"row": row_at(row, flip)}, device_id_type=MESH
        )
    for step in col_steps:
        pl.semaphore_signal(
            sem, inc=1, device_id={"col": (col + step) % 4}, device_id_type=MESH
        )
    pl.semaphore_wait(sem, len(row_flips) + len(col_steps))


def unit_order(col, k):
    table = ((0, 1, 2, 3), (1, 0, 2, 3), (2, 3, 1, 0), (3, 2, 1, 0))
    out = table[3][k]
    for c in (2, 1, 0):
        out = jnp.where(col == c, table[c][k], out)
    return out


X, Y, SIB = 2, 4, 1


def plane_send(view, row, ss, rs):
    for i, flip in enumerate((X, Y, SIB)):
        remote(view(row), view(row), ss(i), rs(i), {"row": row_at(row, flip)}).start()


def plane_forward(view, halves, row, ss, rs):
    first, second = halves
    from_x, from_y = row_at(row, X), row_at(row, Y)
    sib = {"row": row_at(row, SIB)}
    remote(view(from_x), view(from_x), ss(0), rs(0), sib).wait_recv()
    remote(first(from_x), first(from_x), ss(3), rs(3), {"row": from_y}).start()
    remote(view(from_x), view(from_x), ss(5), rs(5), sib).start()
    remote(view(from_y), view(from_y), ss(1), rs(1), sib).wait_recv()
    remote(second(from_y), second(from_y), ss(4), rs(4), {"row": from_x}).start()
    remote(view(from_y), view(from_y), ss(6), rs(6), sib).start()


def plane_last(view, halves, row, ss, rs):
    first, second = halves
    diag = row_at(row, X + Y)
    sib = {"row": row_at(row, SIB)}
    remote(first(diag), first(diag), ss(3), rs(3), sib).wait_recv()
    remote(first(diag), first(diag), ss(7), rs(7), sib).start()
    remote(second(diag), second(diag), ss(4), rs(4), sib).wait_recv()
    remote(second(diag), second(diag), ss(8), rs(8), sib).start()


def plane_finish(view, halves, row, ss, rs):
    first, second = halves
    sib_row = row_at(row, SIB)
    sib = {"row": sib_row}
    whole = view(sib_row)
    remote(whole, whole, ss(2), rs(2), sib).wait_recv()
    for i, flip in ((5, X), (6, Y)):
        block = view(row_at(sib_row, flip))
        remote(block, block, ss(i), rs(i), sib).wait_recv()
    far = row_at(sib_row, X + Y)
    remote(first(far), first(far), ss(7), rs(7), sib).wait_recv()
    remote(second(far), second(far), ss(8), rs(8), sib).wait_recv()
    for i in range(9):
        block = view(row) if i in (0, 1, 2, 5, 6) else (first(row) if i in (3, 7) else second(row))
        remote(block, block, ss(i), rs(i), sib).wait_send()


def pick(ref, cols, halves_rows):
    block, cut = halves_rows

    def at(start, size):
        def view(r):
            rows = pl.ds(pl.multiple_of(r * block + start, 16), size)
            if cols is None:
                return ref.at[rows, :]
            return ref.at[rows, pl.ds(pl.multiple_of(cols[0], 128), cols[1])]

        return view

    return at(0, block), (at(0, cut), at(cut, block - cut))


def gather_kernel(own_a, own_b, own_s, own_c, full_a, full_b, full_s, full_c,
                  zss, zrs, ass, ars, bss, brs, css, crs, s_zs, s_zr, s_ps, s_pr, loc):
    row, col = lax.axis_index("row"), lax.axis_index("col")
    greet(range(1, 6), (1, 2, 3)) if False else greet(range(1, 8), (1, 2, 3))
    block = own_a.shape[0]
    width_a, width_b = own_a.shape[1], own_b.shape[1]
    rows_c = own_c.shape[0]
    cut = block // 2

    def views(c):
        va = pick(full_a, (c * width_a, width_a), (block, cut))
        vb = pick(full_b, (c * width_b, width_b), (block, cut))
        return va, vb

    for i, step in enumerate((1, 2, 3)):
        remote(own_s, full_s.at[col, row], s_zs.at[i], s_zr.at[i], {"col": (col + step) % 4}).start()
    (view_a, _), (view_b, _) = views(col)
    copies = [
        pltpu.make_async_copy(own_a, view_a(row), loc.at[0]),
        pltpu.make_async_copy(own_b, view_b(row), loc.at[1]),
        pltpu.make_async_copy(own_s, full_s.at[col, row], loc.at[2]),
        pltpu.make_async_copy(own_c, full_c.at[pl.ds(row * rows_c, rows_c), :], loc.at[3]),
    ]
    for copy in copies:
        copy.start()

    def along(c, source_a, source_b, right, left):
        (va, _), (vb, _) = views(c)
        for d, (cond, step) in enumerate(((right, 1), (left, 3))):
            @pl.when(cond)
            def _():
                there = {"col": (col + step) % 4}
                remote(source_a, va(row), zss.at[0, c, d], zrs.at[0, c], there).start()
                remote(source_b, vb(row), zss.at[1, c, d], zrs.at[1, c], there).start()

    along(col, own_a, own_b, col < 3, col > 0)
    for copy in copies:
        copy.wait()
    for k in range(4):
        c = unit_order(col, k)
        (va, ha), (vb, hb) = views(c)
        if k > 0:
            remote(va(row), va(row), zss.at[0, c, 0], zrs.at[0, c], {"col": (col + 1) % 4}).wait_recv()
            remote(vb(row), vb(row), zss.at[1, c, 0], zrs.at[1, c], {"col": (col + 1) % 4}).wait_recv()
            along(c, va(row), vb(row), (c < col) & (col < 3), (c > col) & (col > 0))
        plane_send(va, row, lambda i: ass.at[c, i], lambda i: ars.at[c, i])
        plane_send(vb, row, lambda i: bss.at[c, i], lambda i: brs.at[c, i])
        if k > 0:
            p = unit_order(col, k - 1)
            (va, ha), (vb, hb) = views(p)
            plane_forward(va, ha, row, lambda i: ass.at[p, i], lambda i: ars.at[p, i])
            plane_forward(vb, hb, row, lambda i: bss.at[p, i], lambda i: brs.at[p, i])
        if k > 1:
            q = unit_order(col, k - 2)
            (va, ha), (vb, hb) = views(q)
            plane_last(va, ha, row, lambda i: ass.at[q, i], lambda i: ars.at[q, i])
            plane_last(vb, hb, row, lambda i: bss.at[q, i], lambda i: brs.at[q, i])
        if k == 0:
            for i, step in enumerate((3, 2, 1)):
                remote(own_s, full_s.at[(col + step) % 4, row], s_zs.at[i], s_zr.at[i], {"col": (col + 1) % 4}).wait()
            for i in range(1, 8):
                remote(full_s.at[:, row], full_s.at[:, row], s_ps.at[i - 1], s_pr.at[i - 1], {"row": row_at(row, i)}).start()
    vc, hc = pick(full_c, None, (rows_c, rows_c // 2))
    csv, crv = (lambda i: css.at[i]), (lambda i: crs.at[i])
    plane_send(vc, row, csv, crv)
    for k in (3,):
        p = unit_order(col, k)
        (va, ha), (vb, hb) = views(p)
        plane_forward(va, ha, row, lambda i: ass.at[p, i], lambda i: ars.at[p, i])
        plane_forward(vb, hb, row, lambda i: bss.at[p, i], lambda i: brs.at[p, i])
    for k in (2, 3):
        p = unit_order(col, k)
        (va, ha), (vb, hb) = views(p)
        plane_last(va, ha, row, lambda i: ass.at[p, i], lambda i: ars.at[p, i])
        plane_last(vb, hb, row, lambda i: bss.at[p, i], lambda i: brs.at[p, i])
    plane_forward(vc, hc, row, csv, crv)
    plane_last(vc, hc, row, csv, crv)
    for c in range(4):
        (va, ha), (vb, hb) = views(c)
        plane_finish(va, ha, row, lambda i: ass.at[c, i], lambda i: ars.at[c, i])
        plane_finish(vb, hb, row, lambda i: bss.at[c, i], lambda i: brs.at[c, i])
    plane_finish(vc, hc, row, csv, crv)
    for i in range(1, 8):
        there = row_at(row, i)
        remote(full_s.at[:, there], full_s.at[:, there], s_ps.at[i - 1], s_pr.at[i - 1], {"row": there}).wait()
    for k in range(4):
        c = unit_order(col, k)
        (va, ha), (vb, hb) = views(c)
        right = (c <= col) & (col < 3)
        left = (c >= col) & (col > 0)
        for d, cond in enumerate((right, left)):
            @pl.when(cond)
            def _():
                there = {"col": (col + 1) % 4}
                remote(va(row), va(row), zss.at[0, c, d], zrs.at[0, c], there).wait_send()
                remote(vb(row), vb(row), zss.at[1, c, d], zrs.at[1, c], there).wait_send()


def gather_attention(own_a, own_b, own_s, own_c):
    sems = pltpu.SemaphoreType.DMA
    block, rows_c = own_a.shape[0], own_c.shape[0]
    return pl.pallas_call(
        gather_kernel,
        out_shape=(
            jax.ShapeDtypeStruct((block * 8, own_a.shape[1] * 4), own_a.dtype),
            jax.ShapeDtypeStruct((block * 8, own_b.shape[1] * 4), own_b.dtype),
            jax.ShapeDtypeStruct((4, 8) + own_s.shape, own_s.dtype),
            jax.ShapeDtypeStruct((8 * rows_c, own_c.shape[1]), own_c.dtype),
        ),
        in_specs=[ANY] * 4,
        out_specs=(ANY,) * 4,
        scratch_shapes=[
            sems((2, 4, 2)), sems((2, 4)),
            sems((4, 9)), sems((4, 9)), sems((4, 9)), sems((4, 9)),
            sems((9,)), sems((9,)),
            sems((3,)), sems((3,)), sems((7,)), sems((7,)), sems((4,)),
        ],
        compiler_params=pltpu.CompilerParams(collective_id=0, has_side_effects=True),
        cost_estimate=pl.CostEstimate(flops=0, bytes_accessed=200_000_000, transcendentals=0),
    )(own_a, own_b, own_s, own_c)


def spread_kernel(own_c, own_g, full_c, full_g, css, crs, gss, grs, loc):
    row = lax.axis_index("row")
    greet(range(1, 8), ())
    rows_c = own_c.shape[0]
    copies = [
        pltpu.make_async_copy(own_c, full_c.at[pl.ds(row * rows_c, rows_c), :], loc.at[0]),
        pltpu.make_async_copy(own_g, full_g.at[row], loc.at[1]),
    ]
    for copy in copies:
        copy.start()
    for i in range(1, 8):
        remote(own_g, full_g.at[row], gss.at[i - 1], grs.at[i - 1], {"row": row_at(row, i)}).start()
    for copy in copies:
        copy.wait()
    vc, hc = pick(full_c, None, (rows_c, rows_c // 2))
    csv, crv = (lambda i: css.at[i]), (lambda i: crs.at[i])
    plane_send(vc, row, csv, crv)
    plane_forward(vc, hc, row, csv, crv)
    plane_last(vc, hc, row, csv, crv)
    plane_finish(vc, hc, row, csv, crv)
    for i in range(1, 8):
        there = row_at(row, i)
        remote(own_g, full_g.at[there], gss.at[i - 1], grs.at[i - 1], {"row": there}).wait()


def spread_tokens(own_c, own_g):
    sems = pltpu.SemaphoreType.DMA
    return pl.pallas_call(
        spread_kernel,
        out_shape=(
            jax.ShapeDtypeStruct((8 * own_c.shape[0], own_c.shape[1]), own_c.dtype),
            jax.ShapeDtypeStruct((8,) + own_g.shape, own_g.dtype),
        ),
        in_specs=[ANY] * 2,
        out_specs=(ANY,) * 2,
        scratch_shapes=[sems((9,)), sems((9,)), sems((7,)), sems((7,)), sems((2,))],
        compiler_params=pltpu.CompilerParams(collective_id=1, has_side_effects=True),
        cost_estimate=pl.CostEstimate(flops=0, bytes_accessed=100_000_000, transcendentals=0),
    )(own_c, own_g)


def add_into(target, term):
    target[...] = (target[...].astype(jnp.float32) + term[...].astype(jnp.float32)).astype(target.dtype)


def reduce_kernel(grad_a, grad_b, grad_s, sum_a, sum_b, sum_s,
                  own, rec_sib, rec_one, rec_two, rec_z, s_own, s_rec, s_mid, s_zrec,
                  lss, lrs, ss1, rs1, ss2, rs2, zss, zrs, lo, s_ss, s_rs, sz_ss, sz_rs):
    row, col = lax.axis_index("row"), lax.axis_index("col")
    core = row % 2
    chip = row // 2
    cy, cx = chip // 2, chip % 2
    block, width = own.shape[2], own.shape[3]
    width_a = sum_a.shape[1]
    width_b = width - width_a
    cut = block // 2
    greet(range(1, 8), (1, 2, 3))
    sib = {"row": row_at(row, SIB)}
    to_x, to_y = {"row": row_at(row, X)}, {"row": row_at(row, Y)}

    def parts(c, q, of_core):
        rows = pl.ds(pl.multiple_of((q * 2 + of_core) * block, 16), block)
        return (
            grad_a.at[rows, pl.ds(pl.multiple_of(c * width_a, 128), width_a)],
            grad_b.at[rows, pl.ds(pl.multiple_of(c * width_b, 128), width_b)],
        )

    for i in range(1, 8):
        there = row_at(row, i)
        remote(grad_s.at[there], s_rec.at[i - 1], s_ss.at[i - 1], s_rs.at[i - 1], {"row": there}).start()
    def start_first(c, carry):
        for q in range(4):
            pa, pb = parts(c, q, 1 - core)
            remote(pa, rec_sib.at[c, q, :, pl.ds(0, width_a)], ss1.at[c, q, 0], rs1.at[c, q, 0], sib).start()
            remote(pb, rec_sib.at[c, q, :, pl.ds(width_a, width_b)], ss1.at[c, q, 1], rs1.at[c, q, 1], sib).start()
            pa, pb = parts(c, q, core)
            pltpu.make_async_copy(pa, own.at[c, q, :, pl.ds(0, width_a)], lss.at[c, q, 0]).start()
            pltpu.make_async_copy(pb, own.at[c, q, :, pl.ds(width_a, width_b)], lss.at[c, q, 1]).start()
        return carry
    lax.fori_loop(0, 4, start_first, 0)
    own_small = pltpu.make_async_copy(grad_s.at[row], s_own, lo.at[0])
    own_small.start()

    def chip_sum(c):
        for q in range(4):
            pa, pb = parts(c, q, core)
            for i, (p, off, w) in enumerate(((pa, 0, width_a), (pb, width_a, width_b))):
                pltpu.make_async_copy(p, own.at[c, q, :, pl.ds(off, w)], lss.at[c, q, i]).wait()
                remote(p, rec_sib.at[c, q, :, pl.ds(off, w)], ss1.at[c, q, i], rs1.at[c, q, i], sib).wait_recv()
            add_into(own.at[c, q], rec_sib.at[c, q])

    top, low = pl.ds(0, cut), pl.ds(cut, block - cut)

    def one(c):
        for j in range(2):
            yield remote(own.at[c, j * 2 + 1 - cx, top, :], rec_one.at[c, 0, j], ss2.at[c, 0, j], rs2.at[c, 0, j], to_x)
            yield remote(own.at[c, (1 - cy) * 2 + j, low, :], rec_one.at[c, 1, j], ss2.at[c, 1, j], rs2.at[c, 1, j], to_y)

    def one_sum(c):
        for copy in one(c):
            copy.wait_recv()
        for j in range(2):
            add_into(own.at[c, j * 2 + cx, top, :], rec_one.at[c, 0, j])
            add_into(own.at[c, cy * 2 + j, low, :], rec_one.at[c, 1, j])

    def two(c):
        yield remote(own.at[c, (1 - cy) * 2 + cx, top, :], rec_two.at[c, 0], ss2.at[c, 0, 2], rs2.at[c, 0, 2], to_y)
        yield remote(own.at[c, cy * 2 + 1 - cx, low, :], rec_two.at[c, 1], ss2.at[c, 1, 2], rs2.at[c, 1, 2], to_x)

    def two_sum(c):
        for copy in two(c):
            copy.wait_recv()
        add_into(own.at[c, chip, top, :], rec_two.at[c, 0])
        add_into(own.at[c, chip, low, :], rec_two.at[c, 1])

    def column(step):
        there = (col + step) % 4
        return remote(own.at[there, chip], rec_z.at[step - 1], zss.at[step - 1], zrs.at[step - 1], {"col": there})

    def stages(k, carry):
        @pl.when(k < 4)
        def _():
            chip_sum(k)
            for copy in one(k):
                copy.start()
        @pl.when((k >= 1) & (k < 5))
        def _():
            one_sum(k - 1)
            for copy in two(k - 1):
                copy.start()
        @pl.when(k >= 2)
        def _():
            two_sum(k - 2)
        for step in (1, 2, 3):
            @pl.when((k >= 2) & ((col + step) % 4 == k - 2))
            def _():
                column(step).start()
        return carry
    lax.fori_loop(0, 6, stages, 0)

    own_small.wait()
    total = s_own[...]
    for i in range(1, 8):
        there = row_at(row, i)
        remote(grad_s.at[there], s_rec.at[i - 1], s_ss.at[i - 1], s_rs.at[i - 1], {"row": there}).wait()
        total = total + s_rec[i - 1]
    s_mid[...] = total

    def small(step):
        there = (col + step) % 4
        return remote(s_mid.at[there], s_zrec.at[step - 1], sz_ss.at[step - 1], sz_rs.at[step - 1], {"col": there})

    for step in (1, 2, 3):
        small(step).start()
    for step in (1, 2, 3):
        small(step).wait()
    sum_s[...] = s_mid[col] + s_zrec[0] + s_zrec[1] + s_zrec[2]
    for step in (1, 2, 3):
        column(step).wait_recv()
    for start in range(0, block, 32):
        rows = pl.ds(start, 32)
        total = own[col, chip, rows, :].astype(jnp.float32)
        for step in range(3):
            total = total + rec_z[step, rows, :].astype(jnp.float32)
        sum_a[rows, :] = total[:, :width_a]
        sum_b[rows, :] = total[:, width_a:]
    for step in (1, 2, 3):
        column(step).wait_send()

    def sent(c, carry):
        for q in range(4):
            pa, pb = parts(c, q, 1 - core)
            remote(pa, rec_sib.at[c, q, :, pl.ds(0, width_a)], ss1.at[c, q, 0], rs1.at[c, q, 0], sib).wait_send()
            remote(pb, rec_sib.at[c, q, :, pl.ds(width_a, width_b)], ss1.at[c, q, 1], rs1.at[c, q, 1], sib).wait_send()
        for copy in one(c):
            copy.wait_send()
        for copy in two(c):
            copy.wait_send()
        return carry
    lax.fori_loop(0, 4, sent, 0)


def reduce_attention(grad_a, grad_b, grad_s):
    sems = pltpu.SemaphoreType.DMA
    block = grad_a.shape[0] // 8
    width_a, width_b = grad_a.shape[1] // 4, grad_b.shape[1] // 4
    width = width_a + width_b
    cut = block // 2
    low = grad_a.dtype
    vm = pl.BlockSpec(memory_space=pltpu.VMEM)
    small = grad_s.shape[1:]
    return pl.pallas_call(
        reduce_kernel,
        out_shape=(
            jax.ShapeDtypeStruct((block, width_a), jnp.float32),
            jax.ShapeDtypeStruct((block, width_b), jnp.float32),
            jax.ShapeDtypeStruct(small[1:], jnp.float32),
        ),
        in_specs=[ANY] * 3,
        out_specs=(vm,) * 3,
        scratch_shapes=[
            pltpu.VMEM((4, 4, block, width), low),
            pltpu.VMEM((4, 4, block, width), low),
            pltpu.VMEM((4, 2, 2, cut, width), low),
            pltpu.VMEM((4, 2, cut, width), low),
            pltpu.VMEM((3, block, width), low),
            pltpu.VMEM(small, jnp.float32),
            pltpu.VMEM((7,) + small, jnp.float32),
            pltpu.VMEM(small, jnp.float32),
            pltpu.VMEM((3,) + small[1:], jnp.float32),
            sems((4, 4, 2)), sems((1,)),
            sems((4, 4, 2)), sems((4, 4, 2)),
            sems((4, 2, 3)), sems((4, 2, 3)),
            sems((3,)), sems((3,)), sems((1,)),
            sems((7,)), sems((7,)), sems((3,)), sems((3,)),
        ],
        compiler_params=pltpu.CompilerParams(
            collective_id=2, has_side_effects=True, vmem_limit_bytes=48 * 2**20
        ),
        cost_estimate=pl.CostEstimate(flops=0, bytes_accessed=250_000_000, transcendentals=0),
    )(grad_a, grad_b, grad_s)


def rms_factor(rows_in):
    return lax.rsqrt(jnp.mean(rows_in * rows_in, axis=1, keepdims=True) + EPSILON)


def dot(a, b):
    return jnp.dot(a, b, preferred_element_type=jnp.float32)


def dot_t(a, b):
    return lax.dot_general(a, b, (((1,), (1,)), ((), ())), preferred_element_type=jnp.float32)


def t_dot(a, b):
    return lax.dot_general(a, b, (((0,), (0,)), ((), ())), preferred_element_type=jnp.float32)


def on_small_slice():
    return lax.axis_size("row") == 8 and lax.axis_size("col") == 4


def gather_all(own_a, own_b, own_s, own_c):
    if on_small_slice():
        return gather_attention(own_a, own_b, own_s, own_c)
    col_a = lax.all_gather(own_a, "col", axis=1, tiled=True)
    col_b = lax.all_gather(own_b, "col", axis=1, tiled=True)
    small = lax.all_gather(lax.all_gather(own_s, "col", axis=0), "row", axis=1)
    return (
        lax.all_gather(col_a, "row", axis=0, tiled=True),
        lax.all_gather(col_b, "row", axis=0, tiled=True),
        small,
        lax.all_gather(own_c, "row", axis=0, tiled=True),
    )


def spread(own_c, own_g):
    if on_small_slice():
        return spread_tokens(own_c, own_g)
    return (
        lax.all_gather(own_c, "row", axis=0, tiled=True),
        lax.all_gather(own_g, "row", axis=0),
    )


def reduce_all(grad_a, grad_b, grad_s):
    if on_small_slice():
        return reduce_attention(grad_a, grad_b, grad_s)

    def both(g):
        plane = lax.psum_scatter(g, "row", scatter_dimension=0, tiled=True).astype(jnp.float32)
        return lax.psum_scatter(plane, "col", scatter_dimension=1, tiled=True)

    small = lax.psum_scatter(grad_s, "row", scatter_dimension=0, tiled=False)
    return both(grad_a), both(grad_b), lax.psum_scatter(small, "col", scatter_dimension=0, tiled=False)


def masked_scores(queries, heads_of_key, segments, head_scale):
    length = queries.shape[0]
    heads_of_query = queries.reshape(length, KEY_VALUE_HEADS, QUERY_PER_KEY, HEAD_SIZE)
    scores = (
        jnp.einsum("qkgd,skd->kgqs", heads_of_query, heads_of_key, preferred_element_type=jnp.float32)
        * head_scale
    )
    pos = jnp.arange(length, dtype=jnp.int32)
    allowed = (pos[None, :] <= pos[:, None]) & (segments[None, :] == segments[:, None])
    return jnp.where(allowed, scores, NEGATIVE), heads_of_query


def per_device(
    tokens,
    attn_gain,
    w_query,
    w_key,
    w_value,
    w_out,
    expert_gain,
    router,
    w_gate,
    w_up,
    w_down,
    segment_ids,
    expert_ids,
    cotangent,
):
    length, model = tokens.shape
    rows, cols = lax.axis_size("row"), lax.axis_size("col")
    experts = w_gate.shape[0] * rows
    capacity = 2 * length * TOP // experts
    head_scale = HEAD_SIZE ** (-0.5)
    segments = segment_ids.reshape(-1)
    block, width_q = w_query.shape
    width_k = w_key.shape[1]
    width_a = width_q + 2 * width_k
    piece = attn_gain.shape[0]
    router_cols = router.shape[1]

    full_gate = lax.all_gather(w_gate, "col", axis=1, tiled=True)[0]
    full_up = lax.all_gather(w_up, "col", axis=1, tiled=True)[0]
    full_down = lax.all_gather(w_down, "col", axis=1, tiled=True)[0]

    lane = 256

    def row_of(v):
        return jnp.pad(v, ((0, 0), (0, lane - v.shape[1])))

    own_s = jnp.concatenate(
        [row_of(router.T), row_of(attn_gain[None]), row_of(expert_gain[None])], axis=0
    )
    own_s = jnp.pad(own_s, ((0, 16 - own_s.shape[0]), (0, 0)))
    own_a = jnp.concatenate([w_query, w_key, w_value], axis=1)
    full_a, full_out, small, plane_upstream = gather_all(own_a, w_out, own_s, cotangent)
    full_router = small[:, :, :router_cols, :block].transpose(1, 3, 0, 2).reshape(model, experts)
    gain_one = small[:, :, router_cols, :piece].transpose(1, 0, 2).reshape(model).astype(jnp.float32)
    gain_two = small[:, :, router_cols + 1, :piece].transpose(1, 0, 2).reshape(model).astype(jnp.float32)

    rows_f = tokens.astype(jnp.float32)
    factor_one = rms_factor(rows_f)
    normed = (rows_f * factor_one * gain_one).astype(jnp.bfloat16)
    qkv = dot(normed, full_a).astype(jnp.bfloat16).reshape(length, cols, width_a)
    query_rows = qkv[:, :, :width_q].reshape(length, -1)
    rows_of_key = qkv[:, :, width_q : width_q + width_k].reshape(length, -1)
    rows_of_value = qkv[:, :, width_q + width_k :].reshape(length, -1)
    heads_of_key = rows_of_key.reshape(length, KEY_VALUE_HEADS, HEAD_SIZE)
    heads_of_value = rows_of_value.reshape(length, KEY_VALUE_HEADS, HEAD_SIZE)

    scores, heads_of_query = masked_scores(query_rows, heads_of_key, segments, head_scale)
    row_max = jnp.max(scores, axis=-1, keepdims=True)
    expo_rows = jnp.exp(scores - row_max)
    totals = jnp.sum(expo_rows, axis=-1, keepdims=True)
    soft_probs = expo_rows / totals
    probs_low = soft_probs.astype(jnp.bfloat16)
    attended = (
        jnp.einsum("kgqs,skd->qkgd", probs_low, heads_of_value, preferred_element_type=jnp.float32)
        .reshape(length, -1)
        .astype(jnp.bfloat16)
    )
    hidden = rows_f + dot(attended, full_out)
    factor_two = rms_factor(hidden)
    normed_two = (hidden * factor_two * gain_two).astype(jnp.bfloat16)
    logits = dot(normed_two, full_router)

    named = expert_ids[:, :, None] == jnp.arange(experts, dtype=jnp.int32)[None, None, :]
    chosen = jnp.sum(jnp.where(named, logits[:, None, :], 0.0), axis=2)
    gate_probs = jax.nn.softmax(chosen, axis=1)
    gate_table = jnp.sum(jnp.where(named, gate_probs[:, :, None], 0.0), axis=1)
    gate_table = jnp.where(jnp.any(named, axis=1), gate_table, -1.0)
    plane_normed, plane_gate = spread(normed_two, gate_table.T)
    plane_normed = plane_normed.reshape(rows, length, model)
    plane_upstream = plane_upstream.reshape(rows, length, model)
    mine = lax.dynamic_index_in_dim(plane_gate, lax.axis_index("row"), axis=1, keepdims=False)
    routed = mine >= 0.0
    place = jnp.cumsum(routed.astype(jnp.int32), axis=1) - 1
    slots = jnp.arange(capacity, dtype=jnp.int32)
    chosen_rows = (
        (place[:, None, :] == slots[None, :, None]) & routed[:, None, :]
    ).astype(jnp.bfloat16)
    grouped = jnp.einsum(
        "rct,rtd->rcd", chosen_rows, plane_normed, preferred_element_type=jnp.float32
    ).astype(jnp.bfloat16).reshape(rows * capacity, model)
    weighted = (plane_upstream.astype(jnp.float32) * mine[:, :, None]).astype(jnp.bfloat16)
    grouped_grad = jnp.einsum(
        "rct,rtd->rcd", chosen_rows, weighted, preferred_element_type=jnp.float32
    ).astype(jnp.bfloat16).reshape(rows * capacity, model)

    gate_pre = dot(grouped, full_gate)
    up_pre = dot(grouped, full_up)
    sigma = jax.nn.sigmoid(gate_pre)
    silu_gate = gate_pre * sigma
    activation = (silu_gate * up_pre).astype(jnp.bfloat16)
    grad_down_local = t_dot(activation, grouped_grad).astype(jnp.bfloat16)
    grad_down = lax.psum_scatter(grad_down_local, "col", scatter_dimension=0, tiled=True)
    produced = dot(activation, full_down).astype(jnp.bfloat16)
    back_rows = lax.all_to_all(
        produced.reshape(rows, capacity, model), "row", split_axis=0, concat_axis=0, tiled=True
    ).reshape(experts * capacity, model)
    act_grad = dot_t(grouped_grad, full_down)
    up_grad = (act_grad * silu_gate).astype(jnp.bfloat16)
    pre_grad = (act_grad * up_pre * sigma * (1.0 + gate_pre * (1.0 - sigma))).astype(jnp.bfloat16)
    in_grad = (dot_t(pre_grad, full_gate) + dot_t(up_grad, full_up)).astype(jnp.bfloat16)
    back_grad = lax.all_to_all(
        in_grad.reshape(rows, capacity, model), "row", split_axis=0, concat_axis=0, tiled=True
    ).reshape(experts * capacity, model)
    grad_gate_local = t_dot(grouped, pre_grad).astype(jnp.bfloat16)
    grad_gate = lax.psum_scatter(grad_gate_local, "col", scatter_dimension=0, tiled=True)
    grad_up_local = t_dot(grouped, up_grad).astype(jnp.bfloat16)
    grad_up = lax.psum_scatter(grad_up_local, "col", scatter_dimension=0, tiled=True)

    any_named = jnp.any(named, axis=1)
    before = jnp.cumsum(any_named.astype(jnp.int32), axis=0) - 1
    slot_of = jnp.sum(
        jnp.where(named, before[:, None, :] + jnp.arange(experts, dtype=jnp.int32) * capacity, 0),
        axis=2,
    )
    all_slots = jnp.arange(experts * capacity, dtype=jnp.int32)
    from_slot = (slot_of.T[:, :, None] == all_slots[None, None, :]).astype(jnp.bfloat16)
    returned = [dot(from_slot[k], back_rows) for k in range(TOP)]
    upstream = cotangent.astype(jnp.float32)
    output = (
        hidden + sum(returned[k] * gate_probs[:, k : k + 1] for k in range(TOP))
    ).astype(jnp.bfloat16)
    gate_grad = jnp.stack([jnp.sum(returned[k] * upstream, axis=1) for k in range(TOP)], axis=1)
    normed_two_grad = dot(from_slot[0] + from_slot[1], back_grad)
    pair_mean = jnp.sum(gate_probs * gate_grad, axis=1, keepdims=True)
    pair_logit = gate_probs * (gate_grad - pair_mean)
    logit_grad = jnp.sum(jnp.where(named, pair_logit[:, :, None], 0.0), axis=1).astype(jnp.bfloat16)
    grad_router = t_dot(normed_two, logit_grad)
    normed_two_grad = normed_two_grad + dot_t(logit_grad, full_router)
    grad_expert_gain = jnp.sum(normed_two_grad * hidden * factor_two, axis=0)
    scaled_two = normed_two_grad * gain_two
    hidden_grad = (
        upstream
        + factor_two * scaled_two
        - hidden * factor_two**3 * jnp.mean(scaled_two * hidden, axis=1, keepdims=True)
    )
    branch_grad = hidden_grad.astype(jnp.bfloat16)
    grad_out_full = t_dot(attended, branch_grad).astype(jnp.bfloat16)
    attended_grad = dot_t(branch_grad, full_out).astype(jnp.bfloat16)

    gradient_heads = attended_grad.reshape(length, KEY_VALUE_HEADS, QUERY_PER_KEY, HEAD_SIZE)
    value_grad = jnp.einsum(
        "kgqs,qkgd->skd", probs_low, gradient_heads, preferred_element_type=jnp.float32
    )
    prob_grad = jnp.einsum(
        "qkgd,skd->kgqs", gradient_heads, heads_of_value, preferred_element_type=jnp.float32
    )
    delta_sum = jnp.sum(soft_probs * prob_grad, axis=-1, keepdims=True)
    score_grad = (soft_probs * (prob_grad - delta_sum)).astype(jnp.bfloat16)
    query_grad = (
        jnp.einsum("kgqs,skd->qkgd", score_grad, heads_of_key, preferred_element_type=jnp.float32)
        * head_scale
    )
    key_grad = (
        jnp.einsum("kgqs,qkgd->skd", score_grad, heads_of_query, preferred_element_type=jnp.float32)
        * head_scale
    )
    qkv_grad = jnp.concatenate(
        [
            query_grad.astype(jnp.bfloat16).reshape(length, cols, width_q),
            key_grad.astype(jnp.bfloat16).reshape(length, cols, width_k),
            value_grad.astype(jnp.bfloat16).reshape(length, cols, width_k),
        ],
        axis=2,
    ).reshape(length, cols * width_a)
    grad_a_full = t_dot(normed, qkv_grad).astype(jnp.bfloat16)
    normed_grad = dot_t(qkv_grad, full_a)
    grad_attn_gain = jnp.sum(normed_grad * rows_f * factor_one, axis=0)
    scaled_one = normed_grad * gain_one
    d_tokens = (
        hidden_grad
        + factor_one * scaled_one
        - rows_f * factor_one**3 * jnp.mean(scaled_one * rows_f, axis=1, keepdims=True)
    )
    grad_s = jnp.concatenate(
        [
            jnp.pad(
                grad_router.reshape(rows, block, cols, router_cols).transpose(0, 2, 3, 1),
                ((0, 0), (0, 0), (0, 0), (0, lane - block)),
            ),
            jnp.pad(
                jnp.stack([grad_attn_gain, grad_expert_gain])
                .reshape(2, rows, cols, piece)
                .transpose(1, 2, 0, 3),
                ((0, 0), (0, 0), (0, 6 - router_cols), (0, lane - piece)),
            ),
        ],
        axis=2,
    )
    sum_a, sum_out, sum_s = reduce_all(grad_a_full, grad_out_full, grad_s)
    return (
        output,
        d_tokens,
        sum_s[router_cols, :piece],
        sum_a[:, :width_q],
        sum_a[:, width_q : width_q + width_k],
        sum_a[:, width_q + width_k :],
        sum_out,
        sum_s[router_cols + 1, :piece],
        sum_s[:router_cols, :block].T,
        grad_gate.astype(jnp.float32)[None],
        grad_up.astype(jnp.float32)[None],
        grad_down.astype(jnp.float32)[None],
    )


def solution(mesh):
    in_specs = (
        P(("row", "col"), None),
        P(("row", "col")),
        P("row", "col"),
        P("row", "col"),
        P("row", "col"),
        P("row", "col"),
        P(("row", "col")),
        P("row", "col"),
        P("row", "col", None),
        P("row", "col", None),
        P("row", "col", None),
        P(("row", "col"), None),
        P(("row", "col"), None),
        P(("row", "col"), None),
    )
    out_specs = (
        P(("row", "col"), None),
        P(("row", "col"), None),
        P(("row", "col")),
        P("row", "col"),
        P("row", "col"),
        P("row", "col"),
        P("row", "col"),
        P(("row", "col")),
        P("row", "col"),
        P("row", "col", None),
        P("row", "col", None),
        P("row", "col", None),
    )
    return jax.shard_map(
        per_device, mesh=mesh, in_specs=in_specs, out_specs=out_specs, check_vma=False
    )
```

```python
import functools

import jax
import jax.numpy as jnp
from jax import lax
from jax.experimental import pallas as pl
from jax.experimental.pallas import tpu as pltpu
from jax.sharding import PartitionSpec as P

KEY_VALUE_HEADS = 8
HEAD_SIZE = 64
TOP = 2
QUERY_PER_KEY = 3


EPSILON = 1e-05
NEGATIVE = -1e30


MESH = pl.DeviceIdType.MESH
ANY = pl.BlockSpec(memory_space=pl.ANY)


def row_at(row, flip):
    y, x, core = row // 4, (row // 2) % 2, row % 2
    return (
        (y + flip // 4) % 2 * 4 + (x + (flip // 2) % 2) % 2 * 2 + (core + flip % 2) % 2
    )


def remote(source, target, send, receive, device):
    return pltpu.make_async_remote_copy(
        source, target, send, receive, device_id=device, device_id_type=MESH
    )


def greet(row_flips, col_steps):
    row, col = lax.axis_index("row"), lax.axis_index("col")
    sem = pltpu.get_barrier_semaphore()
    for flip in row_flips:
        pl.semaphore_signal(
            sem, inc=1, device_id={"row": row_at(row, flip)}, device_id_type=MESH
        )
    for step in col_steps:
        pl.semaphore_signal(
            sem, inc=1, device_id={"col": (col + step) % 4}, device_id_type=MESH
        )
    pl.semaphore_wait(sem, len(row_flips) + len(col_steps))


def unit_order(col, k):
    table = ((0, 1, 2, 3), (1, 0, 2, 3), (2, 3, 1, 0), (3, 2, 1, 0))
    out = table[3][k]
    for c in (2, 1, 0):
        out = jnp.where(col == c, table[c][k], out)
    return out


X, Y, SIB = 2, 4, 1


def plane_send(view, row, ss, rs, source=None):
    source = view(row) if source is None else source
    for i, flip in enumerate((X, Y, SIB)):
        remote(source, view(row), ss(i), rs(i), {"row": row_at(row, flip)}).start()


def plane_forward(view, halves, row, ss, rs):
    first, second = halves
    from_x, from_y = row_at(row, X), row_at(row, Y)
    sib = {"row": row_at(row, SIB)}
    remote(view(from_x), view(from_x), ss(0), rs(0), sib).wait_recv()
    remote(first(from_x), first(from_x), ss(3), rs(3), {"row": from_y}).start()
    remote(view(from_x), view(from_x), ss(5), rs(5), sib).start()
    remote(view(from_y), view(from_y), ss(1), rs(1), sib).wait_recv()
    remote(second(from_y), second(from_y), ss(4), rs(4), {"row": from_x}).start()
    remote(view(from_y), view(from_y), ss(6), rs(6), sib).start()


def plane_last(view, halves, row, ss, rs):
    first, second = halves
    diag = row_at(row, X + Y)
    sib = {"row": row_at(row, SIB)}
    remote(first(diag), first(diag), ss(3), rs(3), sib).wait_recv()
    remote(first(diag), first(diag), ss(7), rs(7), sib).start()
    remote(second(diag), second(diag), ss(4), rs(4), sib).wait_recv()
    remote(second(diag), second(diag), ss(8), rs(8), sib).start()


def plane_finish(view, halves, row, ss, rs):
    first, second = halves
    sib_row = row_at(row, SIB)
    sib = {"row": sib_row}
    whole = view(sib_row)
    remote(whole, whole, ss(2), rs(2), sib).wait_recv()
    for i, flip in ((5, X), (6, Y)):
        block = view(row_at(sib_row, flip))
        remote(block, block, ss(i), rs(i), sib).wait_recv()
    far = row_at(sib_row, X + Y)
    remote(first(far), first(far), ss(7), rs(7), sib).wait_recv()
    remote(second(far), second(far), ss(8), rs(8), sib).wait_recv()
    for i in range(9):
        block = view(row) if i in (0, 1, 2, 5, 6) else (first(row) if i in (3, 7) else second(row))
        remote(block, block, ss(i), rs(i), sib).wait_send()


def pick(ref, cols, halves_rows):
    block, cut = halves_rows

    def at(start, size):
        def view(r):
            rows = pl.ds(pl.multiple_of(r * block + start, 16), size)
            if cols is None:
                return ref.at[rows, :]
            return ref.at[rows, pl.ds(pl.multiple_of(cols[0], 128), cols[1])]

        return view

    return at(0, block), (at(0, cut), at(cut, block - cut))


def through(source, middle, target, sem):
    return pltpu.make_async_copy(source, middle, sem), pltpu.make_async_copy(middle, target, sem)


def through(source, middle, target, sem):
    return pltpu.make_async_copy(source, middle, sem), pltpu.make_async_copy(middle, target, sem)


def line_kernel(own_a, own_b, own_s, own_c, line_a, line_b, full_s, full_c, mid_a, mid_b, mid_c,
                zss, zrs, css, crs, s_zs, s_zr, s_ps, s_pr, loc):
    row, col = lax.axis_index("row"), lax.axis_index("col")
    width_a, width_b = own_a.shape[1], own_b.shape[1]
    rows_c = own_c.shape[0]
    vc, hc = pick(full_c, None, (rows_c, rows_c // 2))
    csv, crv = (lambda i: css.at[i]), (lambda i: crs.at[i])

    def of_a(c):
        return line_a.at[:, pl.ds(pl.multiple_of(c * width_a, 128), width_a)]

    def of_b(c):
        return line_b.at[:, pl.ds(pl.multiple_of(c * width_b, 128), width_b)]

    copies = [
        through(own_a, mid_a, of_a(col), loc.at[0]),
        through(own_b, mid_b, of_b(col), loc.at[1]),
        through(own_c, mid_c, vc(row), loc.at[2]),
    ]
    for copy, _ in copies:
        copy.start()
    small_copy = pltpu.make_async_copy(own_s, full_s.at[col, row], loc.at[3])
    small_copy.start()
    greet(range(1, 8), (1, 2, 3))

    def along(c, source_a, source_b, right, left):
        for d, (cond, step) in enumerate(((right, 1), (left, 3))):
            @pl.when(cond)
            def _():
                there = {"col": (col + step) % 4}
                remote(source_a, of_a(c), zss.at[0, c, d], zrs.at[0, c], there).start()
                remote(source_b, of_b(c), zss.at[1, c, d], zrs.at[1, c], there).start()

    def arrived(k):
        c = unit_order(col, k)
        there = {"col": (col + 1) % 4}
        remote(of_a(c), of_a(c), zss.at[0, c, 0], zrs.at[0, c], there).wait_recv()
        remote(of_b(c), of_b(c), zss.at[1, c, 0], zrs.at[1, c], there).wait_recv()
        along(c, of_a(c), of_b(c), (c < col) & (col < 3), (c > col) & (col > 0))

    along(col, own_a, own_b, col < 3, col > 0)
    for i, step in enumerate((1, 2, 3)):
        remote(own_s, full_s.at[col, row], s_zs.at[i], s_zr.at[i], {"col": (col + step) % 4}).start()
    plane_send(vc, row, csv, crv, own_c)
    for first, second in copies:
        first.wait()
        second.start()
    small_copy.wait()
    arrived(1)
    for i, step in enumerate((3, 2, 1)):
        remote(own_s, full_s.at[(col + step) % 4, row], s_zs.at[i], s_zr.at[i], {"col": (col + 1) % 4}).wait()
    for i in range(1, 8):
        remote(full_s.at[:, row], full_s.at[:, row], s_ps.at[i - 1], s_pr.at[i - 1], {"row": row_at(row, i)}).start()
    arrived(2)
    plane_forward(vc, hc, row, csv, crv)
    arrived(3)
    plane_last(vc, hc, row, csv, crv)
    for _, second in copies:
        second.wait()
    plane_finish(vc, hc, row, csv, crv)
    for i in range(1, 8):
        there = row_at(row, i)
        remote(full_s.at[:, there], full_s.at[:, there], s_ps.at[i - 1], s_pr.at[i - 1], {"row": there}).wait()
    for k in range(4):
        c = unit_order(col, k)
        right = (c <= col) & (col < 3)
        left = (c >= col) & (col > 0)
        for d, cond in enumerate((right, left)):
            @pl.when(cond)
            def _():
                there = {"col": (col + 1) % 4}
                remote(of_a(c), of_a(c), zss.at[0, c, d], zrs.at[0, c], there).wait_send()
                remote(of_b(c), of_b(c), zss.at[1, c, d], zrs.at[1, c], there).wait_send()


def gather_line(own_a, own_b, own_s, own_c):
    sems = pltpu.SemaphoreType.DMA
    rows_c = own_c.shape[0]
    return pl.pallas_call(
        line_kernel,
        out_shape=(
            jax.ShapeDtypeStruct((own_a.shape[0], own_a.shape[1] * 4), own_a.dtype),
            jax.ShapeDtypeStruct((own_b.shape[0], own_b.shape[1] * 4), own_b.dtype),
            jax.ShapeDtypeStruct((4, 8) + own_s.shape, own_s.dtype),
            jax.ShapeDtypeStruct((8 * rows_c, own_c.shape[1]), own_c.dtype),
        ),
        in_specs=[ANY] * 4,
        out_specs=(ANY,) * 4,
        scratch_shapes=[
            pltpu.VMEM(own_a.shape, own_a.dtype),
            pltpu.VMEM(own_b.shape, own_b.dtype),
            pltpu.VMEM(own_c.shape, own_c.dtype),
            sems((2, 4, 2)), sems((2, 4)),
            sems((9,)), sems((9,)),
            sems((3,)), sems((3,)), sems((7,)), sems((7,)), sems((4,)),
        ],
        compiler_params=pltpu.CompilerParams(collective_id=0, has_side_effects=True),
        cost_estimate=pl.CostEstimate(flops=0, bytes_accessed=1_000_000, transcendentals=0),
    )(own_a, own_b, own_s, own_c)


def plane_kernel(count, *refs):
    row = lax.axis_index("row")
    owns, fulls, mids = refs[:count], refs[count : 2 * count], refs[2 * count : 3 * count]
    ss, rs, loc = refs[3 * count :]
    views, copies = [], []
    for i in range(count):
        block = owns[i].shape[0]
        views.append(pick(fulls[i], None, (block, block // 2)))
        copies.append(through(owns[i], mids[i], views[i][0](row), loc.at[i]))
        copies[i][0].start()
    greet(range(1, 8), ())

    def sems_of(i):
        return (lambda j: ss.at[i, j]), (lambda j: rs.at[i, j])

    for i in range(count):
        plane_send(views[i][0], row, *sems_of(i), owns[i])
    for first, second in copies:
        first.wait()
        second.start()
    for i in range(count):
        plane_forward(*views[i], row, *sems_of(i))
    for i in range(count):
        plane_last(*views[i], row, *sems_of(i))
    for _, second in copies:
        second.wait()
    for i in range(count):
        plane_finish(*views[i], row, *sems_of(i))


def gather_plane(collective, owns):
    sems = pltpu.SemaphoreType.DMA
    count = len(owns)
    return pl.pallas_call(
        functools.partial(plane_kernel, count),
        out_shape=tuple(
            jax.ShapeDtypeStruct((8 * own.shape[0], own.shape[1]), own.dtype) for own in owns
        ),
        in_specs=[ANY] * count,
        out_specs=(ANY,) * count,
        scratch_shapes=[pltpu.VMEM(own.shape, own.dtype) for own in owns]
        + [sems((count, 9)), sems((count, 9)), sems((count,))],
        compiler_params=pltpu.CompilerParams(collective_id=collective, has_side_effects=True),
        cost_estimate=pl.CostEstimate(flops=0, bytes_accessed=1_000_000, transcendentals=0),
    )(*owns)


def spread_kernel(own_c, own_g, full_c, full_g, mid_c, css, crs, gss, grs, loc):
    row = lax.axis_index("row")
    rows_c = own_c.shape[0]
    vc, hc = pick(full_c, None, (rows_c, rows_c // 2))
    csv, crv = (lambda i: css.at[i]), (lambda i: crs.at[i])
    first, second = through(own_c, mid_c, vc(row), loc.at[0])
    first.start()
    own_copy = pltpu.make_async_copy(own_g, full_g.at[row], loc.at[1])
    own_copy.start()
    greet(range(1, 8), ())
    plane_send(vc, row, csv, crv, own_c)
    for i in range(1, 8):
        remote(own_g, full_g.at[row], gss.at[i - 1], grs.at[i - 1], {"row": row_at(row, i)}).start()
    first.wait()
    second.start()
    plane_forward(vc, hc, row, csv, crv)
    plane_last(vc, hc, row, csv, crv)
    second.wait()
    own_copy.wait()
    plane_finish(vc, hc, row, csv, crv)
    for i in range(1, 8):
        there = row_at(row, i)
        remote(own_g, full_g.at[there], gss.at[i - 1], grs.at[i - 1], {"row": there}).wait()


def spread_tokens(own_c, own_g):
    sems = pltpu.SemaphoreType.DMA
    return pl.pallas_call(
        spread_kernel,
        out_shape=(
            jax.ShapeDtypeStruct((8 * own_c.shape[0], own_c.shape[1]), own_c.dtype),
            jax.ShapeDtypeStruct((8,) + own_g.shape, own_g.dtype),
        ),
        in_specs=[ANY] * 2,
        out_specs=(ANY,) * 2,
        scratch_shapes=[
            pltpu.VMEM(own_c.shape, own_c.dtype),
            sems((9,)), sems((9,)), sems((7,)), sems((7,)), sems((2,)),
        ],
        compiler_params=pltpu.CompilerParams(collective_id=1, has_side_effects=True),
        cost_estimate=pl.CostEstimate(flops=0, bytes_accessed=1_000_000, transcendentals=0),
    )(own_c, own_g)


def add_into(target, term):
    target[...] = (target[...].astype(jnp.float32) + term[...].astype(jnp.float32)).astype(target.dtype)


def reduce_kernel(grad_a, grad_b, grad_s, sum_a, sum_b, sum_s,
                  own, rec_sib, rec_one, rec_two, rec_z, s_own, s_rec, s_mid, s_zrec,
                  lss, lrs, ss1, rs1, ss2, rs2, zss, zrs, lo, s_ss, s_rs, sz_ss, sz_rs):
    row, col = lax.axis_index("row"), lax.axis_index("col")
    core = row % 2
    chip = row // 2
    cy, cx = chip // 2, chip % 2
    block, width = own.shape[2], own.shape[3]
    width_a = sum_a.shape[1]
    width_b = width - width_a
    cut = block // 2
    greet(range(1, 8), (1, 2, 3))
    sib = {"row": row_at(row, SIB)}
    to_x, to_y = {"row": row_at(row, X)}, {"row": row_at(row, Y)}

    def parts(c, q, of_core):
        rows = pl.ds(pl.multiple_of((q * 2 + of_core) * block, 16), block)
        return (
            grad_a.at[rows, pl.ds(pl.multiple_of(c * width_a, 128), width_a)],
            grad_b.at[rows, pl.ds(pl.multiple_of(c * width_b, 128), width_b)],
        )

    for i in range(1, 8):
        there = row_at(row, i)
        remote(grad_s.at[there], s_rec.at[i - 1], s_ss.at[i - 1], s_rs.at[i - 1], {"row": there}).start()
    def start_first(k, carry):
        c = (col + 1 + k) % 4
        for q in range(4):
            pa, pb = parts(c, q, 1 - core)
            remote(pa, rec_sib.at[c, q, :, pl.ds(0, width_a)], ss1.at[c, q, 0], rs1.at[c, q, 0], sib).start()
            remote(pb, rec_sib.at[c, q, :, pl.ds(width_a, width_b)], ss1.at[c, q, 1], rs1.at[c, q, 1], sib).start()
            pa, pb = parts(c, q, core)
            pltpu.make_async_copy(pa, own.at[c, q, :, pl.ds(0, width_a)], lss.at[c, q, 0]).start()
            pltpu.make_async_copy(pb, own.at[c, q, :, pl.ds(width_a, width_b)], lss.at[c, q, 1]).start()
        return carry
    lax.fori_loop(0, 4, start_first, 0)
    own_small = pltpu.make_async_copy(grad_s.at[row], s_own, lo.at[0])
    own_small.start()

    def chip_sum(c):
        for q in range(4):
            pa, pb = parts(c, q, core)
            for i, (p, off, w) in enumerate(((pa, 0, width_a), (pb, width_a, width_b))):
                pltpu.make_async_copy(p, own.at[c, q, :, pl.ds(off, w)], lss.at[c, q, i]).wait()
                remote(p, rec_sib.at[c, q, :, pl.ds(off, w)], ss1.at[c, q, i], rs1.at[c, q, i], sib).wait_recv()
            add_into(own.at[c, q], rec_sib.at[c, q])

    top, low = pl.ds(0, cut), pl.ds(cut, block - cut)

    def one(c):
        for j in range(2):
            yield remote(own.at[c, j * 2 + 1 - cx, top, :], rec_one.at[c, 0, j], ss2.at[c, 0, j], rs2.at[c, 0, j], to_x)
            yield remote(own.at[c, (1 - cy) * 2 + j, low, :], rec_one.at[c, 1, j], ss2.at[c, 1, j], rs2.at[c, 1, j], to_y)

    def one_sum(c):
        for copy in one(c):
            copy.wait_recv()
        for j in range(2):
            add_into(own.at[c, j * 2 + cx, top, :], rec_one.at[c, 0, j])
            add_into(own.at[c, cy * 2 + j, low, :], rec_one.at[c, 1, j])

    def two(c):
        yield remote(own.at[c, (1 - cy) * 2 + cx, top, :], rec_two.at[c, 0], ss2.at[c, 0, 2], rs2.at[c, 0, 2], to_y)
        yield remote(own.at[c, cy * 2 + 1 - cx, low, :], rec_two.at[c, 1], ss2.at[c, 1, 2], rs2.at[c, 1, 2], to_x)

    def two_sum(c):
        for copy in two(c):
            copy.wait_recv()
        add_into(own.at[c, chip, top, :], rec_two.at[c, 0])
        add_into(own.at[c, chip, low, :], rec_two.at[c, 1])

    def column(step):
        there = (col + step) % 4
        return remote(own.at[there, chip], rec_z.at[step - 1], zss.at[step - 1], zrs.at[step - 1], {"col": there})

    def nth(k):
        return (col + 1 + k) % 4

    def stages(k, carry):
        @pl.when(k < 4)
        def _():
            chip_sum(nth(k))
            for copy in one(nth(k)):
                copy.start()
        @pl.when((k >= 1) & (k < 5))
        def _():
            one_sum(nth(k - 1))
            for copy in two(nth(k - 1)):
                copy.start()
        @pl.when(k >= 2)
        def _():
            two_sum(nth(k - 2))
        for step in (1, 2, 3):
            @pl.when(k == step + 1)
            def _():
                column(step).start()
        return carry
    lax.fori_loop(0, 6, stages, 0)

    own_small.wait()
    total = s_own[...]
    for i in range(1, 8):
        there = row_at(row, i)
        remote(grad_s.at[there], s_rec.at[i - 1], s_ss.at[i - 1], s_rs.at[i - 1], {"row": there}).wait()
        total = total + s_rec[i - 1]
    s_mid[...] = total

    def small(step):
        there = (col + step) % 4
        return remote(s_mid.at[there], s_zrec.at[step - 1], sz_ss.at[step - 1], sz_rs.at[step - 1], {"col": there})

    for step in (1, 2, 3):
        small(step).start()
    for step in (1, 2, 3):
        small(step).wait()
    sum_s[...] = s_mid[col] + s_zrec[0] + s_zrec[1] + s_zrec[2]
    for step in (1, 2, 3):
        column(step).wait_recv()
    for start in range(0, block, 32):
        rows = pl.ds(start, 32)
        total = own[col, chip, rows, :].astype(jnp.float32)
        for step in range(3):
            total = total + rec_z[step, rows, :].astype(jnp.float32)
        sum_a[rows, :] = total[:, :width_a]
        sum_b[rows, :] = total[:, width_a:]
    for step in (1, 2, 3):
        column(step).wait_send()

    def sent(c, carry):
        for q in range(4):
            pa, pb = parts(c, q, 1 - core)
            remote(pa, rec_sib.at[c, q, :, pl.ds(0, width_a)], ss1.at[c, q, 0], rs1.at[c, q, 0], sib).wait_send()
            remote(pb, rec_sib.at[c, q, :, pl.ds(width_a, width_b)], ss1.at[c, q, 1], rs1.at[c, q, 1], sib).wait_send()
        for copy in one(c):
            copy.wait_send()
        for copy in two(c):
            copy.wait_send()
        return carry
    lax.fori_loop(0, 4, sent, 0)


def reduce_attention(grad_a, grad_b, grad_s):
    sems = pltpu.SemaphoreType.DMA
    block = grad_a.shape[0] // 8
    width_a, width_b = grad_a.shape[1] // 4, grad_b.shape[1] // 4
    width = width_a + width_b
    cut = block // 2
    low = grad_a.dtype
    vm = pl.BlockSpec(memory_space=pltpu.VMEM)
    small = grad_s.shape[1:]
    return pl.pallas_call(
        reduce_kernel,
        out_shape=(
            jax.ShapeDtypeStruct((block, width_a), jnp.float32),
            jax.ShapeDtypeStruct((block, width_b), jnp.float32),
            jax.ShapeDtypeStruct(small[1:], jnp.float32),
        ),
        in_specs=[ANY] * 3,
        out_specs=(vm,) * 3,
        scratch_shapes=[
            pltpu.VMEM((4, 4, block, width), low),
            pltpu.VMEM((4, 4, block, width), low),
            pltpu.VMEM((4, 2, 2, cut, width), low),
            pltpu.VMEM((4, 2, cut, width), low),
            pltpu.VMEM((3, block, width), low),
            pltpu.VMEM(small, jnp.float32),
            pltpu.VMEM((7,) + small, jnp.float32),
            pltpu.VMEM(small, jnp.float32),
            pltpu.VMEM((3,) + small[1:], jnp.float32),
            sems((4, 4, 2)), sems((1,)),
            sems((4, 4, 2)), sems((4, 4, 2)),
            sems((4, 2, 3)), sems((4, 2, 3)),
            sems((3,)), sems((3,)), sems((1,)),
            sems((7,)), sems((7,)), sems((3,)), sems((3,)),
        ],
        compiler_params=pltpu.CompilerParams(
            collective_id=2, has_side_effects=True, vmem_limit_bytes=48 * 2**20
        ),
        cost_estimate=pl.CostEstimate(flops=0, bytes_accessed=1_000_000, transcendentals=0),
    )(grad_a, grad_b, grad_s)


def rms_factor(rows_in):
    return lax.rsqrt(jnp.mean(rows_in * rows_in, axis=1, keepdims=True) + EPSILON)


def dot(a, b):
    return jnp.dot(a, b, preferred_element_type=jnp.float32)


def dot_t(a, b):
    return lax.dot_general(a, b, (((1,), (1,)), ((), ())), preferred_element_type=jnp.float32)


def t_dot(a, b):
    return lax.dot_general(a, b, (((0,), (0,)), ((), ())), preferred_element_type=jnp.float32)


def on_small_slice():
    return lax.axis_size("row") == 8 and lax.axis_size("col") == 4


def gather_all(own_a, own_b, own_s, own_c):
    col_a = lax.all_gather(own_a, "col", axis=1, tiled=True)
    col_b = lax.all_gather(own_b, "col", axis=1, tiled=True)
    small = lax.all_gather(lax.all_gather(own_s, "col", axis=0), "row", axis=1)
    return (
        lax.all_gather(col_a, "row", axis=0, tiled=True),
        lax.all_gather(col_b, "row", axis=0, tiled=True),
        small,
        lax.all_gather(own_c, "row", axis=0, tiled=True),
    )


def spread(own_c, own_g):
    if on_small_slice():
        return spread_tokens(own_c, own_g)
    return (
        lax.all_gather(own_c, "row", axis=0, tiled=True),
        lax.all_gather(own_g, "row", axis=0),
    )


def reduce_all(grad_a, grad_b, grad_s):
    if on_small_slice():
        return reduce_attention(grad_a, grad_b, grad_s)

    def both(g):
        plane = lax.psum_scatter(g, "row", scatter_dimension=0, tiled=True).astype(jnp.float32)
        return lax.psum_scatter(plane, "col", scatter_dimension=1, tiled=True)

    small = lax.psum_scatter(grad_s, "row", scatter_dimension=0, tiled=False)
    return both(grad_a), both(grad_b), lax.psum_scatter(small, "col", scatter_dimension=0, tiled=False)


def masked_scores(queries, heads_of_key, segments, head_scale):
    length = queries.shape[0]
    heads_of_query = queries.reshape(length, KEY_VALUE_HEADS, QUERY_PER_KEY, HEAD_SIZE)
    scores = (
        jnp.einsum("qkgd,skd->kgqs", heads_of_query, heads_of_key, preferred_element_type=jnp.float32)
        * head_scale
    )
    pos = jnp.arange(length, dtype=jnp.int32)
    allowed = (pos[None, :] <= pos[:, None]) & (segments[None, :] == segments[:, None])
    return jnp.where(allowed, scores, NEGATIVE), heads_of_query


def per_device(
    tokens,
    attn_gain,
    w_query,
    w_key,
    w_value,
    w_out,
    expert_gain,
    router,
    w_gate,
    w_up,
    w_down,
    segment_ids,
    expert_ids,
    cotangent,
):
    length, model = tokens.shape
    rows, cols = lax.axis_size("row"), lax.axis_size("col")
    experts = w_gate.shape[0] * rows
    capacity = 2 * length * TOP // experts
    head_scale = HEAD_SIZE ** (-0.5)
    segments = segment_ids.reshape(-1)
    block, width_q = w_query.shape
    width_k = w_key.shape[1]
    width_a = width_q + 2 * width_k
    piece = attn_gain.shape[0]
    router_cols = router.shape[1]

    hidden_units = w_gate.shape[2]
    own_gu = jnp.concatenate([w_gate[0], w_up[0]], axis=1)
    own_down = w_down[0]

    lane = 256

    def row_of(v):
        return jnp.pad(v, ((0, 0), (0, lane - v.shape[1])))

    own_s = jnp.concatenate(
        [row_of(router.T), row_of(attn_gain[None]), row_of(expert_gain[None])], axis=0
    )
    own_s = jnp.pad(own_s, ((0, 16 - own_s.shape[0]), (0, 0)))
    own_a = jnp.concatenate([w_query, w_key, w_value], axis=1)
    if on_small_slice():
        line_a, line_out, small, plane_upstream = gather_line(own_a, w_out, own_s, cotangent)
        own_gu, own_down, line_a, line_out = lax.optimization_barrier(
            (own_gu, own_down, line_a, line_out)
        )
        full_a, full_out = gather_plane(3, (line_a, line_out))
    else:
        full_a, full_out, small, plane_upstream = gather_all(own_a, w_out, own_s, cotangent)
    full_gu = lax.all_gather(own_gu, "col", axis=0, tiled=True)
    full_down = lax.all_gather(own_down, "col", axis=0, tiled=True)
    full_router = small[:, :, :router_cols, :block].transpose(1, 3, 0, 2).reshape(model, experts)
    gain_one = small[:, :, router_cols, :piece].transpose(1, 0, 2).reshape(model).astype(jnp.float32)
    gain_two = small[:, :, router_cols + 1, :piece].transpose(1, 0, 2).reshape(model).astype(jnp.float32)

    rows_f = tokens.astype(jnp.float32)
    factor_one = rms_factor(rows_f)
    normed = (rows_f * factor_one * gain_one).astype(jnp.bfloat16)
    qkv = dot(normed, full_a).astype(jnp.bfloat16).reshape(length, cols, width_a)
    query_rows = qkv[:, :, :width_q].reshape(length, -1)
    rows_of_key = qkv[:, :, width_q : width_q + width_k].reshape(length, -1)
    rows_of_value = qkv[:, :, width_q + width_k :].reshape(length, -1)
    heads_of_key = rows_of_key.reshape(length, KEY_VALUE_HEADS, HEAD_SIZE)
    heads_of_value = rows_of_value.reshape(length, KEY_VALUE_HEADS, HEAD_SIZE)

    scores, heads_of_query = masked_scores(query_rows, heads_of_key, segments, head_scale)
    row_max = jnp.max(scores, axis=-1, keepdims=True)
    expo_rows = jnp.exp(scores - row_max)
    totals = jnp.sum(expo_rows, axis=-1, keepdims=True)
    soft_probs = expo_rows / totals
    probs_low = soft_probs.astype(jnp.bfloat16)
    attended = (
        jnp.einsum("kgqs,skd->qkgd", probs_low, heads_of_value, preferred_element_type=jnp.float32)
        .reshape(length, -1)
        .astype(jnp.bfloat16)
    )
    hidden = rows_f + dot(attended, full_out)
    factor_two = rms_factor(hidden)
    normed_two = (hidden * factor_two * gain_two).astype(jnp.bfloat16)
    logits = dot(normed_two, full_router)

    named = expert_ids[:, :, None] == jnp.arange(experts, dtype=jnp.int32)[None, None, :]
    chosen = jnp.sum(jnp.where(named, logits[:, None, :], 0.0), axis=2)
    gate_probs = jax.nn.softmax(chosen, axis=1)
    gate_table = jnp.sum(jnp.where(named, gate_probs[:, :, None], 0.0), axis=1)
    gate_table = jnp.where(jnp.any(named, axis=1), gate_table, -1.0)
    plane_normed, plane_gate = spread(normed_two, gate_table.T)
    plane_normed = plane_normed.reshape(rows, length, model)
    plane_upstream = plane_upstream.reshape(rows, length, model)
    mine = lax.dynamic_index_in_dim(plane_gate, lax.axis_index("row"), axis=1, keepdims=False)
    routed = mine >= 0.0
    place = jnp.cumsum(routed.astype(jnp.int32), axis=1) - 1
    slots = jnp.arange(capacity, dtype=jnp.int32)
    chosen_rows = (
        (place[:, None, :] == slots[None, :, None]) & routed[:, None, :]
    ).astype(jnp.bfloat16)
    grouped = jnp.einsum(
        "rct,rtd->rcd", chosen_rows, plane_normed, preferred_element_type=jnp.float32
    ).astype(jnp.bfloat16).reshape(rows * capacity, model)
    slot_gate = jnp.sum(
        jnp.where(chosen_rows > 0, mine[:, None, :], 0.0), axis=2
    ).reshape(rows * capacity, 1)
    grouped_up = jnp.einsum(
        "rct,rtd->rcd", chosen_rows, plane_upstream, preferred_element_type=jnp.float32
    ).reshape(rows * capacity, model)
    grouped_grad = (grouped_up * slot_gate).astype(jnp.bfloat16)

    both_pre = dot(grouped, full_gu)
    gate_pre, up_pre = both_pre[:, :hidden_units], both_pre[:, hidden_units:]
    sigma = jax.nn.sigmoid(gate_pre)
    silu_gate = gate_pre * sigma
    activation = (silu_gate * up_pre).astype(jnp.bfloat16)
    grad_down_local = t_dot(activation, grouped_grad).astype(jnp.bfloat16)
    grad_down = lax.psum_scatter(grad_down_local, "col", scatter_dimension=0, tiled=True)
    later_grad, _ = lax.optimization_barrier((grouped_grad, grad_down_local))
    act_grad = dot_t(later_grad, full_down)
    both_grad = jnp.concatenate(
        [
            (act_grad * up_pre * sigma * (1.0 + gate_pre * (1.0 - sigma))).astype(jnp.bfloat16),
            (act_grad * silu_gate).astype(jnp.bfloat16),
        ],
        axis=1,
    )
    in_grad = dot_t(both_grad, full_gu).astype(jnp.bfloat16)
    back_grad = lax.all_to_all(
        in_grad.reshape(rows, capacity, model), "row", split_axis=0, concat_axis=0, tiled=True
    ).reshape(experts * capacity, model)
    later_act, _ = lax.optimization_barrier((activation, in_grad))
    produced = dot(later_act, full_down).astype(jnp.bfloat16)
    slot_gate_grad = jnp.sum(produced.astype(jnp.float32) * grouped_up, axis=1)
    back_gate_grad = lax.all_to_all(
        slot_gate_grad.reshape(rows, 1, capacity), "row", split_axis=0, concat_axis=0, tiled=True
    ).reshape(experts * capacity)
    grad_gu_local = t_dot(grouped, both_grad).astype(jnp.bfloat16)
    grad_gu = lax.psum_scatter(grad_gu_local, "col", scatter_dimension=0, tiled=True)
    produced, back_grad = lax.optimization_barrier((produced, back_grad))
    back_rows = lax.all_to_all(
        produced.reshape(rows, capacity, model), "row", split_axis=0, concat_axis=0, tiled=True
    ).reshape(experts * capacity, model)

    any_named = jnp.any(named, axis=1)
    before = jnp.cumsum(any_named.astype(jnp.int32), axis=0) - 1
    slot_of = jnp.sum(
        jnp.where(named, before[:, None, :] + jnp.arange(experts, dtype=jnp.int32) * capacity, 0),
        axis=2,
    )
    all_slots = jnp.arange(experts * capacity, dtype=jnp.int32)
    is_slot = slot_of.T[:, :, None] == all_slots[None, None, :]
    from_slot = is_slot.astype(jnp.bfloat16)
    gate_grad = jnp.sum(jnp.where(is_slot, back_gate_grad[None, None, :], 0.0), axis=2).T
    returned = [dot(from_slot[k], back_rows) for k in range(TOP)]
    upstream = cotangent.astype(jnp.float32)
    output = (
        hidden + sum(returned[k] * gate_probs[:, k : k + 1] for k in range(TOP))
    ).astype(jnp.bfloat16)
    normed_two_grad = dot(from_slot[0] + from_slot[1], back_grad)
    pair_mean = jnp.sum(gate_probs * gate_grad, axis=1, keepdims=True)
    pair_logit = gate_probs * (gate_grad - pair_mean)
    logit_grad = jnp.sum(jnp.where(named, pair_logit[:, :, None], 0.0), axis=1).astype(jnp.bfloat16)
    grad_router = t_dot(normed_two, logit_grad)
    normed_two_grad = normed_two_grad + dot_t(logit_grad, full_router)
    grad_expert_gain = jnp.sum(normed_two_grad * hidden * factor_two, axis=0)
    scaled_two = normed_two_grad * gain_two
    hidden_grad = (
        upstream
        + factor_two * scaled_two
        - hidden * factor_two**3 * jnp.mean(scaled_two * hidden, axis=1, keepdims=True)
    )
    branch_grad = hidden_grad.astype(jnp.bfloat16)
    grad_out_full = t_dot(attended, branch_grad).astype(jnp.bfloat16)
    attended_grad = dot_t(branch_grad, full_out).astype(jnp.bfloat16)

    gradient_heads = attended_grad.reshape(length, KEY_VALUE_HEADS, QUERY_PER_KEY, HEAD_SIZE)
    value_grad = jnp.einsum(
        "kgqs,qkgd->skd", probs_low, gradient_heads, preferred_element_type=jnp.float32
    )
    prob_grad = jnp.einsum(
        "qkgd,skd->kgqs", gradient_heads, heads_of_value, preferred_element_type=jnp.float32
    )
    delta_sum = jnp.sum(soft_probs * prob_grad, axis=-1, keepdims=True)
    score_grad = (soft_probs * (prob_grad - delta_sum)).astype(jnp.bfloat16)
    query_grad = (
        jnp.einsum("kgqs,skd->qkgd", score_grad, heads_of_key, preferred_element_type=jnp.float32)
        * head_scale
    )
    key_grad = (
        jnp.einsum("kgqs,qkgd->skd", score_grad, heads_of_query, preferred_element_type=jnp.float32)
        * head_scale
    )
    qkv_grad = jnp.concatenate(
        [
            query_grad.astype(jnp.bfloat16).reshape(length, cols, width_q),
            key_grad.astype(jnp.bfloat16).reshape(length, cols, width_k),
            value_grad.astype(jnp.bfloat16).reshape(length, cols, width_k),
        ],
        axis=2,
    ).reshape(length, cols * width_a)
    grad_a_full = t_dot(normed, qkv_grad).astype(jnp.bfloat16)
    normed_grad = dot_t(qkv_grad, full_a)
    grad_attn_gain = jnp.sum(normed_grad * rows_f * factor_one, axis=0)
    scaled_one = normed_grad * gain_one
    d_tokens = (
        hidden_grad
        + factor_one * scaled_one
        - rows_f * factor_one**3 * jnp.mean(scaled_one * rows_f, axis=1, keepdims=True)
    )
    grad_s = jnp.concatenate(
        [
            jnp.pad(
                grad_router.reshape(rows, block, cols, router_cols).transpose(0, 2, 3, 1),
                ((0, 0), (0, 0), (0, 0), (0, lane - block)),
            ),
            jnp.pad(
                jnp.stack([grad_attn_gain, grad_expert_gain])
                .reshape(2, rows, cols, piece)
                .transpose(1, 2, 0, 3),
                ((0, 0), (0, 0), (0, 6 - router_cols), (0, lane - piece)),
            ),
        ],
        axis=2,
    )
    grad_down = grad_down.astype(jnp.float32)[None]
    grad_a_full, d_tokens, output, grad_down = lax.optimization_barrier(
        (grad_a_full, d_tokens, output, grad_down)
    )
    sum_a, sum_out, sum_s = reduce_all(grad_a_full, grad_out_full, grad_s)
    return (
        output,
        d_tokens,
        sum_s[router_cols, :piece],
        sum_a[:, :width_q],
        sum_a[:, width_q : width_q + width_k],
        sum_a[:, width_q + width_k :],
        sum_out,
        sum_s[router_cols + 1, :piece],
        sum_s[:router_cols, :block].T,
        grad_gu[:, :hidden_units].astype(jnp.float32)[None],
        grad_gu[:, hidden_units:].astype(jnp.float32)[None],
        grad_down,
    )


def solution(mesh):
    in_specs = (
        P(("row", "col"), None),
        P(("row", "col")),
        P("row", "col"),
        P("row", "col"),
        P("row", "col"),
        P("row", "col"),
        P(("row", "col")),
        P("row", "col"),
        P("row", "col", None),
        P("row", "col", None),
        P("row", "col", None),
        P(("row", "col"), None),
        P(("row", "col"), None),
        P(("row", "col"), None),
    )
    out_specs = (
        P(("row", "col"), None),
        P(("row", "col"), None),
        P(("row", "col")),
        P("row", "col"),
        P("row", "col"),
        P("row", "col"),
        P("row", "col"),
        P(("row", "col")),
        P("row", "col"),
        P("row", "col", None),
        P("row", "col", None),
        P("row", "col", None),
    )
    return jax.shard_map(
        per_device, mesh=mesh, in_specs=in_specs, out_specs=out_specs, check_vma=False
    )
```

```python
import functools

import jax
import jax.numpy as jnp
from jax import lax
from jax.experimental import pallas as pl
from jax.experimental.pallas import tpu as pltpu
from jax.sharding import PartitionSpec as P

KEY_VALUE_HEADS = 8
HEAD_SIZE = 64
TOP = 2
QUERY_PER_KEY = 3


EPSILON = 1e-05
NEGATIVE = -1e30


MESH = pl.DeviceIdType.MESH
ANY = pl.BlockSpec(memory_space=pl.ANY)


def row_at(row, flip):
    y, x, core = row // 4, (row // 2) % 2, row % 2
    return (
        (y + flip // 4) % 2 * 4 + (x + (flip // 2) % 2) % 2 * 2 + (core + flip % 2) % 2
    )


def remote(source, target, send, receive, device):
    return pltpu.make_async_remote_copy(
        source, target, send, receive, device_id=device, device_id_type=MESH
    )


def greet(row_flips, col_steps):
    row, col = lax.axis_index("row"), lax.axis_index("col")
    sem = pltpu.get_barrier_semaphore()
    for flip in row_flips:
        pl.semaphore_signal(
            sem, inc=1, device_id={"row": row_at(row, flip)}, device_id_type=MESH
        )
    for step in col_steps:
        pl.semaphore_signal(
            sem, inc=1, device_id={"col": (col + step) % 4}, device_id_type=MESH
        )
    pl.semaphore_wait(sem, len(row_flips) + len(col_steps))


def unit_order(col, k):
    table = ((0, 1, 2, 3), (1, 0, 2, 3), (2, 3, 1, 0), (3, 2, 1, 0))
    out = table[3][k]
    for c in (2, 1, 0):
        out = jnp.where(col == c, table[c][k], out)
    return out


X, Y, SIB = 2, 4, 1


def plane_send(view, row, ss, rs, source=None):
    source = view(row) if source is None else source
    for i, flip in enumerate((X, Y, SIB)):
        remote(source, view(row), ss(i), rs(i), {"row": row_at(row, flip)}).start()


def plane_forward(view, halves, row, ss, rs):
    first, second = halves
    from_x, from_y = row_at(row, X), row_at(row, Y)
    sib = {"row": row_at(row, SIB)}
    remote(view(from_x), view(from_x), ss(0), rs(0), sib).wait_recv()
    remote(first(from_x), first(from_x), ss(3), rs(3), {"row": from_y}).start()
    remote(view(from_x), view(from_x), ss(5), rs(5), sib).start()
    remote(view(from_y), view(from_y), ss(1), rs(1), sib).wait_recv()
    remote(second(from_y), second(from_y), ss(4), rs(4), {"row": from_x}).start()
    remote(view(from_y), view(from_y), ss(6), rs(6), sib).start()


def plane_last(view, halves, row, ss, rs):
    first, second = halves
    diag = row_at(row, X + Y)
    sib = {"row": row_at(row, SIB)}
    remote(first(diag), first(diag), ss(3), rs(3), sib).wait_recv()
    remote(first(diag), first(diag), ss(7), rs(7), sib).start()
    remote(second(diag), second(diag), ss(4), rs(4), sib).wait_recv()
    remote(second(diag), second(diag), ss(8), rs(8), sib).start()


def plane_finish(view, halves, row, ss, rs):
    first, second = halves
    sib_row = row_at(row, SIB)
    sib = {"row": sib_row}
    whole = view(sib_row)
    remote(whole, whole, ss(2), rs(2), sib).wait_recv()
    for i, flip in ((5, X), (6, Y)):
        block = view(row_at(sib_row, flip))
        remote(block, block, ss(i), rs(i), sib).wait_recv()
    far = row_at(sib_row, X + Y)
    remote(first(far), first(far), ss(7), rs(7), sib).wait_recv()
    remote(second(far), second(far), ss(8), rs(8), sib).wait_recv()
    for i in range(9):
        block = view(row) if i in (0, 1, 2, 5, 6) else (first(row) if i in (3, 7) else second(row))
        remote(block, block, ss(i), rs(i), sib).wait_send()


def pick(ref, cols, halves_rows):
    block, cut = halves_rows

    def at(start, size):
        def view(r):
            rows = pl.ds(pl.multiple_of(r * block + start, 16), size)
            if cols is None:
                return ref.at[rows, :]
            return ref.at[rows, pl.ds(pl.multiple_of(cols[0], 128), cols[1])]

        return view

    return at(0, block), (at(0, cut), at(cut, block - cut))


def through(source, middle, target, sem):
    return pltpu.make_async_copy(source, middle, sem), pltpu.make_async_copy(middle, target, sem)


def through(source, middle, target, sem):
    return pltpu.make_async_copy(source, middle, sem), pltpu.make_async_copy(middle, target, sem)


def line_kernel(own_a, own_b, own_s, own_c, line_a, line_b, full_s, full_c, mid_a, mid_b, mid_c,
                zss, zrs, css, crs, s_zs, s_zr, s_ps, s_pr, loc):
    row, col = lax.axis_index("row"), lax.axis_index("col")
    width_a, width_b = own_a.shape[1], own_b.shape[1]
    rows_c = own_c.shape[0]
    vc, hc = pick(full_c, None, (rows_c, rows_c // 2))
    csv, crv = (lambda i: css.at[i]), (lambda i: crs.at[i])

    def of_a(c):
        return line_a.at[:, pl.ds(pl.multiple_of(c * width_a, 128), width_a)]

    def of_b(c):
        return line_b.at[:, pl.ds(pl.multiple_of(c * width_b, 128), width_b)]

    copies = [
        through(own_a, mid_a, of_a(col), loc.at[0]),
        through(own_b, mid_b, of_b(col), loc.at[1]),
        through(own_c, mid_c, vc(row), loc.at[2]),
    ]
    for copy, _ in copies:
        copy.start()
    small_copy = pltpu.make_async_copy(own_s, full_s.at[col, row], loc.at[3])
    small_copy.start()
    greet(range(1, 8), (1, 2, 3))

    def along(c, source_a, source_b, right, left):
        for d, (cond, step) in enumerate(((right, 1), (left, 3))):
            @pl.when(cond)
            def _():
                there = {"col": (col + step) % 4}
                remote(source_a, of_a(c), zss.at[0, c, d], zrs.at[0, c], there).start()
                remote(source_b, of_b(c), zss.at[1, c, d], zrs.at[1, c], there).start()

    def arrived(k):
        c = unit_order(col, k)
        there = {"col": (col + 1) % 4}
        remote(of_a(c), of_a(c), zss.at[0, c, 0], zrs.at[0, c], there).wait_recv()
        remote(of_b(c), of_b(c), zss.at[1, c, 0], zrs.at[1, c], there).wait_recv()
        along(c, of_a(c), of_b(c), (c < col) & (col < 3), (c > col) & (col > 0))

    along(col, own_a, own_b, col < 3, col > 0)
    for i, step in enumerate((1, 2, 3)):
        remote(own_s, full_s.at[col, row], s_zs.at[i], s_zr.at[i], {"col": (col + step) % 4}).start()
    plane_send(vc, row, csv, crv, own_c)
    for first, second in copies:
        first.wait()
        second.start()
    small_copy.wait()
    arrived(1)
    for i, step in enumerate((3, 2, 1)):
        remote(own_s, full_s.at[(col + step) % 4, row], s_zs.at[i], s_zr.at[i], {"col": (col + 1) % 4}).wait()
    for i in range(1, 8):
        remote(full_s.at[:, row], full_s.at[:, row], s_ps.at[i - 1], s_pr.at[i - 1], {"row": row_at(row, i)}).start()
    arrived(2)
    plane_forward(vc, hc, row, csv, crv)
    arrived(3)
    plane_last(vc, hc, row, csv, crv)
    for _, second in copies:
        second.wait()
    plane_finish(vc, hc, row, csv, crv)
    for i in range(1, 8):
        there = row_at(row, i)
        remote(full_s.at[:, there], full_s.at[:, there], s_ps.at[i - 1], s_pr.at[i - 1], {"row": there}).wait()
    for k in range(4):
        c = unit_order(col, k)
        right = (c <= col) & (col < 3)
        left = (c >= col) & (col > 0)
        for d, cond in enumerate((right, left)):
            @pl.when(cond)
            def _():
                there = {"col": (col + 1) % 4}
                remote(of_a(c), of_a(c), zss.at[0, c, d], zrs.at[0, c], there).wait_send()
                remote(of_b(c), of_b(c), zss.at[1, c, d], zrs.at[1, c], there).wait_send()


def gather_line(own_a, own_b, own_s, own_c):
    sems = pltpu.SemaphoreType.DMA
    rows_c = own_c.shape[0]
    return pl.pallas_call(
        line_kernel,
        out_shape=(
            jax.ShapeDtypeStruct((own_a.shape[0], own_a.shape[1] * 4), own_a.dtype),
            jax.ShapeDtypeStruct((own_b.shape[0], own_b.shape[1] * 4), own_b.dtype),
            jax.ShapeDtypeStruct((4, 8) + own_s.shape, own_s.dtype),
            jax.ShapeDtypeStruct((8 * rows_c, own_c.shape[1]), own_c.dtype),
        ),
        in_specs=[ANY] * 4,
        out_specs=(ANY,) * 4,
        scratch_shapes=[
            pltpu.VMEM(own_a.shape, own_a.dtype),
            pltpu.VMEM(own_b.shape, own_b.dtype),
            pltpu.VMEM(own_c.shape, own_c.dtype),
            sems((2, 4, 2)), sems((2, 4)),
            sems((9,)), sems((9,)),
            sems((3,)), sems((3,)), sems((7,)), sems((7,)), sems((4,)),
        ],
        compiler_params=pltpu.CompilerParams(collective_id=0, has_side_effects=True),
        cost_estimate=pl.CostEstimate(flops=0, bytes_accessed=1_000_000, transcendentals=0),
    )(own_a, own_b, own_s, own_c)


def plane_kernel(count, *refs):
    row = lax.axis_index("row")
    owns, fulls, mids = refs[:count], refs[count : 2 * count], refs[2 * count : 3 * count]
    ss, rs, loc = refs[3 * count :]
    views, copies = [], []
    for i in range(count):
        block = owns[i].shape[0]
        views.append(pick(fulls[i], None, (block, block // 2)))
        copies.append(through(owns[i], mids[i], views[i][0](row), loc.at[i]))
        copies[i][0].start()
    greet(range(1, 8), ())

    def sems_of(i):
        return (lambda j: ss.at[i, j]), (lambda j: rs.at[i, j])

    for i in range(count):
        plane_send(views[i][0], row, *sems_of(i), owns[i])
    for first, second in copies:
        first.wait()
        second.start()
    for i in range(count):
        plane_forward(*views[i], row, *sems_of(i))
    for i in range(count):
        plane_last(*views[i], row, *sems_of(i))
    for _, second in copies:
        second.wait()
    for i in range(count):
        plane_finish(*views[i], row, *sems_of(i))


def gather_plane(collective, owns):
    sems = pltpu.SemaphoreType.DMA
    count = len(owns)
    return pl.pallas_call(
        functools.partial(plane_kernel, count),
        out_shape=tuple(
            jax.ShapeDtypeStruct((8 * own.shape[0], own.shape[1]), own.dtype) for own in owns
        ),
        in_specs=[ANY] * count,
        out_specs=(ANY,) * count,
        scratch_shapes=[pltpu.VMEM(own.shape, own.dtype) for own in owns]
        + [sems((count, 9)), sems((count, 9)), sems((count,))],
        compiler_params=pltpu.CompilerParams(collective_id=collective, has_side_effects=True),
        cost_estimate=pl.CostEstimate(flops=0, bytes_accessed=1_000_000, transcendentals=0),
    )(*owns)


def spread_kernel(own_c, own_g, full_c, full_g, mid_c, css, crs, gss, grs, loc):
    row = lax.axis_index("row")
    rows_c = own_c.shape[0]
    vc, hc = pick(full_c, None, (rows_c, rows_c // 2))
    csv, crv = (lambda i: css.at[i]), (lambda i: crs.at[i])
    first, second = through(own_c, mid_c, vc(row), loc.at[0])
    first.start()
    own_copy = pltpu.make_async_copy(own_g, full_g.at[row], loc.at[1])
    own_copy.start()
    greet(range(1, 8), ())
    plane_send(vc, row, csv, crv, own_c)
    for i in range(1, 8):
        remote(own_g, full_g.at[row], gss.at[i - 1], grs.at[i - 1], {"row": row_at(row, i)}).start()
    first.wait()
    second.start()
    plane_forward(vc, hc, row, csv, crv)
    plane_last(vc, hc, row, csv, crv)
    second.wait()
    own_copy.wait()
    plane_finish(vc, hc, row, csv, crv)
    for i in range(1, 8):
        there = row_at(row, i)
        remote(own_g, full_g.at[there], gss.at[i - 1], grs.at[i - 1], {"row": there}).wait()


def spread_tokens(own_c, own_g):
    sems = pltpu.SemaphoreType.DMA
    return pl.pallas_call(
        spread_kernel,
        out_shape=(
            jax.ShapeDtypeStruct((8 * own_c.shape[0], own_c.shape[1]), own_c.dtype),
            jax.ShapeDtypeStruct((8,) + own_g.shape, own_g.dtype),
        ),
        in_specs=[ANY] * 2,
        out_specs=(ANY,) * 2,
        scratch_shapes=[
            pltpu.VMEM(own_c.shape, own_c.dtype),
            sems((9,)), sems((9,)), sems((7,)), sems((7,)), sems((2,)),
        ],
        compiler_params=pltpu.CompilerParams(collective_id=1, has_side_effects=True),
        cost_estimate=pl.CostEstimate(flops=0, bytes_accessed=1_000_000, transcendentals=0),
    )(own_c, own_g)


def add_into(target, term):
    target[...] = (target[...].astype(jnp.float32) + term[...].astype(jnp.float32)).astype(target.dtype)


def reduce_kernel(grad_a, grad_b, grad_s, sum_a, sum_b, sum_s,
                  own, rec_sib, rec_one, rec_two, rec_z, s_own, s_rec, s_mid, s_zrec,
                  lss, lrs, ss1, rs1, ss2, rs2, zss, zrs, lo, s_ss, s_rs, sz_ss, sz_rs):
    row, col = lax.axis_index("row"), lax.axis_index("col")
    core = row % 2
    chip = row // 2
    cy, cx = chip // 2, chip % 2
    block, width = own.shape[2], own.shape[3]
    width_a = sum_a.shape[1]
    width_b = width - width_a
    cut = block // 2
    greet(range(1, 8), (1, 2, 3))
    sib = {"row": row_at(row, SIB)}
    to_x, to_y = {"row": row_at(row, X)}, {"row": row_at(row, Y)}

    def parts(c, q, of_core):
        rows = pl.ds(pl.multiple_of((q * 2 + of_core) * block, 16), block)
        return (
            grad_a.at[rows, pl.ds(pl.multiple_of(c * width_a, 128), width_a)],
            grad_b.at[rows, pl.ds(pl.multiple_of(c * width_b, 128), width_b)],
        )

    for i in range(1, 8):
        there = row_at(row, i)
        remote(grad_s.at[there], s_rec.at[i - 1], s_ss.at[i - 1], s_rs.at[i - 1], {"row": there}).start()
    def start_first(k, carry):
        c = (col + 1 + k) % 4
        for q in range(4):
            pa, pb = parts(c, q, 1 - core)
            remote(pa, rec_sib.at[c, q, :, pl.ds(0, width_a)], ss1.at[c, q, 0], rs1.at[c, q, 0], sib).start()
            remote(pb, rec_sib.at[c, q, :, pl.ds(width_a, width_b)], ss1.at[c, q, 1], rs1.at[c, q, 1], sib).start()
            pa, pb = parts(c, q, core)
            pltpu.make_async_copy(pa, own.at[c, q, :, pl.ds(0, width_a)], lss.at[c, q, 0]).start()
            pltpu.make_async_copy(pb, own.at[c, q, :, pl.ds(width_a, width_b)], lss.at[c, q, 1]).start()
        return carry
    lax.fori_loop(0, 4, start_first, 0)
    own_small = pltpu.make_async_copy(grad_s.at[row], s_own, lo.at[0])
    own_small.start()

    def chip_sum(c):
        for q in range(4):
            pa, pb = parts(c, q, core)
            for i, (p, off, w) in enumerate(((pa, 0, width_a), (pb, width_a, width_b))):
                pltpu.make_async_copy(p, own.at[c, q, :, pl.ds(off, w)], lss.at[c, q, i]).wait()
                remote(p, rec_sib.at[c, q, :, pl.ds(off, w)], ss1.at[c, q, i], rs1.at[c, q, i], sib).wait_recv()
            add_into(own.at[c, q], rec_sib.at[c, q])

    top, low = pl.ds(0, cut), pl.ds(cut, block - cut)

    def one(c):
        for j in range(2):
            yield remote(own.at[c, j * 2 + 1 - cx, top, :], rec_one.at[c, 0, j], ss2.at[c, 0, j], rs2.at[c, 0, j], to_x)
            yield remote(own.at[c, (1 - cy) * 2 + j, low, :], rec_one.at[c, 1, j], ss2.at[c, 1, j], rs2.at[c, 1, j], to_y)

    def one_sum(c):
        for copy in one(c):
            copy.wait_recv()
        for j in range(2):
            add_into(own.at[c, j * 2 + cx, top, :], rec_one.at[c, 0, j])
            add_into(own.at[c, cy * 2 + j, low, :], rec_one.at[c, 1, j])

    def two(c):
        yield remote(own.at[c, (1 - cy) * 2 + cx, top, :], rec_two.at[c, 0], ss2.at[c, 0, 2], rs2.at[c, 0, 2], to_y)
        yield remote(own.at[c, cy * 2 + 1 - cx, low, :], rec_two.at[c, 1], ss2.at[c, 1, 2], rs2.at[c, 1, 2], to_x)

    def two_sum(c):
        for copy in two(c):
            copy.wait_recv()
        add_into(own.at[c, chip, top, :], rec_two.at[c, 0])
        add_into(own.at[c, chip, low, :], rec_two.at[c, 1])

    def column(step):
        there = (col + step) % 4
        return remote(own.at[there, chip], rec_z.at[step - 1], zss.at[step - 1], zrs.at[step - 1], {"col": there})

    def nth(k):
        return (col + 1 + k) % 4

    def stages(k, carry):
        @pl.when(k < 4)
        def _():
            chip_sum(nth(k))
            for copy in one(nth(k)):
                copy.start()
        @pl.when((k >= 1) & (k < 5))
        def _():
            one_sum(nth(k - 1))
            for copy in two(nth(k - 1)):
                copy.start()
        @pl.when(k >= 2)
        def _():
            two_sum(nth(k - 2))
        for step in (1, 2, 3):
            @pl.when(k == step + 1)
            def _():
                column(step).start()
        return carry
    lax.fori_loop(0, 6, stages, 0)

    own_small.wait()
    total = s_own[...]
    for i in range(1, 8):
        there = row_at(row, i)
        remote(grad_s.at[there], s_rec.at[i - 1], s_ss.at[i - 1], s_rs.at[i - 1], {"row": there}).wait()
        total = total + s_rec[i - 1]
    s_mid[...] = total

    def small(step):
        there = (col + step) % 4
        return remote(s_mid.at[there], s_zrec.at[step - 1], sz_ss.at[step - 1], sz_rs.at[step - 1], {"col": there})

    for step in (1, 2, 3):
        small(step).start()
    for step in (1, 2, 3):
        small(step).wait()
    sum_s[...] = s_mid[col] + s_zrec[0] + s_zrec[1] + s_zrec[2]
    for step in (1, 2, 3):
        column(step).wait_recv()
    for start in range(0, block, 32):
        rows = pl.ds(start, 32)
        total = own[col, chip, rows, :].astype(jnp.float32)
        for step in range(3):
            total = total + rec_z[step, rows, :].astype(jnp.float32)
        sum_a[rows, :] = total[:, :width_a]
        sum_b[rows, :] = total[:, width_a:]
    for step in (1, 2, 3):
        column(step).wait_send()

    def sent(c, carry):
        for q in range(4):
            pa, pb = parts(c, q, 1 - core)
            remote(pa, rec_sib.at[c, q, :, pl.ds(0, width_a)], ss1.at[c, q, 0], rs1.at[c, q, 0], sib).wait_send()
            remote(pb, rec_sib.at[c, q, :, pl.ds(width_a, width_b)], ss1.at[c, q, 1], rs1.at[c, q, 1], sib).wait_send()
        for copy in one(c):
            copy.wait_send()
        for copy in two(c):
            copy.wait_send()
        return carry
    lax.fori_loop(0, 4, sent, 0)


def reduce_attention(grad_a, grad_b, grad_s):
    sems = pltpu.SemaphoreType.DMA
    block = grad_a.shape[0] // 8
    width_a, width_b = grad_a.shape[1] // 4, grad_b.shape[1] // 4
    width = width_a + width_b
    cut = block // 2
    low = grad_a.dtype
    vm = pl.BlockSpec(memory_space=pltpu.VMEM)
    small = grad_s.shape[1:]
    return pl.pallas_call(
        reduce_kernel,
        out_shape=(
            jax.ShapeDtypeStruct((block, width_a), jnp.float32),
            jax.ShapeDtypeStruct((block, width_b), jnp.float32),
            jax.ShapeDtypeStruct(small[1:], jnp.float32),
        ),
        in_specs=[ANY] * 3,
        out_specs=(vm,) * 3,
        scratch_shapes=[
            pltpu.VMEM((4, 4, block, width), low),
            pltpu.VMEM((4, 4, block, width), low),
            pltpu.VMEM((4, 2, 2, cut, width), low),
            pltpu.VMEM((4, 2, cut, width), low),
            pltpu.VMEM((3, block, width), low),
            pltpu.VMEM(small, jnp.float32),
            pltpu.VMEM((7,) + small, jnp.float32),
            pltpu.VMEM(small, jnp.float32),
            pltpu.VMEM((3,) + small[1:], jnp.float32),
            sems((4, 4, 2)), sems((1,)),
            sems((4, 4, 2)), sems((4, 4, 2)),
            sems((4, 2, 3)), sems((4, 2, 3)),
            sems((3,)), sems((3,)), sems((1,)),
            sems((7,)), sems((7,)), sems((3,)), sems((3,)),
        ],
        compiler_params=pltpu.CompilerParams(
            collective_id=2, has_side_effects=True, vmem_limit_bytes=48 * 2**20
        ),
        cost_estimate=pl.CostEstimate(flops=0, bytes_accessed=1_000_000, transcendentals=0),
    )(grad_a, grad_b, grad_s)


def expert_kernel(key, mine, normed_hbm, upstream_hbm, gu_hbm, own_down,
                  in_ref, prod_ref, gate_grad_ref, grad_gu, sum_down,
                  x_t, ups, gu, down, act, silu, slope, both, gd, rec_right, rec_left, stage, gate,
                  load_sem, src_sem, stage_sem, zss, zrs, rss, rrs):
    col = lax.axis_index("col")
    sources, _, length = key.shape
    slots = in_ref.shape[0]
    capacity = slots // sources
    units = gu.shape[1] // 2
    width = units // 4
    chunk = 256
    x = in_ref
    right_dev, left_dev = {"col": (col + 1) % 4}, {"col": (col + 3) % 4}

    load_gu = pltpu.make_async_copy(gu_hbm, gu, load_sem.at[0])
    load_gu.start()
    load_down = pltpu.make_async_copy(own_down, down.at[col], load_sem.at[1])
    load_down.start()

    def fetch(s, slot):
        rows = pl.ds(pl.multiple_of(s * length, 16), length)
        for i, hbm in enumerate((normed_hbm, upstream_hbm)):
            to = prod_ref.at[pl.ds(pl.multiple_of((slot * 2 + i) * length, 16), length), :]
            yield pltpu.make_async_copy(hbm.at[rows, :], to, src_sem.at[slot, i])

    for copy in fetch(0, 0):
        copy.start()
    greet((), (1, 2, 3))

    def pass_on(c, source, right, left):
        for d, (cond, there) in enumerate(((right, right_dev), (left, left_dev))):
            @pl.when(cond)
            def _():
                remote(source, down.at[c], zss.at[c, d], zrs.at[c], there).start()

    pass_on(col, own_down, col < 3, col > 0)

    def ag_step(s):
        @pl.when(col >= s)
        def _():
            c = col - s
            remote(down.at[c], down.at[c], zss.at[c, 0], zrs.at[c], right_dev).wait_recv()
            @pl.when(col < 3)
            def _():
                remote(down.at[c], down.at[c], zss.at[c, 0], zrs.at[c], right_dev).start()
        @pl.when(col + s < 4)
        def _():
            c = col + s
            remote(down.at[c], down.at[c], zss.at[c, 1], zrs.at[c], left_dev).wait_recv()
            @pl.when(col > 0)
            def _():
                remote(down.at[c], down.at[c], zss.at[c, 1], zrs.at[c], left_dev).start()

    def to_right(d):
        target = rec_right.at[d - 1]
        return remote(target, target, rss.at[0, d - 1], rrs.at[0, d - 1], right_dev)

    def to_left(d):
        target = rec_left.at[d]
        return remote(target, target, rss.at[1, d], rrs.at[1, d], left_dev)

    def from_end(d):
        if d > 0:
            @pl.when(col == 0)
            def _():
                remote(gd.at[d], rec_right.at[d - 1], rss.at[0, d - 1], rrs.at[0, d - 1], right_dev).start()
        if d < 3:
            @pl.when(col == 3)
            def _():
                remote(gd.at[d], rec_left.at[d], rss.at[1, d], rrs.at[1, d], left_dev).start()

    def add_rows(target, term):
        def body(i, carry):
            rows = pl.ds(pl.multiple_of(i * 64, 64), 64)
            total = target[rows, :].astype(jnp.float32) + term[rows, :].astype(jnp.float32)
            target[rows, :] = total.astype(target.dtype)
            return carry
        lax.fori_loop(0, width // 64, body, 0)

    def hop_right(at, d):
        @pl.when(col == at)
        def _():
            to_right(d).wait_recv()
            add_rows(rec_right.at[d - 1], gd.at[d])
            to_right(d).start()

    def hop_left(at, d):
        @pl.when(col == at)
        def _():
            to_left(d).wait_recv()
            add_rows(rec_left.at[d], gd.at[d])
            to_left(d).start()

    def select(s, carry):
        slot = s % 2
        @pl.when(s + 1 < sources)
        def _():
            for copy in fetch(s + 1, 1 - slot):
                copy.start()
        for copy in fetch(s, slot):
            copy.wait()
        chosen = key[s] == lax.broadcasted_iota(jnp.int32, (capacity, length), 0)
        value = jnp.sum(jnp.where(chosen, mine[s], 0.0), axis=1, keepdims=True)
        rows = pl.ds(pl.multiple_of(s * capacity, 16), capacity)
        gate[rows, :] = jnp.broadcast_to(value, (capacity, gate.shape[1]))
        one_hot = jnp.where(chosen, 1.0, 0.0).astype(x.dtype)
        for i, target in enumerate((x, ups)):
            block = prod_ref[pl.ds(pl.multiple_of((slot * 2 + i) * length, 16), length), :]
            target[rows, :] = dot(one_hot, block).astype(target.dtype)
        return carry
    lax.fori_loop(0, sources, select, 0)

    load_gu.wait()

    def forward(c):
        first = pl.ds(c * width, width)
        second = pl.ds(units + c * width, width)
        def body(m, carry):
            rows = pl.ds(pl.multiple_of(m * chunk, chunk), chunk)
            gate_pre = dot(x[rows, :], gu[:, first])
            up_pre = dot(x[rows, :], gu[:, second])
            sigma = jax.nn.sigmoid(gate_pre)
            silu_gate = gate_pre * sigma
            silu[rows, first] = silu_gate
            slope[rows, first] = up_pre * sigma * (1.0 + gate_pre * (1.0 - sigma))
            low = (silu_gate * up_pre).astype(act.dtype)
            act[rows, first] = low
            both[rows, first] = (low.astype(jnp.float32) * gate[rows, 0:1]).astype(both.dtype)
            return carry
        lax.fori_loop(0, slots // chunk, body, 0)
        gd[c] = t_dot(both[:, first], ups[...]).astype(gd.dtype)

    forward(3)
    from_end(3)
    forward(0)
    from_end(0)
    ag_step(1)
    forward(2)
    forward(1)
    for d in (2, 1):
        if d > 0:
            @pl.when(col == 0)
            def _():
                remote(gd.at[d], rec_right.at[d - 1], rss.at[0, d - 1], rrs.at[0, d - 1], right_dev).start()
    for d in (1, 2):
        @pl.when(col == 3)
        def _():
            remote(gd.at[d], rec_left.at[d], rss.at[1, d], rrs.at[1, d], left_dev).start()
    load_down.wait()

    def turn(m, carry):
        rows = pl.ds(pl.multiple_of(m * chunk, chunk), chunk)
        x_t[:, rows] = x[rows, :].T
        return carry
    lax.fori_loop(0, slots // chunk, turn, 0)
    gate_grad_ref[...] = jnp.zeros_like(gate_grad_ref)

    def out_stage(c, slot):
        for i in range(2):
            yield pltpu.make_async_copy(
                stage.at[slot, :, pl.ds(i * width, width)],
                grad_gu.at[:, pl.ds(pl.multiple_of(i * units + c * width, width), width)],
                stage_sem.at[slot, i],
            )

    def backward(k):
        c = unit_order(col, k)
        first = pl.ds(pl.multiple_of(c * width, width), width)
        second = pl.ds(pl.multiple_of(units + c * width, width), width)
        def body(m, carry):
            rows = pl.ds(pl.multiple_of(m * chunk, chunk), chunk)
            plain = dot_t(ups[rows, :], down[c])
            term = jnp.sum(act[rows, first].astype(jnp.float32) * plain, axis=1, keepdims=True)
            gate_grad_ref[rows, :] += jnp.broadcast_to(term, (chunk, gate_grad_ref.shape[1]))
            act_grad = plain * gate[rows, 0:1]
            both[rows, first] = (act_grad * slope[rows, first]).astype(both.dtype)
            both[rows, second] = (act_grad * silu[rows, first]).astype(both.dtype)
            return carry
        lax.fori_loop(0, slots // chunk, body, 0)
        slot = k % 2
        if k >= 2:
            for copy in out_stage(unit_order(col, k - 2), slot):
                copy.wait()
        def grads(i, carry):
            rows = pl.ds(pl.multiple_of(i * chunk, chunk), chunk)
            stage[slot, rows, 0:width] = dot(x_t[rows, :], both[:, first]).astype(stage.dtype)
            stage[slot, rows, width : 2 * width] = dot(x_t[rows, :], both[:, second]).astype(stage.dtype)
            return carry
        lax.fori_loop(0, x_t.shape[0] // chunk, grads, 0)
        for copy in out_stage(c, slot):
            copy.start()

    backward(0)
    ag_step(2)
    hop_right(1, 3)
    hop_left(2, 0)
    backward(1)
    backward(2)
    ag_step(3)
    hop_right(1, 2)
    hop_right(2, 3)
    hop_left(2, 1)
    hop_left(1, 0)
    backward(3)

    def inputs(m, carry):
        rows = pl.ds(pl.multiple_of(m * chunk, chunk), chunk)
        in_ref[rows, :] = dot_t(both[rows, :], gu[...]).astype(in_ref.dtype)
        return carry
    lax.fori_loop(0, slots // chunk, inputs, 0)

    def outputs(m, carry):
        rows = pl.ds(pl.multiple_of(m * chunk, chunk), chunk)
        total = dot(act[rows, 0:width], down[0])
        for c in range(1, 4):
            total = total + dot(act[rows, c * width : (c + 1) * width], down[c])
        prod_ref[rows, :] = total.astype(prod_ref.dtype)
        return carry
    lax.fori_loop(0, slots // chunk, outputs, 0)

    for k in (2, 3):
        for copy in out_stage(unit_order(col, k), k % 2):
            copy.wait()
    for d in range(4):
        @pl.when(col == d)
        def _():
            if d > 0:
                to_right(d).wait_recv()
            if d < 3:
                to_left(d).wait_recv()
            def body(i, carry):
                rows = pl.ds(pl.multiple_of(i * 64, 64), 64)
                total = gd[d, rows, :].astype(jnp.float32)
                if d > 0:
                    total = total + rec_right[d - 1, rows, :].astype(jnp.float32)
                if d < 3:
                    total = total + rec_left[d, rows, :].astype(jnp.float32)
                sum_down[rows, :] = total
                return carry
            lax.fori_loop(0, width // 64, body, 0)
            for e in range(d + 1, 4):
                to_right(e).wait_send()
            for e in range(d):
                to_left(e).wait_send()
            if d < 3:
                for e in range(d + 1):
                    remote(down.at[e], down.at[e], zss.at[e, 0], zrs.at[e], right_dev).wait_send()
            if d > 0:
                for e in range(d, 4):
                    remote(down.at[e], down.at[e], zss.at[e, 1], zrs.at[e], left_dev).wait_send()


def run_expert(key, mine, normed, upstream, full_gu, own_down):
    sources, length = key.shape
    model, units = full_gu.shape[0], full_gu.shape[1] // 2
    width = own_down.shape[0]
    slots = sources * length // 2
    low, f32 = normed.dtype, jnp.float32
    sems = pltpu.SemaphoreType.DMA
    vm = pl.BlockSpec(memory_space=pltpu.VMEM)
    return pl.pallas_call(
        expert_kernel,
        out_shape=(
            jax.ShapeDtypeStruct((slots, model), low),
            jax.ShapeDtypeStruct((slots, model), low),
            jax.ShapeDtypeStruct((slots, 128), f32),
            jax.ShapeDtypeStruct((model, 2 * units), low),
            jax.ShapeDtypeStruct((width, model), f32),
        ),
        in_specs=[vm, vm, ANY, ANY, ANY, ANY],
        out_specs=(vm, vm, vm, ANY, vm),
        scratch_shapes=[
            pltpu.VMEM((model, slots), low),
            pltpu.VMEM((slots, model), low),
            pltpu.VMEM((model, 2 * units), low),
            pltpu.VMEM((4, width, model), low),
            pltpu.VMEM((slots, units), low),
            pltpu.VMEM((slots, units), f32),
            pltpu.VMEM((slots, units), f32),
            pltpu.VMEM((slots, 2 * units), low),
            pltpu.VMEM((4, width, model), low),
            pltpu.VMEM((3, width, model), low),
            pltpu.VMEM((3, width, model), low),
            pltpu.VMEM((2, model, 2 * width), low),
            pltpu.VMEM((slots, 128), f32),
            sems((2,)), sems((2, 2)), sems((2, 2)),
            sems((4, 2)), sems((4,)), sems((2, 3)), sems((2, 3)),
        ],
        compiler_params=pltpu.CompilerParams(
            collective_id=4, has_side_effects=True, vmem_limit_bytes=60 * 2**20
        ),
        cost_estimate=pl.CostEstimate(flops=0, bytes_accessed=1_000_000, transcendentals=0),
    )(key.reshape(sources, 1, length), mine.reshape(sources, 1, length), normed, upstream, full_gu, own_down)


def rms_factor(rows_in):
    return lax.rsqrt(jnp.mean(rows_in * rows_in, axis=1, keepdims=True) + EPSILON)


def dot(a, b):
    return jnp.dot(a, b, preferred_element_type=jnp.float32)


def dot_t(a, b):
    return lax.dot_general(a, b, (((1,), (1,)), ((), ())), preferred_element_type=jnp.float32)


def t_dot(a, b):
    return lax.dot_general(a, b, (((0,), (0,)), ((), ())), preferred_element_type=jnp.float32)


def on_small_slice():
    return lax.axis_size("row") == 8 and lax.axis_size("col") == 4


def gather_all(own_a, own_b, own_s, own_c):
    col_a = lax.all_gather(own_a, "col", axis=1, tiled=True)
    col_b = lax.all_gather(own_b, "col", axis=1, tiled=True)
    small = lax.all_gather(lax.all_gather(own_s, "col", axis=0), "row", axis=1)
    return (
        lax.all_gather(col_a, "row", axis=0, tiled=True),
        lax.all_gather(col_b, "row", axis=0, tiled=True),
        small,
        lax.all_gather(own_c, "row", axis=0, tiled=True),
    )


def spread(own_c, own_g):
    if on_small_slice():
        return spread_tokens(own_c, own_g)
    return (
        lax.all_gather(own_c, "row", axis=0, tiled=True),
        lax.all_gather(own_g, "row", axis=0),
    )


def reduce_all(grad_a, grad_b, grad_s):
    if on_small_slice():
        return reduce_attention(grad_a, grad_b, grad_s)

    def both(g):
        plane = lax.psum_scatter(g, "row", scatter_dimension=0, tiled=True).astype(jnp.float32)
        return lax.psum_scatter(plane, "col", scatter_dimension=1, tiled=True)

    small = lax.psum_scatter(grad_s, "row", scatter_dimension=0, tiled=False)
    return both(grad_a), both(grad_b), lax.psum_scatter(small, "col", scatter_dimension=0, tiled=False)


def expert_elsewhere(place, routed, mine, plane_normed, plane_upstream, full_gu, own_down):
    rows, length = place.shape
    model = plane_normed.shape[1]
    hidden_units = full_gu.shape[1] // 2
    capacity = 2 * length * TOP // rows
    full_down = lax.all_gather(own_down, "col", axis=0, tiled=True)
    chosen_rows = (
        (place[:, None, :] == jnp.arange(capacity, dtype=jnp.int32)[None, :, None]) & routed[:, None, :]
    ).astype(jnp.bfloat16)

    def of_slots(plane):
        return jnp.einsum(
            "rct,rtd->rcd",
            chosen_rows,
            plane.reshape(rows, length, model),
            preferred_element_type=jnp.float32,
        ).astype(jnp.bfloat16).reshape(rows * capacity, model)

    grouped, grouped_up = of_slots(plane_normed), of_slots(plane_upstream)
    slot_gate = jnp.sum(jnp.where(chosen_rows > 0, mine[:, None, :], 0.0), axis=2)
    slot_gate = slot_gate.reshape(rows * capacity, 1)
    grouped_grad = (grouped_up.astype(jnp.float32) * slot_gate).astype(jnp.bfloat16)
    both_pre = dot(grouped, full_gu)
    gate_pre, up_pre = both_pre[:, :hidden_units], both_pre[:, hidden_units:]
    sigma = jax.nn.sigmoid(gate_pre)
    silu_gate = gate_pre * sigma
    activation = (silu_gate * up_pre).astype(jnp.bfloat16)
    grad_down_local = t_dot(activation, grouped_grad).astype(jnp.bfloat16)
    grad_down = lax.psum_scatter(grad_down_local, "col", scatter_dimension=0, tiled=True)
    act_grad = dot_t(grouped_grad, full_down)
    both_grad = jnp.concatenate(
        [
            (act_grad * up_pre * sigma * (1.0 + gate_pre * (1.0 - sigma))).astype(jnp.bfloat16),
            (act_grad * silu_gate).astype(jnp.bfloat16),
        ],
        axis=1,
    )
    in_grad = dot_t(both_grad, full_gu).astype(jnp.bfloat16)
    produced = dot(activation, full_down).astype(jnp.bfloat16)
    slot_gate_grad = jnp.sum(produced.astype(jnp.float32) * grouped_up.astype(jnp.float32), axis=1)
    grad_gu_local = t_dot(grouped, both_grad).astype(jnp.bfloat16)
    return in_grad, produced, slot_gate_grad, grad_gu_local, grad_down.astype(jnp.float32)


def masked_scores(queries, heads_of_key, segments, head_scale):
    length = queries.shape[0]
    heads_of_query = queries.reshape(length, KEY_VALUE_HEADS, QUERY_PER_KEY, HEAD_SIZE)
    scores = (
        jnp.einsum("qkgd,skd->kgqs", heads_of_query, heads_of_key, preferred_element_type=jnp.float32)
        * head_scale
    )
    pos = jnp.arange(length, dtype=jnp.int32)
    allowed = (pos[None, :] <= pos[:, None]) & (segments[None, :] == segments[:, None])
    return jnp.where(allowed, scores, NEGATIVE), heads_of_query


def per_device(
    tokens,
    attn_gain,
    w_query,
    w_key,
    w_value,
    w_out,
    expert_gain,
    router,
    w_gate,
    w_up,
    w_down,
    segment_ids,
    expert_ids,
    cotangent,
):
    length, model = tokens.shape
    rows, cols = lax.axis_size("row"), lax.axis_size("col")
    experts = w_gate.shape[0] * rows
    capacity = 2 * length * TOP // experts
    head_scale = HEAD_SIZE ** (-0.5)
    segments = segment_ids.reshape(-1)
    block, width_q = w_query.shape
    width_k = w_key.shape[1]
    width_a = width_q + 2 * width_k
    piece = attn_gain.shape[0]
    router_cols = router.shape[1]

    hidden_units = w_gate.shape[2]
    own_gu = jnp.concatenate([w_gate[0], w_up[0]], axis=1)
    own_down = w_down[0]

    lane = 256

    def row_of(v):
        return jnp.pad(v, ((0, 0), (0, lane - v.shape[1])))

    own_s = jnp.concatenate(
        [row_of(router.T), row_of(attn_gain[None]), row_of(expert_gain[None])], axis=0
    )
    own_s = jnp.pad(own_s, ((0, 16 - own_s.shape[0]), (0, 0)))
    own_a = jnp.concatenate([w_query, w_key, w_value], axis=1)
    if on_small_slice():
        line_a, line_out, small, plane_upstream = gather_line(own_a, w_out, own_s, cotangent)
        own_gu, own_down, line_a, line_out = lax.optimization_barrier(
            (own_gu, own_down, line_a, line_out)
        )
        full_a, full_out = gather_plane(3, (line_a, line_out))
    else:
        full_a, full_out, small, plane_upstream = gather_all(own_a, w_out, own_s, cotangent)
    full_gu = lax.all_gather(own_gu, "col", axis=0, tiled=True)
    full_router = small[:, :, :router_cols, :block].transpose(1, 3, 0, 2).reshape(model, experts)
    gain_one = small[:, :, router_cols, :piece].transpose(1, 0, 2).reshape(model).astype(jnp.float32)
    gain_two = small[:, :, router_cols + 1, :piece].transpose(1, 0, 2).reshape(model).astype(jnp.float32)

    rows_f = tokens.astype(jnp.float32)
    factor_one = rms_factor(rows_f)
    normed = (rows_f * factor_one * gain_one).astype(jnp.bfloat16)
    qkv = dot(normed, full_a).astype(jnp.bfloat16).reshape(length, cols, width_a)
    query_rows = qkv[:, :, :width_q].reshape(length, -1)
    rows_of_key = qkv[:, :, width_q : width_q + width_k].reshape(length, -1)
    rows_of_value = qkv[:, :, width_q + width_k :].reshape(length, -1)
    heads_of_key = rows_of_key.reshape(length, KEY_VALUE_HEADS, HEAD_SIZE)
    heads_of_value = rows_of_value.reshape(length, KEY_VALUE_HEADS, HEAD_SIZE)

    scores, heads_of_query = masked_scores(query_rows, heads_of_key, segments, head_scale)
    row_max = jnp.max(scores, axis=-1, keepdims=True)
    expo_rows = jnp.exp(scores - row_max)
    totals = jnp.sum(expo_rows, axis=-1, keepdims=True)
    soft_probs = expo_rows / totals
    probs_low = soft_probs.astype(jnp.bfloat16)
    attended = (
        jnp.einsum("kgqs,skd->qkgd", probs_low, heads_of_value, preferred_element_type=jnp.float32)
        .reshape(length, -1)
        .astype(jnp.bfloat16)
    )
    hidden = rows_f + dot(attended, full_out)
    factor_two = rms_factor(hidden)
    normed_two = (hidden * factor_two * gain_two).astype(jnp.bfloat16)
    logits = dot(normed_two, full_router)

    named = expert_ids[:, :, None] == jnp.arange(experts, dtype=jnp.int32)[None, None, :]
    chosen = jnp.sum(jnp.where(named, logits[:, None, :], 0.0), axis=2)
    gate_probs = jax.nn.softmax(chosen, axis=1)
    gate_table = jnp.sum(jnp.where(named, gate_probs[:, :, None], 0.0), axis=1)
    gate_table = jnp.where(jnp.any(named, axis=1), gate_table, -1.0)
    plane_normed, plane_gate = spread(normed_two, gate_table.T)
    mine = lax.dynamic_index_in_dim(plane_gate, lax.axis_index("row"), axis=1, keepdims=False)
    routed = mine >= 0.0
    place = jnp.cumsum(routed.astype(jnp.int32), axis=1) - 1
    if on_small_slice():
        in_grad, produced, slot_gate_grad, grad_gu_local, grad_down = run_expert(
            jnp.where(routed, place, -1), mine, plane_normed, plane_upstream, full_gu, own_down
        )
        slot_gate_grad = slot_gate_grad[:, 0]
    else:
        in_grad, produced, slot_gate_grad, grad_gu_local, grad_down = expert_elsewhere(
            place, routed, mine, plane_normed, plane_upstream, full_gu, own_down
        )
    grad_gu = lax.psum_scatter(grad_gu_local, "col", scatter_dimension=0, tiled=True)
    back_grad = lax.all_to_all(
        in_grad.reshape(rows, capacity, model), "row", split_axis=0, concat_axis=0, tiled=True
    ).reshape(experts * capacity, model)
    back_gate_grad = lax.all_to_all(
        slot_gate_grad.reshape(rows, 1, capacity), "row", split_axis=0, concat_axis=0, tiled=True
    ).reshape(experts * capacity)
    produced, back_grad = lax.optimization_barrier((produced, back_grad))
    back_rows = lax.all_to_all(
        produced.reshape(rows, capacity, model), "row", split_axis=0, concat_axis=0, tiled=True
    ).reshape(experts * capacity, model)

    any_named = jnp.any(named, axis=1)
    before = jnp.cumsum(any_named.astype(jnp.int32), axis=0) - 1
    slot_of = jnp.sum(
        jnp.where(named, before[:, None, :] + jnp.arange(experts, dtype=jnp.int32) * capacity, 0),
        axis=2,
    )
    all_slots = jnp.arange(experts * capacity, dtype=jnp.int32)
    is_slot = slot_of.T[:, :, None] == all_slots[None, None, :]
    from_slot = is_slot.astype(jnp.bfloat16)
    gate_grad = jnp.sum(jnp.where(is_slot, back_gate_grad[None, None, :], 0.0), axis=2).T
    returned = [dot(from_slot[k], back_rows) for k in range(TOP)]
    upstream = cotangent.astype(jnp.float32)
    output = (
        hidden + sum(returned[k] * gate_probs[:, k : k + 1] for k in range(TOP))
    ).astype(jnp.bfloat16)
    normed_two_grad = dot(from_slot[0] + from_slot[1], back_grad)
    pair_mean = jnp.sum(gate_probs * gate_grad, axis=1, keepdims=True)
    pair_logit = gate_probs * (gate_grad - pair_mean)
    logit_grad = jnp.sum(jnp.where(named, pair_logit[:, :, None], 0.0), axis=1).astype(jnp.bfloat16)
    grad_router = t_dot(normed_two, logit_grad)
    normed_two_grad = normed_two_grad + dot_t(logit_grad, full_router)
    grad_expert_gain = jnp.sum(normed_two_grad * hidden * factor_two, axis=0)
    scaled_two = normed_two_grad * gain_two
    hidden_grad = (
        upstream
        + factor_two * scaled_two
        - hidden * factor_two**3 * jnp.mean(scaled_two * hidden, axis=1, keepdims=True)
    )
    branch_grad = hidden_grad.astype(jnp.bfloat16)
    grad_out_full = t_dot(attended, branch_grad).astype(jnp.bfloat16)
    attended_grad = dot_t(branch_grad, full_out).astype(jnp.bfloat16)

    gradient_heads = attended_grad.reshape(length, KEY_VALUE_HEADS, QUERY_PER_KEY, HEAD_SIZE)
    value_grad = jnp.einsum(
        "kgqs,qkgd->skd", probs_low, gradient_heads, preferred_element_type=jnp.float32
    )
    prob_grad = jnp.einsum(
        "qkgd,skd->kgqs", gradient_heads, heads_of_value, preferred_element_type=jnp.float32
    )
    delta_sum = jnp.sum(soft_probs * prob_grad, axis=-1, keepdims=True)
    score_grad = (soft_probs * (prob_grad - delta_sum)).astype(jnp.bfloat16)
    query_grad = (
        jnp.einsum("kgqs,skd->qkgd", score_grad, heads_of_key, preferred_element_type=jnp.float32)
        * head_scale
    )
    key_grad = (
        jnp.einsum("kgqs,qkgd->skd", score_grad, heads_of_query, preferred_element_type=jnp.float32)
        * head_scale
    )
    qkv_grad = jnp.concatenate(
        [
            query_grad.astype(jnp.bfloat16).reshape(length, cols, width_q),
            key_grad.astype(jnp.bfloat16).reshape(length, cols, width_k),
            value_grad.astype(jnp.bfloat16).reshape(length, cols, width_k),
        ],
        axis=2,
    ).reshape(length, cols * width_a)
    grad_a_full = t_dot(normed, qkv_grad).astype(jnp.bfloat16)
    normed_grad = dot_t(qkv_grad, full_a)
    grad_attn_gain = jnp.sum(normed_grad * rows_f * factor_one, axis=0)
    scaled_one = normed_grad * gain_one
    d_tokens = (
        hidden_grad
        + factor_one * scaled_one
        - rows_f * factor_one**3 * jnp.mean(scaled_one * rows_f, axis=1, keepdims=True)
    )
    grad_s = jnp.concatenate(
        [
            jnp.pad(
                grad_router.reshape(rows, block, cols, router_cols).transpose(0, 2, 3, 1),
                ((0, 0), (0, 0), (0, 0), (0, lane - block)),
            ),
            jnp.pad(
                jnp.stack([grad_attn_gain, grad_expert_gain])
                .reshape(2, rows, cols, piece)
                .transpose(1, 2, 0, 3),
                ((0, 0), (0, 0), (0, 6 - router_cols), (0, lane - piece)),
            ),
        ],
        axis=2,
    )
    grad_a_full, d_tokens, output = lax.optimization_barrier((grad_a_full, d_tokens, output))
    sum_a, sum_out, sum_s = reduce_all(grad_a_full, grad_out_full, grad_s)
    return (
        output,
        d_tokens,
        sum_s[router_cols, :piece],
        sum_a[:, :width_q],
        sum_a[:, width_q : width_q + width_k],
        sum_a[:, width_q + width_k :],
        sum_out,
        sum_s[router_cols + 1, :piece],
        sum_s[:router_cols, :block].T,
        grad_gu[:, :hidden_units].astype(jnp.float32)[None],
        grad_gu[:, hidden_units:].astype(jnp.float32)[None],
        grad_down[None],
    )


def solution(mesh):
    in_specs = (
        P(("row", "col"), None),
        P(("row", "col")),
        P("row", "col"),
        P("row", "col"),
        P("row", "col"),
        P("row", "col"),
        P(("row", "col")),
        P("row", "col"),
        P("row", "col", None),
        P("row", "col", None),
        P("row", "col", None),
        P(("row", "col"), None),
        P(("row", "col"), None),
        P(("row", "col"), None),
    )
    out_specs = (
        P(("row", "col"), None),
        P(("row", "col"), None),
        P(("row", "col")),
        P("row", "col"),
        P("row", "col"),
        P("row", "col"),
        P("row", "col"),
        P(("row", "col")),
        P("row", "col"),
        P("row", "col", None),
        P("row", "col", None),
        P("row", "col", None),
    )
    return jax.shard_map(
        per_device, mesh=mesh, in_specs=in_specs, out_specs=out_specs, check_vma=False
    )
```

```python
import functools

import jax
import jax.numpy as jnp
from jax import lax
from jax.experimental import pallas as pl
from jax.experimental.pallas import tpu as pltpu
from jax.sharding import PartitionSpec as P

KEY_VALUE_HEADS = 8
HEAD_SIZE = 64
TOP = 2
QUERY_PER_KEY = 3


EPSILON = 1e-05
NEGATIVE = -1e30


MESH = pl.DeviceIdType.MESH
ANY = pl.BlockSpec(memory_space=pl.ANY)


def row_at(row, flip):
    y, x, core = row // 4, (row // 2) % 2, row % 2
    return (
        (y + flip // 4) % 2 * 4 + (x + (flip // 2) % 2) % 2 * 2 + (core + flip % 2) % 2
    )


def remote(source, target, send, receive, device):
    return pltpu.make_async_remote_copy(
        source, target, send, receive, device_id=device, device_id_type=MESH
    )


def greet(row_flips, col_steps):
    row, col = lax.axis_index("row"), lax.axis_index("col")
    sem = pltpu.get_barrier_semaphore()
    for flip in row_flips:
        pl.semaphore_signal(
            sem, inc=1, device_id={"row": row_at(row, flip)}, device_id_type=MESH
        )
    for step in col_steps:
        pl.semaphore_signal(
            sem, inc=1, device_id={"col": (col + step) % 4}, device_id_type=MESH
        )
    pl.semaphore_wait(sem, len(row_flips) + len(col_steps))


def unit_order(col, k):
    table = ((0, 1, 2, 3), (1, 0, 2, 3), (2, 3, 1, 0), (3, 2, 1, 0))
    out = table[3][k]
    for c in (2, 1, 0):
        out = jnp.where(col == c, table[c][k], out)
    return out


def unit_at(col, k):
    end = (col == 0) | (col == 3)
    ends = jnp.where(col == 0, k, 3 - k)
    middle = jnp.where(k == 0, col, jnp.where(k == 3, jnp.where(col == 1, 3, 0), jnp.where(col == 1, 2 * k - 2, 5 - 2 * k)))
    return jnp.where(end, ends, middle)


X, Y, SIB = 2, 4, 1


def plane_send(view, row, ss, rs, source=None):
    source = view(row) if source is None else source
    for i, flip in enumerate((X, Y, SIB)):
        remote(source, view(row), ss(i), rs(i), {"row": row_at(row, flip)}).start()


def plane_forward(view, halves, row, ss, rs):
    first, second = halves
    from_x, from_y = row_at(row, X), row_at(row, Y)
    sib = {"row": row_at(row, SIB)}
    remote(view(from_x), view(from_x), ss(0), rs(0), sib).wait_recv()
    remote(first(from_x), first(from_x), ss(3), rs(3), {"row": from_y}).start()
    remote(view(from_x), view(from_x), ss(5), rs(5), sib).start()
    remote(view(from_y), view(from_y), ss(1), rs(1), sib).wait_recv()
    remote(second(from_y), second(from_y), ss(4), rs(4), {"row": from_x}).start()
    remote(view(from_y), view(from_y), ss(6), rs(6), sib).start()


def plane_last(view, halves, row, ss, rs):
    first, second = halves
    diag = row_at(row, X + Y)
    sib = {"row": row_at(row, SIB)}
    remote(first(diag), first(diag), ss(3), rs(3), sib).wait_recv()
    remote(first(diag), first(diag), ss(7), rs(7), sib).start()
    remote(second(diag), second(diag), ss(4), rs(4), sib).wait_recv()
    remote(second(diag), second(diag), ss(8), rs(8), sib).start()


def plane_finish(view, halves, row, ss, rs):
    first, second = halves
    sib_row = row_at(row, SIB)
    sib = {"row": sib_row}
    whole = view(sib_row)
    remote(whole, whole, ss(2), rs(2), sib).wait_recv()
    for i, flip in ((5, X), (6, Y)):
        block = view(row_at(sib_row, flip))
        remote(block, block, ss(i), rs(i), sib).wait_recv()
    far = row_at(sib_row, X + Y)
    remote(first(far), first(far), ss(7), rs(7), sib).wait_recv()
    remote(second(far), second(far), ss(8), rs(8), sib).wait_recv()
    for i in range(9):
        block = view(row) if i in (0, 1, 2, 5, 6) else (first(row) if i in (3, 7) else second(row))
        remote(block, block, ss(i), rs(i), sib).wait_send()


def pick(ref, cols, halves_rows):
    block, cut = halves_rows

    def at(start, size):
        def view(r):
            rows = pl.ds(pl.multiple_of(r * block + start, 16), size)
            if cols is None:
                return ref.at[rows, :]
            return ref.at[rows, pl.ds(pl.multiple_of(cols[0], 128), cols[1])]

        return view

    return at(0, block), (at(0, cut), at(cut, block - cut))


def through(source, middle, target, sem):
    return pltpu.make_async_copy(source, middle, sem), pltpu.make_async_copy(middle, target, sem)


def through(source, middle, target, sem):
    return pltpu.make_async_copy(source, middle, sem), pltpu.make_async_copy(middle, target, sem)


def line_kernel(own_a, own_b, own_s, own_c, line_a, line_b, full_s, full_c, mid_a, mid_b, mid_c,
                zss, zrs, css, crs, s_zs, s_zr, s_ps, s_pr, loc):
    row, col = lax.axis_index("row"), lax.axis_index("col")
    width_a, width_b = own_a.shape[1], own_b.shape[1]
    rows_c = own_c.shape[0]
    vc, hc = pick(full_c, None, (rows_c, rows_c // 2))
    csv, crv = (lambda i: css.at[i]), (lambda i: crs.at[i])

    def of_a(c):
        return line_a.at[:, pl.ds(pl.multiple_of(c * width_a, 128), width_a)]

    def of_b(c):
        return line_b.at[:, pl.ds(pl.multiple_of(c * width_b, 128), width_b)]

    copies = [
        through(own_a, mid_a, of_a(col), loc.at[0]),
        through(own_b, mid_b, of_b(col), loc.at[1]),
        through(own_c, mid_c, vc(row), loc.at[2]),
    ]
    for copy, _ in copies:
        copy.start()
    small_copy = pltpu.make_async_copy(own_s, full_s.at[col, row], loc.at[3])
    small_copy.start()
    greet(range(1, 8), (1, 2, 3))

    def along(c, source_a, source_b, right, left):
        for d, (cond, step) in enumerate(((right, 1), (left, 3))):
            @pl.when(cond)
            def _():
                there = {"col": (col + step) % 4}
                remote(source_a, of_a(c), zss.at[0, c, d], zrs.at[0, c], there).start()
                remote(source_b, of_b(c), zss.at[1, c, d], zrs.at[1, c], there).start()

    def arrived(k):
        c = unit_order(col, k)
        there = {"col": (col + 1) % 4}
        remote(of_a(c), of_a(c), zss.at[0, c, 0], zrs.at[0, c], there).wait_recv()
        remote(of_b(c), of_b(c), zss.at[1, c, 0], zrs.at[1, c], there).wait_recv()
        along(c, of_a(c), of_b(c), (c < col) & (col < 3), (c > col) & (col > 0))

    along(col, own_a, own_b, col < 3, col > 0)
    for i, step in enumerate((1, 2, 3)):
        remote(own_s, full_s.at[col, row], s_zs.at[i], s_zr.at[i], {"col": (col + step) % 4}).start()
    plane_send(vc, row, csv, crv, own_c)
    for first, second in copies:
        first.wait()
        second.start()
    small_copy.wait()
    arrived(1)
    for i, step in enumerate((3, 2, 1)):
        remote(own_s, full_s.at[(col + step) % 4, row], s_zs.at[i], s_zr.at[i], {"col": (col + 1) % 4}).wait()
    for i in range(1, 8):
        remote(full_s.at[:, row], full_s.at[:, row], s_ps.at[i - 1], s_pr.at[i - 1], {"row": row_at(row, i)}).start()
    arrived(2)
    plane_forward(vc, hc, row, csv, crv)
    arrived(3)
    plane_last(vc, hc, row, csv, crv)
    for _, second in copies:
        second.wait()
    plane_finish(vc, hc, row, csv, crv)
    for i in range(1, 8):
        there = row_at(row, i)
        remote(full_s.at[:, there], full_s.at[:, there], s_ps.at[i - 1], s_pr.at[i - 1], {"row": there}).wait()
    for k in range(4):
        c = unit_order(col, k)
        right = (c <= col) & (col < 3)
        left = (c >= col) & (col > 0)
        for d, cond in enumerate((right, left)):
            @pl.when(cond)
            def _():
                there = {"col": (col + 1) % 4}
                remote(of_a(c), of_a(c), zss.at[0, c, d], zrs.at[0, c], there).wait_send()
                remote(of_b(c), of_b(c), zss.at[1, c, d], zrs.at[1, c], there).wait_send()


def gather_line(own_a, own_b, own_s, own_c):
    sems = pltpu.SemaphoreType.DMA
    rows_c = own_c.shape[0]
    return pl.pallas_call(
        line_kernel,
        out_shape=(
            jax.ShapeDtypeStruct((own_a.shape[0], own_a.shape[1] * 4), own_a.dtype),
            jax.ShapeDtypeStruct((own_b.shape[0], own_b.shape[1] * 4), own_b.dtype),
            jax.ShapeDtypeStruct((4, 8) + own_s.shape, own_s.dtype),
            jax.ShapeDtypeStruct((8 * rows_c, own_c.shape[1]), own_c.dtype),
        ),
        in_specs=[ANY] * 4,
        out_specs=(ANY,) * 4,
        scratch_shapes=[
            pltpu.VMEM(own_a.shape, own_a.dtype),
            pltpu.VMEM(own_b.shape, own_b.dtype),
            pltpu.VMEM(own_c.shape, own_c.dtype),
            sems((2, 4, 2)), sems((2, 4)),
            sems((9,)), sems((9,)),
            sems((3,)), sems((3,)), sems((7,)), sems((7,)), sems((4,)),
        ],
        compiler_params=pltpu.CompilerParams(collective_id=0, has_side_effects=True),
        cost_estimate=pl.CostEstimate(flops=0, bytes_accessed=1_000_000, transcendentals=0),
    )(own_a, own_b, own_s, own_c)


def plane_kernel(count, *refs):
    row = lax.axis_index("row")
    owns, fulls, mids = refs[:count], refs[count : 2 * count], refs[2 * count : 3 * count]
    ss, rs, loc = refs[3 * count :]
    views, copies = [], []
    for i in range(count):
        block = owns[i].shape[0]
        views.append(pick(fulls[i], None, (block, block // 2)))
        copies.append(through(owns[i], mids[i], views[i][0](row), loc.at[i]))
        copies[i][0].start()
    greet(range(1, 8), ())

    def sems_of(i):
        return (lambda j: ss.at[i, j]), (lambda j: rs.at[i, j])

    for i in range(count):
        plane_send(views[i][0], row, *sems_of(i), owns[i])
    for first, second in copies:
        first.wait()
        second.start()
    for i in range(count):
        plane_forward(*views[i], row, *sems_of(i))
    for i in range(count):
        plane_last(*views[i], row, *sems_of(i))
    for _, second in copies:
        second.wait()
    for i in range(count):
        plane_finish(*views[i], row, *sems_of(i))


def gather_plane(collective, owns):
    sems = pltpu.SemaphoreType.DMA
    count = len(owns)
    return pl.pallas_call(
        functools.partial(plane_kernel, count),
        out_shape=tuple(
            jax.ShapeDtypeStruct((8 * own.shape[0], own.shape[1]), own.dtype) for own in owns
        ),
        in_specs=[ANY] * count,
        out_specs=(ANY,) * count,
        scratch_shapes=[pltpu.VMEM(own.shape, own.dtype) for own in owns]
        + [sems((count, 9)), sems((count, 9)), sems((count,))],
        compiler_params=pltpu.CompilerParams(collective_id=collective, has_side_effects=True),
        cost_estimate=pl.CostEstimate(flops=0, bytes_accessed=1_000_000, transcendentals=0),
    )(*owns)


def spread_kernel(own_c, own_g, full_c, full_g, mid_c, css, crs, gss, grs, loc):
    row = lax.axis_index("row")
    rows_c = own_c.shape[0]
    vc, hc = pick(full_c, None, (rows_c, rows_c // 2))
    csv, crv = (lambda i: css.at[i]), (lambda i: crs.at[i])
    first, second = through(own_c, mid_c, vc(row), loc.at[0])
    first.start()
    own_copy = pltpu.make_async_copy(own_g, full_g.at[row], loc.at[1])
    own_copy.start()
    greet(range(1, 8), ())
    plane_send(vc, row, csv, crv, own_c)
    for i in range(1, 8):
        remote(own_g, full_g.at[row], gss.at[i - 1], grs.at[i - 1], {"row": row_at(row, i)}).start()
    first.wait()
    second.start()
    plane_forward(vc, hc, row, csv, crv)
    plane_last(vc, hc, row, csv, crv)
    second.wait()
    own_copy.wait()
    plane_finish(vc, hc, row, csv, crv)
    for i in range(1, 8):
        there = row_at(row, i)
        remote(own_g, full_g.at[there], gss.at[i - 1], grs.at[i - 1], {"row": there}).wait()


def spread_tokens(own_c, own_g):
    sems = pltpu.SemaphoreType.DMA
    return pl.pallas_call(
        spread_kernel,
        out_shape=(
            jax.ShapeDtypeStruct((8 * own_c.shape[0], own_c.shape[1]), own_c.dtype),
            jax.ShapeDtypeStruct((8,) + own_g.shape, own_g.dtype),
        ),
        in_specs=[ANY] * 2,
        out_specs=(ANY,) * 2,
        scratch_shapes=[
            pltpu.VMEM(own_c.shape, own_c.dtype),
            sems((9,)), sems((9,)), sems((7,)), sems((7,)), sems((2,)),
        ],
        compiler_params=pltpu.CompilerParams(collective_id=1, has_side_effects=True),
        cost_estimate=pl.CostEstimate(flops=0, bytes_accessed=1_000_000, transcendentals=0),
    )(own_c, own_g)


def add_into(target, term):
    def body(i, carry):
        rows = pl.ds(pl.multiple_of(i * 32, 32), 32)
        total = target[rows, :].astype(jnp.float32) + term[rows, :].astype(jnp.float32)
        target[rows, :] = total.astype(target.dtype)
        return carry
    lax.fori_loop(0, target.shape[0] // 32, body, 0)


def expert_kernel(key, mine, normed_hbm, upstream_hbm, gu_hbm, own_down,
                  in_ref, prod_ref, gate_grad_out, grad_gu, sum_down,
                  gate_grad_ref, x_t, ups, gu, down, act, silu, slope, both, gd, rec_right, rec_left, stage, gate,
                  load_sem, src_sem, stage_sem, zss, zrs, rss, rrs):
    col = lax.axis_index("col")
    sources, _, length = key.shape
    slots = in_ref.shape[0]
    capacity = slots // sources
    units = gu.shape[1] // 2
    width = units // 4
    chunk = 256
    x = in_ref
    right_dev, left_dev = {"col": (col + 1) % 4}, {"col": (col + 3) % 4}

    load_gu = pltpu.make_async_copy(gu_hbm, gu, load_sem.at[0])
    load_gu.start()
    load_down = pltpu.make_async_copy(own_down, down.at[col], load_sem.at[1])
    load_down.start()

    def fetch(s, slot):
        rows = pl.ds(pl.multiple_of(s * length, 16), length)
        for i, hbm in enumerate((normed_hbm, upstream_hbm)):
            to = prod_ref.at[pl.ds(pl.multiple_of((slot * 2 + i) * length, 16), length), :]
            yield pltpu.make_async_copy(hbm.at[rows, :], to, src_sem.at[slot, i])

    for copy in fetch(0, 0):
        copy.start()
    greet((), (1, 2, 3))

    def pass_on(c, source, right, left):
        for d, (cond, there) in enumerate(((right, right_dev), (left, left_dev))):
            @pl.when(cond)
            def _():
                remote(source, down.at[c], zss.at[c, d], zrs.at[c], there).start()

    pass_on(col, own_down, col < 3, col > 0)

    def ag_step(s):
        @pl.when(col >= s)
        def _():
            c = col - s
            remote(down.at[c], down.at[c], zss.at[c, 0], zrs.at[c], right_dev).wait_recv()
            @pl.when(col < 3)
            def _():
                remote(down.at[c], down.at[c], zss.at[c, 0], zrs.at[c], right_dev).start()
        @pl.when(col + s < 4)
        def _():
            c = col + s
            remote(down.at[c], down.at[c], zss.at[c, 1], zrs.at[c], left_dev).wait_recv()
            @pl.when(col > 0)
            def _():
                remote(down.at[c], down.at[c], zss.at[c, 1], zrs.at[c], left_dev).start()

    def to_right(d):
        target = rec_right.at[d - 1]
        return remote(target, target, rss.at[0, d - 1], rrs.at[0, d - 1], right_dev)

    def to_left(d):
        target = rec_left.at[d]
        return remote(target, target, rss.at[1, d], rrs.at[1, d], left_dev)

    def from_end(d):
        @pl.when((col == 0) & (d > 0))
        def _():
            remote(gd.at[d], rec_right.at[d - 1], rss.at[0, d - 1], rrs.at[0, d - 1], right_dev).start()
        @pl.when((col == 3) & (d < 3))
        def _():
            remote(gd.at[d], rec_left.at[d], rss.at[1, d], rrs.at[1, d], left_dev).start()

    def add_rows(target, term):
        def body(i, carry):
            rows = pl.ds(pl.multiple_of(i * 64, 64), 64)
            total = target[rows, :].astype(jnp.float32) + term[rows, :].astype(jnp.float32)
            target[rows, :] = total.astype(target.dtype)
            return carry
        lax.fori_loop(0, width // 64, body, 0)

    def hop_right(d):
        to_right(d).wait_recv()
        add_rows(rec_right.at[d - 1], gd.at[d])
        to_right(d).start()

    def hop_left(d):
        to_left(d).wait_recv()
        add_rows(rec_left.at[d], gd.at[d])
        to_left(d).start()

    def select(s, carry):
        slot = s % 2
        @pl.when(s + 1 < sources)
        def _():
            for copy in fetch(s + 1, 1 - slot):
                copy.start()
        for copy in fetch(s, slot):
            copy.wait()
        chosen = key[s] == lax.broadcasted_iota(jnp.int32, (capacity, length), 0)
        value = jnp.sum(jnp.where(chosen, mine[s], 0.0), axis=1, keepdims=True)
        rows = pl.ds(pl.multiple_of(s * capacity, 16), capacity)
        gate[rows, :] = jnp.broadcast_to(value, (capacity, gate.shape[1]))
        one_hot = jnp.where(chosen, 1.0, 0.0).astype(x.dtype)
        for i, target in enumerate((x, ups)):
            block = prod_ref[pl.ds(pl.multiple_of((slot * 2 + i) * length, 16), length), :]
            target[rows, :] = dot(one_hot, block).astype(target.dtype)
        return carry
    lax.fori_loop(0, sources, select, 0)

    load_gu.wait()

    def forward(c):
        first = pl.ds(pl.multiple_of(c * width, width), width)
        second = pl.ds(pl.multiple_of(units + c * width, width), width)
        def body(m, carry):
            rows = pl.ds(pl.multiple_of(m * chunk, chunk), chunk)
            gate_pre = dot(x[rows, :], gu[:, first])
            up_pre = dot(x[rows, :], gu[:, second])
            sigma = jax.nn.sigmoid(gate_pre)
            silu_gate = gate_pre * sigma
            silu[rows, first] = silu_gate
            slope[rows, first] = up_pre * sigma * (1.0 + gate_pre * (1.0 - sigma))
            low = (silu_gate * up_pre).astype(act.dtype)
            act[rows, first] = low
            both[rows, first] = (low.astype(jnp.float32) * gate[rows, 0:1]).astype(both.dtype)
            return carry
        lax.fori_loop(0, slots // chunk, body, 0)
        gd[c] = t_dot(both[:, first], ups[...]).astype(gd.dtype)

    def forward_step(i, carry):
        c = jnp.where(i < 2, 3 - 3 * i, 4 - i)
        forward(c)
        pl.when((i < 2) | (col == 0))(lambda: from_end(c))
        pl.when(i == 1)(lambda: ag_step(1))
        @pl.when((i == 3) & (col == 3))
        def _():
            from_end(1)
            from_end(2)
        return carry
    lax.fori_loop(0, 4, forward_step, 0)
    load_down.wait()

    def turn(m, carry):
        rows = pl.ds(pl.multiple_of(m * chunk, chunk), chunk)
        x_t[:, rows] = x[rows, :].T
        return carry
    lax.fori_loop(0, slots // chunk, turn, 0)
    gate_grad_ref[...] = jnp.zeros_like(gate_grad_ref)

    def out_stage(c, slot):
        for i in range(2):
            yield pltpu.make_async_copy(
                stage.at[slot, :, pl.ds(i * width, width)],
                grad_gu.at[:, pl.ds(pl.multiple_of(i * units + c * width, width), width)],
                stage_sem.at[slot, i],
            )

    def backward(k):
        c = unit_at(col, k)
        first = pl.ds(pl.multiple_of(c * width, width), width)
        second = pl.ds(pl.multiple_of(units + c * width, width), width)
        def body(m, carry):
            rows = pl.ds(pl.multiple_of(m * chunk, chunk), chunk)
            plain = dot_t(ups[rows, :], down[c])
            term = jnp.sum(act[rows, first].astype(jnp.float32) * plain, axis=1, keepdims=True)
            gate_grad_ref[rows, :] += jnp.broadcast_to(term, (chunk, gate_grad_ref.shape[1]))
            act_grad = plain * gate[rows, 0:1]
            both[rows, first] = (act_grad * slope[rows, first]).astype(both.dtype)
            both[rows, second] = (act_grad * silu[rows, first]).astype(both.dtype)
            return carry
        lax.fori_loop(0, slots // chunk, body, 0)
        slot = k % 2
        @pl.when(k >= 2)
        def _():
            for copy in out_stage(unit_at(col, k - 2), slot):
                copy.wait()
        def grads(i, carry):
            rows = pl.ds(pl.multiple_of(i * chunk, chunk), chunk)
            stage[slot, rows, 0:width] = dot(x_t[rows, :], both[:, first]).astype(stage.dtype)
            stage[slot, rows, width : 2 * width] = dot(x_t[rows, :], both[:, second]).astype(stage.dtype)
            return carry
        lax.fori_loop(0, x_t.shape[0] // chunk, grads, 0)
        for copy in out_stage(c, slot):
            copy.start()

    def backward_step(k, carry):
        backward(k)
        pl.when(k == 0)(lambda: ag_step(2))
        pl.when((k == 0) & (col == 1))(lambda: hop_right(3))
        pl.when((k == 0) & (col == 2))(lambda: hop_left(0))
        pl.when(k == 2)(lambda: ag_step(3))
        @pl.when((k == 2) & (col == 1))
        def _():
            hop_right(2)
            hop_left(0)
        @pl.when((k == 2) & (col == 2))
        def _():
            hop_right(3)
            hop_left(1)
        return carry
    lax.fori_loop(0, 4, backward_step, 0)

    def inputs(m, carry):
        rows = pl.ds(pl.multiple_of(m * chunk, chunk), chunk)
        in_ref[rows, :] = dot_t(both[rows, :], gu[...]).astype(in_ref.dtype)
        return carry
    lax.fori_loop(0, slots // chunk, inputs, 0)

    def outputs(m, carry):
        rows = pl.ds(pl.multiple_of(m * chunk, chunk), chunk)
        total = dot(act[rows, 0:width], down[0])
        for c in range(1, 4):
            total = total + dot(act[rows, c * width : (c + 1) * width], down[c])
        prod_ref[rows, :] = total.astype(prod_ref.dtype)
        return carry
    lax.fori_loop(0, slots // chunk, outputs, 0)

    turned = gate_grad_ref[...].T
    for s in range(sources):
        gate_grad_out[s] = turned[0:1, s * capacity : (s + 1) * capacity]
    for k in (2, 3):
        for copy in out_stage(unit_at(col, k), k % 2):
            copy.wait()
    pl.when(col > 0)(lambda: to_right(col).wait_recv())
    pl.when(col < 3)(lambda: to_left(col).wait_recv())

    def to_sum(i, carry):
        rows = pl.ds(pl.multiple_of(i * 64, 64), 64)
        sum_down[rows, :] = gd[col, rows, :].astype(jnp.float32)
        @pl.when(col > 0)
        def _():
            sum_down[rows, :] += rec_right[jnp.maximum(col - 1, 0), rows, :].astype(jnp.float32)
        @pl.when(col < 3)
        def _():
            sum_down[rows, :] += rec_left[jnp.minimum(col, 2), rows, :].astype(jnp.float32)
        return carry
    lax.fori_loop(0, width // 64, to_sum, 0)

    def sent(e, carry):
        pl.when(e > col)(lambda: to_right(e).wait_send())
        pl.when(e < col)(lambda: to_left(e).wait_send())
        @pl.when((col < 3) & (e <= col))
        def _():
            remote(down.at[e], down.at[e], zss.at[e, 0], zrs.at[e], right_dev).wait_send()
        @pl.when((col > 0) & (e >= col))
        def _():
            remote(down.at[e], down.at[e], zss.at[e, 1], zrs.at[e], left_dev).wait_send()
        return carry
    lax.fori_loop(0, 4, sent, 0)


def run_expert(key, mine, normed, upstream, full_gu, own_down):
    sources, length = key.shape
    model, units = full_gu.shape[0], full_gu.shape[1] // 2
    width = own_down.shape[0]
    slots = sources * length // 2
    low, f32 = normed.dtype, jnp.float32
    sems = pltpu.SemaphoreType.DMA
    vm = pl.BlockSpec(memory_space=pltpu.VMEM)
    return pl.pallas_call(
        expert_kernel,
        out_shape=(
            jax.ShapeDtypeStruct((slots, model), low),
            jax.ShapeDtypeStruct((slots, model), low),
            jax.ShapeDtypeStruct((sources, 1, slots // sources), f32),
            jax.ShapeDtypeStruct((model, 2 * units), low),
            jax.ShapeDtypeStruct((width, model), f32),
        ),
        in_specs=[vm, vm, ANY, ANY, ANY, ANY],
        out_specs=(vm, vm, vm, ANY, vm),
        scratch_shapes=[
            pltpu.VMEM((slots, 128), f32),
            pltpu.VMEM((model, slots), low),
            pltpu.VMEM((slots, model), low),
            pltpu.VMEM((model, 2 * units), low),
            pltpu.VMEM((4, width, model), low),
            pltpu.VMEM((slots, units), low),
            pltpu.VMEM((slots, units), f32),
            pltpu.VMEM((slots, units), f32),
            pltpu.VMEM((slots, 2 * units), low),
            pltpu.VMEM((4, width, model), low),
            pltpu.VMEM((3, width, model), low),
            pltpu.VMEM((3, width, model), low),
            pltpu.VMEM((2, model, 2 * width), low),
            pltpu.VMEM((slots, 128), f32),
            sems((2,)), sems((2, 2)), sems((2, 2)),
            sems((4, 2)), sems((4,)), sems((2, 3)), sems((2, 3)),
        ],
        compiler_params=pltpu.CompilerParams(
            collective_id=4, has_side_effects=True, vmem_limit_bytes=60 * 2**20
        ),
        cost_estimate=pl.CostEstimate(flops=0, bytes_accessed=1_000_000, transcendentals=0),
    )(key.reshape(sources, 1, length), mine.reshape(sources, 1, length), normed, upstream, full_gu, own_down)


def backward_kernel(slot_of, gates, ids, router_p, gain_one, gain_two, lse, seg_row, seg_col,
                    gate_grad, in_grad, produced, hidden_hbm, tokens_hbm, cot_hbm, normed_hbm, attended_hbm,
                    two_hbm, qkv_hbm, full_a_hbm, full_out_hbm,
                    out_ref, d_tokens, sum_a, sum_b, sum_s,
                    rec_in, rec_gate, rec_prod, hidden, tokens, cot, two, qkv, full_a, full_out,
                    n_t, a_t, branch, bias, out_rows, grad_c, qg, lgs, small,
                    own, sib_out, rec_sib, rec_one, rec_two, rec_z, s_rec, s_mid, s_zrec,
                    load, in_ss, in_rs, g_ss, g_rs, pr_ss, pr_rs, loc,
                    ss1, rs1, ss2, rs2, zss, zrs, s_ss, s_rs, sz_ss, sz_rs):
    row, col = lax.axis_index("row"), lax.axis_index("col")
    core = row % 2
    chip = row // 2
    cy, cx = chip // 2, chip % 2
    length, model = hidden.shape
    capacity = rec_in.shape[0] // 8
    block = own.shape[2]
    width_a, width_b = sum_a.shape[1], sum_b.shape[1]
    cut = block // 2
    half = length // 2
    f32, low = jnp.float32, branch.dtype
    sib = {"row": row_at(row, SIB)}
    to_x, to_y = {"row": row_at(row, X)}, {"row": row_at(row, Y)}

    def each_flip(function):
        def body(i, carry):
            function(7 - i)
            return carry
        lax.fori_loop(0, 7, body, 0)

    def block_of(r):
        return pl.ds(pl.multiple_of(r * capacity, 16), capacity)

    own_in = pltpu.make_async_copy(in_grad.at[block_of(row), :], rec_in.at[block_of(row), :], loc.at[0])
    own_gate = pltpu.make_async_copy(gate_grad.at[row], rec_gate.at[row], loc.at[1])
    own_prod = pltpu.make_async_copy(produced.at[block_of(row), :], rec_prod.at[block_of(row), :], loc.at[2])
    loads = [
        pltpu.make_async_copy(source, target, load.at[i])
        for i, (source, target) in enumerate((
            (normed_hbm, branch), (attended_hbm, out_ref), (hidden_hbm, hidden), (cot_hbm, cot), (two_hbm, two),
            (qkv_hbm, qkv), (tokens_hbm, tokens), (full_out_hbm, full_out), (full_a_hbm, full_a),
        ))
    ]
    greet(range(1, 8), (1, 2, 3))

    def back(flip):
        there = row_at(row, flip)
        device = {"row": there}
        return (
            remote(in_grad.at[block_of(there), :], rec_in.at[block_of(row), :],
                   in_ss.at[flip - 1], in_rs.at[flip - 1], device),
            remote(gate_grad.at[there], rec_gate.at[row], g_ss.at[flip - 1], g_rs.at[flip - 1], device),
        )

    def back_prod(flip):
        there = row_at(row, flip)
        return remote(produced.at[block_of(there), :], rec_prod.at[block_of(row), :],
                      pr_ss.at[flip - 1], pr_rs.at[flip - 1], {"row": there})

    each_flip(lambda flip: [copy.start() for copy in back(flip)])
    for copy in (own_in, own_gate, own_prod):
        copy.start()
    for copy in loads:
        copy.start()
    loads[0].wait()
    n_t[...] = branch[...].T
    loads[1].wait()
    a_t[...] = out_ref[...].T
    key_pos = lax.broadcasted_iota(jnp.int32, (length, length), 0)
    query_pos = lax.broadcasted_iota(jnp.int32, (length, length), 1)
    allowed = (key_pos <= query_pos) & (seg_col[...] == seg_row[...])
    bias[...] = jnp.where(allowed, 0.0, NEGATIVE)
    small[...] = jnp.zeros_like(small)
    for copy in loads[2:]:
        copy.wait()
    for copy in (own_in, own_gate):
        copy.wait()
    each_flip(lambda flip: [copy.wait_recv() for copy in back(flip)])
    each_flip(lambda flip: back_prod(flip).start())

    all_gate = jnp.concatenate([rec_gate[e] for e in range(8)], axis=1)
    wide = rec_in.shape[0]
    lanes = lgs.shape[1]

    def at_slot(rows, k):
        return slot_of[rows, k : k + 1] == lax.broadcasted_iota(jnp.int32, (half, wide), 1)

    def to_hidden(m, carry):
        rows = pl.ds(pl.multiple_of(m * half, half), half)
        first, second = at_slot(rows, 0), at_slot(rows, 1)
        picked = jnp.where(first | second, 1.0, 0.0).astype(low)
        two_grad = dot(picked, rec_in[...])
        grad_0 = jnp.sum(jnp.where(first, all_gate, 0.0), axis=1, keepdims=True)
        grad_1 = jnp.sum(jnp.where(second, all_gate, 0.0), axis=1, keepdims=True)
        gate_0, gate_1 = gates[rows, 0:1], gates[rows, 1:2]
        mean = gate_0 * grad_0 + gate_1 * grad_1
        lane = lax.broadcasted_iota(jnp.int32, (half, lanes), 1)
        logit_grad = jnp.where(lane == ids[rows, 0:1], gate_0 * (grad_0 - mean), 0.0)
        logit_grad = logit_grad + jnp.where(lane == ids[rows, 1:2], gate_1 * (grad_1 - mean), 0.0)
        logit_grad = logit_grad.astype(low)
        lgs[rows, :] = logit_grad
        two_grad = two_grad + dot_t(logit_grad, router_p[...])
        h = hidden[rows, :]
        factor = lax.rsqrt(jnp.mean(h * h, axis=1, keepdims=True) + EPSILON)
        small[9:10, :] += jnp.sum(two_grad * h * factor, axis=0, keepdims=True)
        scaled = two_grad * gain_two[...]
        inner = jnp.mean(scaled * h, axis=1, keepdims=True)
        grad = cot[rows, :].astype(f32) + factor * scaled - h * (factor * factor * factor * inner)
        d_tokens[rows, :] = grad
        branch[rows, :] = grad.astype(low)
        return carry
    lax.fori_loop(0, 2, to_hidden, 0)
    small[0:8, :] = t_dot(lgs[...], two[...])[0:8, :]

    def nth(k):
        return (col + 1 + k) % 4

    lanes_of = {"a": pl.ds(0, width_a), "b": pl.ds(width_a, width_b)}
    part_at = {"a": 0, "b": 1}

    def to_sibling(part, c, q):
        view = lanes_of[part]
        i = part_at[part]
        return remote(sib_out.at[c, q, :, view], rec_sib.at[c, q, :, view], ss1.at[c, q, i], rs1.at[c, q, i], sib)

    def weight_grads(part, c, left, right):
        view = lanes_of[part]
        def body(q, carry):
            theirs = pl.ds(pl.multiple_of((q * 2 + 1 - core) * block, 16), block)
            sib_out[c, q, :, view] = dot(left[theirs, :], right()).astype(low)
            to_sibling(part, c, q).start()
            mine = pl.ds(pl.multiple_of((q * 2 + core) * block, 16), block)
            own[c, q, :, view] = dot(left[mine, :], right()).astype(low)
            return carry
        lax.fori_loop(0, 4, body, 0)

    def cols_b(c):
        return pl.ds(pl.multiple_of(c * width_b, 128), width_b)

    def attend_back(c):
        span_c = width_b // QUERY_PER_KEY
        for i in range(QUERY_PER_KEY):
            for u in range(2):
                rows = pl.ds(pl.multiple_of(c * width_b + (u * QUERY_PER_KEY + i) * HEAD_SIZE, HEAD_SIZE), HEAD_SIZE)
                out_rows[(2 * i + u) * HEAD_SIZE : (2 * i + u + 1) * HEAD_SIZE, :] = full_out[rows, :]
        grad_c[...] = dot_t(branch[...], out_rows[...]).astype(low)
        at_c = pl.multiple_of(c * width_a, 128)
        key = qkv[:, pl.ds(at_c + width_b, span_c)]
        value = qkv[:, pl.ds(at_c + width_b + span_c, span_c)]
        first = lax.broadcasted_iota(jnp.int32, (length, span_c), 1) < HEAD_SIZE
        none = jnp.zeros_like(key)
        keys = (jnp.where(first, key, none), jnp.where(first, none, key))
        values = (jnp.where(first, value, none), jnp.where(first, none, value))
        scale = HEAD_SIZE ** (-0.5)
        key_grads = [jnp.zeros((length, span_c), f32) for _ in range(2)]
        value_grads = [jnp.zeros((length, span_c), f32) for _ in range(2)]
        for i in range(QUERY_PER_KEY):
            q_i = qkv[:, pl.ds(at_c + i * span_c, span_c)]
            g_i = grad_c[:, i * span_c : (i + 1) * span_c]
            q_grad = jnp.zeros((length, span_c), f32)
            for u in range(2):
                log_total = lse[c * 2 + u, :, i * length : (i + 1) * length]
                probs = jnp.exp(dot_t(keys[u], q_i) * scale + bias[...] - log_total)
                prob_grad = dot_t(values[u], g_i)
                delta = jnp.sum(probs * prob_grad, axis=0, keepdims=True)
                score_grad = (probs * (prob_grad - delta)).astype(low)
                value_grads[u] += dot(probs.astype(low), g_i)
                key_grads[u] += dot(score_grad, q_i)
                q_grad += t_dot(score_grad, keys[u])
            qg[c, :, i * span_c : (i + 1) * span_c] = (q_grad * scale).astype(low)
        key_grad = jnp.where(first, key_grads[0], key_grads[1]) * scale
        qg[c, :, width_b : width_b + span_c] = key_grad.astype(low)
        qg[c, :, width_b + span_c : width_a] = jnp.where(first, value_grads[0], value_grads[1]).astype(low)

    top, bottom = pl.ds(0, cut), pl.ds(cut, block - cut)

    def one(part, c):
        view, i = lanes_of[part], part_at[part]
        for j in range(2):
            yield remote(own.at[c, j * 2 + 1 - cx, top, view], rec_one.at[c, 0, j, :, view],
                         ss2.at[c, i, 0, j], rs2.at[c, i, 0, j], to_x)
            yield remote(own.at[c, (1 - cy) * 2 + j, bottom, view], rec_one.at[c, 1, j, :, view],
                         ss2.at[c, i, 1, j], rs2.at[c, i, 1, j], to_y)

    def two_step(part, c):
        view, i = lanes_of[part], part_at[part]
        yield remote(own.at[c, (1 - cy) * 2 + cx, top, view], rec_two.at[c, 0, :, view],
                     ss2.at[c, i, 0, 2], rs2.at[c, i, 0, 2], to_y)
        yield remote(own.at[c, cy * 2 + 1 - cx, bottom, view], rec_two.at[c, 1, :, view],
                     ss2.at[c, i, 1, 2], rs2.at[c, i, 1, 2], to_x)

    def column(part, step):
        there = (col + step) % 4
        view, i = lanes_of[part], part_at[part]
        return remote(own.at[there, chip, :, view], rec_z.at[step - 1, :, view],
                      zss.at[i, step - 1], zrs.at[i, step - 1], {"col": there})

    def stage_one(part, k):
        c, view = nth(k), lanes_of[part]
        def body(q, carry):
            to_sibling(part, c, q).wait_recv()
            add_into(own.at[c, q, :, view], rec_sib.at[c, q, :, view])
            return carry
        lax.fori_loop(0, 4, body, 0)
        for copy in one(part, c):
            copy.start()

    def stage_two(part, k):
        c, view = nth(k), lanes_of[part]
        for copy in one(part, c):
            copy.wait_recv()
        for j in range(2):
            add_into(own.at[c, j * 2 + cx, top, view], rec_one.at[c, 0, j, :, view])
            add_into(own.at[c, cy * 2 + j, bottom, view], rec_one.at[c, 1, j, :, view])
        for copy in two_step(part, c):
            copy.start()

    def stage_three(part, k):
        c, view = nth(k), lanes_of[part]
        for copy in two_step(part, c):
            copy.wait_recv()
        add_into(own.at[c, chip, top, view], rec_two.at[c, 0, :, view])
        add_into(own.at[c, chip, bottom, view], rec_two.at[c, 1, :, view])
        pl.when(k < 3)(lambda: column(part, k + 1).start())

    def out_grads(k, carry):
        c = nth(k)
        weight_grads("b", c, a_t, lambda: branch[:, cols_b(c)])
        pl.when(k >= 1)(lambda: stage_one("b", k - 1))
        pl.when(k >= 2)(lambda: stage_two("b", k - 2))
        pl.when(k >= 3)(lambda: stage_three("b", k - 3))
        return carry
    lax.fori_loop(0, 4, out_grads, 0)

    def input_grads(k, carry):
        c = nth(k)
        attend_back(c)
        weight_grads("a", c, n_t, lambda: qg[c])
        pl.when(k == 0)(lambda: stage_one("b", k + 3))
        pl.when(k >= 1)(lambda: stage_one("a", k - 1))
        pl.when(k <= 1)(lambda: stage_two("b", k + 2))
        pl.when(k >= 2)(lambda: stage_two("a", k - 2))
        pl.when(k <= 2)(lambda: stage_three("b", k + 1))
        pl.when(k >= 3)(lambda: stage_three("a", k - 3))
        return carry
    lax.fori_loop(0, 4, input_grads, 0)
    stage_one("a", 3)
    stage_two("a", 2)
    stage_three("a", 1)

    def to_tokens(m, carry):
        rows = pl.ds(pl.multiple_of(m * half, half), half)
        grad = dot_t(qg[0, rows, :], full_a[:, 0:width_a])
        for c in range(1, 4):
            grad = grad + dot_t(qg[c, rows, :], full_a[:, c * width_a : (c + 1) * width_a])
        x = tokens[rows, :].astype(f32)
        factor = lax.rsqrt(jnp.mean(x * x, axis=1, keepdims=True) + EPSILON)
        small[8:9, :] += jnp.sum(grad * x * factor, axis=0, keepdims=True)
        scaled = grad * gain_one[...]
        inner = jnp.mean(scaled * x, axis=1, keepdims=True)
        d_tokens[rows, :] += factor * scaled - x * (factor * factor * factor * inner)
        return carry
    lax.fori_loop(0, 2, to_tokens, 0)

    span = s_mid.shape[1]

    def small_plane(flip):
        there = row_at(row, flip)
        view = small.at[:, pl.ds(pl.multiple_of((there // 2) * span, 128), span)]
        return remote(view, s_rec.at[flip - 1], s_ss.at[flip - 1], s_rs.at[flip - 1], {"row": there})

    def small_column(step):
        return remote(s_mid, s_zrec.at[step - 1], sz_ss.at[step - 1], sz_rs.at[step - 1], {"col": (col + step) % 4})

    each_flip(lambda flip: small_plane(flip).start())
    stage_two("a", 3)
    stage_three("a", 2)
    s_mid[...] = small[:, pl.ds(pl.multiple_of(chip * span, 128), span)]

    def add_small(flip):
        small_plane(flip).wait_recv()
        s_mid[...] += s_rec[flip - 1]

    each_flip(add_small)
    for step in (1, 2, 3):
        small_column(step).start()
    stage_three("a", 3)

    own_prod.wait()
    each_flip(lambda flip: back_prod(flip).wait_recv())

    def to_output(m, carry):
        rows = pl.ds(pl.multiple_of(m * half, half), half)
        total = hidden[rows, :]
        for k in range(2):
            picked = jnp.where(at_slot(rows, k), 1.0, 0.0).astype(low)
            total = total + dot(picked, rec_prod[...]) * gates[rows, k : k + 1]
        out_ref[rows, :] = total.astype(low)
        return carry
    lax.fori_loop(0, 2, to_output, 0)

    total = s_mid[...]
    for step in (1, 2, 3):
        small_column(step).wait_recv()
        total = total + s_zrec[step - 1]
    sum_s[...] = total
    for part in ("b", "a"):
        for step in (1, 2, 3):
            column(part, step).wait_recv()

    def to_sums(i, carry):
        rows = pl.ds(pl.multiple_of(i * 32, 32), 32)
        total = own[col, chip, rows, :].astype(f32)
        for step in range(3):
            total = total + rec_z[step, rows, :].astype(f32)
        sum_a[rows, :] = total[:, :width_a]
        sum_b[rows, :] = total[:, width_a:]
        return carry
    lax.fori_loop(0, block // 32, to_sums, 0)


    def all_sent(flip):
        for copy in back(flip):
            copy.wait_send()
        back_prod(flip).wait_send()
        small_plane(flip).wait_send()

    each_flip(all_sent)
    for step in (1, 2, 3):
        small_column(step).wait_send()
        column("a", step).wait_send()
        column("b", step).wait_send()

    def sent(c, carry):
        for part in ("a", "b"):
            def body(q, carry):
                to_sibling(part, c, q).wait_send()
                return carry
            lax.fori_loop(0, 4, body, 0)
            for copy in one(part, c):
                copy.wait_send()
            for copy in two_step(part, c):
                copy.wait_send()
        return carry
    lax.fori_loop(0, 4, sent, 0)


def run_backward(slot_of, gates, ids, router, gain_one, gain_two, lse, segments, gate_grad, in_grad, produced,
                 hidden, tokens, cotangent, normed, attended, normed_two, qkv, full_a, full_out):
    sems = pltpu.SemaphoreType.DMA
    length, model = tokens.shape
    block = full_a.shape[0] // 8
    width_a, width_b = full_a.shape[1] // 4, full_out.shape[1] // 4
    width = width_a + width_b
    cut = block // 2
    low, f32 = tokens.dtype, jnp.float32
    vm = pl.BlockSpec(memory_space=pltpu.VMEM)
    slots = in_grad.shape[0]
    capacity = slots // 8
    span = model // 4
    router_p = jnp.pad(router, ((0, 0), (0, 128 - router.shape[1])))
    v = pltpu.VMEM
    rows_low = v((length, model), low)
    return pl.pallas_call(
        backward_kernel,
        out_shape=(
            jax.ShapeDtypeStruct((length, model), low),
            jax.ShapeDtypeStruct((length, model), f32),
            jax.ShapeDtypeStruct((block, width_a), f32),
            jax.ShapeDtypeStruct((block, width_b), f32),
            jax.ShapeDtypeStruct((16, span), f32),
        ),
        in_specs=[vm] * 9 + [ANY] * 12,
        out_specs=(vm,) * 5,
        scratch_shapes=[
            v((slots, model), low), v((8, 1, capacity), f32), v((slots, model), low),
            v((length, model), f32), rows_low, rows_low, rows_low,
            v(qkv.shape, low), v(full_a.shape, low), v(full_out.shape, low),
            v((model, length), low), v((model, length), low), rows_low,
            v((length, length), f32), v((width_b, model), low), v((length, width_b), low), v((4, length, width_a), low),
            v((length, 128), low), v((16, model), f32),
            v((4, 4, block, width), low), v((4, 4, block, width), low), v((4, 4, block, width), low),
            v((4, 2, 2, cut, width), low), v((4, 2, cut, width), low), v((3, block, width), low),
            v((7, 16, span), f32), v((16, span), f32), v((3, 16, span), f32),
            sems((9,)), sems((7,)), sems((7,)), sems((7,)), sems((7,)), sems((7,)), sems((7,)), sems((3,)),
            sems((4, 4, 2)), sems((4, 4, 2)), sems((4, 2, 2, 3)), sems((4, 2, 2, 3)),
            sems((2, 3)), sems((2, 3)), sems((7,)), sems((7,)), sems((3,)), sems((3,)),
        ],
        compiler_params=pltpu.CompilerParams(
            collective_id=2, has_side_effects=True, vmem_limit_bytes=60 * 2**20
        ),
        cost_estimate=pl.CostEstimate(flops=0, bytes_accessed=1_000_000, transcendentals=0),
    )(slot_of, gates, ids, router_p, gain_one[None], gain_two[None], lse, segments.reshape(1, length),
      segments.reshape(length, 1), gate_grad, in_grad, produced, hidden, tokens, cotangent, normed, attended,
      normed_two, qkv, full_a, full_out)


def rms_factor(rows_in):
    return lax.rsqrt(jnp.mean(rows_in * rows_in, axis=1, keepdims=True) + EPSILON)


def dot(a, b):
    return jnp.dot(a, b, preferred_element_type=jnp.float32)


def dot_t(a, b):
    return lax.dot_general(a, b, (((1,), (1,)), ((), ())), preferred_element_type=jnp.float32)


def t_dot(a, b):
    return lax.dot_general(a, b, (((0,), (0,)), ((), ())), preferred_element_type=jnp.float32)


def on_small_slice():
    return lax.axis_size("row") == 8 and lax.axis_size("col") == 4


def pair_heads(a):
    if not on_small_slice():
        return a
    a = a.reshape(a.shape[0], -1, 2, QUERY_PER_KEY, HEAD_SIZE)
    return a.transpose(0, 1, 3, 2, 4).reshape(a.shape[0], -1)


def part_heads(a):
    a = a.reshape(a.shape[0], -1, QUERY_PER_KEY, 2, HEAD_SIZE)
    return a.transpose(0, 1, 3, 2, 4).reshape(a.shape[0], -1)


def gather_all(own_a, own_b, own_s, own_c):
    col_a = lax.all_gather(own_a, "col", axis=1, tiled=True)
    col_b = lax.all_gather(own_b, "col", axis=1, tiled=True)
    small = lax.all_gather(lax.all_gather(own_s, "col", axis=0), "row", axis=1)
    return (
        lax.all_gather(col_a, "row", axis=0, tiled=True),
        lax.all_gather(col_b, "row", axis=0, tiled=True),
        small,
        lax.all_gather(own_c, "row", axis=0, tiled=True),
    )


def spread(own_c, own_g):
    if on_small_slice():
        return spread_tokens(own_c, own_g)
    return (
        lax.all_gather(own_c, "row", axis=0, tiled=True),
        lax.all_gather(own_g, "row", axis=0),
    )


def reduce_all(grad_a, grad_b, grad_s):
    def both(g):
        plane = lax.psum_scatter(g, "row", scatter_dimension=0, tiled=True).astype(jnp.float32)
        return lax.psum_scatter(plane, "col", scatter_dimension=1, tiled=True)

    small = lax.psum_scatter(grad_s, "row", scatter_dimension=0, tiled=False)
    return both(grad_a), both(grad_b), lax.psum_scatter(small, "col", scatter_dimension=0, tiled=False)


def expert_elsewhere(place, routed, mine, plane_normed, plane_upstream, full_gu, own_down):
    rows, length = place.shape
    model = plane_normed.shape[1]
    hidden_units = full_gu.shape[1] // 2
    capacity = 2 * length * TOP // rows
    full_down = lax.all_gather(own_down, "col", axis=0, tiled=True)
    chosen_rows = (
        (place[:, None, :] == jnp.arange(capacity, dtype=jnp.int32)[None, :, None]) & routed[:, None, :]
    ).astype(jnp.bfloat16)

    def of_slots(plane):
        return jnp.einsum(
            "rct,rtd->rcd",
            chosen_rows,
            plane.reshape(rows, length, model),
            preferred_element_type=jnp.float32,
        ).astype(jnp.bfloat16).reshape(rows * capacity, model)

    grouped, grouped_up = of_slots(plane_normed), of_slots(plane_upstream)
    slot_gate = jnp.sum(jnp.where(chosen_rows > 0, mine[:, None, :], 0.0), axis=2)
    slot_gate = slot_gate.reshape(rows * capacity, 1)
    grouped_grad = (grouped_up.astype(jnp.float32) * slot_gate).astype(jnp.bfloat16)
    both_pre = dot(grouped, full_gu)
    gate_pre, up_pre = both_pre[:, :hidden_units], both_pre[:, hidden_units:]
    sigma = jax.nn.sigmoid(gate_pre)
    silu_gate = gate_pre * sigma
    activation = (silu_gate * up_pre).astype(jnp.bfloat16)
    grad_down_local = t_dot(activation, grouped_grad).astype(jnp.bfloat16)
    grad_down = lax.psum_scatter(grad_down_local, "col", scatter_dimension=0, tiled=True)
    act_grad = dot_t(grouped_grad, full_down)
    both_grad = jnp.concatenate(
        [
            (act_grad * up_pre * sigma * (1.0 + gate_pre * (1.0 - sigma))).astype(jnp.bfloat16),
            (act_grad * silu_gate).astype(jnp.bfloat16),
        ],
        axis=1,
    )
    in_grad = dot_t(both_grad, full_gu).astype(jnp.bfloat16)
    produced = dot(activation, full_down).astype(jnp.bfloat16)
    slot_gate_grad = jnp.sum(produced.astype(jnp.float32) * grouped_up.astype(jnp.float32), axis=1)
    grad_gu_local = t_dot(grouped, both_grad).astype(jnp.bfloat16)
    return in_grad, produced, slot_gate_grad, grad_gu_local, grad_down.astype(jnp.float32)


def masked_scores(queries, heads_of_key, segments, head_scale):
    length = queries.shape[0]
    heads_of_query = queries.reshape(length, KEY_VALUE_HEADS, QUERY_PER_KEY, HEAD_SIZE)
    scores = (
        jnp.einsum("qkgd,skd->kgqs", heads_of_query, heads_of_key, preferred_element_type=jnp.float32)
        * head_scale
    )
    pos = jnp.arange(length, dtype=jnp.int32)
    allowed = (pos[None, :] <= pos[:, None]) & (segments[None, :] == segments[:, None])
    return jnp.where(allowed, scores, NEGATIVE), heads_of_query


def per_device(
    tokens,
    attn_gain,
    w_query,
    w_key,
    w_value,
    w_out,
    expert_gain,
    router,
    w_gate,
    w_up,
    w_down,
    segment_ids,
    expert_ids,
    cotangent,
):
    length, model = tokens.shape
    rows, cols = lax.axis_size("row"), lax.axis_size("col")
    experts = w_gate.shape[0] * rows
    capacity = 2 * length * TOP // experts
    head_scale = HEAD_SIZE ** (-0.5)
    segments = segment_ids.reshape(-1)
    block, width_q = w_query.shape
    width_k = w_key.shape[1]
    width_a = width_q + 2 * width_k
    piece = attn_gain.shape[0]
    router_cols = router.shape[1]

    hidden_units = w_gate.shape[2]
    own_gu = jnp.concatenate([w_gate[0], w_up[0]], axis=1)
    own_down = w_down[0]

    lane = 256

    def row_of(v):
        return jnp.pad(v, ((0, 0), (0, lane - v.shape[1])))

    own_s = jnp.concatenate(
        [row_of(router.T), row_of(attn_gain[None]), row_of(expert_gain[None])], axis=0
    )
    own_s = jnp.pad(own_s, ((0, 16 - own_s.shape[0]), (0, 0)))
    own_a = jnp.concatenate([pair_heads(w_query), w_key, w_value], axis=1)
    if on_small_slice():
        line_a, line_out, small, plane_upstream = gather_line(own_a, w_out, own_s, cotangent)
        own_gu, own_down, line_a, line_out = lax.optimization_barrier(
            (own_gu, own_down, line_a, line_out)
        )
        full_a, full_out = gather_plane(3, (line_a, line_out))
    else:
        full_a, full_out, small, plane_upstream = gather_all(own_a, w_out, own_s, cotangent)
    full_gu = lax.all_gather(own_gu, "col", axis=0, tiled=True)
    full_router = small[:, :, :router_cols, :block].transpose(1, 3, 0, 2).reshape(model, experts)
    gain_one = small[:, :, router_cols, :piece].transpose(1, 0, 2).reshape(model).astype(jnp.float32)
    gain_two = small[:, :, router_cols + 1, :piece].transpose(1, 0, 2).reshape(model).astype(jnp.float32)

    rows_f = tokens.astype(jnp.float32)
    factor_one = rms_factor(rows_f)
    normed = (rows_f * factor_one * gain_one).astype(jnp.bfloat16)
    flat_qkv = dot(normed, full_a).astype(jnp.bfloat16)
    qkv = flat_qkv.reshape(length, cols, width_a)
    query_rows = qkv[:, :, :width_q].reshape(length, -1)
    if on_small_slice():
        query_rows = part_heads(query_rows)
    rows_of_key = qkv[:, :, width_q : width_q + width_k].reshape(length, -1)
    rows_of_value = qkv[:, :, width_q + width_k :].reshape(length, -1)
    heads_of_key = rows_of_key.reshape(length, KEY_VALUE_HEADS, HEAD_SIZE)
    heads_of_value = rows_of_value.reshape(length, KEY_VALUE_HEADS, HEAD_SIZE)

    scores, heads_of_query = masked_scores(query_rows, heads_of_key, segments, head_scale)
    row_max = jnp.max(scores, axis=-1, keepdims=True)
    expo_rows = jnp.exp(scores - row_max)
    totals = jnp.sum(expo_rows, axis=-1, keepdims=True)
    soft_probs = expo_rows / totals
    probs_low = soft_probs.astype(jnp.bfloat16)
    attended = (
        jnp.einsum("kgqs,skd->qkgd", probs_low, heads_of_value, preferred_element_type=jnp.float32)
        .reshape(length, -1)
        .astype(jnp.bfloat16)
    )
    hidden = rows_f + dot(attended, full_out)
    factor_two = rms_factor(hidden)
    normed_two = (hidden * factor_two * gain_two).astype(jnp.bfloat16)
    logits = dot(normed_two, full_router)

    named = expert_ids[:, :, None] == jnp.arange(experts, dtype=jnp.int32)[None, None, :]
    chosen = jnp.sum(jnp.where(named, logits[:, None, :], 0.0), axis=2)
    gate_probs = jax.nn.softmax(chosen, axis=1)
    gate_table = jnp.sum(jnp.where(named, gate_probs[:, :, None], 0.0), axis=1)
    gate_table = jnp.where(jnp.any(named, axis=1), gate_table, -1.0)
    plane_normed, plane_gate = spread(normed_two, gate_table.T)
    mine = lax.dynamic_index_in_dim(plane_gate, lax.axis_index("row"), axis=1, keepdims=False)
    routed = mine >= 0.0
    place = jnp.cumsum(routed.astype(jnp.int32), axis=1) - 1
    any_named = jnp.any(named, axis=1)
    before = jnp.cumsum(any_named.astype(jnp.int32), axis=0) - 1
    slot_of = jnp.sum(
        jnp.where(named, before[:, None, :] + jnp.arange(experts, dtype=jnp.int32) * capacity, 0),
        axis=2,
    )
    if on_small_slice():
        in_grad, produced, slot_gate_grad, grad_gu_local, grad_down = run_expert(
            jnp.where(routed, place, -1), mine, plane_normed, plane_upstream, full_gu, own_down
        )
        grad_gu = lax.psum_scatter(grad_gu_local, "col", scatter_dimension=0, tiled=True)
        lse = (row_max + jnp.log(totals)).reshape(KEY_VALUE_HEADS, 1, QUERY_PER_KEY * length)
        output, d_tokens, sum_a, sum_out, sum_s = run_backward(
            slot_of, gate_probs, expert_ids, full_router, gain_one, gain_two, lse, segments,
            slot_gate_grad, in_grad, produced, hidden, tokens, cotangent, normed, attended, normed_two,
            flat_qkv, full_a, full_out,
        )
        core = lax.axis_index("row") % 2
        col = lax.axis_index("col")
        own_router = lax.dynamic_slice(sum_s, (col * router_cols, core * block), (router_cols, block))
        own_gains = lax.dynamic_slice(sum_s, (experts, core * block + col * piece), (2, piece))
        return (
            output,
            d_tokens,
            own_gains[0],
            part_heads(sum_a[:, :width_q]),
            sum_a[:, width_q : width_q + width_k],
            sum_a[:, width_q + width_k :],
            sum_out,
            own_gains[1],
            own_router.T,
            grad_gu[:, :hidden_units].astype(jnp.float32)[None],
            grad_gu[:, hidden_units:].astype(jnp.float32)[None],
            grad_down[None],
        )
    else:
        in_grad, produced, slot_gate_grad, grad_gu_local, grad_down = expert_elsewhere(
            place, routed, mine, plane_normed, plane_upstream, full_gu, own_down
        )
    grad_gu = lax.psum_scatter(grad_gu_local, "col", scatter_dimension=0, tiled=True)
    back_grad = lax.all_to_all(
        in_grad.reshape(rows, capacity, model), "row", split_axis=0, concat_axis=0, tiled=True
    ).reshape(experts * capacity, model)
    back_gate_grad = lax.all_to_all(
        slot_gate_grad.reshape(rows, 1, capacity), "row", split_axis=0, concat_axis=0, tiled=True
    ).reshape(experts * capacity)
    produced, back_grad = lax.optimization_barrier((produced, back_grad))
    back_rows = lax.all_to_all(
        produced.reshape(rows, capacity, model), "row", split_axis=0, concat_axis=0, tiled=True
    ).reshape(experts * capacity, model)

    all_slots = jnp.arange(experts * capacity, dtype=jnp.int32)
    is_slot = slot_of.T[:, :, None] == all_slots[None, None, :]
    from_slot = is_slot.astype(jnp.bfloat16)
    gate_grad = jnp.sum(jnp.where(is_slot, back_gate_grad[None, None, :], 0.0), axis=2).T
    returned = [dot(from_slot[k], back_rows) for k in range(TOP)]
    upstream = cotangent.astype(jnp.float32)
    output = (
        hidden + sum(returned[k] * gate_probs[:, k : k + 1] for k in range(TOP))
    ).astype(jnp.bfloat16)
    normed_two_grad = dot(from_slot[0] + from_slot[1], back_grad)
    pair_mean = jnp.sum(gate_probs * gate_grad, axis=1, keepdims=True)
    pair_logit = gate_probs * (gate_grad - pair_mean)
    logit_grad = jnp.sum(jnp.where(named, pair_logit[:, :, None], 0.0), axis=1).astype(jnp.bfloat16)
    grad_router = t_dot(normed_two, logit_grad)
    normed_two_grad = normed_two_grad + dot_t(logit_grad, full_router)
    grad_expert_gain = jnp.sum(normed_two_grad * hidden * factor_two, axis=0)
    scaled_two = normed_two_grad * gain_two
    hidden_grad = (
        upstream
        + factor_two * scaled_two
        - hidden * factor_two**3 * jnp.mean(scaled_two * hidden, axis=1, keepdims=True)
    )
    branch_grad = hidden_grad.astype(jnp.bfloat16)
    grad_out_full = t_dot(attended, branch_grad).astype(jnp.bfloat16)
    attended_grad = dot_t(branch_grad, full_out).astype(jnp.bfloat16)

    gradient_heads = attended_grad.reshape(length, KEY_VALUE_HEADS, QUERY_PER_KEY, HEAD_SIZE)
    value_grad = jnp.einsum(
        "kgqs,qkgd->skd", probs_low, gradient_heads, preferred_element_type=jnp.float32
    )
    prob_grad = jnp.einsum(
        "qkgd,skd->kgqs", gradient_heads, heads_of_value, preferred_element_type=jnp.float32
    )
    delta_sum = jnp.sum(soft_probs * prob_grad, axis=-1, keepdims=True)
    score_grad = (soft_probs * (prob_grad - delta_sum)).astype(jnp.bfloat16)
    query_grad = (
        jnp.einsum("kgqs,skd->qkgd", score_grad, heads_of_key, preferred_element_type=jnp.float32)
        * head_scale
    )
    key_grad = (
        jnp.einsum("kgqs,qkgd->skd", score_grad, heads_of_query, preferred_element_type=jnp.float32)
        * head_scale
    )
    qkv_grad = jnp.concatenate(
        [
            query_grad.astype(jnp.bfloat16).reshape(length, cols, width_q),
            key_grad.astype(jnp.bfloat16).reshape(length, cols, width_k),
            value_grad.astype(jnp.bfloat16).reshape(length, cols, width_k),
        ],
        axis=2,
    ).reshape(length, cols * width_a)
    grad_a_full = t_dot(normed, qkv_grad).astype(jnp.bfloat16)
    normed_grad = dot_t(qkv_grad, full_a)
    grad_attn_gain = jnp.sum(normed_grad * rows_f * factor_one, axis=0)
    scaled_one = normed_grad * gain_one
    d_tokens = (
        hidden_grad
        + factor_one * scaled_one
        - rows_f * factor_one**3 * jnp.mean(scaled_one * rows_f, axis=1, keepdims=True)
    )
    grad_s = jnp.concatenate(
        [
            jnp.pad(
                grad_router.reshape(rows, block, cols, router_cols).transpose(0, 2, 3, 1),
                ((0, 0), (0, 0), (0, 0), (0, lane - block)),
            ),
            jnp.pad(
                jnp.stack([grad_attn_gain, grad_expert_gain])
                .reshape(2, rows, cols, piece)
                .transpose(1, 2, 0, 3),
                ((0, 0), (0, 0), (0, 6 - router_cols), (0, lane - piece)),
            ),
        ],
        axis=2,
    )
    grad_a_full, d_tokens, output = lax.optimization_barrier((grad_a_full, d_tokens, output))
    sum_a, sum_out, sum_s = reduce_all(grad_a_full, grad_out_full, grad_s)
    return (
        output,
        d_tokens,
        sum_s[router_cols, :piece],
        sum_a[:, :width_q],
        sum_a[:, width_q : width_q + width_k],
        sum_a[:, width_q + width_k :],
        sum_out,
        sum_s[router_cols + 1, :piece],
        sum_s[:router_cols, :block].T,
        grad_gu[:, :hidden_units].astype(jnp.float32)[None],
        grad_gu[:, hidden_units:].astype(jnp.float32)[None],
        grad_down[None],
    )


def solution(mesh):
    in_specs = (
        P(("row", "col"), None),
        P(("row", "col")),
        P("row", "col"),
        P("row", "col"),
        P("row", "col"),
        P("row", "col"),
        P(("row", "col")),
        P("row", "col"),
        P("row", "col", None),
        P("row", "col", None),
        P("row", "col", None),
        P(("row", "col"), None),
        P(("row", "col"), None),
        P(("row", "col"), None),
    )
    out_specs = (
        P(("row", "col"), None),
        P(("row", "col"), None),
        P(("row", "col")),
        P("row", "col"),
        P("row", "col"),
        P("row", "col"),
        P("row", "col"),
        P(("row", "col")),
        P("row", "col"),
        P("row", "col", None),
        P("row", "col", None),
        P("row", "col", None),
    )
    return jax.shard_map(
        per_device, mesh=mesh, in_specs=in_specs, out_specs=out_specs, check_vma=False
    )
```

```python
import functools

import jax
import jax.numpy as jnp
from jax import lax
from jax.experimental import pallas as pl
from jax.experimental.pallas import tpu as pltpu
from jax.sharding import PartitionSpec as P

KEY_VALUE_HEADS = 8
HEAD_SIZE = 64
TOP = 2
QUERY_PER_KEY = 3


EPSILON = 1e-05
NEGATIVE = -1e30


MESH = pl.DeviceIdType.MESH
ANY = pl.BlockSpec(memory_space=pl.ANY)


def row_at(row, flip):
    y, x, core = row // 4, (row // 2) % 2, row % 2
    return (
        (y + flip // 4) % 2 * 4 + (x + (flip // 2) % 2) % 2 * 2 + (core + flip % 2) % 2
    )


def remote(source, target, send, receive, device):
    return pltpu.make_async_remote_copy(
        source, target, send, receive, device_id=device, device_id_type=MESH
    )


def greet(row_flips, col_steps):
    row, col = lax.axis_index("row"), lax.axis_index("col")
    sem = pltpu.get_barrier_semaphore()
    for flip in row_flips:
        pl.semaphore_signal(
            sem, inc=1, device_id={"row": row_at(row, flip)}, device_id_type=MESH
        )
    for step in col_steps:
        pl.semaphore_signal(
            sem, inc=1, device_id={"col": (col + step) % 4}, device_id_type=MESH
        )
    pl.semaphore_wait(sem, len(row_flips) + len(col_steps))


def unit_order(col, k):
    table = ((0, 1, 2, 3), (1, 0, 2, 3), (2, 3, 1, 0), (3, 2, 1, 0))
    out = table[3][k]
    for c in (2, 1, 0):
        out = jnp.where(col == c, table[c][k], out)
    return out


def unit_at(col, k):
    end = (col == 0) | (col == 3)
    ends = jnp.where(col == 0, k, 3 - k)
    middle = jnp.where(k == 0, col, jnp.where(k == 3, jnp.where(col == 1, 3, 0), jnp.where(col == 1, 2 * k - 2, 5 - 2 * k)))
    return jnp.where(end, ends, middle)


X, Y, SIB = 2, 4, 1


def plane_send(view, row, ss, rs, source=None):
    source = view(row) if source is None else source
    for i, flip in enumerate((X, Y, SIB)):
        remote(source, view(row), ss(i), rs(i), {"row": row_at(row, flip)}).start()


def plane_forward(view, halves, row, ss, rs):
    first, second = halves
    from_x, from_y = row_at(row, X), row_at(row, Y)
    sib = {"row": row_at(row, SIB)}
    remote(view(from_x), view(from_x), ss(0), rs(0), sib).wait_recv()
    remote(first(from_x), first(from_x), ss(3), rs(3), {"row": from_y}).start()
    remote(view(from_x), view(from_x), ss(5), rs(5), sib).start()
    remote(view(from_y), view(from_y), ss(1), rs(1), sib).wait_recv()
    remote(second(from_y), second(from_y), ss(4), rs(4), {"row": from_x}).start()
    remote(view(from_y), view(from_y), ss(6), rs(6), sib).start()


def plane_last(view, halves, row, ss, rs):
    first, second = halves
    diag = row_at(row, X + Y)
    sib = {"row": row_at(row, SIB)}
    remote(first(diag), first(diag), ss(3), rs(3), sib).wait_recv()
    remote(first(diag), first(diag), ss(7), rs(7), sib).start()
    remote(second(diag), second(diag), ss(4), rs(4), sib).wait_recv()
    remote(second(diag), second(diag), ss(8), rs(8), sib).start()


def plane_finish(view, halves, row, ss, rs):
    first, second = halves
    sib_row = row_at(row, SIB)
    sib = {"row": sib_row}
    whole = view(sib_row)
    remote(whole, whole, ss(2), rs(2), sib).wait_recv()
    for i, flip in ((5, X), (6, Y)):
        block = view(row_at(sib_row, flip))
        remote(block, block, ss(i), rs(i), sib).wait_recv()
    far = row_at(sib_row, X + Y)
    remote(first(far), first(far), ss(7), rs(7), sib).wait_recv()
    remote(second(far), second(far), ss(8), rs(8), sib).wait_recv()
    for i in range(9):
        block = view(row) if i in (0, 1, 2, 5, 6) else (first(row) if i in (3, 7) else second(row))
        remote(block, block, ss(i), rs(i), sib).wait_send()


def pick(ref, cols, halves_rows):
    block, cut = halves_rows

    def at(start, size):
        def view(r):
            rows = pl.ds(pl.multiple_of(r * block + start, 16), size)
            if cols is None:
                return ref.at[rows, :]
            return ref.at[rows, pl.ds(pl.multiple_of(cols[0], 128), cols[1])]

        return view

    return at(0, block), (at(0, cut), at(cut, block - cut))


def through(source, middle, target, sem):
    return pltpu.make_async_copy(source, middle, sem), pltpu.make_async_copy(middle, target, sem)


def through(source, middle, target, sem):
    return pltpu.make_async_copy(source, middle, sem), pltpu.make_async_copy(middle, target, sem)


def line_kernel(own_a, own_b, own_s, own_c, w_gate, w_up, line_a, line_b, full_s, full_c, own_gu, mid_a, mid_b, mid_c, mid_gu,
                zss, zrs, css, crs, s_zs, s_zr, s_ps, s_pr, loc):
    row, col = lax.axis_index("row"), lax.axis_index("col")
    width_a, width_b = own_a.shape[1], own_b.shape[1]
    rows_c = own_c.shape[0]
    vc, hc = pick(full_c, None, (rows_c, rows_c // 2))
    csv, crv = (lambda i: css.at[i]), (lambda i: crs.at[i])

    def of_a(c):
        return line_a.at[:, pl.ds(pl.multiple_of(c * width_a, 128), width_a)]

    def of_b(c):
        return line_b.at[:, pl.ds(pl.multiple_of(c * width_b, 128), width_b)]

    copies = [
        through(own_a, mid_a, of_a(col), loc.at[0]),
        through(own_b, mid_b, of_b(col), loc.at[1]),
        through(own_c, mid_c, vc(row), loc.at[2]),
    ]
    for copy, _ in copies:
        copy.start()
    small_copy = pltpu.make_async_copy(own_s, full_s.at[col, row], loc.at[3])
    small_copy.start()
    units = w_gate.shape[1]
    to_gu = [
        pltpu.make_async_copy(w, mid_gu.at[:, pl.ds(i * units, units)], loc.at[4 + i])
        for i, w in enumerate((w_gate, w_up))
    ]
    from_gu = pltpu.make_async_copy(mid_gu, own_gu, loc.at[6])
    greet(range(1, 8), (1, 2, 3))

    def along(c, source_a, source_b, right, left):
        for d, (cond, step) in enumerate(((right, 1), (left, 3))):
            @pl.when(cond)
            def _():
                there = {"col": (col + step) % 4}
                remote(source_a, of_a(c), zss.at[0, c, d], zrs.at[0, c], there).start()
                remote(source_b, of_b(c), zss.at[1, c, d], zrs.at[1, c], there).start()

    def arrived(k):
        c = unit_order(col, k)
        there = {"col": (col + 1) % 4}
        remote(of_a(c), of_a(c), zss.at[0, c, 0], zrs.at[0, c], there).wait_recv()
        remote(of_b(c), of_b(c), zss.at[1, c, 0], zrs.at[1, c], there).wait_recv()
        along(c, of_a(c), of_b(c), (c < col) & (col < 3), (c > col) & (col > 0))

    along(col, own_a, own_b, col < 3, col > 0)
    for i, step in enumerate((1, 2, 3)):
        remote(own_s, full_s.at[col, row], s_zs.at[i], s_zr.at[i], {"col": (col + step) % 4}).start()
    plane_send(vc, row, csv, crv, own_c)
    for copy in to_gu:
        copy.start()
    for first, second in copies:
        first.wait()
        second.start()
    small_copy.wait()
    for copy in to_gu:
        copy.wait()
    from_gu.start()
    arrived(1)
    for i, step in enumerate((3, 2, 1)):
        remote(own_s, full_s.at[(col + step) % 4, row], s_zs.at[i], s_zr.at[i], {"col": (col + 1) % 4}).wait()
    for i in range(1, 8):
        remote(full_s.at[:, row], full_s.at[:, row], s_ps.at[i - 1], s_pr.at[i - 1], {"row": row_at(row, i)}).start()
    arrived(2)
    plane_forward(vc, hc, row, csv, crv)
    arrived(3)
    plane_last(vc, hc, row, csv, crv)
    for _, second in copies:
        second.wait()
    from_gu.wait()
    plane_finish(vc, hc, row, csv, crv)
    for i in range(1, 8):
        there = row_at(row, i)
        remote(full_s.at[:, there], full_s.at[:, there], s_ps.at[i - 1], s_pr.at[i - 1], {"row": there}).wait()
    for k in range(4):
        c = unit_order(col, k)
        right = (c <= col) & (col < 3)
        left = (c >= col) & (col > 0)
        for d, cond in enumerate((right, left)):
            @pl.when(cond)
            def _():
                there = {"col": (col + 1) % 4}
                remote(of_a(c), of_a(c), zss.at[0, c, d], zrs.at[0, c], there).wait_send()
                remote(of_b(c), of_b(c), zss.at[1, c, d], zrs.at[1, c], there).wait_send()


def gather_line(own_a, own_b, own_s, own_c, w_gate, w_up):
    sems = pltpu.SemaphoreType.DMA
    rows_c = own_c.shape[0]
    return pl.pallas_call(
        line_kernel,
        out_shape=(
            jax.ShapeDtypeStruct((own_a.shape[0], own_a.shape[1] * 4), own_a.dtype),
            jax.ShapeDtypeStruct((own_b.shape[0], own_b.shape[1] * 4), own_b.dtype),
            jax.ShapeDtypeStruct((4, 8) + own_s.shape, own_s.dtype),
            jax.ShapeDtypeStruct((8 * rows_c, own_c.shape[1]), own_c.dtype),
            jax.ShapeDtypeStruct((w_gate.shape[0], 2 * w_gate.shape[1]), w_gate.dtype),
        ),
        in_specs=[ANY] * 6,
        out_specs=(ANY,) * 5,
        scratch_shapes=[
            pltpu.VMEM(own_a.shape, own_a.dtype),
            pltpu.VMEM(own_b.shape, own_b.dtype),
            pltpu.VMEM(own_c.shape, own_c.dtype),
            pltpu.VMEM((w_gate.shape[0], 2 * w_gate.shape[1]), w_gate.dtype),
            sems((2, 4, 2)), sems((2, 4)),
            sems((9,)), sems((9,)),
            sems((3,)), sems((3,)), sems((7,)), sems((7,)), sems((7,)),
        ],
        compiler_params=pltpu.CompilerParams(collective_id=0, has_side_effects=True),
        cost_estimate=pl.CostEstimate(flops=0, bytes_accessed=1_000_000, transcendentals=0),
    )(own_a, own_b, own_s, own_c, w_gate, w_up)


def plane_kernel(count, *refs):
    row = lax.axis_index("row")
    owns, fulls, mids = refs[:count], refs[count : 2 * count], refs[2 * count : 3 * count]
    ss, rs, loc = refs[3 * count :]
    views, copies = [], []
    for i in range(count):
        block = owns[i].shape[0]
        views.append(pick(fulls[i], None, (block, block // 2)))
        copies.append(through(owns[i], mids[i], views[i][0](row), loc.at[i]))
        copies[i][0].start()
    greet(range(1, 8), ())

    def sems_of(i):
        return (lambda j: ss.at[i, j]), (lambda j: rs.at[i, j])

    for i in range(count):
        plane_send(views[i][0], row, *sems_of(i), owns[i])
    for first, second in copies:
        first.wait()
        second.start()
    for i in range(count):
        plane_forward(*views[i], row, *sems_of(i))
    for i in range(count):
        plane_last(*views[i], row, *sems_of(i))
    for _, second in copies:
        second.wait()
    for i in range(count):
        plane_finish(*views[i], row, *sems_of(i))


def gather_plane(collective, owns):
    sems = pltpu.SemaphoreType.DMA
    count = len(owns)
    return pl.pallas_call(
        functools.partial(plane_kernel, count),
        out_shape=tuple(
            jax.ShapeDtypeStruct((8 * own.shape[0], own.shape[1]), own.dtype) for own in owns
        ),
        in_specs=[ANY] * count,
        out_specs=(ANY,) * count,
        scratch_shapes=[pltpu.VMEM(own.shape, own.dtype) for own in owns]
        + [sems((count, 9)), sems((count, 9)), sems((count,))],
        compiler_params=pltpu.CompilerParams(collective_id=collective, has_side_effects=True),
        cost_estimate=pl.CostEstimate(flops=0, bytes_accessed=1_000_000, transcendentals=0),
    )(*owns)


def spread_kernel(own_c, own_g, full_c, full_g, mid_c, css, crs, gss, grs, loc):
    row = lax.axis_index("row")
    rows_c = own_c.shape[0]
    vc, hc = pick(full_c, None, (rows_c, rows_c // 2))
    csv, crv = (lambda i: css.at[i]), (lambda i: crs.at[i])
    first, second = through(own_c, mid_c, vc(row), loc.at[0])
    first.start()
    own_copy = pltpu.make_async_copy(own_g, full_g.at[row], loc.at[1])
    own_copy.start()
    greet(range(1, 8), ())
    plane_send(vc, row, csv, crv, own_c)
    for i in range(1, 8):
        remote(own_g, full_g.at[row], gss.at[i - 1], grs.at[i - 1], {"row": row_at(row, i)}).start()
    first.wait()
    second.start()
    plane_forward(vc, hc, row, csv, crv)
    plane_last(vc, hc, row, csv, crv)
    second.wait()
    own_copy.wait()
    plane_finish(vc, hc, row, csv, crv)
    for i in range(1, 8):
        there = row_at(row, i)
        remote(own_g, full_g.at[there], gss.at[i - 1], grs.at[i - 1], {"row": there}).wait()


def spread_tokens(own_c, own_g):
    sems = pltpu.SemaphoreType.DMA
    return pl.pallas_call(
        spread_kernel,
        out_shape=(
            jax.ShapeDtypeStruct((8 * own_c.shape[0], own_c.shape[1]), own_c.dtype),
            jax.ShapeDtypeStruct((8,) + own_g.shape, own_g.dtype),
        ),
        in_specs=[ANY] * 2,
        out_specs=(ANY,) * 2,
        scratch_shapes=[
            pltpu.VMEM(own_c.shape, own_c.dtype),
            sems((9,)), sems((9,)), sems((7,)), sems((7,)), sems((2,)),
        ],
        compiler_params=pltpu.CompilerParams(collective_id=1, has_side_effects=True),
        cost_estimate=pl.CostEstimate(flops=0, bytes_accessed=1_000_000, transcendentals=0),
    )(own_c, own_g)


def add_into(target, term):
    def body(i, carry):
        rows = pl.ds(pl.multiple_of(i * 32, 32), 32)
        total = target[rows, :].astype(jnp.float32) + term[rows, :].astype(jnp.float32)
        target[rows, :] = total.astype(target.dtype)
        return carry
    lax.fori_loop(0, target.shape[0] // 32, body, 0)


def finish_kernel(count, *refs):
    for source, target in zip(refs[:count], refs[count + 1 : 2 * count + 1]):
        target[...] = source[...]
    gu, gate, up = refs[count], refs[2 * count + 1], refs[2 * count + 2]
    gate[...] = gu[:, : gate.shape[1]].astype(gate.dtype)
    up[...] = gu[:, gate.shape[1] :].astype(up.dtype)


def finish(arrays, grad_gu):
    steps = 4

    def spec(a, columns=None):
        return pl.BlockSpec((a.shape[0] // steps, columns or a.shape[1]), lambda i: (i, 0))

    units = grad_gu.shape[1] // 2
    half = jax.ShapeDtypeStruct((grad_gu.shape[0], units), jnp.float32)
    return pl.pallas_call(
        functools.partial(finish_kernel, len(arrays)),
        grid=(steps,),
        out_shape=tuple(jax.ShapeDtypeStruct(a.shape, a.dtype) for a in arrays) + (half, half),
        in_specs=[spec(a) for a in arrays] + [spec(grad_gu)],
        out_specs=tuple(spec(a) for a in arrays) + (spec(half), spec(half)),
    )(*arrays, grad_gu)


def expert_kernel(key, mine, normed_hbm, upstream_hbm, gu_hbm, own_down,
                  in_ref, prod_ref, gate_grad_out, grad_gu, sum_down, back_far,
                  gate_grad_ref, x_t, ups, gu, down, act, silu, slope, both, gd, rec_right, rec_left, stage, gate,
                  load_sem, src_sem, stage_sem, zss, zrs, rss, rrs, fss, frs):
    row, col = lax.axis_index("row"), lax.axis_index("col")
    sources, _, length = key.shape
    slots = in_ref.shape[0]
    capacity = slots // sources
    units = gu.shape[1] // 2
    width = units // 4
    chunk = 256
    x = in_ref
    right_dev, left_dev = {"col": (col + 1) % 4}, {"col": (col + 3) % 4}

    load_gu = pltpu.make_async_copy(gu_hbm, gu, load_sem.at[0])
    load_gu.start()
    load_down = pltpu.make_async_copy(own_down, down.at[col], load_sem.at[1])
    load_down.start()

    def fetch(s, slot):
        rows = pl.ds(pl.multiple_of(s * length, 16), length)
        for i, hbm in enumerate((normed_hbm, upstream_hbm)):
            to = prod_ref.at[pl.ds(pl.multiple_of((slot * 2 + i) * length, 16), length), :]
            yield pltpu.make_async_copy(hbm.at[rows, :], to, src_sem.at[slot, i])

    for copy in fetch(0, 0):
        copy.start()
    greet((X + Y, X + Y + SIB), (1, 2, 3))

    def pass_on(c, source, right, left):
        for d, (cond, there) in enumerate(((right, right_dev), (left, left_dev))):
            @pl.when(cond)
            def _():
                remote(source, down.at[c], zss.at[c, d], zrs.at[c], there).start()

    pass_on(col, own_down, col < 3, col > 0)

    def ag_step(s):
        @pl.when(col >= s)
        def _():
            c = col - s
            remote(down.at[c], down.at[c], zss.at[c, 0], zrs.at[c], right_dev).wait_recv()
            @pl.when(col < 3)
            def _():
                remote(down.at[c], down.at[c], zss.at[c, 0], zrs.at[c], right_dev).start()
        @pl.when(col + s < 4)
        def _():
            c = col + s
            remote(down.at[c], down.at[c], zss.at[c, 1], zrs.at[c], left_dev).wait_recv()
            @pl.when(col > 0)
            def _():
                remote(down.at[c], down.at[c], zss.at[c, 1], zrs.at[c], left_dev).start()

    def to_right(d):
        target = rec_right.at[d - 1]
        return remote(target, target, rss.at[0, d - 1], rrs.at[0, d - 1], right_dev)

    def to_left(d):
        target = rec_left.at[d]
        return remote(target, target, rss.at[1, d], rrs.at[1, d], left_dev)

    def from_end(d):
        @pl.when((col == 0) & (d > 0))
        def _():
            remote(gd.at[d], rec_right.at[d - 1], rss.at[0, d - 1], rrs.at[0, d - 1], right_dev).start()
        @pl.when((col == 3) & (d < 3))
        def _():
            remote(gd.at[d], rec_left.at[d], rss.at[1, d], rrs.at[1, d], left_dev).start()

    def add_rows(target, term):
        def body(i, carry):
            rows = pl.ds(pl.multiple_of(i * 64, 64), 64)
            total = target[rows, :].astype(jnp.float32) + term[rows, :].astype(jnp.float32)
            target[rows, :] = total.astype(target.dtype)
            return carry
        lax.fori_loop(0, width // 64, body, 0)

    def hop_right(d):
        to_right(d).wait_recv()
        add_rows(rec_right.at[d - 1], gd.at[d])
        to_right(d).start()

    def hop_left(d):
        to_left(d).wait_recv()
        add_rows(rec_left.at[d], gd.at[d])
        to_left(d).start()

    def select(s, carry):
        slot = s % 2
        @pl.when(s + 1 < sources)
        def _():
            for copy in fetch(s + 1, 1 - slot):
                copy.start()
        for copy in fetch(s, slot):
            copy.wait()
        chosen = key[s] == lax.broadcasted_iota(jnp.int32, (capacity, length), 0)
        value = jnp.sum(jnp.where(chosen, mine[s], 0.0), axis=1, keepdims=True)
        rows = pl.ds(pl.multiple_of(s * capacity, 16), capacity)
        gate[rows, :] = jnp.broadcast_to(value, (capacity, gate.shape[1]))
        one_hot = jnp.where(chosen, 1.0, 0.0).astype(x.dtype)
        for i, target in enumerate((x, ups)):
            block = prod_ref[pl.ds(pl.multiple_of((slot * 2 + i) * length, 16), length), :]
            target[rows, :] = dot(one_hot, block).astype(target.dtype)
        return carry
    lax.fori_loop(0, sources, select, 0)

    load_gu.wait()

    def forward(c):
        first = pl.ds(pl.multiple_of(c * width, width), width)
        second = pl.ds(pl.multiple_of(units + c * width, width), width)
        def body(m, carry):
            rows = pl.ds(pl.multiple_of(m * chunk, chunk), chunk)
            gate_pre = dot(x[rows, :], gu[:, first])
            up_pre = dot(x[rows, :], gu[:, second])
            sigma = jax.nn.sigmoid(gate_pre)
            silu_gate = gate_pre * sigma
            silu[rows, first] = silu_gate
            slope[rows, first] = up_pre * sigma * (1.0 + gate_pre * (1.0 - sigma))
            low = (silu_gate * up_pre).astype(act.dtype)
            act[rows, first] = low
            both[rows, first] = (low.astype(jnp.float32) * gate[rows, 0:1]).astype(both.dtype)
            return carry
        lax.fori_loop(0, slots // chunk, body, 0)
        gd[c] = t_dot(both[:, first], ups[...]).astype(gd.dtype)

    def forward_step(i, carry):
        c = jnp.where(i < 2, 3 - 3 * i, 4 - i)
        forward(c)
        pl.when((i < 2) | (col == 0))(lambda: from_end(c))
        pl.when(i == 1)(lambda: ag_step(1))
        @pl.when((i == 3) & (col == 3))
        def _():
            from_end(1)
            from_end(2)
        return carry
    lax.fori_loop(0, 4, forward_step, 0)
    load_down.wait()

    def turn(m, carry):
        rows = pl.ds(pl.multiple_of(m * chunk, chunk), chunk)
        x_t[:, rows] = x[rows, :].T
        return carry
    lax.fori_loop(0, slots // chunk, turn, 0)
    gate_grad_ref[...] = jnp.zeros_like(gate_grad_ref)

    def out_stage(c, slot):
        for i in range(2):
            yield pltpu.make_async_copy(
                stage.at[slot, :, pl.ds(i * width, width)],
                grad_gu.at[:, pl.ds(pl.multiple_of(i * units + c * width, width), width)],
                stage_sem.at[slot, i],
            )

    def far(j):
        there = row_at(row, X + Y + j)
        rows = pl.ds(pl.multiple_of(there * capacity, 16), capacity)
        return remote(in_ref.at[rows, :], back_far.at[j], fss.at[j], frs.at[j], {"row": there})

    def inputs(i, carry):
        chip = row_at(row, 2 * (3 - i)) // 2
        rows = pl.ds(pl.multiple_of(chip * 2 * capacity, 16), 2 * capacity)
        in_ref[rows, :] = dot_t(both[rows, :], gu[...]).astype(in_ref.dtype)
        return carry

    def backward(k):
        c = unit_at(col, k)
        first = pl.ds(pl.multiple_of(c * width, width), width)
        second = pl.ds(pl.multiple_of(units + c * width, width), width)
        def body(m, carry):
            rows = pl.ds(pl.multiple_of(m * chunk, chunk), chunk)
            plain = dot_t(ups[rows, :], down[c])
            term = jnp.sum(act[rows, first].astype(jnp.float32) * plain, axis=1, keepdims=True)
            gate_grad_ref[rows, :] += jnp.broadcast_to(term, (chunk, gate_grad_ref.shape[1]))
            act_grad = plain * gate[rows, 0:1]
            both[rows, first] = (act_grad * slope[rows, first]).astype(both.dtype)
            both[rows, second] = (act_grad * silu[rows, first]).astype(both.dtype)
            return carry
        lax.fori_loop(0, slots // chunk, body, 0)
        @pl.when(k == 3)
        def _():
            inputs(0, 0)
            far(0).start()
            far(1).start()
        slot = k % 2
        @pl.when(k >= 2)
        def _():
            for copy in out_stage(unit_at(col, k - 2), slot):
                copy.wait()
        def grads(i, carry):
            rows = pl.ds(pl.multiple_of(i * chunk, chunk), chunk)
            stage[slot, rows, 0:width] = dot(x_t[rows, :], both[:, first]).astype(stage.dtype)
            stage[slot, rows, width : 2 * width] = dot(x_t[rows, :], both[:, second]).astype(stage.dtype)
            return carry
        lax.fori_loop(0, x_t.shape[0] // chunk, grads, 0)
        for copy in out_stage(c, slot):
            copy.start()

    def backward_step(k, carry):
        backward(k)
        pl.when(k == 0)(lambda: ag_step(2))
        pl.when((k == 0) & (col == 1))(lambda: hop_right(3))
        pl.when((k == 0) & (col == 2))(lambda: hop_left(0))
        pl.when(k == 2)(lambda: ag_step(3))
        @pl.when((k == 2) & (col == 1))
        def _():
            hop_right(2)
            hop_left(0)
        @pl.when((k == 2) & (col == 2))
        def _():
            hop_right(3)
            hop_left(1)
        return carry
    lax.fori_loop(0, 4, backward_step, 0)

    lax.fori_loop(1, sources // 2, inputs, 0)

    def outputs(m, carry):
        rows = pl.ds(pl.multiple_of(m * chunk, chunk), chunk)
        total = dot(act[rows, 0:width], down[0])
        for c in range(1, 4):
            total = total + dot(act[rows, c * width : (c + 1) * width], down[c])
        prod_ref[rows, :] = total.astype(prod_ref.dtype)
        return carry
    lax.fori_loop(0, slots // chunk, outputs, 0)

    turned = gate_grad_ref[...].T
    for s in range(sources):
        gate_grad_out[s] = turned[0:1, s * capacity : (s + 1) * capacity]
    for k in (2, 3):
        for copy in out_stage(unit_at(col, k), k % 2):
            copy.wait()
    pl.when(col > 0)(lambda: to_right(col).wait_recv())
    pl.when(col < 3)(lambda: to_left(col).wait_recv())

    def to_sum(i, carry):
        rows = pl.ds(pl.multiple_of(i * 64, 64), 64)
        sum_down[rows, :] = gd[col, rows, :].astype(jnp.float32)
        @pl.when(col > 0)
        def _():
            sum_down[rows, :] += rec_right[jnp.maximum(col - 1, 0), rows, :].astype(jnp.float32)
        @pl.when(col < 3)
        def _():
            sum_down[rows, :] += rec_left[jnp.minimum(col, 2), rows, :].astype(jnp.float32)
        return carry
    lax.fori_loop(0, width // 64, to_sum, 0)

    def sent(e, carry):
        pl.when(e > col)(lambda: to_right(e).wait_send())
        pl.when(e < col)(lambda: to_left(e).wait_send())
        @pl.when((col < 3) & (e <= col))
        def _():
            remote(down.at[e], down.at[e], zss.at[e, 0], zrs.at[e], right_dev).wait_send()
        @pl.when((col > 0) & (e >= col))
        def _():
            remote(down.at[e], down.at[e], zss.at[e, 1], zrs.at[e], left_dev).wait_send()
        return carry
    lax.fori_loop(0, 4, sent, 0)
    for j in range(2):
        far(j).wait()


def run_expert(key, mine, normed, upstream, full_gu, own_down):
    sources, length = key.shape
    model, units = full_gu.shape[0], full_gu.shape[1] // 2
    width = own_down.shape[0]
    slots = sources * length // 2
    low, f32 = normed.dtype, jnp.float32
    sems = pltpu.SemaphoreType.DMA
    vm = pl.BlockSpec(memory_space=pltpu.VMEM)
    return pl.pallas_call(
        expert_kernel,
        out_shape=(
            jax.ShapeDtypeStruct((slots, model), low),
            jax.ShapeDtypeStruct((slots, model), low),
            jax.ShapeDtypeStruct((sources, 1, slots // sources), f32),
            jax.ShapeDtypeStruct((model, 2 * units), low),
            jax.ShapeDtypeStruct((width, model), f32),
            jax.ShapeDtypeStruct((2, slots // sources, model), low),
        ),
        in_specs=[vm, vm, ANY, ANY, ANY, ANY],
        out_specs=(vm, vm, vm, ANY, vm, ANY),
        scratch_shapes=[
            pltpu.VMEM((slots, 128), f32),
            pltpu.VMEM((model, slots), low),
            pltpu.VMEM((slots, model), low),
            pltpu.VMEM((model, 2 * units), low),
            pltpu.VMEM((4, width, model), low),
            pltpu.VMEM((slots, units), low),
            pltpu.VMEM((slots, units), f32),
            pltpu.VMEM((slots, units), f32),
            pltpu.VMEM((slots, 2 * units), low),
            pltpu.VMEM((4, width, model), low),
            pltpu.VMEM((3, width, model), low),
            pltpu.VMEM((3, width, model), low),
            pltpu.VMEM((2, model, 2 * width), low),
            pltpu.VMEM((slots, 128), f32),
            sems((2,)), sems((2, 2)), sems((2, 2)),
            sems((4, 2)), sems((4,)), sems((2, 3)), sems((2, 3)), sems((2,)), sems((2,)),
        ],
        compiler_params=pltpu.CompilerParams(
            collective_id=4, has_side_effects=True, vmem_limit_bytes=60 * 2**20
        ),
        cost_estimate=pl.CostEstimate(flops=0, bytes_accessed=1_000_000, transcendentals=0),
    )(key.reshape(sources, 1, length), mine.reshape(sources, 1, length), normed, upstream, full_gu, own_down)


def backward_kernel(table, router_p, gain_one, gain_two, lse,
                    gate_grad, in_grad, back_far, produced, hidden_hbm, tokens_hbm, cot_hbm, normed_hbm, attended_hbm,
                    two_hbm, qkv_hbm, full_a_hbm, full_out_hbm,
                    out_ref, d_tokens, sum_q, sum_k, sum_v, sum_b, sum_s,
                    cols, rec_in, rec_gate, rec_prod, hidden, tokens, cot, two, qkv, full_a, full_out,
                    n_t, a_t, branch, bias, out_rows, grad_c, qg, lgs, small,
                    own, sib_out, rec_sib, rec_one, rec_two, rec_z, s_rec, s_mid, s_zrec,
                    load, in_ss, in_rs, g_ss, g_rs, pr_ss, pr_rs, loc, far_sem,
                    ss1, rs1, ss2, rs2, zss, zrs, s_ss, s_rs, sz_ss, sz_rs):
    row, col = lax.axis_index("row"), lax.axis_index("col")
    core = row % 2
    chip = row // 2
    cy, cx = chip // 2, chip % 2
    length, model = hidden.shape
    capacity = rec_in.shape[0] // 8
    block = own.shape[2]
    width_b = sum_b.shape[1]
    width_a = own.shape[3] - width_b
    cut = block // 2
    half = length // 2
    f32, low = jnp.float32, branch.dtype
    sib = {"row": row_at(row, SIB)}
    to_x, to_y = {"row": row_at(row, X)}, {"row": row_at(row, Y)}

    def each_flip(function):
        def body(i, carry):
            function(7 - i)
            return carry
        lax.fori_loop(0, 7, body, 0)

    def block_of(r):
        return pl.ds(pl.multiple_of(r * capacity, 16), capacity)

    own_in = pltpu.make_async_copy(in_grad.at[block_of(row), :], rec_in.at[block_of(row), :], loc.at[0])
    own_gate = pltpu.make_async_copy(gate_grad.at[row], rec_gate.at[row], loc.at[1])
    own_prod = pltpu.make_async_copy(produced.at[block_of(row), :], rec_prod.at[block_of(row), :], loc.at[2])
    loads = [
        pltpu.make_async_copy(source, target, load.at[i])
        for i, (source, target) in enumerate((
            (normed_hbm, branch), (attended_hbm, out_ref), (hidden_hbm, hidden), (cot_hbm, cot), (two_hbm, two),
            (qkv_hbm, qkv), (tokens_hbm, tokens), (full_out_hbm, full_out), (full_a_hbm, full_a),
        ))
    ]
    greet(range(1, 8), (1, 2, 3))

    far_in = [
        pltpu.make_async_copy(back_far.at[j], rec_in.at[block_of(row_at(row, X + Y + j)), :], far_sem.at[j])
        for j in range(2)
    ]

    def back(flip):
        there = row_at(row, flip)
        return remote(in_grad.at[block_of(there), :], rec_in.at[block_of(row), :],
                      in_ss.at[flip - 1], in_rs.at[flip - 1], {"row": there})

    def back_gate(flip):
        there = row_at(row, flip)
        return remote(gate_grad.at[there], rec_gate.at[row], g_ss.at[flip - 1], g_rs.at[flip - 1], {"row": there})

    def each_near(function):
        def body(i, carry):
            function(5 - i)
            return carry
        lax.fori_loop(0, 5, body, 0)

    def back_prod(flip):
        there = row_at(row, flip)
        return remote(produced.at[block_of(there), :], rec_prod.at[block_of(row), :],
                      pr_ss.at[flip - 1], pr_rs.at[flip - 1], {"row": there})

    each_near(lambda flip: back(flip).start())
    each_flip(lambda flip: back_gate(flip).start())
    for copy in (own_in, own_gate, own_prod, *far_in):
        copy.start()
    cols[...] = table[...].T
    for copy in loads:
        copy.start()
    loads[0].wait()
    n_t[...] = branch[...].T
    loads[1].wait()
    a_t[...] = out_ref[...].T
    key_pos = lax.broadcasted_iota(jnp.int32, (length, length), 0)
    query_pos = lax.broadcasted_iota(jnp.int32, (length, length), 1)
    allowed = (key_pos <= query_pos) & (cols[:, 6:7] == table[6:7, :])
    bias[...] = jnp.where(allowed, 0.0, NEGATIVE)
    small[...] = jnp.zeros_like(small)
    for copy in loads[2:]:
        copy.wait()
    for copy in (own_in, own_gate, *far_in):
        copy.wait()
    each_flip(lambda flip: back_gate(flip).wait_recv())
    each_near(lambda flip: back(flip).wait_recv())

    all_gate = jnp.concatenate([rec_gate[e] for e in range(8)], axis=1)
    wide = rec_in.shape[0]
    lanes = lgs.shape[1]

    def at_slot(rows, k):
        return cols[rows, k : k + 1] == lax.broadcasted_iota(jnp.int32, (half, wide), 1).astype(f32)

    def to_hidden(m, carry):
        rows = pl.ds(pl.multiple_of(m * half, half), half)
        first, second = at_slot(rows, 0), at_slot(rows, 1)
        picked = jnp.where(first | second, 1.0, 0.0).astype(low)
        two_grad = dot(picked, rec_in[...])
        grad_0 = jnp.sum(jnp.where(first, all_gate, 0.0), axis=1, keepdims=True)
        grad_1 = jnp.sum(jnp.where(second, all_gate, 0.0), axis=1, keepdims=True)
        gate_0, gate_1 = cols[rows, 4:5], cols[rows, 5:6]
        mean = gate_0 * grad_0 + gate_1 * grad_1
        lane = lax.broadcasted_iota(jnp.int32, (half, lanes), 1).astype(f32)
        logit_grad = jnp.where(lane == cols[rows, 2:3], gate_0 * (grad_0 - mean), 0.0)
        logit_grad = logit_grad + jnp.where(lane == cols[rows, 3:4], gate_1 * (grad_1 - mean), 0.0)
        logit_grad = logit_grad.astype(low)
        lgs[rows, :] = logit_grad
        two_grad = two_grad + dot_t(logit_grad, router_p[...])
        h = hidden[rows, :]
        factor = lax.rsqrt(jnp.mean(h * h, axis=1, keepdims=True) + EPSILON)
        small[9:10, :] += jnp.sum(two_grad * h * factor, axis=0, keepdims=True)
        scaled = two_grad * gain_two[...]
        inner = jnp.mean(scaled * h, axis=1, keepdims=True)
        grad = cot[rows, :].astype(f32) + factor * scaled - h * (factor * factor * factor * inner)
        d_tokens[rows, :] = grad
        branch[rows, :] = grad.astype(low)
        return carry
    lax.fori_loop(0, 2, to_hidden, 0)
    small[0:8, :] = t_dot(lgs[...], two[...])[0:8, :]

    def nth(k):
        return (col + 1 + k) % 4

    lanes_of = {"a": pl.ds(0, width_a), "b": pl.ds(width_a, width_b)}
    part_at = {"a": 0, "b": 1}

    def to_sibling(part, c, q):
        view = lanes_of[part]
        i = part_at[part]
        return remote(sib_out.at[c, q, :, view], rec_sib.at[c, q, :, view], ss1.at[c, q, i], rs1.at[c, q, i], sib)

    def weight_grads(part, c, left, right):
        view = lanes_of[part]
        def body(q, carry):
            theirs = pl.ds(pl.multiple_of((q * 2 + 1 - core) * block, 16), block)
            sib_out[c, q, :, view] = dot(left[theirs, :], right()).astype(low)
            to_sibling(part, c, q).start()
            mine = pl.ds(pl.multiple_of((q * 2 + core) * block, 16), block)
            own[c, q, :, view] = dot(left[mine, :], right()).astype(low)
            return carry
        lax.fori_loop(0, 4, body, 0)

    def cols_b(c):
        return pl.ds(pl.multiple_of(c * width_b, 128), width_b)

    def attend_back(c):
        span_c = width_b // QUERY_PER_KEY
        for i in range(QUERY_PER_KEY):
            for u in range(2):
                rows = pl.ds(pl.multiple_of(c * width_b + (u * QUERY_PER_KEY + i) * HEAD_SIZE, HEAD_SIZE), HEAD_SIZE)
                out_rows[(2 * i + u) * HEAD_SIZE : (2 * i + u + 1) * HEAD_SIZE, :] = full_out[rows, :]
        grad_c[...] = dot_t(branch[...], out_rows[...]).astype(low)
        at_c = pl.multiple_of(c * width_a, 128)
        key = qkv[:, pl.ds(at_c + width_b, span_c)]
        value = qkv[:, pl.ds(at_c + width_b + span_c, span_c)]
        first = lax.broadcasted_iota(jnp.int32, (length, span_c), 1) < HEAD_SIZE
        none = jnp.zeros_like(key)
        keys = (jnp.where(first, key, none), jnp.where(first, none, key))
        values = (jnp.where(first, value, none), jnp.where(first, none, value))
        scale = HEAD_SIZE ** (-0.5)
        key_grads = [jnp.zeros((length, span_c), f32) for _ in range(2)]
        value_grads = [jnp.zeros((length, span_c), f32) for _ in range(2)]
        for i in range(QUERY_PER_KEY):
            q_i = qkv[:, pl.ds(at_c + i * span_c, span_c)]
            g_i = grad_c[:, i * span_c : (i + 1) * span_c]
            q_grad = jnp.zeros((length, span_c), f32)
            for u in range(2):
                log_total = lse[c * 2 + u, :, i * length : (i + 1) * length]
                probs = jnp.exp(dot_t(keys[u], q_i) * scale + bias[...] - log_total)
                prob_grad = dot_t(values[u], g_i)
                delta = jnp.sum(probs * prob_grad, axis=0, keepdims=True)
                score_grad = (probs * (prob_grad - delta)).astype(low)
                value_grads[u] += dot(probs.astype(low), g_i)
                key_grads[u] += dot(score_grad, q_i)
                q_grad += t_dot(score_grad, keys[u])
            qg[c, :, i * span_c : (i + 1) * span_c] = (q_grad * scale).astype(low)
        key_grad = jnp.where(first, key_grads[0], key_grads[1]) * scale
        qg[c, :, width_b : width_b + span_c] = key_grad.astype(low)
        qg[c, :, width_b + span_c : width_a] = jnp.where(first, value_grads[0], value_grads[1]).astype(low)

    top, bottom = pl.ds(0, cut), pl.ds(cut, block - cut)

    def one(part, c):
        view, i = lanes_of[part], part_at[part]
        for j in range(2):
            yield remote(own.at[c, j * 2 + 1 - cx, top, view], rec_one.at[c, 0, j, :, view],
                         ss2.at[c, i, 0, j], rs2.at[c, i, 0, j], to_x)
            yield remote(own.at[c, (1 - cy) * 2 + j, bottom, view], rec_one.at[c, 1, j, :, view],
                         ss2.at[c, i, 1, j], rs2.at[c, i, 1, j], to_y)

    def two_step(part, c):
        view, i = lanes_of[part], part_at[part]
        yield remote(own.at[c, (1 - cy) * 2 + cx, top, view], rec_two.at[c, 0, :, view],
                     ss2.at[c, i, 0, 2], rs2.at[c, i, 0, 2], to_y)
        yield remote(own.at[c, cy * 2 + 1 - cx, bottom, view], rec_two.at[c, 1, :, view],
                     ss2.at[c, i, 1, 2], rs2.at[c, i, 1, 2], to_x)

    def column(part, step):
        there = (col + step) % 4
        view, i = lanes_of[part], part_at[part]
        return remote(own.at[there, chip, :, view], rec_z.at[step - 1, :, view],
                      zss.at[i, step - 1], zrs.at[i, step - 1], {"col": there})

    def stage_one(part, k):
        c, view = nth(k), lanes_of[part]
        def body(q, carry):
            to_sibling(part, c, q).wait_recv()
            add_into(own.at[c, q, :, view], rec_sib.at[c, q, :, view])
            return carry
        lax.fori_loop(0, 4, body, 0)
        for copy in one(part, c):
            copy.start()

    def stage_two(part, k):
        c, view = nth(k), lanes_of[part]
        for copy in one(part, c):
            copy.wait_recv()
        for j in range(2):
            add_into(own.at[c, j * 2 + cx, top, view], rec_one.at[c, 0, j, :, view])
            add_into(own.at[c, cy * 2 + j, bottom, view], rec_one.at[c, 1, j, :, view])
        for copy in two_step(part, c):
            copy.start()

    def stage_three(part, k):
        c, view = nth(k), lanes_of[part]
        for copy in two_step(part, c):
            copy.wait_recv()
        add_into(own.at[c, chip, top, view], rec_two.at[c, 0, :, view])
        add_into(own.at[c, chip, bottom, view], rec_two.at[c, 1, :, view])
        pl.when(k < 3)(lambda: column(part, k + 1).start())

    def out_grads(k, carry):
        c = nth(k)
        weight_grads("b", c, a_t, lambda: branch[:, cols_b(c)])
        pl.when(k >= 1)(lambda: stage_one("b", k - 1))
        pl.when(k >= 2)(lambda: stage_two("b", k - 2))
        pl.when(k >= 3)(lambda: stage_three("b", k - 3))
        return carry
    lax.fori_loop(0, 4, out_grads, 0)

    def input_grads(k, carry):
        c = nth(k)
        attend_back(c)
        weight_grads("a", c, n_t, lambda: qg[c])
        pl.when(k == 0)(lambda: stage_one("b", k + 3))
        pl.when(k >= 1)(lambda: stage_one("a", k - 1))
        pl.when(k <= 1)(lambda: stage_two("b", k + 2))
        pl.when(k >= 2)(lambda: stage_two("a", k - 2))
        pl.when(k <= 2)(lambda: stage_three("b", k + 1))
        pl.when(k >= 3)(lambda: stage_three("a", k - 3))
        return carry
    lax.fori_loop(0, 4, input_grads, 0)
    stage_one("a", 3)
    each_flip(lambda flip: back_prod(flip).start())
    stage_two("a", 2)
    stage_three("a", 1)

    def to_tokens(m, carry):
        rows = pl.ds(pl.multiple_of(m * half, half), half)
        grad = dot_t(qg[0, rows, :], full_a[:, 0:width_a])
        for c in range(1, 4):
            grad = grad + dot_t(qg[c, rows, :], full_a[:, c * width_a : (c + 1) * width_a])
        x = tokens[rows, :].astype(f32)
        factor = lax.rsqrt(jnp.mean(x * x, axis=1, keepdims=True) + EPSILON)
        small[8:9, :] += jnp.sum(grad * x * factor, axis=0, keepdims=True)
        scaled = grad * gain_one[...]
        inner = jnp.mean(scaled * x, axis=1, keepdims=True)
        d_tokens[rows, :] += factor * scaled - x * (factor * factor * factor * inner)
        return carry
    lax.fori_loop(0, 2, to_tokens, 0)

    span = s_mid.shape[1]

    def small_plane(flip):
        there = row_at(row, flip)
        view = small.at[:, pl.ds(pl.multiple_of((there // 2) * span, 128), span)]
        return remote(view, s_rec.at[flip - 1], s_ss.at[flip - 1], s_rs.at[flip - 1], {"row": there})

    def small_column(step):
        return remote(s_mid, s_zrec.at[step - 1], sz_ss.at[step - 1], sz_rs.at[step - 1], {"col": (col + step) % 4})

    each_flip(lambda flip: small_plane(flip).start())
    stage_two("a", 3)
    stage_three("a", 2)
    s_mid[...] = small[:, pl.ds(pl.multiple_of(chip * span, 128), span)]

    def add_small(flip):
        small_plane(flip).wait_recv()
        s_mid[...] += s_rec[flip - 1]

    each_flip(add_small)
    for step in (1, 2, 3):
        small_column(step).start()
    stage_three("a", 3)

    own_prod.wait()
    each_flip(lambda flip: back_prod(flip).wait_recv())

    def to_output(m, carry):
        rows = pl.ds(pl.multiple_of(m * half, half), half)
        total = hidden[rows, :]
        for k in range(2):
            picked = jnp.where(at_slot(rows, k), 1.0, 0.0).astype(low)
            total = total + dot(picked, rec_prod[...]) * cols[rows, 4 + k : 5 + k]
        out_ref[rows, :] = total.astype(low)
        return carry
    lax.fori_loop(0, 2, to_output, 0)

    total = s_mid[...]
    for step in (1, 2, 3):
        small_column(step).wait_recv()
        total = total + s_zrec[step - 1]
    sum_s[...] = total
    for part in ("b", "a"):
        for step in (1, 2, 3):
            column(part, step).wait_recv()

    def to_sums(i, carry):
        rows = pl.ds(pl.multiple_of(i * 32, 32), 32)
        total = own[col, chip, rows, :].astype(f32)
        for step in range(3):
            total = total + rec_z[step, rows, :].astype(f32)
        span_c = width_b // QUERY_PER_KEY
        zero, one_, two_ = (total[:, i * span_c : (i + 1) * span_c] for i in range(QUERY_PER_KEY))
        turned = pltpu.roll(one_, HEAD_SIZE, 1)
        first = lax.broadcasted_iota(jnp.int32, zero.shape, 1) < HEAD_SIZE
        sum_q[rows, 0:span_c] = jnp.where(first, zero, turned)
        sum_q[rows, span_c : 2 * span_c] = jnp.where(first, two_, zero)
        sum_q[rows, 2 * span_c : width_b] = jnp.where(first, turned, two_)
        sum_k[rows, :] = total[:, width_b : width_b + span_c]
        sum_v[rows, :] = total[:, width_b + span_c : width_a]
        sum_b[rows, :] = total[:, width_a:]
        return carry
    lax.fori_loop(0, block // 32, to_sums, 0)


    each_near(lambda flip: back(flip).wait_send())

    def all_sent(flip):
        back_gate(flip).wait_send()
        back_prod(flip).wait_send()
        small_plane(flip).wait_send()

    each_flip(all_sent)
    for step in (1, 2, 3):
        small_column(step).wait_send()
        column("a", step).wait_send()
        column("b", step).wait_send()

    def sent(c, carry):
        for part in ("a", "b"):
            def body(q, carry):
                to_sibling(part, c, q).wait_send()
                return carry
            lax.fori_loop(0, 4, body, 0)
            for copy in one(part, c):
                copy.wait_send()
            for copy in two_step(part, c):
                copy.wait_send()
        return carry
    lax.fori_loop(0, 4, sent, 0)


def run_backward(slot_of, gates, ids, router, gain_one, gain_two, lse, segments, gate_grad, in_grad, back_far, produced,
                 hidden, tokens, cotangent, normed, attended, normed_two, qkv, full_a, full_out):
    table = jnp.concatenate(
        [slot_of.T.astype(jnp.float32), ids.T.astype(jnp.float32), gates.T, segments[None].astype(jnp.float32),
         jnp.zeros((1, segments.shape[0]), jnp.float32)], axis=0)
    sems = pltpu.SemaphoreType.DMA
    length, model = tokens.shape
    block = full_a.shape[0] // 8
    width_a, width_b = full_a.shape[1] // 4, full_out.shape[1] // 4
    width = width_a + width_b
    cut = block // 2
    low, f32 = tokens.dtype, jnp.float32
    vm = pl.BlockSpec(memory_space=pltpu.VMEM)
    slots = in_grad.shape[0]
    capacity = slots // 8
    span = model // 4
    router_p = jnp.pad(router, ((0, 0), (0, 128 - router.shape[1])))
    v = pltpu.VMEM
    rows_low = v((length, model), low)
    return pl.pallas_call(
        backward_kernel,
        out_shape=(
            jax.ShapeDtypeStruct((length, model), low),
            jax.ShapeDtypeStruct((length, model), f32),
            jax.ShapeDtypeStruct((block, width_b), f32),
            jax.ShapeDtypeStruct((block, (width_a - width_b) // 2), f32),
            jax.ShapeDtypeStruct((block, (width_a - width_b) // 2), f32),
            jax.ShapeDtypeStruct((block, width_b), f32),
            jax.ShapeDtypeStruct((16, span), f32),
        ),
        in_specs=[vm] * 5 + [ANY] * 13,
        out_specs=(vm,) * 7,
        scratch_shapes=[
            v((length, 8), f32), v((slots, model), low), v((8, 1, capacity), f32), v((slots, model), low),
            v((length, model), f32), rows_low, rows_low, rows_low,
            v(qkv.shape, low), v(full_a.shape, low), v(full_out.shape, low),
            v((model, length), low), v((model, length), low), rows_low,
            v((length, length), f32), v((width_b, model), low), v((length, width_b), low), v((4, length, width_a), low),
            v((length, 128), low), v((16, model), f32),
            v((4, 4, block, width), low), v((4, 4, block, width), low), v((4, 4, block, width), low),
            v((4, 2, 2, cut, width), low), v((4, 2, cut, width), low), v((3, block, width), low),
            v((7, 16, span), f32), v((16, span), f32), v((3, 16, span), f32),
            sems((9,)), sems((7,)), sems((7,)), sems((7,)), sems((7,)), sems((7,)), sems((7,)), sems((3,)), sems((2,)),
            sems((4, 4, 2)), sems((4, 4, 2)), sems((4, 2, 2, 3)), sems((4, 2, 2, 3)),
            sems((2, 3)), sems((2, 3)), sems((7,)), sems((7,)), sems((3,)), sems((3,)),
        ],
        compiler_params=pltpu.CompilerParams(
            collective_id=2, has_side_effects=True, vmem_limit_bytes=60 * 2**20
        ),
        cost_estimate=pl.CostEstimate(flops=0, bytes_accessed=1_000_000, transcendentals=0),
    )(table, router_p, gain_one, gain_two, lse, gate_grad, in_grad, back_far, produced, hidden, tokens,
      cotangent, normed, attended, normed_two, qkv, full_a, full_out)


def rms_factor(rows_in):
    return lax.rsqrt(jnp.mean(rows_in * rows_in, axis=1, keepdims=True) + EPSILON)


def dot(a, b):
    return jnp.dot(a, b, preferred_element_type=jnp.float32)


def dot_t(a, b):
    return lax.dot_general(a, b, (((1,), (1,)), ((), ())), preferred_element_type=jnp.float32)


def t_dot(a, b):
    return lax.dot_general(a, b, (((0,), (0,)), ((), ())), preferred_element_type=jnp.float32)


def on_small_slice():
    return lax.axis_size("row") == 8 and lax.axis_size("col") == 4


def pair_heads(a):
    if not on_small_slice():
        return a
    a = a.reshape(a.shape[0], -1, 2, QUERY_PER_KEY, HEAD_SIZE)
    return a.transpose(0, 1, 3, 2, 4).reshape(a.shape[0], -1)


def part_heads(a):
    a = a.reshape(a.shape[0], -1, QUERY_PER_KEY, 2, HEAD_SIZE)
    return a.transpose(0, 1, 3, 2, 4).reshape(a.shape[0], -1)


def gather_all(own_a, own_b, own_s, own_c):
    col_a = lax.all_gather(own_a, "col", axis=1, tiled=True)
    col_b = lax.all_gather(own_b, "col", axis=1, tiled=True)
    small = lax.all_gather(lax.all_gather(own_s, "col", axis=0), "row", axis=1)
    return (
        lax.all_gather(col_a, "row", axis=0, tiled=True),
        lax.all_gather(col_b, "row", axis=0, tiled=True),
        small,
        lax.all_gather(own_c, "row", axis=0, tiled=True),
    )


def spread(own_c, own_g):
    if on_small_slice():
        return spread_tokens(own_c, own_g)
    return (
        lax.all_gather(own_c, "row", axis=0, tiled=True),
        lax.all_gather(own_g, "row", axis=0),
    )


def reduce_all(grad_a, grad_b, grad_s):
    def both(g):
        plane = lax.psum_scatter(g, "row", scatter_dimension=0, tiled=True).astype(jnp.float32)
        return lax.psum_scatter(plane, "col", scatter_dimension=1, tiled=True)

    small = lax.psum_scatter(grad_s, "row", scatter_dimension=0, tiled=False)
    return both(grad_a), both(grad_b), lax.psum_scatter(small, "col", scatter_dimension=0, tiled=False)


def expert_elsewhere(place, routed, mine, plane_normed, plane_upstream, full_gu, own_down):
    rows, length = place.shape
    model = plane_normed.shape[1]
    hidden_units = full_gu.shape[1] // 2
    capacity = 2 * length * TOP // rows
    full_down = lax.all_gather(own_down, "col", axis=0, tiled=True)
    chosen_rows = (
        (place[:, None, :] == jnp.arange(capacity, dtype=jnp.int32)[None, :, None]) & routed[:, None, :]
    ).astype(jnp.bfloat16)

    def of_slots(plane):
        return jnp.einsum(
            "rct,rtd->rcd",
            chosen_rows,
            plane.reshape(rows, length, model),
            preferred_element_type=jnp.float32,
        ).astype(jnp.bfloat16).reshape(rows * capacity, model)

    grouped, grouped_up = of_slots(plane_normed), of_slots(plane_upstream)
    slot_gate = jnp.sum(jnp.where(chosen_rows > 0, mine[:, None, :], 0.0), axis=2)
    slot_gate = slot_gate.reshape(rows * capacity, 1)
    grouped_grad = (grouped_up.astype(jnp.float32) * slot_gate).astype(jnp.bfloat16)
    both_pre = dot(grouped, full_gu)
    gate_pre, up_pre = both_pre[:, :hidden_units], both_pre[:, hidden_units:]
    sigma = jax.nn.sigmoid(gate_pre)
    silu_gate = gate_pre * sigma
    activation = (silu_gate * up_pre).astype(jnp.bfloat16)
    grad_down_local = t_dot(activation, grouped_grad).astype(jnp.bfloat16)
    grad_down = lax.psum_scatter(grad_down_local, "col", scatter_dimension=0, tiled=True)
    act_grad = dot_t(grouped_grad, full_down)
    both_grad = jnp.concatenate(
        [
            (act_grad * up_pre * sigma * (1.0 + gate_pre * (1.0 - sigma))).astype(jnp.bfloat16),
            (act_grad * silu_gate).astype(jnp.bfloat16),
        ],
        axis=1,
    )
    in_grad = dot_t(both_grad, full_gu).astype(jnp.bfloat16)
    produced = dot(activation, full_down).astype(jnp.bfloat16)
    slot_gate_grad = jnp.sum(produced.astype(jnp.float32) * grouped_up.astype(jnp.float32), axis=1)
    grad_gu_local = t_dot(grouped, both_grad).astype(jnp.bfloat16)
    return in_grad, produced, slot_gate_grad, grad_gu_local, grad_down.astype(jnp.float32)


def masked_scores(queries, heads_of_key, segments, head_scale):
    length = queries.shape[0]
    heads_of_query = queries.reshape(length, KEY_VALUE_HEADS, QUERY_PER_KEY, HEAD_SIZE)
    scores = (
        jnp.einsum("qkgd,skd->kgqs", heads_of_query, heads_of_key, preferred_element_type=jnp.float32)
        * head_scale
    )
    pos = jnp.arange(length, dtype=jnp.int32)
    allowed = (pos[None, :] <= pos[:, None]) & (segments[None, :] == segments[:, None])
    return jnp.where(allowed, scores, NEGATIVE), heads_of_query


def per_device(
    tokens,
    attn_gain,
    w_query,
    w_key,
    w_value,
    w_out,
    expert_gain,
    router,
    w_gate,
    w_up,
    w_down,
    segment_ids,
    expert_ids,
    cotangent,
):
    length, model = tokens.shape
    rows, cols = lax.axis_size("row"), lax.axis_size("col")
    experts = w_gate.shape[0] * rows
    capacity = 2 * length * TOP // experts
    head_scale = HEAD_SIZE ** (-0.5)
    segments = segment_ids.reshape(-1)
    block, width_q = w_query.shape
    width_k = w_key.shape[1]
    width_a = width_q + 2 * width_k
    piece = attn_gain.shape[0]
    router_cols = router.shape[1]

    hidden_units = w_gate.shape[2]
    own_down = w_down[0]

    lane = 256

    def row_of(v):
        return jnp.pad(v, ((0, 0), (0, lane - v.shape[1])))

    own_s = jnp.concatenate(
        [row_of(router.T), row_of(attn_gain[None]), row_of(expert_gain[None])], axis=0
    )
    own_s = jnp.pad(own_s, ((0, 16 - own_s.shape[0]), (0, 0)))
    own_a = jnp.concatenate([pair_heads(w_query), w_key, w_value], axis=1)
    if on_small_slice():
        line_a, line_out, small, plane_upstream, own_gu = gather_line(
            own_a, w_out, own_s, cotangent, w_gate[0], w_up[0]
        )
        full_a, full_out = gather_plane(3, (line_a, line_out))
    else:
        own_gu = jnp.concatenate([w_gate[0], w_up[0]], axis=1)
        full_a, full_out, small, plane_upstream = gather_all(own_a, w_out, own_s, cotangent)
    full_gu = lax.all_gather(own_gu, "col", axis=0, tiled=True)
    full_router = small[:, :, :router_cols, :block].transpose(1, 3, 0, 2).reshape(model, experts)
    gain_one = small[:, :, router_cols, :piece].transpose(1, 0, 2).reshape(1, model).astype(jnp.float32)
    gain_two = small[:, :, router_cols + 1, :piece].transpose(1, 0, 2).reshape(1, model).astype(jnp.float32)

    rows_f = tokens.astype(jnp.float32)
    factor_one = rms_factor(rows_f)
    normed = (rows_f * factor_one * gain_one).astype(jnp.bfloat16)
    flat_qkv = dot(normed, full_a).astype(jnp.bfloat16)
    qkv = flat_qkv.reshape(length, cols, width_a)
    query_rows = qkv[:, :, :width_q].reshape(length, -1)
    if on_small_slice():
        query_rows = part_heads(query_rows)
    rows_of_key = qkv[:, :, width_q : width_q + width_k].reshape(length, -1)
    rows_of_value = qkv[:, :, width_q + width_k :].reshape(length, -1)
    heads_of_key = rows_of_key.reshape(length, KEY_VALUE_HEADS, HEAD_SIZE)
    heads_of_value = rows_of_value.reshape(length, KEY_VALUE_HEADS, HEAD_SIZE)

    scores, heads_of_query = masked_scores(query_rows, heads_of_key, segments, head_scale)
    row_max = jnp.max(scores, axis=-1, keepdims=True)
    expo_rows = jnp.exp(scores - row_max)
    totals = jnp.sum(expo_rows, axis=-1, keepdims=True)
    soft_probs = expo_rows / totals
    probs_low = soft_probs.astype(jnp.bfloat16)
    attended = (
        jnp.einsum("kgqs,skd->qkgd", probs_low, heads_of_value, preferred_element_type=jnp.float32)
        .reshape(length, -1)
        .astype(jnp.bfloat16)
    )
    hidden = rows_f + dot(attended, full_out)
    factor_two = rms_factor(hidden)
    normed_two = (hidden * factor_two * gain_two).astype(jnp.bfloat16)
    logits = dot(normed_two, full_router)

    named = expert_ids[:, :, None] == jnp.arange(experts, dtype=jnp.int32)[None, None, :]
    chosen = jnp.sum(jnp.where(named, logits[:, None, :], 0.0), axis=2)
    gate_probs = jax.nn.softmax(chosen, axis=1)
    gate_table = jnp.sum(jnp.where(named, gate_probs[:, :, None], 0.0), axis=1)
    gate_table = jnp.where(jnp.any(named, axis=1), gate_table, -1.0)
    plane_normed, plane_gate = spread(normed_two, gate_table.T)
    mine = lax.dynamic_index_in_dim(plane_gate, lax.axis_index("row"), axis=1, keepdims=False)
    routed = mine >= 0.0
    place = jnp.cumsum(routed.astype(jnp.int32), axis=1) - 1
    any_named = jnp.any(named, axis=1)
    before = jnp.cumsum(any_named.astype(jnp.int32), axis=0) - 1
    slot_of = jnp.sum(
        jnp.where(named, before[:, None, :] + jnp.arange(experts, dtype=jnp.int32) * capacity, 0),
        axis=2,
    )
    if on_small_slice():
        in_grad, produced, slot_gate_grad, grad_gu_local, grad_down, back_far = run_expert(
            jnp.where(routed, place, -1), mine, plane_normed, plane_upstream, full_gu, own_down
        )
        grad_gu = lax.psum_scatter(grad_gu_local, "col", scatter_dimension=0, tiled=True)
        lse = (row_max + jnp.log(totals)).reshape(KEY_VALUE_HEADS, 1, QUERY_PER_KEY * length)
        output, d_tokens, sum_q, sum_k, sum_v, sum_out, sum_s = run_backward(
            slot_of, gate_probs, expert_ids, full_router, gain_one, gain_two, lse, segments,
            slot_gate_grad, in_grad, back_far, produced, hidden, tokens, cotangent, normed, attended, normed_two,
            flat_qkv, full_a, full_out,
        )
        core = lax.axis_index("row") % 2
        col = lax.axis_index("col")
        own_router = lax.dynamic_slice(sum_s, (col * router_cols, core * block), (router_cols, block))
        own_gains = lax.dynamic_slice(sum_s, (experts, core * block + col * piece), (2, piece))
        output, d_tokens, sum_q, sum_k, sum_v, sum_out, grad_down, grad_gate, grad_up = finish(
            (output, d_tokens, sum_q, sum_k, sum_v, sum_out, grad_down), grad_gu
        )
        return (
            output,
            d_tokens,
            own_gains[0],
            sum_q,
            sum_k,
            sum_v,
            sum_out,
            own_gains[1],
            own_router.T,
            grad_gate[None],
            grad_up[None],
            grad_down[None],
        )
    else:
        in_grad, produced, slot_gate_grad, grad_gu_local, grad_down = expert_elsewhere(
            place, routed, mine, plane_normed, plane_upstream, full_gu, own_down
        )
    grad_gu = lax.psum_scatter(grad_gu_local, "col", scatter_dimension=0, tiled=True)
    back_grad = lax.all_to_all(
        in_grad.reshape(rows, capacity, model), "row", split_axis=0, concat_axis=0, tiled=True
    ).reshape(experts * capacity, model)
    back_gate_grad = lax.all_to_all(
        slot_gate_grad.reshape(rows, 1, capacity), "row", split_axis=0, concat_axis=0, tiled=True
    ).reshape(experts * capacity)
    produced, back_grad = lax.optimization_barrier((produced, back_grad))
    back_rows = lax.all_to_all(
        produced.reshape(rows, capacity, model), "row", split_axis=0, concat_axis=0, tiled=True
    ).reshape(experts * capacity, model)

    all_slots = jnp.arange(experts * capacity, dtype=jnp.int32)
    is_slot = slot_of.T[:, :, None] == all_slots[None, None, :]
    from_slot = is_slot.astype(jnp.bfloat16)
    gate_grad = jnp.sum(jnp.where(is_slot, back_gate_grad[None, None, :], 0.0), axis=2).T
    returned = [dot(from_slot[k], back_rows) for k in range(TOP)]
    upstream = cotangent.astype(jnp.float32)
    output = (
        hidden + sum(returned[k] * gate_probs[:, k : k + 1] for k in range(TOP))
    ).astype(jnp.bfloat16)
    normed_two_grad = dot(from_slot[0] + from_slot[1], back_grad)
    pair_mean = jnp.sum(gate_probs * gate_grad, axis=1, keepdims=True)
    pair_logit = gate_probs * (gate_grad - pair_mean)
    logit_grad = jnp.sum(jnp.where(named, pair_logit[:, :, None], 0.0), axis=1).astype(jnp.bfloat16)
    grad_router = t_dot(normed_two, logit_grad)
    normed_two_grad = normed_two_grad + dot_t(logit_grad, full_router)
    grad_expert_gain = jnp.sum(normed_two_grad * hidden * factor_two, axis=0)
    scaled_two = normed_two_grad * gain_two
    hidden_grad = (
        upstream
        + factor_two * scaled_two
        - hidden * factor_two**3 * jnp.mean(scaled_two * hidden, axis=1, keepdims=True)
    )
    branch_grad = hidden_grad.astype(jnp.bfloat16)
    grad_out_full = t_dot(attended, branch_grad).astype(jnp.bfloat16)
    attended_grad = dot_t(branch_grad, full_out).astype(jnp.bfloat16)

    gradient_heads = attended_grad.reshape(length, KEY_VALUE_HEADS, QUERY_PER_KEY, HEAD_SIZE)
    value_grad = jnp.einsum(
        "kgqs,qkgd->skd", probs_low, gradient_heads, preferred_element_type=jnp.float32
    )
    prob_grad = jnp.einsum(
        "qkgd,skd->kgqs", gradient_heads, heads_of_value, preferred_element_type=jnp.float32
    )
    delta_sum = jnp.sum(soft_probs * prob_grad, axis=-1, keepdims=True)
    score_grad = (soft_probs * (prob_grad - delta_sum)).astype(jnp.bfloat16)
    query_grad = (
        jnp.einsum("kgqs,skd->qkgd", score_grad, heads_of_key, preferred_element_type=jnp.float32)
        * head_scale
    )
    key_grad = (
        jnp.einsum("kgqs,qkgd->skd", score_grad, heads_of_query, preferred_element_type=jnp.float32)
        * head_scale
    )
    qkv_grad = jnp.concatenate(
        [
            query_grad.astype(jnp.bfloat16).reshape(length, cols, width_q),
            key_grad.astype(jnp.bfloat16).reshape(length, cols, width_k),
            value_grad.astype(jnp.bfloat16).reshape(length, cols, width_k),
        ],
        axis=2,
    ).reshape(length, cols * width_a)
    grad_a_full = t_dot(normed, qkv_grad).astype(jnp.bfloat16)
    normed_grad = dot_t(qkv_grad, full_a)
    grad_attn_gain = jnp.sum(normed_grad * rows_f * factor_one, axis=0)
    scaled_one = normed_grad * gain_one
    d_tokens = (
        hidden_grad
        + factor_one * scaled_one
        - rows_f * factor_one**3 * jnp.mean(scaled_one * rows_f, axis=1, keepdims=True)
    )
    grad_s = jnp.concatenate(
        [
            jnp.pad(
                grad_router.reshape(rows, block, cols, router_cols).transpose(0, 2, 3, 1),
                ((0, 0), (0, 0), (0, 0), (0, lane - block)),
            ),
            jnp.pad(
                jnp.stack([grad_attn_gain, grad_expert_gain])
                .reshape(2, rows, cols, piece)
                .transpose(1, 2, 0, 3),
                ((0, 0), (0, 0), (0, 6 - router_cols), (0, lane - piece)),
            ),
        ],
        axis=2,
    )
    grad_a_full, d_tokens, output = lax.optimization_barrier((grad_a_full, d_tokens, output))
    sum_a, sum_out, sum_s = reduce_all(grad_a_full, grad_out_full, grad_s)
    return (
        output,
        d_tokens,
        sum_s[router_cols, :piece],
        sum_a[:, :width_q],
        sum_a[:, width_q : width_q + width_k],
        sum_a[:, width_q + width_k :],
        sum_out,
        sum_s[router_cols + 1, :piece],
        sum_s[:router_cols, :block].T,
        grad_gu[:, :hidden_units].astype(jnp.float32)[None],
        grad_gu[:, hidden_units:].astype(jnp.float32)[None],
        grad_down[None],
    )


def solution(mesh):
    in_specs = (
        P(("row", "col"), None),
        P(("row", "col")),
        P("row", "col"),
        P("row", "col"),
        P("row", "col"),
        P("row", "col"),
        P(("row", "col")),
        P("row", "col"),
        P("row", "col", None),
        P("row", "col", None),
        P("row", "col", None),
        P(("row", "col"), None),
        P(("row", "col"), None),
        P(("row", "col"), None),
    )
    out_specs = (
        P(("row", "col"), None),
        P(("row", "col"), None),
        P(("row", "col")),
        P("row", "col"),
        P("row", "col"),
        P("row", "col"),
        P("row", "col"),
        P(("row", "col")),
        P("row", "col"),
        P("row", "col", None),
        P("row", "col", None),
        P("row", "col", None),
    )
    return jax.shard_map(
        per_device, mesh=mesh, in_specs=in_specs, out_specs=out_specs, check_vma=False
    )
```

```python
import functools

import jax
import jax.numpy as jnp
from jax import lax
from jax.experimental import pallas as pl
from jax.experimental.pallas import tpu as pltpu
from jax.sharding import PartitionSpec as P

KEY_VALUE_HEADS = 8
HEAD_SIZE = 64
TOP = 2
QUERY_PER_KEY = 3


EPSILON = 1e-05
NEGATIVE = -1e30


MESH = pl.DeviceIdType.MESH
ANY = pl.BlockSpec(memory_space=pl.ANY)


def row_at(row, flip):
    y, x, core = row // 4, (row // 2) % 2, row % 2
    return (
        (y + flip // 4) % 2 * 4 + (x + (flip // 2) % 2) % 2 * 2 + (core + flip % 2) % 2
    )


def remote(source, target, send, receive, device):
    return pltpu.make_async_remote_copy(
        source, target, send, receive, device_id=device, device_id_type=MESH
    )


def greet(row_flips, col_steps):
    row, col = lax.axis_index("row"), lax.axis_index("col")
    sem = pltpu.get_barrier_semaphore()
    for flip in row_flips:
        pl.semaphore_signal(
            sem, inc=1, device_id={"row": row_at(row, flip)}, device_id_type=MESH
        )
    for step in col_steps:
        pl.semaphore_signal(
            sem, inc=1, device_id={"col": (col + step) % 4}, device_id_type=MESH
        )
    pl.semaphore_wait(sem, len(row_flips) + len(col_steps))


def unit_order(col, k):
    table = ((0, 1, 2, 3), (1, 0, 2, 3), (2, 3, 1, 0), (3, 2, 1, 0))
    out = table[3][k]
    for c in (2, 1, 0):
        out = jnp.where(col == c, table[c][k], out)
    return out


def unit_at(col, k):
    end = (col == 0) | (col == 3)
    ends = jnp.where(col == 0, k, 3 - k)
    middle = jnp.where(k == 0, col, jnp.where(k == 3, jnp.where(col == 1, 3, 0), jnp.where(col == 1, 2 * k - 2, 5 - 2 * k)))
    return jnp.where(end, ends, middle)


X, Y, SIB = 2, 4, 1


def plane_send(view, row, ss, rs, source=None):
    source = view(row) if source is None else source
    for i, flip in enumerate((X, Y, SIB)):
        remote(source, view(row), ss(i), rs(i), {"row": row_at(row, flip)}).start()


def plane_forward(view, halves, row, ss, rs):
    first, second = halves
    from_x, from_y = row_at(row, X), row_at(row, Y)
    sib = {"row": row_at(row, SIB)}
    remote(view(from_x), view(from_x), ss(0), rs(0), sib).wait_recv()
    remote(first(from_x), first(from_x), ss(3), rs(3), {"row": from_y}).start()
    remote(view(from_x), view(from_x), ss(5), rs(5), sib).start()
    remote(view(from_y), view(from_y), ss(1), rs(1), sib).wait_recv()
    remote(second(from_y), second(from_y), ss(4), rs(4), {"row": from_x}).start()
    remote(view(from_y), view(from_y), ss(6), rs(6), sib).start()


def plane_last(view, halves, row, ss, rs):
    first, second = halves
    diag = row_at(row, X + Y)
    sib = {"row": row_at(row, SIB)}
    remote(first(diag), first(diag), ss(3), rs(3), sib).wait_recv()
    remote(first(diag), first(diag), ss(7), rs(7), sib).start()
    remote(second(diag), second(diag), ss(4), rs(4), sib).wait_recv()
    remote(second(diag), second(diag), ss(8), rs(8), sib).start()


def plane_finish(view, halves, row, ss, rs):
    first, second = halves
    sib_row = row_at(row, SIB)
    sib = {"row": sib_row}
    whole = view(sib_row)
    remote(whole, whole, ss(2), rs(2), sib).wait_recv()
    for i, flip in ((5, X), (6, Y)):
        block = view(row_at(sib_row, flip))
        remote(block, block, ss(i), rs(i), sib).wait_recv()
    far = row_at(sib_row, X + Y)
    remote(first(far), first(far), ss(7), rs(7), sib).wait_recv()
    remote(second(far), second(far), ss(8), rs(8), sib).wait_recv()
    for i in range(9):
        block = view(row) if i in (0, 1, 2, 5, 6) else (first(row) if i in (3, 7) else second(row))
        remote(block, block, ss(i), rs(i), sib).wait_send()


def pick(ref, cols, halves_rows):
    block, cut = halves_rows

    def at(start, size):
        def view(r):
            rows = pl.ds(pl.multiple_of(r * block + start, 16), size)
            if cols is None:
                return ref.at[rows, :]
            return ref.at[rows, pl.ds(pl.multiple_of(cols[0], 128), cols[1])]

        return view

    return at(0, block), (at(0, cut), at(cut, block - cut))


def through(source, middle, target, sem):
    return pltpu.make_async_copy(source, middle, sem), pltpu.make_async_copy(middle, target, sem)


def through(source, middle, target, sem):
    return pltpu.make_async_copy(source, middle, sem), pltpu.make_async_copy(middle, target, sem)


def line_kernel(own_a, own_b, own_s, own_c, w_gate, w_up, line_a, line_b, full_s, full_c, own_gu, mid_a, mid_b, mid_c, mid_gu,
                zss, zrs, css, crs, s_zs, s_zr, s_ps, s_pr, loc):
    row, col = lax.axis_index("row"), lax.axis_index("col")
    width_a, width_b = own_a.shape[1], own_b.shape[1]
    rows_c = own_c.shape[0]
    vc, hc = pick(full_c, None, (rows_c, rows_c // 2))
    csv, crv = (lambda i: css.at[i]), (lambda i: crs.at[i])

    def of_a(c):
        return line_a.at[:, pl.ds(pl.multiple_of(c * width_a, 128), width_a)]

    def of_b(c):
        return line_b.at[:, pl.ds(pl.multiple_of(c * width_b, 128), width_b)]

    copies = [
        through(own_a, mid_a, of_a(col), loc.at[0]),
        through(own_b, mid_b, of_b(col), loc.at[1]),
        through(own_c, mid_c, vc(row), loc.at[2]),
    ]
    for copy, _ in copies:
        copy.start()
    small_copy = pltpu.make_async_copy(own_s, full_s.at[col, row], loc.at[3])
    small_copy.start()
    units = w_gate.shape[1]
    to_gu = [
        pltpu.make_async_copy(w, mid_gu.at[:, pl.ds(i * units, units)], loc.at[4 + i])
        for i, w in enumerate((w_gate, w_up))
    ]
    from_gu = pltpu.make_async_copy(mid_gu, own_gu, loc.at[6])
    greet(range(1, 8), (1, 2, 3))

    def along(c, source_a, source_b, right, left):
        for d, (cond, step) in enumerate(((right, 1), (left, 3))):
            @pl.when(cond)
            def _():
                there = {"col": (col + step) % 4}
                remote(source_a, of_a(c), zss.at[0, c, d], zrs.at[0, c], there).start()
                remote(source_b, of_b(c), zss.at[1, c, d], zrs.at[1, c], there).start()

    def arrived(k):
        c = unit_order(col, k)
        there = {"col": (col + 1) % 4}
        remote(of_a(c), of_a(c), zss.at[0, c, 0], zrs.at[0, c], there).wait_recv()
        remote(of_b(c), of_b(c), zss.at[1, c, 0], zrs.at[1, c], there).wait_recv()
        along(c, of_a(c), of_b(c), (c < col) & (col < 3), (c > col) & (col > 0))

    along(col, own_a, own_b, col < 3, col > 0)
    for i, step in enumerate((1, 2, 3)):
        remote(own_s, full_s.at[col, row], s_zs.at[i], s_zr.at[i], {"col": (col + step) % 4}).start()
    plane_send(vc, row, csv, crv, own_c)
    for copy in to_gu:
        copy.start()
    for first, second in copies:
        first.wait()
        second.start()
    small_copy.wait()
    for copy in to_gu:
        copy.wait()
    from_gu.start()
    arrived(1)
    for i, step in enumerate((3, 2, 1)):
        remote(own_s, full_s.at[(col + step) % 4, row], s_zs.at[i], s_zr.at[i], {"col": (col + 1) % 4}).wait()
    for i in range(1, 8):
        remote(full_s.at[:, row], full_s.at[:, row], s_ps.at[i - 1], s_pr.at[i - 1], {"row": row_at(row, i)}).start()
    arrived(2)
    plane_forward(vc, hc, row, csv, crv)
    arrived(3)
    plane_last(vc, hc, row, csv, crv)
    for _, second in copies:
        second.wait()
    from_gu.wait()
    plane_finish(vc, hc, row, csv, crv)
    for i in range(1, 8):
        there = row_at(row, i)
        remote(full_s.at[:, there], full_s.at[:, there], s_ps.at[i - 1], s_pr.at[i - 1], {"row": there}).wait()
    for k in range(4):
        c = unit_order(col, k)
        right = (c <= col) & (col < 3)
        left = (c >= col) & (col > 0)
        for d, cond in enumerate((right, left)):
            @pl.when(cond)
            def _():
                there = {"col": (col + 1) % 4}
                remote(of_a(c), of_a(c), zss.at[0, c, d], zrs.at[0, c], there).wait_send()
                remote(of_b(c), of_b(c), zss.at[1, c, d], zrs.at[1, c], there).wait_send()


def gather_line(own_a, own_b, own_s, own_c, w_gate, w_up):
    sems = pltpu.SemaphoreType.DMA
    rows_c = own_c.shape[0]
    return pl.pallas_call(
        line_kernel,
        out_shape=(
            jax.ShapeDtypeStruct((own_a.shape[0], own_a.shape[1] * 4), own_a.dtype),
            jax.ShapeDtypeStruct((own_b.shape[0], own_b.shape[1] * 4), own_b.dtype),
            jax.ShapeDtypeStruct((4, 8) + own_s.shape, own_s.dtype),
            jax.ShapeDtypeStruct((8 * rows_c, own_c.shape[1]), own_c.dtype),
            jax.ShapeDtypeStruct((w_gate.shape[0], 2 * w_gate.shape[1]), w_gate.dtype),
        ),
        in_specs=[ANY] * 6,
        out_specs=(ANY,) * 5,
        scratch_shapes=[
            pltpu.VMEM(own_a.shape, own_a.dtype),
            pltpu.VMEM(own_b.shape, own_b.dtype),
            pltpu.VMEM(own_c.shape, own_c.dtype),
            pltpu.VMEM((w_gate.shape[0], 2 * w_gate.shape[1]), w_gate.dtype),
            sems((2, 4, 2)), sems((2, 4)),
            sems((9,)), sems((9,)),
            sems((3,)), sems((3,)), sems((7,)), sems((7,)), sems((7,)),
        ],
        compiler_params=pltpu.CompilerParams(collective_id=0, has_side_effects=True),
        cost_estimate=pl.CostEstimate(flops=0, bytes_accessed=1_000_000, transcendentals=0),
    )(own_a, own_b, own_s, own_c, w_gate, w_up)


def plane_kernel(count, *refs):
    row = lax.axis_index("row")
    owns, fulls, mids = refs[:count], refs[count : 2 * count], refs[2 * count : 3 * count]
    ss, rs, loc = refs[3 * count :]
    views, copies = [], []
    for i in range(count):
        block = owns[i].shape[0]
        views.append(pick(fulls[i], None, (block, block // 2)))
        copies.append(through(owns[i], mids[i], views[i][0](row), loc.at[i]))
        copies[i][0].start()
    greet(range(1, 8), ())

    def sems_of(i):
        return (lambda j: ss.at[i, j]), (lambda j: rs.at[i, j])

    for i in range(count):
        plane_send(views[i][0], row, *sems_of(i), owns[i])
    for first, second in copies:
        first.wait()
        second.start()
    for i in range(count):
        plane_forward(*views[i], row, *sems_of(i))
    for i in range(count):
        plane_last(*views[i], row, *sems_of(i))
    for _, second in copies:
        second.wait()
    for i in range(count):
        plane_finish(*views[i], row, *sems_of(i))


def gather_plane(collective, owns):
    sems = pltpu.SemaphoreType.DMA
    count = len(owns)
    return pl.pallas_call(
        functools.partial(plane_kernel, count),
        out_shape=tuple(
            jax.ShapeDtypeStruct((8 * own.shape[0], own.shape[1]), own.dtype) for own in owns
        ),
        in_specs=[ANY] * count,
        out_specs=(ANY,) * count,
        scratch_shapes=[pltpu.VMEM(own.shape, own.dtype) for own in owns]
        + [sems((count, 9)), sems((count, 9)), sems((count,))],
        compiler_params=pltpu.CompilerParams(collective_id=collective, has_side_effects=True),
        cost_estimate=pl.CostEstimate(flops=0, bytes_accessed=1_000_000, transcendentals=0),
    )(*owns)


def spread_kernel(own_c, own_g, full_c, full_g, mid_c, css, crs, gss, grs, loc):
    row = lax.axis_index("row")
    rows_c = own_c.shape[0]
    vc, hc = pick(full_c, None, (rows_c, rows_c // 2))
    csv, crv = (lambda i: css.at[i]), (lambda i: crs.at[i])
    first, second = through(own_c, mid_c, vc(row), loc.at[0])
    first.start()
    own_copy = pltpu.make_async_copy(own_g, full_g.at[row], loc.at[1])
    own_copy.start()
    greet(range(1, 8), ())
    plane_send(vc, row, csv, crv, own_c)
    for i in range(1, 8):
        remote(own_g, full_g.at[row], gss.at[i - 1], grs.at[i - 1], {"row": row_at(row, i)}).start()
    first.wait()
    second.start()
    plane_forward(vc, hc, row, csv, crv)
    plane_last(vc, hc, row, csv, crv)
    second.wait()
    own_copy.wait()
    plane_finish(vc, hc, row, csv, crv)
    for i in range(1, 8):
        there = row_at(row, i)
        remote(own_g, full_g.at[there], gss.at[i - 1], grs.at[i - 1], {"row": there}).wait()


def spread_tokens(own_c, own_g):
    sems = pltpu.SemaphoreType.DMA
    return pl.pallas_call(
        spread_kernel,
        out_shape=(
            jax.ShapeDtypeStruct((8 * own_c.shape[0], own_c.shape[1]), own_c.dtype),
            jax.ShapeDtypeStruct((8,) + own_g.shape, own_g.dtype),
        ),
        in_specs=[ANY] * 2,
        out_specs=(ANY,) * 2,
        scratch_shapes=[
            pltpu.VMEM(own_c.shape, own_c.dtype),
            sems((9,)), sems((9,)), sems((7,)), sems((7,)), sems((2,)),
        ],
        compiler_params=pltpu.CompilerParams(collective_id=1, has_side_effects=True),
        cost_estimate=pl.CostEstimate(flops=0, bytes_accessed=1_000_000, transcendentals=0),
    )(own_c, own_g)


def add_into(target, term):
    def body(i, carry):
        rows = pl.ds(pl.multiple_of(i * 32, 32), 32)
        total = target[rows, :].astype(jnp.float32) + term[rows, :].astype(jnp.float32)
        target[rows, :] = total.astype(target.dtype)
        return carry
    lax.fori_loop(0, target.shape[0] // 32, body, 0)


def finish_kernel(count, experts, block, piece, *refs):
    for source, target in zip(refs[:count], refs[count + 2 : 2 * count + 2]):
        target[...] = source[...]
    gu, sums = refs[count : count + 2]
    gate, up, router, gain_a, gain_e, turned = refs[2 * count + 2 :]
    gate[...] = gu[:, : gate.shape[1]].astype(gate.dtype)
    up[...] = gu[:, gate.shape[1] :].astype(up.dtype)

    @pl.when(pl.program_id(0) == 0)
    def _():
        core, col = lax.axis_index("row") % 2, lax.axis_index("col")
        turned[...] = sums[...].T
        mine = turned[pl.ds(pl.multiple_of(core * block, 8), block), :].T
        rows = lax.broadcasted_iota(jnp.int32, mine.shape, 0)
        for j in range(router.shape[0]):
            at = col * router.shape[0] + j
            router[j : j + 1, :] = jnp.sum(jnp.where(rows == at, mine, 0.0), axis=0, keepdims=True)
        own = turned[pl.ds(pl.multiple_of(core * block + col * piece, 8), piece), :].T
        gain_a[...] = own[experts : experts + 1, :]
        gain_e[...] = own[experts + 1 : experts + 2, :]


def finish(arrays, grad_gu, sums, block, piece, router_cols):
    steps = 4
    experts = router_cols * 4

    def spec(a):
        return pl.BlockSpec((a.shape[0] // steps, a.shape[1]), lambda i: (i, 0))

    def once(a):
        return pl.BlockSpec(a.shape, lambda i: (0, 0))

    f32 = jnp.float32
    half = jax.ShapeDtypeStruct((grad_gu.shape[0], grad_gu.shape[1] // 2), f32)
    small = [jax.ShapeDtypeStruct(shape, f32) for shape in ((router_cols, block), (1, piece), (1, piece))]
    return pl.pallas_call(
        functools.partial(finish_kernel, len(arrays), experts, block, piece),
        grid=(steps,),
        out_shape=(*(jax.ShapeDtypeStruct(a.shape, a.dtype) for a in arrays), half, half, *small),
        in_specs=[*(spec(a) for a in arrays), spec(grad_gu), once(sums)],
        out_specs=(*(spec(a) for a in arrays), spec(half), spec(half), *(once(a) for a in small)),
        scratch_shapes=[pltpu.VMEM((sums.shape[1], sums.shape[0]), f32)],
    )(*arrays, grad_gu, sums)


def expert_kernel(key, mine, normed_hbm, upstream_hbm, gu_hbm, own_down,
                  in_ref, prod_ref, gate_grad_out, grad_gu, sum_down, back_far,
                  gate_grad_ref, x_t, ups, gu, down, act, silu, slope, both, gd, rec_right, rec_left, stage, gate,
                  load_sem, src_sem, stage_sem, zss, zrs, rss, rrs, fss, frs):
    row, col = lax.axis_index("row"), lax.axis_index("col")
    sources, _, length = key.shape
    slots = in_ref.shape[0]
    capacity = slots // sources
    units = gu.shape[1] // 2
    width = units // 4
    chunk = 256
    x = in_ref
    right_dev, left_dev = {"col": (col + 1) % 4}, {"col": (col + 3) % 4}

    load_gu = pltpu.make_async_copy(gu_hbm, gu, load_sem.at[0])
    load_gu.start()
    load_down = pltpu.make_async_copy(own_down, down.at[col], load_sem.at[1])
    load_down.start()

    def fetch(s, slot):
        rows = pl.ds(pl.multiple_of(s * length, 16), length)
        for i, hbm in enumerate((normed_hbm, upstream_hbm)):
            to = prod_ref.at[pl.ds(pl.multiple_of((slot * 2 + i) * length, 16), length), :]
            yield pltpu.make_async_copy(hbm.at[rows, :], to, src_sem.at[slot, i])

    for copy in fetch(0, 0):
        copy.start()
    greet((X + Y, X + Y + SIB), (1, 2, 3))

    def pass_on(c, source, right, left):
        for d, (cond, there) in enumerate(((right, right_dev), (left, left_dev))):
            @pl.when(cond)
            def _():
                remote(source, down.at[c], zss.at[c, d], zrs.at[c], there).start()

    pass_on(col, own_down, col < 3, col > 0)

    def ag_step(s):
        @pl.when(col >= s)
        def _():
            c = col - s
            remote(down.at[c], down.at[c], zss.at[c, 0], zrs.at[c], right_dev).wait_recv()
            @pl.when(col < 3)
            def _():
                remote(down.at[c], down.at[c], zss.at[c, 0], zrs.at[c], right_dev).start()
        @pl.when(col + s < 4)
        def _():
            c = col + s
            remote(down.at[c], down.at[c], zss.at[c, 1], zrs.at[c], left_dev).wait_recv()
            @pl.when(col > 0)
            def _():
                remote(down.at[c], down.at[c], zss.at[c, 1], zrs.at[c], left_dev).start()

    def to_right(d):
        target = rec_right.at[d - 1]
        return remote(target, target, rss.at[0, d - 1], rrs.at[0, d - 1], right_dev)

    def to_left(d):
        target = rec_left.at[d]
        return remote(target, target, rss.at[1, d], rrs.at[1, d], left_dev)

    def from_end(d):
        @pl.when((col == 0) & (d > 0))
        def _():
            remote(gd.at[d], rec_right.at[d - 1], rss.at[0, d - 1], rrs.at[0, d - 1], right_dev).start()
        @pl.when((col == 3) & (d < 3))
        def _():
            remote(gd.at[d], rec_left.at[d], rss.at[1, d], rrs.at[1, d], left_dev).start()

    def add_rows(target, term):
        def body(i, carry):
            rows = pl.ds(pl.multiple_of(i * 64, 64), 64)
            total = target[rows, :].astype(jnp.float32) + term[rows, :].astype(jnp.float32)
            target[rows, :] = total.astype(target.dtype)
            return carry
        lax.fori_loop(0, width // 64, body, 0)

    def hop_right(d):
        to_right(d).wait_recv()
        add_rows(rec_right.at[d - 1], gd.at[d])
        to_right(d).start()

    def hop_left(d):
        to_left(d).wait_recv()
        add_rows(rec_left.at[d], gd.at[d])
        to_left(d).start()

    def select(s, carry):
        slot = s % 2
        @pl.when(s + 1 < sources)
        def _():
            for copy in fetch(s + 1, 1 - slot):
                copy.start()
        for copy in fetch(s, slot):
            copy.wait()
        chosen = key[s] == lax.broadcasted_iota(jnp.int32, (capacity, length), 0)
        value = jnp.sum(jnp.where(chosen, mine[s], 0.0), axis=1, keepdims=True)
        rows = pl.ds(pl.multiple_of(s * capacity, 16), capacity)
        gate[rows, :] = jnp.broadcast_to(value, (capacity, gate.shape[1]))
        one_hot = jnp.where(chosen, 1.0, 0.0).astype(x.dtype)
        for i, target in enumerate((x, ups)):
            block = prod_ref[pl.ds(pl.multiple_of((slot * 2 + i) * length, 16), length), :]
            target[rows, :] = dot(one_hot, block).astype(target.dtype)
        return carry
    lax.fori_loop(0, sources, select, 0)

    load_gu.wait()

    def forward(c):
        first = pl.ds(pl.multiple_of(c * width, width), width)
        second = pl.ds(pl.multiple_of(units + c * width, width), width)
        def body(m, carry):
            rows = pl.ds(pl.multiple_of(m * chunk, chunk), chunk)
            gate_pre = dot(x[rows, :], gu[:, first])
            up_pre = dot(x[rows, :], gu[:, second])
            sigma = jax.nn.sigmoid(gate_pre)
            silu_gate = gate_pre * sigma
            silu[rows, first] = silu_gate
            slope[rows, first] = up_pre * sigma * (1.0 + gate_pre * (1.0 - sigma))
            low = (silu_gate * up_pre).astype(act.dtype)
            act[rows, first] = low
            both[rows, first] = (low.astype(jnp.float32) * gate[rows, 0:1]).astype(both.dtype)
            return carry
        lax.fori_loop(0, slots // chunk, body, 0)
        gd[c] = t_dot(both[:, first], ups[...]).astype(gd.dtype)

    def forward_step(i, carry):
        c = jnp.where(i < 2, 3 - 3 * i, 4 - i)
        forward(c)
        pl.when((i < 2) | (col == 0))(lambda: from_end(c))
        pl.when(i == 1)(lambda: ag_step(1))
        @pl.when((i == 3) & (col == 3))
        def _():
            from_end(1)
            from_end(2)
        return carry
    lax.fori_loop(0, 4, forward_step, 0)
    load_down.wait()

    def turn(m, carry):
        rows = pl.ds(pl.multiple_of(m * chunk, chunk), chunk)
        x_t[:, rows] = x[rows, :].T
        return carry
    lax.fori_loop(0, slots // chunk, turn, 0)
    gate_grad_ref[...] = jnp.zeros_like(gate_grad_ref)

    def out_stage(c, slot):
        for i in range(2):
            yield pltpu.make_async_copy(
                stage.at[slot, :, pl.ds(i * width, width)],
                grad_gu.at[:, pl.ds(pl.multiple_of(i * units + c * width, width), width)],
                stage_sem.at[slot, i],
            )

    def far(j):
        there = row_at(row, X + Y + j)
        rows = pl.ds(pl.multiple_of(there * capacity, 16), capacity)
        return remote(in_ref.at[rows, :], back_far.at[j], fss.at[j], frs.at[j], {"row": there})

    def inputs(i, carry):
        chip = row_at(row, 2 * (3 - i)) // 2
        rows = pl.ds(pl.multiple_of(chip * 2 * capacity, 16), 2 * capacity)
        in_ref[rows, :] = dot_t(both[rows, :], gu[...]).astype(in_ref.dtype)
        return carry

    def backward(k):
        c = unit_at(col, k)
        first = pl.ds(pl.multiple_of(c * width, width), width)
        second = pl.ds(pl.multiple_of(units + c * width, width), width)
        def body(m, carry):
            rows = pl.ds(pl.multiple_of(m * chunk, chunk), chunk)
            plain = dot_t(ups[rows, :], down[c])
            term = jnp.sum(act[rows, first].astype(jnp.float32) * plain, axis=1, keepdims=True)
            gate_grad_ref[rows, :] += jnp.broadcast_to(term, (chunk, gate_grad_ref.shape[1]))
            act_grad = plain * gate[rows, 0:1]
            both[rows, first] = (act_grad * slope[rows, first]).astype(both.dtype)
            both[rows, second] = (act_grad * silu[rows, first]).astype(both.dtype)
            return carry
        lax.fori_loop(0, slots // chunk, body, 0)
        @pl.when(k == 3)
        def _():
            inputs(0, 0)
            far(0).start()
            far(1).start()
        slot = k % 2
        @pl.when(k >= 2)
        def _():
            for copy in out_stage(unit_at(col, k - 2), slot):
                copy.wait()
        def grads(i, carry):
            rows = pl.ds(pl.multiple_of(i * chunk, chunk), chunk)
            stage[slot, rows, 0:width] = dot(x_t[rows, :], both[:, first]).astype(stage.dtype)
            stage[slot, rows, width : 2 * width] = dot(x_t[rows, :], both[:, second]).astype(stage.dtype)
            return carry
        lax.fori_loop(0, x_t.shape[0] // chunk, grads, 0)
        for copy in out_stage(c, slot):
            copy.start()

    def backward_step(k, carry):
        backward(k)
        pl.when(k == 0)(lambda: ag_step(2))
        pl.when((k == 0) & (col == 1))(lambda: hop_right(3))
        pl.when((k == 0) & (col == 2))(lambda: hop_left(0))
        pl.when(k == 2)(lambda: ag_step(3))
        @pl.when((k == 2) & (col == 1))
        def _():
            hop_right(2)
            hop_left(0)
        @pl.when((k == 2) & (col == 2))
        def _():
            hop_right(3)
            hop_left(1)
        return carry
    lax.fori_loop(0, 4, backward_step, 0)

    lax.fori_loop(1, sources // 2, inputs, 0)

    def outputs(m, carry):
        rows = pl.ds(pl.multiple_of(m * chunk, chunk), chunk)
        total = dot(act[rows, 0:width], down[0])
        for c in range(1, 4):
            total = total + dot(act[rows, c * width : (c + 1) * width], down[c])
        prod_ref[rows, :] = total.astype(prod_ref.dtype)
        return carry
    lax.fori_loop(0, slots // chunk, outputs, 0)

    turned = gate_grad_ref[...].T
    for s in range(sources):
        gate_grad_out[s] = turned[0:1, s * capacity : (s + 1) * capacity]
    for k in (2, 3):
        for copy in out_stage(unit_at(col, k), k % 2):
            copy.wait()
    pl.when(col > 0)(lambda: to_right(col).wait_recv())
    pl.when(col < 3)(lambda: to_left(col).wait_recv())

    def to_sum(i, carry):
        rows = pl.ds(pl.multiple_of(i * 64, 64), 64)
        sum_down[rows, :] = gd[col, rows, :].astype(jnp.float32)
        @pl.when(col > 0)
        def _():
            sum_down[rows, :] += rec_right[jnp.maximum(col - 1, 0), rows, :].astype(jnp.float32)
        @pl.when(col < 3)
        def _():
            sum_down[rows, :] += rec_left[jnp.minimum(col, 2), rows, :].astype(jnp.float32)
        return carry
    lax.fori_loop(0, width // 64, to_sum, 0)

    def sent(e, carry):
        pl.when(e > col)(lambda: to_right(e).wait_send())
        pl.when(e < col)(lambda: to_left(e).wait_send())
        @pl.when((col < 3) & (e <= col))
        def _():
            remote(down.at[e], down.at[e], zss.at[e, 0], zrs.at[e], right_dev).wait_send()
        @pl.when((col > 0) & (e >= col))
        def _():
            remote(down.at[e], down.at[e], zss.at[e, 1], zrs.at[e], left_dev).wait_send()
        return carry
    lax.fori_loop(0, 4, sent, 0)
    for j in range(2):
        far(j).wait()


def run_expert(key, mine, normed, upstream, full_gu, own_down):
    sources, length = key.shape
    model, units = full_gu.shape[0], full_gu.shape[1] // 2
    width = own_down.shape[0]
    slots = sources * length // 2
    low, f32 = normed.dtype, jnp.float32
    sems = pltpu.SemaphoreType.DMA
    vm = pl.BlockSpec(memory_space=pltpu.VMEM)
    return pl.pallas_call(
        expert_kernel,
        out_shape=(
            jax.ShapeDtypeStruct((slots, model), low),
            jax.ShapeDtypeStruct((slots, model), low),
            jax.ShapeDtypeStruct((sources, 1, slots // sources), f32),
            jax.ShapeDtypeStruct((model, 2 * units), low),
            jax.ShapeDtypeStruct((width, model), f32),
            jax.ShapeDtypeStruct((2, slots // sources, model), low),
        ),
        in_specs=[vm, vm, ANY, ANY, ANY, ANY],
        out_specs=(vm, vm, vm, ANY, vm, ANY),
        scratch_shapes=[
            pltpu.VMEM((slots, 128), f32),
            pltpu.VMEM((model, slots), low),
            pltpu.VMEM((slots, model), low),
            pltpu.VMEM((model, 2 * units), low),
            pltpu.VMEM((4, width, model), low),
            pltpu.VMEM((slots, units), low),
            pltpu.VMEM((slots, units), f32),
            pltpu.VMEM((slots, units), f32),
            pltpu.VMEM((slots, 2 * units), low),
            pltpu.VMEM((4, width, model), low),
            pltpu.VMEM((3, width, model), low),
            pltpu.VMEM((3, width, model), low),
            pltpu.VMEM((2, model, 2 * width), low),
            pltpu.VMEM((slots, 128), f32),
            sems((2,)), sems((2, 2)), sems((2, 2)),
            sems((4, 2)), sems((4,)), sems((2, 3)), sems((2, 3)), sems((2,)), sems((2,)),
        ],
        compiler_params=pltpu.CompilerParams(
            collective_id=4, has_side_effects=True, vmem_limit_bytes=60 * 2**20
        ),
        cost_estimate=pl.CostEstimate(flops=0, bytes_accessed=1_000_000, transcendentals=0),
    )(key.reshape(sources, 1, length), mine.reshape(sources, 1, length), normed, upstream, full_gu, own_down)


def backward_kernel(table, router_p, gains, lse,
                    gate_grad, in_grad, back_far, produced, hidden_hbm, tokens_hbm, cot_hbm, normed_hbm, attended_hbm,
                    two_hbm, qkv_hbm, full_a_hbm, full_out_hbm,
                    out_ref, d_tokens, sum_q, sum_k, sum_v, sum_b, sum_s,
                    cols, rec_in, rec_gate, rec_prod, hidden, tokens, cot, two, qkv, full_a, full_out,
                    n_t, a_t, branch, bias, out_rows, grad_c, qg, lgs, small,
                    own, sib_out, rec_sib, rec_one, rec_two, rec_z, s_rec, s_mid, s_zrec,
                    load, in_ss, in_rs, g_ss, g_rs, pr_ss, pr_rs, loc, far_sem,
                    ss1, rs1, ss2, rs2, zss, zrs, s_ss, s_rs, sz_ss, sz_rs):
    row, col = lax.axis_index("row"), lax.axis_index("col")
    core = row % 2
    chip = row // 2
    cy, cx = chip // 2, chip % 2
    length, model = hidden.shape
    capacity = rec_in.shape[0] // 8
    block = own.shape[2]
    width_b = sum_b.shape[1]
    width_a = own.shape[3] - width_b
    cut = block // 2
    half = length // 2
    f32, low = jnp.float32, branch.dtype
    sib = {"row": row_at(row, SIB)}
    to_x, to_y = {"row": row_at(row, X)}, {"row": row_at(row, Y)}

    def each_flip(function):
        def body(i, carry):
            function(7 - i)
            return carry
        lax.fori_loop(0, 7, body, 0)

    def block_of(r):
        return pl.ds(pl.multiple_of(r * capacity, 16), capacity)

    own_in = pltpu.make_async_copy(in_grad.at[block_of(row), :], rec_in.at[block_of(row), :], loc.at[0])
    own_gate = pltpu.make_async_copy(gate_grad.at[row], rec_gate.at[row], loc.at[1])
    own_prod = pltpu.make_async_copy(produced.at[block_of(row), :], rec_prod.at[block_of(row), :], loc.at[2])
    loads = [
        pltpu.make_async_copy(source, target, load.at[i])
        for i, (source, target) in enumerate((
            (normed_hbm, branch), (attended_hbm, a_t), (hidden_hbm, hidden), (cot_hbm, cot), (two_hbm, two),
            (qkv_hbm, qkv), (tokens_hbm, tokens), (full_out_hbm, full_out), (full_a_hbm, full_a),
        ))
    ]
    greet(range(1, 8), (1, 2, 3))

    far_in = [
        pltpu.make_async_copy(back_far.at[j], rec_in.at[block_of(row_at(row, X + Y + j)), :], far_sem.at[j])
        for j in range(2)
    ]

    def back(flip):
        there = row_at(row, flip)
        return remote(in_grad.at[block_of(there), :], rec_in.at[block_of(row), :],
                      in_ss.at[flip - 1], in_rs.at[flip - 1], {"row": there})

    def back_gate(flip):
        there = row_at(row, flip)
        return remote(gate_grad.at[there], rec_gate.at[row], g_ss.at[flip - 1], g_rs.at[flip - 1], {"row": there})

    def each_near(function):
        def body(i, carry):
            function(5 - i)
            return carry
        lax.fori_loop(0, 5, body, 0)

    def back_prod(flip):
        there = row_at(row, flip)
        return remote(produced.at[block_of(there), :], rec_prod.at[block_of(row), :],
                      pr_ss.at[flip - 1], pr_rs.at[flip - 1], {"row": there})

    each_near(lambda flip: back(flip).start())
    each_flip(lambda flip: back_gate(flip).start())
    for copy in (own_in, own_gate, own_prod, *far_in):
        copy.start()
    cols[...] = table[...].T
    for copy in loads:
        copy.start()
    loads[0].wait()
    n_t[...] = branch[...].T
    key_pos = lax.broadcasted_iota(jnp.int32, (length, length), 0)
    query_pos = lax.broadcasted_iota(jnp.int32, (length, length), 1)
    allowed = (key_pos <= query_pos) & (cols[:, 6:7] == table[6:7, :])
    bias[...] = jnp.where(allowed, 0.0, NEGATIVE)
    small[...] = jnp.zeros_like(small)
    for copy in loads[1:]:
        copy.wait()
    for copy in (own_in, own_gate, *far_in):
        copy.wait()
    each_flip(lambda flip: back_gate(flip).wait_recv())
    each_near(lambda flip: back(flip).wait_recv())

    all_gate = jnp.concatenate([rec_gate[e] for e in range(8)], axis=1)
    wide = rec_in.shape[0]
    lanes = lgs.shape[1]

    def at_slot(rows, k):
        return cols[rows, k : k + 1] == lax.broadcasted_iota(jnp.int32, (half, wide), 1).astype(f32)

    def to_hidden(m, carry):
        rows = pl.ds(pl.multiple_of(m * half, half), half)
        first, second = at_slot(rows, 0), at_slot(rows, 1)
        picked = jnp.where(first | second, 1.0, 0.0).astype(low)
        two_grad = dot(picked, rec_in[...])
        grad_0 = jnp.sum(jnp.where(first, all_gate, 0.0), axis=1, keepdims=True)
        grad_1 = jnp.sum(jnp.where(second, all_gate, 0.0), axis=1, keepdims=True)
        gate_0, gate_1 = cols[rows, 4:5], cols[rows, 5:6]
        mean = gate_0 * grad_0 + gate_1 * grad_1
        lane = lax.broadcasted_iota(jnp.int32, (half, lanes), 1).astype(f32)
        logit_grad = jnp.where(lane == cols[rows, 2:3], gate_0 * (grad_0 - mean), 0.0)
        logit_grad = logit_grad + jnp.where(lane == cols[rows, 3:4], gate_1 * (grad_1 - mean), 0.0)
        logit_grad = logit_grad.astype(low)
        lgs[rows, :] = logit_grad
        two_grad = two_grad + dot_t(logit_grad, router_p[...])
        h = hidden[rows, :]
        factor = lax.rsqrt(jnp.mean(h * h, axis=1, keepdims=True) + EPSILON)
        small[9:10, :] += jnp.sum(two_grad * h * factor, axis=0, keepdims=True)
        scaled = two_grad * gains[1:2, :]
        inner = jnp.mean(scaled * h, axis=1, keepdims=True)
        grad = cot[rows, :].astype(f32) + factor * scaled - h * (factor * factor * factor * inner)
        d_tokens[rows, :] = grad
        branch[rows, :] = grad.astype(low)
        return carry
    lax.fori_loop(0, 2, to_hidden, 0)
    small[0:8, :] = t_dot(lgs[...], two[...])[0:8, :]

    def nth(k):
        return (col + 1 + k) % 4

    lanes_of = {"a": pl.ds(0, width_a), "b": pl.ds(width_a, width_b)}
    part_at = {"a": 0, "b": 1}

    def to_sibling(part, c, q):
        view = lanes_of[part]
        i = part_at[part]
        return remote(sib_out.at[c, q, :, view], rec_sib.at[c, q, :, view], ss1.at[c, q, i], rs1.at[c, q, i], sib)

    def weight_grads(part, c, left, right):
        view = lanes_of[part]
        def body(q, carry):
            theirs = pl.ds(pl.multiple_of((q * 2 + 1 - core) * block, 16), block)
            sib_out[c, q, :, view] = dot(left[theirs, :], right()).astype(low)
            to_sibling(part, c, q).start()
            mine = pl.ds(pl.multiple_of((q * 2 + core) * block, 16), block)
            own[c, q, :, view] = dot(left[mine, :], right()).astype(low)
            return carry
        lax.fori_loop(0, 4, body, 0)

    def cols_b(c):
        return pl.ds(pl.multiple_of(c * width_b, 128), width_b)

    def attend_back(c):
        span_c = width_b // QUERY_PER_KEY
        for i in range(QUERY_PER_KEY):
            for u in range(2):
                rows = pl.ds(pl.multiple_of(c * width_b + (u * QUERY_PER_KEY + i) * HEAD_SIZE, HEAD_SIZE), HEAD_SIZE)
                out_rows[(2 * i + u) * HEAD_SIZE : (2 * i + u + 1) * HEAD_SIZE, :] = full_out[rows, :]
        grad_c[...] = dot_t(branch[...], out_rows[...]).astype(low)
        at_c = pl.multiple_of(c * width_a, 128)
        key = qkv[:, pl.ds(at_c + width_b, span_c)]
        value = qkv[:, pl.ds(at_c + width_b + span_c, span_c)]
        first = lax.broadcasted_iota(jnp.int32, (length, span_c), 1) < HEAD_SIZE
        none = jnp.zeros_like(key)
        keys = (jnp.where(first, key, none), jnp.where(first, none, key))
        values = (jnp.where(first, value, none), jnp.where(first, none, value))
        scale = HEAD_SIZE ** (-0.5)
        key_grads = [jnp.zeros((length, span_c), f32) for _ in range(2)]
        value_grads = [jnp.zeros((length, span_c), f32) for _ in range(2)]
        for i in range(QUERY_PER_KEY):
            q_i = qkv[:, pl.ds(at_c + i * span_c, span_c)]
            g_i = grad_c[:, i * span_c : (i + 1) * span_c]
            q_grad = jnp.zeros((length, span_c), f32)
            for u in range(2):
                log_total = lse[c * 2 + u, :, i * length : (i + 1) * length]
                probs = jnp.exp(dot_t(keys[u], q_i) * scale + bias[...] - log_total)
                prob_grad = dot_t(values[u], g_i)
                delta = jnp.sum(probs * prob_grad, axis=0, keepdims=True)
                score_grad = (probs * (prob_grad - delta)).astype(low)
                value_grads[u] += dot(probs.astype(low), g_i)
                key_grads[u] += dot(score_grad, q_i)
                q_grad += t_dot(score_grad, keys[u])
            qg[c, :, i * span_c : (i + 1) * span_c] = (q_grad * scale).astype(low)
        key_grad = jnp.where(first, key_grads[0], key_grads[1]) * scale
        qg[c, :, width_b : width_b + span_c] = key_grad.astype(low)
        qg[c, :, width_b + span_c : width_a] = jnp.where(first, value_grads[0], value_grads[1]).astype(low)

    top, bottom = pl.ds(0, cut), pl.ds(cut, block - cut)

    def one(part, c):
        view, i = lanes_of[part], part_at[part]
        for j in range(2):
            yield remote(own.at[c, j * 2 + 1 - cx, top, view], rec_one.at[c, 0, j, :, view],
                         ss2.at[c, i, 0, j], rs2.at[c, i, 0, j], to_x)
            yield remote(own.at[c, (1 - cy) * 2 + j, bottom, view], rec_one.at[c, 1, j, :, view],
                         ss2.at[c, i, 1, j], rs2.at[c, i, 1, j], to_y)

    def two_step(part, c):
        view, i = lanes_of[part], part_at[part]
        yield remote(own.at[c, (1 - cy) * 2 + cx, top, view], rec_two.at[c, 0, :, view],
                     ss2.at[c, i, 0, 2], rs2.at[c, i, 0, 2], to_y)
        yield remote(own.at[c, cy * 2 + 1 - cx, bottom, view], rec_two.at[c, 1, :, view],
                     ss2.at[c, i, 1, 2], rs2.at[c, i, 1, 2], to_x)

    def column(part, step):
        there = (col + step) % 4
        view, i = lanes_of[part], part_at[part]
        return remote(own.at[there, chip, :, view], rec_z.at[step - 1, :, view],
                      zss.at[i, step - 1], zrs.at[i, step - 1], {"col": there})

    def stage_one(part, k):
        c, view = nth(k), lanes_of[part]
        def body(q, carry):
            to_sibling(part, c, q).wait_recv()
            add_into(own.at[c, q, :, view], rec_sib.at[c, q, :, view])
            return carry
        lax.fori_loop(0, 4, body, 0)
        for copy in one(part, c):
            copy.start()

    def stage_two(part, k):
        c, view = nth(k), lanes_of[part]
        for copy in one(part, c):
            copy.wait_recv()
        for j in range(2):
            add_into(own.at[c, j * 2 + cx, top, view], rec_one.at[c, 0, j, :, view])
            add_into(own.at[c, cy * 2 + j, bottom, view], rec_one.at[c, 1, j, :, view])
        for copy in two_step(part, c):
            copy.start()

    def stage_three(part, k):
        c, view = nth(k), lanes_of[part]
        for copy in two_step(part, c):
            copy.wait_recv()
        add_into(own.at[c, chip, top, view], rec_two.at[c, 0, :, view])
        add_into(own.at[c, chip, bottom, view], rec_two.at[c, 1, :, view])
        pl.when(k < 3)(lambda: column(part, k + 1).start())

    def out_grads(k, carry):
        c = nth(k)
        weight_grads("b", c, a_t, lambda: branch[:, cols_b(c)])
        pl.when(k >= 1)(lambda: stage_one("b", k - 1))
        pl.when(k >= 2)(lambda: stage_two("b", k - 2))
        pl.when(k >= 3)(lambda: stage_three("b", k - 3))
        return carry
    lax.fori_loop(0, 4, out_grads, 0)

    def input_grads(k, carry):
        c = nth(k)
        attend_back(c)
        weight_grads("a", c, n_t, lambda: qg[c])
        pl.when(k == 0)(lambda: stage_one("b", k + 3))
        pl.when(k >= 1)(lambda: stage_one("a", k - 1))
        pl.when(k <= 1)(lambda: stage_two("b", k + 2))
        pl.when(k >= 2)(lambda: stage_two("a", k - 2))
        pl.when(k <= 2)(lambda: stage_three("b", k + 1))
        pl.when(k >= 3)(lambda: stage_three("a", k - 3))
        return carry
    lax.fori_loop(0, 4, input_grads, 0)
    stage_one("a", 3)
    each_flip(lambda flip: back_prod(flip).start())
    stage_two("a", 2)
    stage_three("a", 1)

    def to_tokens(m, carry):
        rows = pl.ds(pl.multiple_of(m * half, half), half)
        grad = dot_t(qg[0, rows, :], full_a[:, 0:width_a])
        for c in range(1, 4):
            grad = grad + dot_t(qg[c, rows, :], full_a[:, c * width_a : (c + 1) * width_a])
        x = tokens[rows, :].astype(f32)
        factor = lax.rsqrt(jnp.mean(x * x, axis=1, keepdims=True) + EPSILON)
        small[8:9, :] += jnp.sum(grad * x * factor, axis=0, keepdims=True)
        scaled = grad * gains[0:1, :]
        inner = jnp.mean(scaled * x, axis=1, keepdims=True)
        d_tokens[rows, :] += factor * scaled - x * (factor * factor * factor * inner)
        return carry
    lax.fori_loop(0, 2, to_tokens, 0)

    span = s_mid.shape[1]

    def small_plane(flip):
        there = row_at(row, flip)
        view = small.at[:, pl.ds(pl.multiple_of((there // 2) * span, 128), span)]
        return remote(view, s_rec.at[flip - 1], s_ss.at[flip - 1], s_rs.at[flip - 1], {"row": there})

    def small_column(step):
        return remote(s_mid, s_zrec.at[step - 1], sz_ss.at[step - 1], sz_rs.at[step - 1], {"col": (col + step) % 4})

    each_flip(lambda flip: small_plane(flip).start())
    stage_two("a", 3)
    stage_three("a", 2)
    s_mid[...] = small[:, pl.ds(pl.multiple_of(chip * span, 128), span)]

    def add_small(flip):
        small_plane(flip).wait_recv()
        s_mid[...] += s_rec[flip - 1]

    each_flip(add_small)
    for step in (1, 2, 3):
        small_column(step).start()
    stage_three("a", 3)

    own_prod.wait()
    each_flip(lambda flip: back_prod(flip).wait_recv())

    def to_output(m, carry):
        rows = pl.ds(pl.multiple_of(m * half, half), half)
        total = hidden[rows, :]
        for k in range(2):
            picked = jnp.where(at_slot(rows, k), 1.0, 0.0).astype(low)
            total = total + dot(picked, rec_prod[...]) * cols[rows, 4 + k : 5 + k]
        out_ref[rows, :] = total.astype(low)
        return carry
    lax.fori_loop(0, 2, to_output, 0)

    total = s_mid[...]
    for step in (1, 2, 3):
        small_column(step).wait_recv()
        total = total + s_zrec[step - 1]
    sum_s[...] = total
    for part in ("b", "a"):
        for step in (1, 2, 3):
            column(part, step).wait_recv()

    def to_sums(i, carry):
        rows = pl.ds(pl.multiple_of(i * 32, 32), 32)
        total = own[col, chip, rows, :].astype(f32)
        for step in range(3):
            total = total + rec_z[step, rows, :].astype(f32)
        span_c = width_b // QUERY_PER_KEY
        zero, one_, two_ = (total[:, i * span_c : (i + 1) * span_c] for i in range(QUERY_PER_KEY))
        turned = pltpu.roll(one_, HEAD_SIZE, 1)
        first = lax.broadcasted_iota(jnp.int32, zero.shape, 1) < HEAD_SIZE
        sum_q[rows, 0:span_c] = jnp.where(first, zero, turned)
        sum_q[rows, span_c : 2 * span_c] = jnp.where(first, two_, zero)
        sum_q[rows, 2 * span_c : width_b] = jnp.where(first, turned, two_)
        sum_k[rows, :] = total[:, width_b : width_b + span_c]
        sum_v[rows, :] = total[:, width_b + span_c : width_a]
        sum_b[rows, :] = total[:, width_a:]
        return carry
    lax.fori_loop(0, block // 32, to_sums, 0)


    each_near(lambda flip: back(flip).wait_send())

    def all_sent(flip):
        back_gate(flip).wait_send()
        back_prod(flip).wait_send()
        small_plane(flip).wait_send()

    each_flip(all_sent)
    for step in (1, 2, 3):
        small_column(step).wait_send()
        column("a", step).wait_send()
        column("b", step).wait_send()

    def sent(c, carry):
        for part in ("a", "b"):
            def body(q, carry):
                to_sibling(part, c, q).wait_send()
                return carry
            lax.fori_loop(0, 4, body, 0)
            for copy in one(part, c):
                copy.wait_send()
            for copy in two_step(part, c):
                copy.wait_send()
        return carry
    lax.fori_loop(0, 4, sent, 0)


def run_backward(slot_of, gates, ids, router, gains, lse, segments, gate_grad, in_grad, back_far, produced,
                 hidden, tokens, cotangent, normed, attended, normed_two, qkv, full_a, full_out):
    table = jnp.concatenate(
        [slot_of.T.astype(jnp.float32), ids.T.astype(jnp.float32), gates.T, segments[None].astype(jnp.float32),
         jnp.zeros((1, segments.shape[0]), jnp.float32)], axis=0)
    sems = pltpu.SemaphoreType.DMA
    length, model = tokens.shape
    block = full_a.shape[0] // 8
    width_a, width_b = full_a.shape[1] // 4, full_out.shape[1] // 4
    width = width_a + width_b
    cut = block // 2
    low, f32 = tokens.dtype, jnp.float32
    vm = pl.BlockSpec(memory_space=pltpu.VMEM)
    slots = in_grad.shape[0]
    capacity = slots // 8
    span = model // 4
    router_p = jnp.pad(router, ((0, 0), (0, 128 - router.shape[1])))
    v = pltpu.VMEM
    rows_low = v((length, model), low)
    return pl.pallas_call(
        backward_kernel,
        out_shape=(
            jax.ShapeDtypeStruct((length, model), low),
            jax.ShapeDtypeStruct((length, model), f32),
            jax.ShapeDtypeStruct((block, width_b), f32),
            jax.ShapeDtypeStruct((block, (width_a - width_b) // 2), f32),
            jax.ShapeDtypeStruct((block, (width_a - width_b) // 2), f32),
            jax.ShapeDtypeStruct((block, width_b), f32),
            jax.ShapeDtypeStruct((16, span), f32),
        ),
        in_specs=[vm] * 4 + [ANY] * 13,
        out_specs=(vm,) * 7,
        scratch_shapes=[
            v((length, 8), f32), v((slots, model), low), v((8, 1, capacity), f32), v((slots, model), low),
            v((length, model), f32), rows_low, rows_low, rows_low,
            v(qkv.shape, low), v(full_a.shape, low), v(full_out.shape, low),
            v((model, length), low), v((model, length), low), rows_low,
            v((length, length), f32), v((width_b, model), low), v((length, width_b), low), v((4, length, width_a), low),
            v((length, 128), low), v((16, model), f32),
            v((4, 4, block, width), low), v((4, 4, block, width), low), v((4, 4, block, width), low),
            v((4, 2, 2, cut, width), low), v((4, 2, cut, width), low), v((3, block, width), low),
            v((7, 16, span), f32), v((16, span), f32), v((3, 16, span), f32),
            sems((9,)), sems((7,)), sems((7,)), sems((7,)), sems((7,)), sems((7,)), sems((7,)), sems((3,)), sems((2,)),
            sems((4, 4, 2)), sems((4, 4, 2)), sems((4, 2, 2, 3)), sems((4, 2, 2, 3)),
            sems((2, 3)), sems((2, 3)), sems((7,)), sems((7,)), sems((3,)), sems((3,)),
        ],
        compiler_params=pltpu.CompilerParams(
            collective_id=2, has_side_effects=True, vmem_limit_bytes=60 * 2**20
        ),
        cost_estimate=pl.CostEstimate(flops=0, bytes_accessed=1_000_000, transcendentals=0),
    )(table, router_p, gains, lse, gate_grad, in_grad, back_far, produced, hidden, tokens,
      cotangent, normed, attended, normed_two, qkv, full_a, full_out)


def rms_factor(rows_in):
    return lax.rsqrt(jnp.mean(rows_in * rows_in, axis=1, keepdims=True) + EPSILON)


def dot(a, b):
    return jnp.dot(a, b, preferred_element_type=jnp.float32)


def dot_t(a, b):
    return lax.dot_general(a, b, (((1,), (1,)), ((), ())), preferred_element_type=jnp.float32)


def t_dot(a, b):
    return lax.dot_general(a, b, (((0,), (0,)), ((), ())), preferred_element_type=jnp.float32)


def on_small_slice():
    return lax.axis_size("row") == 8 and lax.axis_size("col") == 4


def pair_heads(a):
    if not on_small_slice():
        return [a]
    heads = [a[:, i * HEAD_SIZE : (i + 1) * HEAD_SIZE] for i in range(a.shape[1] // HEAD_SIZE)]
    return [heads[u * QUERY_PER_KEY + i] for i in range(QUERY_PER_KEY) for u in range(2)]


def part_heads(a):
    a = a.reshape(a.shape[0], -1, QUERY_PER_KEY, 2, HEAD_SIZE)
    return a.transpose(0, 1, 3, 2, 4).reshape(a.shape[0], -1)


def gather_all(own_a, own_b, own_s, own_c):
    col_a = lax.all_gather(own_a, "col", axis=1, tiled=True)
    col_b = lax.all_gather(own_b, "col", axis=1, tiled=True)
    small = lax.all_gather(lax.all_gather(own_s, "col", axis=0), "row", axis=1)
    return (
        lax.all_gather(col_a, "row", axis=0, tiled=True),
        lax.all_gather(col_b, "row", axis=0, tiled=True),
        small,
        lax.all_gather(own_c, "row", axis=0, tiled=True),
    )


def spread(own_c, own_g):
    if on_small_slice():
        return spread_tokens(own_c, own_g)
    return (
        lax.all_gather(own_c, "row", axis=0, tiled=True),
        lax.all_gather(own_g, "row", axis=0),
    )


def reduce_all(grad_a, grad_b, grad_s):
    def both(g):
        plane = lax.psum_scatter(g, "row", scatter_dimension=0, tiled=True).astype(jnp.float32)
        return lax.psum_scatter(plane, "col", scatter_dimension=1, tiled=True)

    small = lax.psum_scatter(grad_s, "row", scatter_dimension=0, tiled=False)
    return both(grad_a), both(grad_b), lax.psum_scatter(small, "col", scatter_dimension=0, tiled=False)


def expert_elsewhere(place, routed, mine, plane_normed, plane_upstream, full_gu, own_down):
    rows, length = place.shape
    model = plane_normed.shape[1]
    hidden_units = full_gu.shape[1] // 2
    capacity = 2 * length * TOP // rows
    full_down = lax.all_gather(own_down, "col", axis=0, tiled=True)
    chosen_rows = (
        (place[:, None, :] == jnp.arange(capacity, dtype=jnp.int32)[None, :, None]) & routed[:, None, :]
    ).astype(jnp.bfloat16)

    def of_slots(plane):
        return jnp.einsum(
            "rct,rtd->rcd",
            chosen_rows,
            plane.reshape(rows, length, model),
            preferred_element_type=jnp.float32,
        ).astype(jnp.bfloat16).reshape(rows * capacity, model)

    grouped, grouped_up = of_slots(plane_normed), of_slots(plane_upstream)
    slot_gate = jnp.sum(jnp.where(chosen_rows > 0, mine[:, None, :], 0.0), axis=2)
    slot_gate = slot_gate.reshape(rows * capacity, 1)
    grouped_grad = (grouped_up.astype(jnp.float32) * slot_gate).astype(jnp.bfloat16)
    both_pre = dot(grouped, full_gu)
    gate_pre, up_pre = both_pre[:, :hidden_units], both_pre[:, hidden_units:]
    sigma = jax.nn.sigmoid(gate_pre)
    silu_gate = gate_pre * sigma
    activation = (silu_gate * up_pre).astype(jnp.bfloat16)
    grad_down_local = t_dot(activation, grouped_grad).astype(jnp.bfloat16)
    grad_down = lax.psum_scatter(grad_down_local, "col", scatter_dimension=0, tiled=True)
    act_grad = dot_t(grouped_grad, full_down)
    both_grad = jnp.concatenate(
        [
            (act_grad * up_pre * sigma * (1.0 + gate_pre * (1.0 - sigma))).astype(jnp.bfloat16),
            (act_grad * silu_gate).astype(jnp.bfloat16),
        ],
        axis=1,
    )
    in_grad = dot_t(both_grad, full_gu).astype(jnp.bfloat16)
    produced = dot(activation, full_down).astype(jnp.bfloat16)
    slot_gate_grad = jnp.sum(produced.astype(jnp.float32) * grouped_up.astype(jnp.float32), axis=1)
    grad_gu_local = t_dot(grouped, both_grad).astype(jnp.bfloat16)
    return in_grad, produced, slot_gate_grad, grad_gu_local, grad_down.astype(jnp.float32)


def masked_scores(queries, heads_of_key, segments, head_scale):
    length = queries.shape[0]
    heads_of_query = queries.reshape(length, KEY_VALUE_HEADS, QUERY_PER_KEY, HEAD_SIZE)
    scores = (
        jnp.einsum("qkgd,skd->kgqs", heads_of_query, heads_of_key, preferred_element_type=jnp.float32)
        * head_scale
    )
    pos = jnp.arange(length, dtype=jnp.int32)
    allowed = (pos[None, :] <= pos[:, None]) & (segments[None, :] == segments[:, None])
    return jnp.where(allowed, scores, NEGATIVE), heads_of_query


def per_device(
    tokens,
    attn_gain,
    w_query,
    w_key,
    w_value,
    w_out,
    expert_gain,
    router,
    w_gate,
    w_up,
    w_down,
    segment_ids,
    expert_ids,
    cotangent,
):
    length, model = tokens.shape
    rows, cols = lax.axis_size("row"), lax.axis_size("col")
    experts = w_gate.shape[0] * rows
    capacity = 2 * length * TOP // experts
    head_scale = HEAD_SIZE ** (-0.5)
    segments = segment_ids.reshape(-1)
    block, width_q = w_query.shape
    width_k = w_key.shape[1]
    width_a = width_q + 2 * width_k
    piece = attn_gain.shape[0]
    router_cols = router.shape[1]

    hidden_units = w_gate.shape[2]
    own_down = w_down[0]

    lane = 256

    def at_row(v, row):
        return jnp.pad(v, ((row, 16 - row - v.shape[0]), (0, lane - v.shape[1])))

    own_s = (
        at_row(router.T, 0)
        + at_row(attn_gain[None], router_cols)
        + at_row(expert_gain[None], router_cols + 1)
    )
    own_a = jnp.concatenate([*pair_heads(w_query), w_key, w_value], axis=1)
    if on_small_slice():
        line_a, line_out, small, plane_upstream, own_gu = gather_line(
            own_a, w_out, own_s, cotangent, w_gate[0], w_up[0]
        )
        full_a, full_out = gather_plane(3, (line_a, line_out))
    else:
        own_gu = jnp.concatenate([w_gate[0], w_up[0]], axis=1)
        full_a, full_out, small, plane_upstream = gather_all(own_a, w_out, own_s, cotangent)
    full_gu = lax.all_gather(own_gu, "col", axis=0, tiled=True)
    full_router = small[:, :, :router_cols, :block].transpose(1, 3, 0, 2).reshape(model, experts)
    gains = (
        small[:, :, router_cols : router_cols + 2, :piece].transpose(2, 1, 0, 3).reshape(2, model).astype(jnp.float32)
    )
    gain_one, gain_two = gains[0:1], gains[1:2]

    rows_f = tokens.astype(jnp.float32)
    factor_one = rms_factor(rows_f)
    normed = (rows_f * factor_one * gain_one).astype(jnp.bfloat16)
    flat_qkv = dot(normed, full_a).astype(jnp.bfloat16)
    qkv = flat_qkv.reshape(length, cols, width_a)
    query_rows = qkv[:, :, :width_q].reshape(length, -1)
    if on_small_slice():
        query_rows = part_heads(query_rows)
    rows_of_key = qkv[:, :, width_q : width_q + width_k].reshape(length, -1)
    rows_of_value = qkv[:, :, width_q + width_k :].reshape(length, -1)
    heads_of_key = rows_of_key.reshape(length, KEY_VALUE_HEADS, HEAD_SIZE)
    heads_of_value = rows_of_value.reshape(length, KEY_VALUE_HEADS, HEAD_SIZE)

    scores, heads_of_query = masked_scores(query_rows, heads_of_key, segments, head_scale)
    row_max = jnp.max(scores, axis=-1, keepdims=True)
    expo_rows = jnp.exp(scores - row_max)
    totals = jnp.sum(expo_rows, axis=-1, keepdims=True)
    soft_probs = expo_rows / totals
    probs_low = soft_probs.astype(jnp.bfloat16)
    attended = (
        jnp.einsum("kgqs,skd->qkgd", probs_low, heads_of_value, preferred_element_type=jnp.float32)
        .reshape(length, -1)
        .astype(jnp.bfloat16)
    )
    hidden = rows_f + dot(attended, full_out)
    factor_two = rms_factor(hidden)
    normed_two = (hidden * factor_two * gain_two).astype(jnp.bfloat16)
    logits = dot(normed_two, full_router)

    named = expert_ids[:, :, None] == jnp.arange(experts, dtype=jnp.int32)[None, None, :]
    chosen = jnp.sum(jnp.where(named, logits[:, None, :], 0.0), axis=2)
    gate_probs = jax.nn.softmax(chosen, axis=1)
    gate_table = jnp.sum(jnp.where(named, gate_probs[:, :, None], 0.0), axis=1)
    gate_table = jnp.where(jnp.any(named, axis=1), gate_table, -1.0)
    plane_normed, plane_gate = spread(normed_two, gate_table.T)
    mine = lax.dynamic_index_in_dim(plane_gate, lax.axis_index("row"), axis=1, keepdims=False)
    routed = mine >= 0.0
    place = jnp.cumsum(routed.astype(jnp.int32), axis=1) - 1
    any_named = jnp.any(named, axis=1)
    before = jnp.cumsum(any_named.astype(jnp.int32), axis=0) - 1
    slot_of = jnp.sum(
        jnp.where(named, before[:, None, :] + jnp.arange(experts, dtype=jnp.int32) * capacity, 0),
        axis=2,
    )
    if on_small_slice():
        in_grad, produced, slot_gate_grad, grad_gu_local, grad_down, back_far = run_expert(
            jnp.where(routed, place, -1), mine, plane_normed, plane_upstream, full_gu, own_down
        )
        grad_gu = lax.psum_scatter(grad_gu_local, "col", scatter_dimension=0, tiled=True)
        lse = (row_max + jnp.log(totals)).reshape(KEY_VALUE_HEADS, 1, QUERY_PER_KEY * length)
        output, d_tokens, sum_q, sum_k, sum_v, sum_out, sum_s = run_backward(
            slot_of, gate_probs, expert_ids, full_router, gains, lse, segments,
            slot_gate_grad, in_grad, back_far, produced, hidden, tokens, cotangent, normed, attended.T, normed_two,
            flat_qkv, full_a, full_out,
        )
        output, d_tokens, sum_q, sum_k, sum_v, sum_out, grad_down, grad_gate, grad_up, own_router, gain_a, gain_e = finish(
            (output, d_tokens, sum_q, sum_k, sum_v, sum_out, grad_down), grad_gu, sum_s, block, piece, router_cols
        )
        return (
            output,
            d_tokens,
            gain_a.reshape(piece),
            sum_q,
            sum_k,
            sum_v,
            sum_out,
            gain_e.reshape(piece),
            own_router.T,
            grad_gate[None],
            grad_up[None],
            grad_down[None],
        )
    else:
        in_grad, produced, slot_gate_grad, grad_gu_local, grad_down = expert_elsewhere(
            place, routed, mine, plane_normed, plane_upstream, full_gu, own_down
        )
    grad_gu = lax.psum_scatter(grad_gu_local, "col", scatter_dimension=0, tiled=True)
    back_grad = lax.all_to_all(
        in_grad.reshape(rows, capacity, model), "row", split_axis=0, concat_axis=0, tiled=True
    ).reshape(experts * capacity, model)
    back_gate_grad = lax.all_to_all(
        slot_gate_grad.reshape(rows, 1, capacity), "row", split_axis=0, concat_axis=0, tiled=True
    ).reshape(experts * capacity)
    produced, back_grad = lax.optimization_barrier((produced, back_grad))
    back_rows = lax.all_to_all(
        produced.reshape(rows, capacity, model), "row", split_axis=0, concat_axis=0, tiled=True
    ).reshape(experts * capacity, model)

    all_slots = jnp.arange(experts * capacity, dtype=jnp.int32)
    is_slot = slot_of.T[:, :, None] == all_slots[None, None, :]
    from_slot = is_slot.astype(jnp.bfloat16)
    gate_grad = jnp.sum(jnp.where(is_slot, back_gate_grad[None, None, :], 0.0), axis=2).T
    returned = [dot(from_slot[k], back_rows) for k in range(TOP)]
    upstream = cotangent.astype(jnp.float32)
    output = (
        hidden + sum(returned[k] * gate_probs[:, k : k + 1] for k in range(TOP))
    ).astype(jnp.bfloat16)
    normed_two_grad = dot(from_slot[0] + from_slot[1], back_grad)
    pair_mean = jnp.sum(gate_probs * gate_grad, axis=1, keepdims=True)
    pair_logit = gate_probs * (gate_grad - pair_mean)
    logit_grad = jnp.sum(jnp.where(named, pair_logit[:, :, None], 0.0), axis=1).astype(jnp.bfloat16)
    grad_router = t_dot(normed_two, logit_grad)
    normed_two_grad = normed_two_grad + dot_t(logit_grad, full_router)
    grad_expert_gain = jnp.sum(normed_two_grad * hidden * factor_two, axis=0)
    scaled_two = normed_two_grad * gain_two
    hidden_grad = (
        upstream
        + factor_two * scaled_two
        - hidden * factor_two**3 * jnp.mean(scaled_two * hidden, axis=1, keepdims=True)
    )
    branch_grad = hidden_grad.astype(jnp.bfloat16)
    grad_out_full = t_dot(attended, branch_grad).astype(jnp.bfloat16)
    attended_grad = dot_t(branch_grad, full_out).astype(jnp.bfloat16)

    gradient_heads = attended_grad.reshape(length, KEY_VALUE_HEADS, QUERY_PER_KEY, HEAD_SIZE)
    value_grad = jnp.einsum(
        "kgqs,qkgd->skd", probs_low, gradient_heads, preferred_element_type=jnp.float32
    )
    prob_grad = jnp.einsum(
        "qkgd,skd->kgqs", gradient_heads, heads_of_value, preferred_element_type=jnp.float32
    )
    delta_sum = jnp.sum(soft_probs * prob_grad, axis=-1, keepdims=True)
    score_grad = (soft_probs * (prob_grad - delta_sum)).astype(jnp.bfloat16)
    query_grad = (
        jnp.einsum("kgqs,skd->qkgd", score_grad, heads_of_key, preferred_element_type=jnp.float32)
        * head_scale
    )
    key_grad = (
        jnp.einsum("kgqs,qkgd->skd", score_grad, heads_of_query, preferred_element_type=jnp.float32)
        * head_scale
    )
    qkv_grad = jnp.concatenate(
        [
            query_grad.astype(jnp.bfloat16).reshape(length, cols, width_q),
            key_grad.astype(jnp.bfloat16).reshape(length, cols, width_k),
            value_grad.astype(jnp.bfloat16).reshape(length, cols, width_k),
        ],
        axis=2,
    ).reshape(length, cols * width_a)
    grad_a_full = t_dot(normed, qkv_grad).astype(jnp.bfloat16)
    normed_grad = dot_t(qkv_grad, full_a)
    grad_attn_gain = jnp.sum(normed_grad * rows_f * factor_one, axis=0)
    scaled_one = normed_grad * gain_one
    d_tokens = (
        hidden_grad
        + factor_one * scaled_one
        - rows_f * factor_one**3 * jnp.mean(scaled_one * rows_f, axis=1, keepdims=True)
    )
    grad_s = jnp.concatenate(
        [
            jnp.pad(
                grad_router.reshape(rows, block, cols, router_cols).transpose(0, 2, 3, 1),
                ((0, 0), (0, 0), (0, 0), (0, lane - block)),
            ),
            jnp.pad(
                jnp.stack([grad_attn_gain, grad_expert_gain])
                .reshape(2, rows, cols, piece)
                .transpose(1, 2, 0, 3),
                ((0, 0), (0, 0), (0, 6 - router_cols), (0, lane - piece)),
            ),
        ],
        axis=2,
    )
    grad_a_full, d_tokens, output = lax.optimization_barrier((grad_a_full, d_tokens, output))
    sum_a, sum_out, sum_s = reduce_all(grad_a_full, grad_out_full, grad_s)
    return (
        output,
        d_tokens,
        sum_s[router_cols, :piece],
        sum_a[:, :width_q],
        sum_a[:, width_q : width_q + width_k],
        sum_a[:, width_q + width_k :],
        sum_out,
        sum_s[router_cols + 1, :piece],
        sum_s[:router_cols, :block].T,
        grad_gu[:, :hidden_units].astype(jnp.float32)[None],
        grad_gu[:, hidden_units:].astype(jnp.float32)[None],
        grad_down[None],
    )


def solution(mesh):
    in_specs = (
        P(("row", "col"), None),
        P(("row", "col")),
        P("row", "col"),
        P("row", "col"),
        P("row", "col"),
        P("row", "col"),
        P(("row", "col")),
        P("row", "col"),
        P("row", "col", None),
        P("row", "col", None),
        P("row", "col", None),
        P(("row", "col"), None),
        P(("row", "col"), None),
        P(("row", "col"), None),
    )
    out_specs = (
        P(("row", "col"), None),
        P(("row", "col"), None),
        P(("row", "col")),
        P("row", "col"),
        P("row", "col"),
        P("row", "col"),
        P("row", "col"),
        P(("row", "col")),
        P("row", "col"),
        P("row", "col", None),
        P("row", "col", None),
        P("row", "col", None),
    )
    return jax.shard_map(
        per_device, mesh=mesh, in_specs=in_specs, out_specs=out_specs, check_vma=False
    )
```

```python
import functools

import jax
import jax.numpy as jnp
from jax import lax
from jax.experimental import pallas as pl
from jax.experimental.pallas import tpu as pltpu
from jax.sharding import PartitionSpec as P

KEY_VALUE_HEADS = 8
HEAD_SIZE = 64
TOP = 2
QUERY_PER_KEY = 3


EPSILON = 1e-05
NEGATIVE = -1e30


MESH = pl.DeviceIdType.MESH
ANY = pl.BlockSpec(memory_space=pl.ANY)


def row_at(row, flip):
    y, x, core = row // 4, (row // 2) % 2, row % 2
    return (
        (y + flip // 4) % 2 * 4 + (x + (flip // 2) % 2) % 2 * 2 + (core + flip % 2) % 2
    )


def remote(source, target, send, receive, device):
    return pltpu.make_async_remote_copy(
        source, target, send, receive, device_id=device, device_id_type=MESH
    )


def greet(row_flips, col_steps):
    row, col = lax.axis_index("row"), lax.axis_index("col")
    sem = pltpu.get_barrier_semaphore()
    for flip in row_flips:
        pl.semaphore_signal(
            sem, inc=1, device_id={"row": row_at(row, flip)}, device_id_type=MESH
        )
    for step in col_steps:
        pl.semaphore_signal(
            sem, inc=1, device_id={"col": (col + step) % 4}, device_id_type=MESH
        )
    pl.semaphore_wait(sem, len(row_flips) + len(col_steps))


def unit_order(col, k):
    table = ((0, 1, 2, 3), (1, 0, 2, 3), (2, 3, 1, 0), (3, 2, 1, 0))
    out = table[3][k]
    for c in (2, 1, 0):
        out = jnp.where(col == c, table[c][k], out)
    return out


def unit_at(col, k):
    end = (col == 0) | (col == 3)
    ends = jnp.where(col == 0, k, 3 - k)
    middle = jnp.where(k == 0, col, jnp.where(k == 3, jnp.where(col == 1, 3, 0), jnp.where(col == 1, 2 * k - 2, 5 - 2 * k)))
    return jnp.where(end, ends, middle)


X, Y, SIB = 2, 4, 1


def plane_send(view, row, ss, rs, source=None):
    source = view(row) if source is None else source
    for i, flip in enumerate((X, Y, SIB)):
        remote(source, view(row), ss(i), rs(i), {"row": row_at(row, flip)}).start()


def plane_forward(view, halves, row, ss, rs):
    first, second = halves
    from_x, from_y = row_at(row, X), row_at(row, Y)
    sib = {"row": row_at(row, SIB)}
    remote(view(from_x), view(from_x), ss(0), rs(0), sib).wait_recv()
    remote(first(from_x), first(from_x), ss(3), rs(3), {"row": from_y}).start()
    remote(view(from_x), view(from_x), ss(5), rs(5), sib).start()
    remote(view(from_y), view(from_y), ss(1), rs(1), sib).wait_recv()
    remote(second(from_y), second(from_y), ss(4), rs(4), {"row": from_x}).start()
    remote(view(from_y), view(from_y), ss(6), rs(6), sib).start()


def plane_last(view, halves, row, ss, rs):
    first, second = halves
    diag = row_at(row, X + Y)
    sib = {"row": row_at(row, SIB)}
    remote(first(diag), first(diag), ss(3), rs(3), sib).wait_recv()
    remote(first(diag), first(diag), ss(7), rs(7), sib).start()
    remote(second(diag), second(diag), ss(4), rs(4), sib).wait_recv()
    remote(second(diag), second(diag), ss(8), rs(8), sib).start()


def plane_finish(view, halves, row, ss, rs):
    first, second = halves
    sib_row = row_at(row, SIB)
    sib = {"row": sib_row}
    whole = view(sib_row)
    remote(whole, whole, ss(2), rs(2), sib).wait_recv()
    for i, flip in ((5, X), (6, Y)):
        block = view(row_at(sib_row, flip))
        remote(block, block, ss(i), rs(i), sib).wait_recv()
    far = row_at(sib_row, X + Y)
    remote(first(far), first(far), ss(7), rs(7), sib).wait_recv()
    remote(second(far), second(far), ss(8), rs(8), sib).wait_recv()
    for i in range(9):
        block = view(row) if i in (0, 1, 2, 5, 6) else (first(row) if i in (3, 7) else second(row))
        remote(block, block, ss(i), rs(i), sib).wait_send()


def pick(ref, cols, halves_rows):
    block, cut = halves_rows

    def at(start, size):
        def view(r):
            rows = pl.ds(pl.multiple_of(r * block + start, 16), size)
            if cols is None:
                return ref.at[rows, :]
            return ref.at[rows, pl.ds(pl.multiple_of(cols[0], 128), cols[1])]

        return view

    return at(0, block), (at(0, cut), at(cut, block - cut))


def through(source, middle, target, sem):
    return pltpu.make_async_copy(source, middle, sem), pltpu.make_async_copy(middle, target, sem)


def through(source, middle, target, sem):
    return pltpu.make_async_copy(source, middle, sem), pltpu.make_async_copy(middle, target, sem)


def line_kernel(own_a, own_b, own_s, own_c, w_gate, w_up, line_a, line_b, full_s, full_c, own_gu, mid_a, mid_b, mid_c, mid_gu,
                zss, zrs, css, crs, s_zs, s_zr, s_ps, s_pr, loc):
    row, col = lax.axis_index("row"), lax.axis_index("col")
    width_a, width_b = own_a.shape[1], own_b.shape[1]
    rows_c = own_c.shape[0]
    vc, hc = pick(full_c, None, (rows_c, rows_c // 2))
    csv, crv = (lambda i: css.at[i]), (lambda i: crs.at[i])

    def of_a(c):
        return line_a.at[:, pl.ds(pl.multiple_of(c * width_a, 128), width_a)]

    def of_b(c):
        return line_b.at[:, pl.ds(pl.multiple_of(c * width_b, 128), width_b)]

    copies = [
        through(own_a, mid_a, of_a(col), loc.at[0]),
        through(own_b, mid_b, of_b(col), loc.at[1]),
        through(own_c, mid_c, vc(row), loc.at[2]),
    ]
    for copy, _ in copies:
        copy.start()
    small_copy = pltpu.make_async_copy(own_s, full_s.at[col, row], loc.at[3])
    small_copy.start()
    units = w_gate.shape[1]
    to_gu = [
        pltpu.make_async_copy(w, mid_gu.at[:, pl.ds(i * units, units)], loc.at[4 + i])
        for i, w in enumerate((w_gate, w_up))
    ]
    from_gu = pltpu.make_async_copy(mid_gu, own_gu, loc.at[6])
    greet(range(1, 8), (1, 2, 3))

    def along(i, c, source, target, right, left):
        for d, (cond, step) in enumerate(((right, 1), (left, 3))):
            @pl.when(cond)
            def _():
                remote(source, target, zss.at[i, c, d], zrs.at[i, c], {"col": (col + step) % 4}).start()

    def arrived(k):
        c = unit_order(col, k)
        for i, view in enumerate((of_a(c), of_b(c))):
            remote(view, view, zss.at[i, c, 0], zrs.at[i, c], {"col": (col + 1) % 4}).wait_recv()
            along(i, c, view, view, (c < col) & (col < 3), (c > col) & (col > 0))

    along(0, col, own_a, of_a(col), col < 3, col > 0)
    along(1, col, own_b, of_b(col), col < 3, col > 0)
    for i, step in enumerate((1, 2, 3)):
        remote(own_s, full_s.at[col, row], s_zs.at[i], s_zr.at[i], {"col": (col + step) % 4}).start()
    plane_send(vc, row, csv, crv, own_c)
    for copy in to_gu:
        copy.start()
    for first, second in copies:
        first.wait()
        second.start()
    small_copy.wait()
    for copy in to_gu:
        copy.wait()
    from_gu.start()
    arrived(1)
    for i, step in enumerate((3, 2, 1)):
        remote(own_s, full_s.at[(col + step) % 4, row], s_zs.at[i], s_zr.at[i], {"col": (col + 1) % 4}).wait()
    for i in range(1, 8):
        remote(full_s.at[:, row], full_s.at[:, row], s_ps.at[i - 1], s_pr.at[i - 1], {"row": row_at(row, i)}).start()
    arrived(2)
    plane_forward(vc, hc, row, csv, crv)
    arrived(3)
    plane_last(vc, hc, row, csv, crv)
    for _, second in copies:
        second.wait()
    from_gu.wait()
    plane_finish(vc, hc, row, csv, crv)
    for i in range(1, 8):
        there = row_at(row, i)
        remote(full_s.at[:, there], full_s.at[:, there], s_ps.at[i - 1], s_pr.at[i - 1], {"row": there}).wait()
    for k in range(4):
        c = unit_order(col, k)
        right = (c <= col) & (col < 3)
        left = (c >= col) & (col > 0)
        for d, cond in enumerate((right, left)):
            @pl.when(cond)
            def _():
                there = {"col": (col + 1) % 4}
                remote(of_a(c), of_a(c), zss.at[0, c, d], zrs.at[0, c], there).wait_send()
                remote(of_b(c), of_b(c), zss.at[1, c, d], zrs.at[1, c], there).wait_send()


def gather_line(own_a, own_b, own_s, own_c, w_gate, w_up):
    sems = pltpu.SemaphoreType.DMA
    rows_c = own_c.shape[0]
    return pl.pallas_call(
        line_kernel,
        out_shape=(
            jax.ShapeDtypeStruct((own_a.shape[0], own_a.shape[1] * 4), own_a.dtype),
            jax.ShapeDtypeStruct((own_b.shape[0], own_b.shape[1] * 4), own_b.dtype),
            jax.ShapeDtypeStruct((4, 8) + own_s.shape, own_s.dtype),
            jax.ShapeDtypeStruct((8 * rows_c, own_c.shape[1]), own_c.dtype),
            jax.ShapeDtypeStruct((w_gate.shape[0], 2 * w_gate.shape[1]), w_gate.dtype),
        ),
        in_specs=[ANY] * 6,
        out_specs=(ANY,) * 5,
        scratch_shapes=[
            pltpu.VMEM(own_a.shape, own_a.dtype),
            pltpu.VMEM(own_b.shape, own_b.dtype),
            pltpu.VMEM(own_c.shape, own_c.dtype),
            pltpu.VMEM((w_gate.shape[0], 2 * w_gate.shape[1]), w_gate.dtype),
            sems((2, 4, 2)), sems((2, 4)),
            sems((9,)), sems((9,)),
            sems((3,)), sems((3,)), sems((7,)), sems((7,)), sems((7,)),
        ],
        compiler_params=pltpu.CompilerParams(collective_id=0, has_side_effects=True),
        cost_estimate=pl.CostEstimate(flops=0, bytes_accessed=1_000_000, transcendentals=0),
    )(own_a, own_b, own_s, own_c, w_gate, w_up)


def plane_kernel(count, *refs):
    row = lax.axis_index("row")
    owns, fulls, mids = refs[:count], refs[count : 2 * count], refs[2 * count : 3 * count]
    ss, rs, loc = refs[3 * count :]
    views, copies = [], []
    for i in range(count):
        block = owns[i].shape[0]
        views.append(pick(fulls[i], None, (block, block // 2)))
        copies.append(through(owns[i], mids[i], views[i][0](row), loc.at[i]))
        copies[i][0].start()
    greet(range(1, 8), ())

    def sems_of(i):
        return (lambda j: ss.at[i, j]), (lambda j: rs.at[i, j])

    for i in range(count):
        plane_send(views[i][0], row, *sems_of(i), owns[i])
    for first, second in copies:
        first.wait()
        second.start()
    for i in range(count):
        plane_forward(*views[i], row, *sems_of(i))
    for i in range(count):
        plane_last(*views[i], row, *sems_of(i))
    for _, second in copies:
        second.wait()
    for i in range(count):
        plane_finish(*views[i], row, *sems_of(i))


def gather_plane(collective, owns):
    sems = pltpu.SemaphoreType.DMA
    count = len(owns)
    return pl.pallas_call(
        functools.partial(plane_kernel, count),
        out_shape=tuple(
            jax.ShapeDtypeStruct((8 * own.shape[0], own.shape[1]), own.dtype) for own in owns
        ),
        in_specs=[ANY] * count,
        out_specs=(ANY,) * count,
        scratch_shapes=[pltpu.VMEM(own.shape, own.dtype) for own in owns]
        + [sems((count, 9)), sems((count, 9)), sems((count,))],
        compiler_params=pltpu.CompilerParams(collective_id=collective, has_side_effects=True),
        cost_estimate=pl.CostEstimate(flops=0, bytes_accessed=1_000_000, transcendentals=0),
    )(*owns)


def spread_kernel(own_c, own_g, full_c, full_g, mid_c, css, crs, gss, grs, loc):
    row = lax.axis_index("row")
    rows_c = own_c.shape[0]
    vc, hc = pick(full_c, None, (rows_c, rows_c // 2))
    csv, crv = (lambda i: css.at[i]), (lambda i: crs.at[i])
    first, second = through(own_c, mid_c, vc(row), loc.at[0])
    first.start()
    own_copy = pltpu.make_async_copy(own_g, full_g.at[row], loc.at[1])
    own_copy.start()
    greet(range(1, 8), ())
    plane_send(vc, row, csv, crv, own_c)
    for i in range(1, 8):
        remote(own_g, full_g.at[row], gss.at[i - 1], grs.at[i - 1], {"row": row_at(row, i)}).start()
    first.wait()
    second.start()
    plane_forward(vc, hc, row, csv, crv)
    plane_last(vc, hc, row, csv, crv)
    second.wait()
    own_copy.wait()
    plane_finish(vc, hc, row, csv, crv)
    for i in range(1, 8):
        there = row_at(row, i)
        remote(own_g, full_g.at[there], gss.at[i - 1], grs.at[i - 1], {"row": there}).wait()


def spread_tokens(own_c, own_g):
    sems = pltpu.SemaphoreType.DMA
    return pl.pallas_call(
        spread_kernel,
        out_shape=(
            jax.ShapeDtypeStruct((8 * own_c.shape[0], own_c.shape[1]), own_c.dtype),
            jax.ShapeDtypeStruct((8,) + own_g.shape, own_g.dtype),
        ),
        in_specs=[ANY] * 2,
        out_specs=(ANY,) * 2,
        scratch_shapes=[
            pltpu.VMEM(own_c.shape, own_c.dtype),
            sems((9,)), sems((9,)), sems((7,)), sems((7,)), sems((2,)),
        ],
        compiler_params=pltpu.CompilerParams(collective_id=1, has_side_effects=True),
        cost_estimate=pl.CostEstimate(flops=0, bytes_accessed=1_000_000, transcendentals=0),
    )(own_c, own_g)


def add_into(target, term):
    def body(i, carry):
        rows = pl.ds(pl.multiple_of(i * 32, 32), 32)
        total = target[rows, :].astype(jnp.float32) + term[rows, :].astype(jnp.float32)
        target[rows, :] = total.astype(target.dtype)
        return carry
    lax.fori_loop(0, target.shape[0] // 32, body, 0)


def finish_kernel(count, experts, block, piece, *refs):
    for source, target in zip(refs[:count], refs[count + 2 : 2 * count + 2]):
        target[...] = source[...]
    gu, sums = refs[count : count + 2]
    gate, up, router, gain_a, gain_e, turned = refs[2 * count + 2 :]
    gate[...] = gu[:, : gate.shape[1]].astype(gate.dtype)
    up[...] = gu[:, gate.shape[1] :].astype(up.dtype)

    @pl.when(pl.program_id(0) == 0)
    def _():
        core, col = lax.axis_index("row") % 2, lax.axis_index("col")
        turned[...] = sums[...].T
        mine = turned[pl.ds(pl.multiple_of(core * block, 8), block), :].T
        rows = lax.broadcasted_iota(jnp.int32, mine.shape, 0)
        for j in range(router.shape[0]):
            at = col * router.shape[0] + j
            router[j : j + 1, :] = jnp.sum(jnp.where(rows == at, mine, 0.0), axis=0, keepdims=True)
        own = turned[pl.ds(pl.multiple_of(core * block + col * piece, 8), piece), :].T
        gain_a[...] = own[experts : experts + 1, :]
        gain_e[...] = own[experts + 1 : experts + 2, :]


def finish(arrays, grad_gu, sums, block, piece, router_cols):
    steps = 2
    experts = router_cols * 4

    def spec(a):
        return pl.BlockSpec((a.shape[0] // steps, a.shape[1]), lambda i: (i, 0))

    def once(a):
        return pl.BlockSpec(a.shape, lambda i: (0, 0))

    f32 = jnp.float32
    half = jax.ShapeDtypeStruct((grad_gu.shape[0], grad_gu.shape[1] // 2), f32)
    small = [jax.ShapeDtypeStruct(shape, f32) for shape in ((router_cols, block), (1, piece), (1, piece))]
    return pl.pallas_call(
        functools.partial(finish_kernel, len(arrays), experts, block, piece),
        grid=(steps,),
        out_shape=(*(jax.ShapeDtypeStruct(a.shape, a.dtype) for a in arrays), half, half, *small),
        in_specs=[*(spec(a) for a in arrays), spec(grad_gu), once(sums)],
        out_specs=(*(spec(a) for a in arrays), spec(half), spec(half), *(once(a) for a in small)),
        scratch_shapes=[pltpu.VMEM((sums.shape[1], sums.shape[0]), f32)],
    )(*arrays, grad_gu, sums)


def expert_kernel(key, mine, normed_hbm, upstream_hbm, gu_hbm, own_down,
                  in_out, prod_out, gate_grad_out, grad_gu, sum_down, back_far,
                  in_ref, prod_ref, gate_grad_ref, x_t, ups, gu, down, act, silu, slope, both, gd, rec_right, rec_left, stage, gate,
                  load_sem, src_sem, stage_sem, zss, zrs, rss, rrs, fss, frs, in_sem, prod_sem):
    row, col = lax.axis_index("row"), lax.axis_index("col")
    sources, _, length = key.shape
    slots = in_ref.shape[0]
    capacity = slots // sources
    units = gu.shape[1] // 2
    width = units // 4
    chunk = 256
    x = in_ref
    right_dev, left_dev = {"col": (col + 1) % 4}, {"col": (col + 3) % 4}

    load_gu = pltpu.make_async_copy(gu_hbm, gu, load_sem.at[0])
    load_gu.start()
    load_down = pltpu.make_async_copy(own_down, down.at[col], load_sem.at[1])
    load_down.start()

    def fetch(s, slot):
        rows = pl.ds(pl.multiple_of(s * length, 16), length)
        for i, hbm in enumerate((normed_hbm, upstream_hbm)):
            to = prod_ref.at[pl.ds(pl.multiple_of((slot * 2 + i) * length, 16), length), :]
            yield pltpu.make_async_copy(hbm.at[rows, :], to, src_sem.at[slot, i])

    for copy in fetch(0, 0):
        copy.start()
    greet((X + Y, X + Y + SIB), (1, 2, 3))

    def pass_on(c, source, right, left):
        for d, (cond, there) in enumerate(((right, right_dev), (left, left_dev))):
            @pl.when(cond)
            def _():
                remote(source, down.at[c], zss.at[c, d], zrs.at[c], there).start()

    pass_on(col, own_down, col < 3, col > 0)

    def ag_step(s):
        @pl.when(col >= s)
        def _():
            c = col - s
            remote(down.at[c], down.at[c], zss.at[c, 0], zrs.at[c], right_dev).wait_recv()
            @pl.when(col < 3)
            def _():
                remote(down.at[c], down.at[c], zss.at[c, 0], zrs.at[c], right_dev).start()
        @pl.when(col + s < 4)
        def _():
            c = col + s
            remote(down.at[c], down.at[c], zss.at[c, 1], zrs.at[c], left_dev).wait_recv()
            @pl.when(col > 0)
            def _():
                remote(down.at[c], down.at[c], zss.at[c, 1], zrs.at[c], left_dev).start()

    def to_right(d):
        target = rec_right.at[d - 1]
        return remote(target, target, rss.at[0, d - 1], rrs.at[0, d - 1], right_dev)

    def to_left(d):
        target = rec_left.at[d]
        return remote(target, target, rss.at[1, d], rrs.at[1, d], left_dev)

    def from_end(d):
        @pl.when((col == 0) & (d > 0))
        def _():
            remote(gd.at[d], rec_right.at[d - 1], rss.at[0, d - 1], rrs.at[0, d - 1], right_dev).start()
        @pl.when((col == 3) & (d < 3))
        def _():
            remote(gd.at[d], rec_left.at[d], rss.at[1, d], rrs.at[1, d], left_dev).start()

    def add_rows(target, term):
        def body(i, carry):
            rows = pl.ds(pl.multiple_of(i * 64, 64), 64)
            total = target[rows, :].astype(jnp.float32) + term[rows, :].astype(jnp.float32)
            target[rows, :] = total.astype(target.dtype)
            return carry
        lax.fori_loop(0, width // 64, body, 0)

    def hop_right(d):
        to_right(d).wait_recv()
        add_rows(rec_right.at[d - 1], gd.at[d])
        to_right(d).start()

    def hop_left(d):
        to_left(d).wait_recv()
        add_rows(rec_left.at[d], gd.at[d])
        to_left(d).start()

    def select(s, carry):
        slot = s % 2
        @pl.when(s + 1 < sources)
        def _():
            for copy in fetch(s + 1, 1 - slot):
                copy.start()
        for copy in fetch(s, slot):
            copy.wait()
        chosen = key[s] == lax.broadcasted_iota(jnp.int32, (capacity, length), 0)
        value = jnp.sum(jnp.where(chosen, mine[s], 0.0), axis=1, keepdims=True)
        rows = pl.ds(pl.multiple_of(s * capacity, 16), capacity)
        gate[rows, :] = jnp.broadcast_to(value, (capacity, gate.shape[1]))
        one_hot = jnp.where(chosen, 1.0, 0.0).astype(x.dtype)
        for i, target in enumerate((x, ups)):
            block = prod_ref[pl.ds(pl.multiple_of((slot * 2 + i) * length, 16), length), :]
            target[rows, :] = dot(one_hot, block).astype(target.dtype)
        return carry
    lax.fori_loop(0, sources, select, 0)

    load_gu.wait()

    def forward(c):
        first = pl.ds(pl.multiple_of(c * width, width), width)
        second = pl.ds(pl.multiple_of(units + c * width, width), width)
        def body(m, carry):
            rows = pl.ds(pl.multiple_of(m * chunk, chunk), chunk)
            gate_pre = dot(x[rows, :], gu[:, first])
            up_pre = dot(x[rows, :], gu[:, second])
            sigma = jax.nn.sigmoid(gate_pre)
            silu_gate = gate_pre * sigma
            silu[rows, first] = silu_gate
            slope[rows, first] = up_pre * sigma * (1.0 + gate_pre * (1.0 - sigma))
            low = (silu_gate * up_pre).astype(act.dtype)
            act[rows, first] = low
            both[rows, first] = (low.astype(jnp.float32) * gate[rows, 0:1]).astype(both.dtype)
            return carry
        lax.fori_loop(0, slots // chunk, body, 0)
        gd[c] = t_dot(both[:, first], ups[...]).astype(gd.dtype)

    def forward_step(i, carry):
        c = jnp.where(i < 2, 3 - 3 * i, 4 - i)
        forward(c)
        pl.when((i < 2) | (col == 0))(lambda: from_end(c))
        pl.when(i == 1)(lambda: ag_step(1))
        @pl.when((i == 3) & (col == 3))
        def _():
            from_end(1)
            from_end(2)
        return carry
    lax.fori_loop(0, 4, forward_step, 0)
    load_down.wait()

    def turn(m, carry):
        rows = pl.ds(pl.multiple_of(m * chunk, chunk), chunk)
        x_t[:, rows] = x[rows, :].T
        return carry
    lax.fori_loop(0, slots // chunk, turn, 0)
    gate_grad_ref[...] = jnp.zeros_like(gate_grad_ref)

    def out_stage(c, slot):
        for i in range(2):
            yield pltpu.make_async_copy(
                stage.at[slot, :, pl.ds(i * width, width)],
                grad_gu.at[:, pl.ds(pl.multiple_of(i * units + c * width, width), width)],
                stage_sem.at[slot, i],
            )

    def far(j):
        there = row_at(row, X + Y + j)
        rows = pl.ds(pl.multiple_of(there * capacity, 16), capacity)
        return remote(in_ref.at[rows, :], back_far.at[j], fss.at[j], frs.at[j], {"row": there})

    def of_chip(i):
        chip = row_at(row, 2 * (3 - i)) // 2
        rows = pl.ds(pl.multiple_of(chip * 2 * capacity, 16), 2 * capacity)
        return rows, pltpu.make_async_copy(in_ref.at[rows, :], in_out.at[rows, :], in_sem.at[i])

    def inputs(i, carry):
        rows, copy = of_chip(i)
        in_ref[rows, :] = dot_t(both[rows, :], gu[...]).astype(in_ref.dtype)
        copy.start()
        return carry

    def backward(k):
        c = unit_at(col, k)
        first = pl.ds(pl.multiple_of(c * width, width), width)
        second = pl.ds(pl.multiple_of(units + c * width, width), width)
        def body(m, carry):
            rows = pl.ds(pl.multiple_of(m * chunk, chunk), chunk)
            plain = dot_t(ups[rows, :], down[c])
            term = jnp.sum(act[rows, first].astype(jnp.float32) * plain, axis=1, keepdims=True)
            gate_grad_ref[rows, :] += jnp.broadcast_to(term, (chunk, gate_grad_ref.shape[1]))
            act_grad = plain * gate[rows, 0:1]
            both[rows, first] = (act_grad * slope[rows, first]).astype(both.dtype)
            both[rows, second] = (act_grad * silu[rows, first]).astype(both.dtype)
            return carry
        lax.fori_loop(0, slots // chunk, body, 0)
        @pl.when(k == 3)
        def _():
            inputs(0, 0)
            far(0).start()
            far(1).start()
        slot = k % 2
        @pl.when(k >= 2)
        def _():
            for copy in out_stage(unit_at(col, k - 2), slot):
                copy.wait()
        def grads(i, carry):
            rows = pl.ds(pl.multiple_of(i * chunk, chunk), chunk)
            stage[slot, rows, 0:width] = dot(x_t[rows, :], both[:, first]).astype(stage.dtype)
            stage[slot, rows, width : 2 * width] = dot(x_t[rows, :], both[:, second]).astype(stage.dtype)
            return carry
        lax.fori_loop(0, x_t.shape[0] // chunk, grads, 0)
        for copy in out_stage(c, slot):
            copy.start()

    def backward_step(k, carry):
        backward(k)
        pl.when(k == 0)(lambda: ag_step(2))
        pl.when((k == 0) & (col == 1))(lambda: hop_right(3))
        pl.when((k == 0) & (col == 2))(lambda: hop_left(0))
        pl.when(k == 2)(lambda: ag_step(3))
        @pl.when((k == 2) & (col == 1))
        def _():
            hop_right(2)
            hop_left(0)
        @pl.when((k == 2) & (col == 2))
        def _():
            hop_right(3)
            hop_left(1)
        return carry
    lax.fori_loop(0, 4, backward_step, 0)

    lax.fori_loop(1, sources // 2, inputs, 0)

    def outputs(m, carry):
        rows = pl.ds(pl.multiple_of(m * chunk, chunk), chunk)
        total = dot(act[rows, 0:width], down[0])
        for c in range(1, 4):
            total = total + dot(act[rows, c * width : (c + 1) * width], down[c])
        prod_ref[rows, :] = total.astype(prod_ref.dtype)
        pltpu.make_async_copy(prod_ref.at[rows, :], prod_out.at[rows, :], prod_sem.at[m]).start()
        return carry
    lax.fori_loop(0, slots // chunk, outputs, 0)

    turned = gate_grad_ref[...].T
    for s in range(sources):
        gate_grad_out[s] = turned[0:1, s * capacity : (s + 1) * capacity]
    for k in (2, 3):
        for copy in out_stage(unit_at(col, k), k % 2):
            copy.wait()
    pl.when(col > 0)(lambda: to_right(col).wait_recv())
    pl.when(col < 3)(lambda: to_left(col).wait_recv())

    def to_sum(i, carry):
        rows = pl.ds(pl.multiple_of(i * 64, 64), 64)
        sum_down[rows, :] = gd[col, rows, :].astype(jnp.float32)
        @pl.when(col > 0)
        def _():
            sum_down[rows, :] += rec_right[jnp.maximum(col - 1, 0), rows, :].astype(jnp.float32)
        @pl.when(col < 3)
        def _():
            sum_down[rows, :] += rec_left[jnp.minimum(col, 2), rows, :].astype(jnp.float32)
        return carry
    lax.fori_loop(0, width // 64, to_sum, 0)

    def sent(e, carry):
        pl.when(e > col)(lambda: to_right(e).wait_send())
        pl.when(e < col)(lambda: to_left(e).wait_send())
        @pl.when((col < 3) & (e <= col))
        def _():
            remote(down.at[e], down.at[e], zss.at[e, 0], zrs.at[e], right_dev).wait_send()
        @pl.when((col > 0) & (e >= col))
        def _():
            remote(down.at[e], down.at[e], zss.at[e, 1], zrs.at[e], left_dev).wait_send()
        return carry
    lax.fori_loop(0, 4, sent, 0)
    for j in range(2):
        far(j).wait()

    def written(i, carry):
        of_chip(i)[1].wait()
        rows = pl.ds(pl.multiple_of(i * chunk, chunk), chunk)
        pltpu.make_async_copy(prod_ref.at[rows, :], prod_out.at[rows, :], prod_sem.at[i]).wait()
        return carry
    lax.fori_loop(0, 4, written, 0)


def run_expert(key, mine, normed, upstream, full_gu, own_down):
    sources, length = key.shape
    model, units = full_gu.shape[0], full_gu.shape[1] // 2
    width = own_down.shape[0]
    slots = sources * length // 2
    low, f32 = normed.dtype, jnp.float32
    sems = pltpu.SemaphoreType.DMA
    vm = pl.BlockSpec(memory_space=pltpu.VMEM)
    return pl.pallas_call(
        expert_kernel,
        out_shape=(
            jax.ShapeDtypeStruct((slots, model), low),
            jax.ShapeDtypeStruct((slots, model), low),
            jax.ShapeDtypeStruct((sources, 1, slots // sources), f32),
            jax.ShapeDtypeStruct((model, 2 * units), low),
            jax.ShapeDtypeStruct((width, model), f32),
            jax.ShapeDtypeStruct((2, slots // sources, model), low),
        ),
        in_specs=[vm, vm, ANY, ANY, ANY, ANY],
        out_specs=(ANY, ANY, vm, ANY, vm, ANY),
        scratch_shapes=[
            pltpu.VMEM((slots, model), low),
            pltpu.VMEM((slots, model), low),
            pltpu.VMEM((slots, 128), f32),
            pltpu.VMEM((model, slots), low),
            pltpu.VMEM((slots, model), low),
            pltpu.VMEM((model, 2 * units), low),
            pltpu.VMEM((4, width, model), low),
            pltpu.VMEM((slots, units), low),
            pltpu.VMEM((slots, units), f32),
            pltpu.VMEM((slots, units), f32),
            pltpu.VMEM((slots, 2 * units), low),
            pltpu.VMEM((4, width, model), low),
            pltpu.VMEM((3, width, model), low),
            pltpu.VMEM((3, width, model), low),
            pltpu.VMEM((2, model, 2 * width), low),
            pltpu.VMEM((slots, 128), f32),
            sems((2,)), sems((2, 2)), sems((2, 2)),
            sems((4, 2)), sems((4,)), sems((2, 3)), sems((2, 3)), sems((2,)), sems((2,)), sems((4,)), sems((4,)),
        ],
        compiler_params=pltpu.CompilerParams(
            collective_id=4, has_side_effects=True, vmem_limit_bytes=60 * 2**20
        ),
        cost_estimate=pl.CostEstimate(flops=0, bytes_accessed=1_000_000, transcendentals=0),
    )(key.reshape(sources, 1, length), mine.reshape(sources, 1, length), normed, upstream, full_gu, own_down)


def backward_kernel(table, router_p, gains, lse,
                    gate_grad, in_grad, back_far, produced, hidden_hbm, tokens_hbm, cot_hbm, normed_hbm, attended_hbm,
                    two_hbm, qkv_hbm, full_a_hbm, full_out_hbm,
                    out_hbm, d_hbm, sum_q, sum_k, sum_v, sum_b, sum_s,
                    out_ref, d_tokens, cols, rec_in, rec_gate, rec_prod, hidden, tokens, cot, two, qkv, full_a, full_out,
                    n_t, a_t, branch, bias, out_rows, grad_c, qg, lgs, small,
                    own, sib_out, rec_sib, rec_one, rec_two, rec_z, s_rec, s_mid, s_zrec,
                    load, in_ss, in_rs, g_ss, g_rs, pr_ss, pr_rs, loc, far_sem, write,
                    ss1, rs1, ss2, rs2, zss, zrs, s_ss, s_rs, sz_ss, sz_rs):
    row, col = lax.axis_index("row"), lax.axis_index("col")
    core = row % 2
    chip = row // 2
    cy, cx = chip // 2, chip % 2
    length, model = hidden.shape
    capacity = rec_in.shape[0] // 8
    block = own.shape[2]
    width_b = sum_b.shape[1]
    width_a = own.shape[3] - width_b
    cut = block // 2
    half = length // 2
    f32, low = jnp.float32, branch.dtype
    sib = {"row": row_at(row, SIB)}
    to_x, to_y = {"row": row_at(row, X)}, {"row": row_at(row, Y)}

    def each_flip(function):
        def body(i, carry):
            function(7 - i)
            return carry
        lax.fori_loop(0, 7, body, 0)

    def block_of(r):
        return pl.ds(pl.multiple_of(r * capacity, 16), capacity)

    own_in = pltpu.make_async_copy(in_grad.at[block_of(row), :], rec_in.at[block_of(row), :], loc.at[0])
    own_gate = pltpu.make_async_copy(gate_grad.at[row], rec_gate.at[row], loc.at[1])
    own_prod = pltpu.make_async_copy(produced.at[block_of(row), :], rec_prod.at[block_of(row), :], loc.at[2])
    loads = [
        pltpu.make_async_copy(source, target, load.at[i])
        for i, (source, target) in enumerate((
            (normed_hbm, branch), (attended_hbm, a_t), (hidden_hbm, hidden), (cot_hbm, cot), (two_hbm, two),
            (qkv_hbm, qkv), (tokens_hbm, tokens), (full_out_hbm, full_out), (full_a_hbm, full_a),
        ))
    ]
    greet(range(1, 8), (1, 2, 3))

    far_in = [
        pltpu.make_async_copy(back_far.at[j], rec_in.at[block_of(row_at(row, X + Y + j)), :], far_sem.at[j])
        for j in range(2)
    ]

    def back(flip):
        there = row_at(row, flip)
        return remote(in_grad.at[block_of(there), :], rec_in.at[block_of(row), :],
                      in_ss.at[flip - 1], in_rs.at[flip - 1], {"row": there})

    def back_gate(flip):
        there = row_at(row, flip)
        return remote(gate_grad.at[there], rec_gate.at[row], g_ss.at[flip - 1], g_rs.at[flip - 1], {"row": there})

    def each_near(function):
        def body(i, carry):
            function(5 - i)
            return carry
        lax.fori_loop(0, 5, body, 0)

    def back_prod(flip):
        there = row_at(row, flip)
        return remote(produced.at[block_of(there), :], rec_prod.at[block_of(row), :],
                      pr_ss.at[flip - 1], pr_rs.at[flip - 1], {"row": there})

    each_near(lambda flip: back(flip).start())
    each_flip(lambda flip: back_gate(flip).start())
    for copy in (own_in, own_gate, own_prod, *far_in):
        copy.start()
    cols[...] = table[...].T
    for copy in loads:
        copy.start()
    loads[0].wait()
    n_t[...] = branch[...].T
    key_pos = lax.broadcasted_iota(jnp.int32, (length, length), 0)
    query_pos = lax.broadcasted_iota(jnp.int32, (length, length), 1)
    allowed = (key_pos <= query_pos) & (cols[:, 6:7] == table[6:7, :])
    bias[...] = jnp.where(allowed, 0.0, NEGATIVE)
    small[...] = jnp.zeros_like(small)
    for copy in loads[1:]:
        copy.wait()
    for copy in (own_in, own_gate, *far_in):
        copy.wait()
    each_flip(lambda flip: back_gate(flip).wait_recv())
    each_near(lambda flip: back(flip).wait_recv())

    all_gate = jnp.concatenate([rec_gate[e] for e in range(8)], axis=1)
    wide = rec_in.shape[0]
    lanes = lgs.shape[1]

    def at_slot(rows, k):
        return cols[rows, k : k + 1] == lax.broadcasted_iota(jnp.int32, (half, wide), 1).astype(f32)

    def to_hidden(m, carry):
        rows = pl.ds(pl.multiple_of(m * half, half), half)
        first, second = at_slot(rows, 0), at_slot(rows, 1)
        picked = jnp.where(first | second, 1.0, 0.0).astype(low)
        two_grad = dot(picked, rec_in[...])
        grad_0 = jnp.sum(jnp.where(first, all_gate, 0.0), axis=1, keepdims=True)
        grad_1 = jnp.sum(jnp.where(second, all_gate, 0.0), axis=1, keepdims=True)
        gate_0, gate_1 = cols[rows, 4:5], cols[rows, 5:6]
        mean = gate_0 * grad_0 + gate_1 * grad_1
        lane = lax.broadcasted_iota(jnp.int32, (half, lanes), 1).astype(f32)
        logit_grad = jnp.where(lane == cols[rows, 2:3], gate_0 * (grad_0 - mean), 0.0)
        logit_grad = logit_grad + jnp.where(lane == cols[rows, 3:4], gate_1 * (grad_1 - mean), 0.0)
        logit_grad = logit_grad.astype(low)
        lgs[rows, :] = logit_grad
        two_grad = two_grad + dot_t(logit_grad, router_p[...])
        h = hidden[rows, :]
        factor = lax.rsqrt(jnp.mean(h * h, axis=1, keepdims=True) + EPSILON)
        small[9:10, :] += jnp.sum(two_grad * h * factor, axis=0, keepdims=True)
        scaled = two_grad * gains[1:2, :]
        inner = jnp.mean(scaled * h, axis=1, keepdims=True)
        grad = cot[rows, :].astype(f32) + factor * scaled - h * (factor * factor * factor * inner)
        d_tokens[rows, :] = grad
        branch[rows, :] = grad.astype(low)
        return carry
    lax.fori_loop(0, 2, to_hidden, 0)
    small[0:8, :] = t_dot(lgs[...], two[...])[0:8, :]

    def nth(k):
        return (col + 1 + k) % 4

    lanes_of = {"a": pl.ds(0, width_a), "b": pl.ds(width_a, width_b)}
    part_at = {"a": 0, "b": 1}

    def to_sibling(part, c, q):
        view = lanes_of[part]
        i = part_at[part]
        return remote(sib_out.at[c, q, :, view], rec_sib.at[c, q, :, view], ss1.at[c, q, i], rs1.at[c, q, i], sib)

    def weight_grads(part, c, left, right):
        view = lanes_of[part]
        def body(q, carry):
            theirs = pl.ds(pl.multiple_of((q * 2 + 1 - core) * block, 16), block)
            sib_out[c, q, :, view] = dot(left[theirs, :], right()).astype(low)
            to_sibling(part, c, q).start()
            mine = pl.ds(pl.multiple_of((q * 2 + core) * block, 16), block)
            own[c, q, :, view] = dot(left[mine, :], right()).astype(low)
            return carry
        lax.fori_loop(0, 4, body, 0)

    def cols_b(c):
        return pl.ds(pl.multiple_of(c * width_b, 128), width_b)

    def attend_back(c):
        span_c = width_b // QUERY_PER_KEY
        for i in range(QUERY_PER_KEY):
            for u in range(2):
                rows = pl.ds(pl.multiple_of(c * width_b + (u * QUERY_PER_KEY + i) * HEAD_SIZE, HEAD_SIZE), HEAD_SIZE)
                out_rows[(2 * i + u) * HEAD_SIZE : (2 * i + u + 1) * HEAD_SIZE, :] = full_out[rows, :]
        grad_c[...] = dot_t(branch[...], out_rows[...]).astype(low)
        at_c = pl.multiple_of(c * width_a, 128)
        key = qkv[:, pl.ds(at_c + width_b, span_c)]
        value = qkv[:, pl.ds(at_c + width_b + span_c, span_c)]
        first = lax.broadcasted_iota(jnp.int32, (length, span_c), 1) < HEAD_SIZE
        none = jnp.zeros_like(key)
        keys = (jnp.where(first, key, none), jnp.where(first, none, key))
        values = (jnp.where(first, value, none), jnp.where(first, none, value))
        scale = HEAD_SIZE ** (-0.5)
        key_grads = [jnp.zeros((length, span_c), f32) for _ in range(2)]
        value_grads = [jnp.zeros((length, span_c), f32) for _ in range(2)]
        for i in range(QUERY_PER_KEY):
            q_i = qkv[:, pl.ds(at_c + i * span_c, span_c)]
            g_i = grad_c[:, i * span_c : (i + 1) * span_c]
            q_grad = jnp.zeros((length, span_c), f32)
            for u in range(2):
                log_total = lse[c * 2 + u, :, i * length : (i + 1) * length]
                probs = jnp.exp(dot_t(keys[u], q_i) * scale + bias[...] - log_total)
                prob_grad = dot_t(values[u], g_i)
                delta = jnp.sum(probs * prob_grad, axis=0, keepdims=True)
                score_grad = (probs * (prob_grad - delta)).astype(low)
                value_grads[u] += dot(probs.astype(low), g_i)
                key_grads[u] += dot(score_grad, q_i)
                q_grad += t_dot(score_grad, keys[u])
            qg[c, :, i * span_c : (i + 1) * span_c] = (q_grad * scale).astype(low)
        key_grad = jnp.where(first, key_grads[0], key_grads[1]) * scale
        qg[c, :, width_b : width_b + span_c] = key_grad.astype(low)
        qg[c, :, width_b + span_c : width_a] = jnp.where(first, value_grads[0], value_grads[1]).astype(low)

    top, bottom = pl.ds(0, cut), pl.ds(cut, block - cut)

    def one(part, c):
        view, i = lanes_of[part], part_at[part]
        for j in range(2):
            yield remote(own.at[c, j * 2 + 1 - cx, top, view], rec_one.at[c, 0, j, :, view],
                         ss2.at[c, i, 0, j], rs2.at[c, i, 0, j], to_x)
            yield remote(own.at[c, (1 - cy) * 2 + j, bottom, view], rec_one.at[c, 1, j, :, view],
                         ss2.at[c, i, 1, j], rs2.at[c, i, 1, j], to_y)

    def two_step(part, c):
        view, i = lanes_of[part], part_at[part]
        yield remote(own.at[c, (1 - cy) * 2 + cx, top, view], rec_two.at[c, 0, :, view],
                     ss2.at[c, i, 0, 2], rs2.at[c, i, 0, 2], to_y)
        yield remote(own.at[c, cy * 2 + 1 - cx, bottom, view], rec_two.at[c, 1, :, view],
                     ss2.at[c, i, 1, 2], rs2.at[c, i, 1, 2], to_x)

    def column(part, step):
        there = (col + step) % 4
        view, i = lanes_of[part], part_at[part]
        return remote(own.at[there, chip, :, view], rec_z.at[step - 1, :, view],
                      zss.at[i, step - 1], zrs.at[i, step - 1], {"col": there})

    def stage_one(part, k):
        c, view = nth(k), lanes_of[part]
        def body(q, carry):
            to_sibling(part, c, q).wait_recv()
            add_into(own.at[c, q, :, view], rec_sib.at[c, q, :, view])
            return carry
        lax.fori_loop(0, 4, body, 0)
        for copy in one(part, c):
            copy.start()

    def stage_two(part, k):
        c, view = nth(k), lanes_of[part]
        for copy in one(part, c):
            copy.wait_recv()
        for j in range(2):
            add_into(own.at[c, j * 2 + cx, top, view], rec_one.at[c, 0, j, :, view])
            add_into(own.at[c, cy * 2 + j, bottom, view], rec_one.at[c, 1, j, :, view])
        for copy in two_step(part, c):
            copy.start()

    def stage_three(part, k):
        c, view = nth(k), lanes_of[part]
        for copy in two_step(part, c):
            copy.wait_recv()
        add_into(own.at[c, chip, top, view], rec_two.at[c, 0, :, view])
        add_into(own.at[c, chip, bottom, view], rec_two.at[c, 1, :, view])
        pl.when(k < 3)(lambda: column(part, k + 1).start())

    def out_grads(k, carry):
        c = nth(k)
        weight_grads("b", c, a_t, lambda: branch[:, cols_b(c)])
        pl.when(k >= 1)(lambda: stage_one("b", k - 1))
        pl.when(k >= 2)(lambda: stage_two("b", k - 2))
        pl.when(k >= 3)(lambda: stage_three("b", k - 3))
        return carry
    lax.fori_loop(0, 4, out_grads, 0)

    def input_grads(k, carry):
        c = nth(k)
        attend_back(c)
        weight_grads("a", c, n_t, lambda: qg[c])
        pl.when(k == 0)(lambda: stage_one("b", k + 3))
        pl.when(k >= 1)(lambda: stage_one("a", k - 1))
        pl.when(k <= 1)(lambda: stage_two("b", k + 2))
        pl.when(k >= 2)(lambda: stage_two("a", k - 2))
        pl.when(k <= 2)(lambda: stage_three("b", k + 1))
        pl.when(k >= 3)(lambda: stage_three("a", k - 3))
        return carry
    lax.fori_loop(0, 4, input_grads, 0)
    stage_one("a", 3)
    each_flip(lambda flip: back_prod(flip).start())
    stage_two("a", 2)
    stage_three("a", 1)

    def to_tokens(m, carry):
        rows = pl.ds(pl.multiple_of(m * half, half), half)
        grad = dot_t(qg[0, rows, :], full_a[:, 0:width_a])
        for c in range(1, 4):
            grad = grad + dot_t(qg[c, rows, :], full_a[:, c * width_a : (c + 1) * width_a])
        x = tokens[rows, :].astype(f32)
        factor = lax.rsqrt(jnp.mean(x * x, axis=1, keepdims=True) + EPSILON)
        small[8:9, :] += jnp.sum(grad * x * factor, axis=0, keepdims=True)
        scaled = grad * gains[0:1, :]
        inner = jnp.mean(scaled * x, axis=1, keepdims=True)
        d_tokens[rows, :] += factor * scaled - x * (factor * factor * factor * inner)
        return carry
    lax.fori_loop(0, 2, to_tokens, 0)
    write_tokens = pltpu.make_async_copy(d_tokens, d_hbm, write.at[0])
    write_tokens.start()

    span = s_mid.shape[1]

    def small_plane(flip):
        there = row_at(row, flip)
        view = small.at[:, pl.ds(pl.multiple_of((there // 2) * span, 128), span)]
        return remote(view, s_rec.at[flip - 1], s_ss.at[flip - 1], s_rs.at[flip - 1], {"row": there})

    def small_column(step):
        return remote(s_mid, s_zrec.at[step - 1], sz_ss.at[step - 1], sz_rs.at[step - 1], {"col": (col + step) % 4})

    each_flip(lambda flip: small_plane(flip).start())
    stage_two("a", 3)
    stage_three("a", 2)
    s_mid[...] = small[:, pl.ds(pl.multiple_of(chip * span, 128), span)]

    def add_small(flip):
        small_plane(flip).wait_recv()
        s_mid[...] += s_rec[flip - 1]

    each_flip(add_small)
    for step in (1, 2, 3):
        small_column(step).start()
    stage_three("a", 3)

    own_prod.wait()
    each_flip(lambda flip: back_prod(flip).wait_recv())

    def to_output(m, carry):
        rows = pl.ds(pl.multiple_of(m * half, half), half)
        total = hidden[rows, :]
        for k in range(2):
            picked = jnp.where(at_slot(rows, k), 1.0, 0.0).astype(low)
            total = total + dot(picked, rec_prod[...]) * cols[rows, 4 + k : 5 + k]
        out_ref[rows, :] = total.astype(low)
        return carry
    lax.fori_loop(0, 2, to_output, 0)
    write_output = pltpu.make_async_copy(out_ref, out_hbm, write.at[1])
    write_output.start()

    total = s_mid[...]
    for step in (1, 2, 3):
        small_column(step).wait_recv()
        total = total + s_zrec[step - 1]
    sum_s[...] = total
    for part in ("b", "a"):
        for step in (1, 2, 3):
            column(part, step).wait_recv()

    def to_sums(i, carry):
        rows = pl.ds(pl.multiple_of(i * 32, 32), 32)
        total = own[col, chip, rows, :].astype(f32)
        for step in range(3):
            total = total + rec_z[step, rows, :].astype(f32)
        span_c = width_b // QUERY_PER_KEY
        zero, one_, two_ = (total[:, i * span_c : (i + 1) * span_c] for i in range(QUERY_PER_KEY))
        turned = pltpu.roll(one_, HEAD_SIZE, 1)
        first = lax.broadcasted_iota(jnp.int32, zero.shape, 1) < HEAD_SIZE
        sum_q[rows, 0:span_c] = jnp.where(first, zero, turned)
        sum_q[rows, span_c : 2 * span_c] = jnp.where(first, two_, zero)
        sum_q[rows, 2 * span_c : width_b] = jnp.where(first, turned, two_)
        sum_k[rows, :] = total[:, width_b : width_b + span_c]
        sum_v[rows, :] = total[:, width_b + span_c : width_a]
        sum_b[rows, :] = total[:, width_a:]
        return carry
    lax.fori_loop(0, block // 32, to_sums, 0)

    write_tokens.wait()
    write_output.wait()

    each_near(lambda flip: back(flip).wait_send())

    def all_sent(flip):
        back_gate(flip).wait_send()
        back_prod(flip).wait_send()
        small_plane(flip).wait_send()

    each_flip(all_sent)
    for step in (1, 2, 3):
        small_column(step).wait_send()
        column("a", step).wait_send()
        column("b", step).wait_send()

    def sent(c, carry):
        for part in ("a", "b"):
            def body(q, carry):
                to_sibling(part, c, q).wait_send()
                return carry
            lax.fori_loop(0, 4, body, 0)
            for copy in one(part, c):
                copy.wait_send()
            for copy in two_step(part, c):
                copy.wait_send()
        return carry
    lax.fori_loop(0, 4, sent, 0)


def run_backward(slot_of, gates, ids, router, gains, lse, segments, gate_grad, in_grad, back_far, produced,
                 hidden, tokens, cotangent, normed, attended, normed_two, qkv, full_a, full_out):
    table = jnp.concatenate(
        [slot_of.T.astype(jnp.float32), ids.T.astype(jnp.float32), gates.T, segments[None].astype(jnp.float32),
         jnp.zeros((1, segments.shape[0]), jnp.float32)], axis=0)
    sems = pltpu.SemaphoreType.DMA
    length, model = tokens.shape
    block = full_a.shape[0] // 8
    width_a, width_b = full_a.shape[1] // 4, full_out.shape[1] // 4
    width = width_a + width_b
    cut = block // 2
    low, f32 = tokens.dtype, jnp.float32
    vm = pl.BlockSpec(memory_space=pltpu.VMEM)
    slots = in_grad.shape[0]
    capacity = slots // 8
    span = model // 4
    router_p = jnp.pad(router, ((0, 0), (0, 128 - router.shape[1])))
    v = pltpu.VMEM
    rows_low = v((length, model), low)
    return pl.pallas_call(
        backward_kernel,
        out_shape=(
            jax.ShapeDtypeStruct((length, model), low),
            jax.ShapeDtypeStruct((length, model), f32),
            jax.ShapeDtypeStruct((block, width_b), f32),
            jax.ShapeDtypeStruct((block, (width_a - width_b) // 2), f32),
            jax.ShapeDtypeStruct((block, (width_a - width_b) // 2), f32),
            jax.ShapeDtypeStruct((block, width_b), f32),
            jax.ShapeDtypeStruct((16, span), f32),
        ),
        in_specs=[vm] * 4 + [ANY] * 13,
        out_specs=(ANY, ANY) + (vm,) * 5,
        scratch_shapes=[
            rows_low, v((length, model), f32), v((length, 8), f32), v((slots, model), low), v((8, 1, capacity), f32), v((slots, model), low),
            v((length, model), f32), rows_low, rows_low, rows_low,
            v(qkv.shape, low), v(full_a.shape, low), v(full_out.shape, low),
            v((model, length), low), v((model, length), low), rows_low,
            v((length, length), f32), v((width_b, model), low), v((length, width_b), low), v((4, length, width_a), low),
            v((length, 128), low), v((16, model), f32),
            v((4, 4, block, width), low), v((4, 4, block, width), low), v((4, 4, block, width), low),
            v((4, 2, 2, cut, width), low), v((4, 2, cut, width), low), v((3, block, width), low),
            v((7, 16, span), f32), v((16, span), f32), v((3, 16, span), f32),
            sems((9,)), sems((7,)), sems((7,)), sems((7,)), sems((7,)), sems((7,)), sems((7,)), sems((3,)), sems((2,)), sems((2,)),
            sems((4, 4, 2)), sems((4, 4, 2)), sems((4, 2, 2, 3)), sems((4, 2, 2, 3)),
            sems((2, 3)), sems((2, 3)), sems((7,)), sems((7,)), sems((3,)), sems((3,)),
        ],
        compiler_params=pltpu.CompilerParams(
            collective_id=2, has_side_effects=True, vmem_limit_bytes=60 * 2**20
        ),
        cost_estimate=pl.CostEstimate(flops=0, bytes_accessed=1_000_000, transcendentals=0),
    )(table, router_p, gains, lse, gate_grad, in_grad, back_far, produced, hidden, tokens,
      cotangent, normed, attended, normed_two, qkv, full_a, full_out)


def rms_factor(rows_in):
    return lax.rsqrt(jnp.mean(rows_in * rows_in, axis=1, keepdims=True) + EPSILON)


def dot(a, b):
    return jnp.dot(a, b, preferred_element_type=jnp.float32)


def dot_t(a, b):
    return lax.dot_general(a, b, (((1,), (1,)), ((), ())), preferred_element_type=jnp.float32)


def t_dot(a, b):
    return lax.dot_general(a, b, (((0,), (0,)), ((), ())), preferred_element_type=jnp.float32)


def on_small_slice():
    return lax.axis_size("row") == 8 and lax.axis_size("col") == 4


def pair_heads(a):
    if not on_small_slice():
        return [a]
    heads = [a[:, i * HEAD_SIZE : (i + 1) * HEAD_SIZE] for i in range(a.shape[1] // HEAD_SIZE)]
    return [heads[u * QUERY_PER_KEY + i] for i in range(QUERY_PER_KEY) for u in range(2)]


def part_heads(a):
    a = a.reshape(a.shape[0], -1, QUERY_PER_KEY, 2, HEAD_SIZE)
    return a.transpose(0, 1, 3, 2, 4).reshape(a.shape[0], -1)


def gather_all(own_a, own_b, own_s, own_c):
    col_a = lax.all_gather(own_a, "col", axis=1, tiled=True)
    col_b = lax.all_gather(own_b, "col", axis=1, tiled=True)
    small = lax.all_gather(lax.all_gather(own_s, "col", axis=0), "row", axis=1)
    return (
        lax.all_gather(col_a, "row", axis=0, tiled=True),
        lax.all_gather(col_b, "row", axis=0, tiled=True),
        small,
        lax.all_gather(own_c, "row", axis=0, tiled=True),
    )


def spread(own_c, own_g):
    if on_small_slice():
        return spread_tokens(own_c, own_g)
    return (
        lax.all_gather(own_c, "row", axis=0, tiled=True),
        lax.all_gather(own_g, "row", axis=0),
    )


def reduce_all(grad_a, grad_b, grad_s):
    def both(g):
        plane = lax.psum_scatter(g, "row", scatter_dimension=0, tiled=True).astype(jnp.float32)
        return lax.psum_scatter(plane, "col", scatter_dimension=1, tiled=True)

    small = lax.psum_scatter(grad_s, "row", scatter_dimension=0, tiled=False)
    return both(grad_a), both(grad_b), lax.psum_scatter(small, "col", scatter_dimension=0, tiled=False)


def expert_elsewhere(place, routed, mine, plane_normed, plane_upstream, full_gu, own_down):
    rows, length = place.shape
    model = plane_normed.shape[1]
    hidden_units = full_gu.shape[1] // 2
    capacity = 2 * length * TOP // rows
    full_down = lax.all_gather(own_down, "col", axis=0, tiled=True)
    chosen_rows = (
        (place[:, None, :] == jnp.arange(capacity, dtype=jnp.int32)[None, :, None]) & routed[:, None, :]
    ).astype(jnp.bfloat16)

    def of_slots(plane):
        return jnp.einsum(
            "rct,rtd->rcd",
            chosen_rows,
            plane.reshape(rows, length, model),
            preferred_element_type=jnp.float32,
        ).astype(jnp.bfloat16).reshape(rows * capacity, model)

    grouped, grouped_up = of_slots(plane_normed), of_slots(plane_upstream)
    slot_gate = jnp.sum(jnp.where(chosen_rows > 0, mine[:, None, :], 0.0), axis=2)
    slot_gate = slot_gate.reshape(rows * capacity, 1)
    grouped_grad = (grouped_up.astype(jnp.float32) * slot_gate).astype(jnp.bfloat16)
    both_pre = dot(grouped, full_gu)
    gate_pre, up_pre = both_pre[:, :hidden_units], both_pre[:, hidden_units:]
    sigma = jax.nn.sigmoid(gate_pre)
    silu_gate = gate_pre * sigma
    activation = (silu_gate * up_pre).astype(jnp.bfloat16)
    grad_down_local = t_dot(activation, grouped_grad).astype(jnp.bfloat16)
    grad_down = lax.psum_scatter(grad_down_local, "col", scatter_dimension=0, tiled=True)
    act_grad = dot_t(grouped_grad, full_down)
    both_grad = jnp.concatenate(
        [
            (act_grad * up_pre * sigma * (1.0 + gate_pre * (1.0 - sigma))).astype(jnp.bfloat16),
            (act_grad * silu_gate).astype(jnp.bfloat16),
        ],
        axis=1,
    )
    in_grad = dot_t(both_grad, full_gu).astype(jnp.bfloat16)
    produced = dot(activation, full_down).astype(jnp.bfloat16)
    slot_gate_grad = jnp.sum(produced.astype(jnp.float32) * grouped_up.astype(jnp.float32), axis=1)
    grad_gu_local = t_dot(grouped, both_grad).astype(jnp.bfloat16)
    return in_grad, produced, slot_gate_grad, grad_gu_local, grad_down.astype(jnp.float32)


def masked_scores(queries, heads_of_key, segments, head_scale):
    length = queries.shape[0]
    heads_of_query = queries.reshape(length, KEY_VALUE_HEADS, QUERY_PER_KEY, HEAD_SIZE)
    scores = (
        jnp.einsum("qkgd,skd->kgqs", heads_of_query, heads_of_key, preferred_element_type=jnp.float32)
        * head_scale
    )
    pos = jnp.arange(length, dtype=jnp.int32)
    allowed = (pos[None, :] <= pos[:, None]) & (segments[None, :] == segments[:, None])
    return jnp.where(allowed, scores, NEGATIVE), heads_of_query


def per_device(
    tokens,
    attn_gain,
    w_query,
    w_key,
    w_value,
    w_out,
    expert_gain,
    router,
    w_gate,
    w_up,
    w_down,
    segment_ids,
    expert_ids,
    cotangent,
):
    length, model = tokens.shape
    rows, cols = lax.axis_size("row"), lax.axis_size("col")
    experts = w_gate.shape[0] * rows
    capacity = 2 * length * TOP // experts
    head_scale = HEAD_SIZE ** (-0.5)
    segments = segment_ids.reshape(-1)
    block, width_q = w_query.shape
    width_k = w_key.shape[1]
    width_a = width_q + 2 * width_k
    piece = attn_gain.shape[0]
    router_cols = router.shape[1]

    hidden_units = w_gate.shape[2]
    own_down = w_down[0]

    lane = 256

    def at_row(v, row):
        return jnp.pad(v, ((row, 16 - row - v.shape[0]), (0, lane - v.shape[1])))

    own_s = (
        at_row(router.T, 0)
        + at_row(attn_gain[None], router_cols)
        + at_row(expert_gain[None], router_cols + 1)
    )
    own_a = jnp.concatenate([*pair_heads(w_query), w_key, w_value], axis=1)
    if on_small_slice():
        line_a, line_out, small, plane_upstream, own_gu = gather_line(
            own_a, w_out, own_s, cotangent, w_gate[0], w_up[0]
        )
        full_a, full_out = gather_plane(3, (line_a, line_out))
    else:
        own_gu = jnp.concatenate([w_gate[0], w_up[0]], axis=1)
        full_a, full_out, small, plane_upstream = gather_all(own_a, w_out, own_s, cotangent)
    full_gu = lax.all_gather(own_gu, "col", axis=0, tiled=True)
    full_router = small[:, :, :router_cols, :block].transpose(1, 3, 0, 2).reshape(model, experts)
    gains = (
        small[:, :, router_cols : router_cols + 2, :piece].transpose(2, 1, 0, 3).reshape(2, model).astype(jnp.float32)
    )
    gain_one, gain_two = gains[0:1], gains[1:2]

    rows_f = tokens.astype(jnp.float32)
    factor_one = rms_factor(rows_f)
    normed = (rows_f * factor_one * gain_one).astype(jnp.bfloat16)
    flat_qkv = dot(normed, full_a).astype(jnp.bfloat16)
    qkv = flat_qkv.reshape(length, cols, width_a)
    query_rows = qkv[:, :, :width_q].reshape(length, -1)
    if on_small_slice():
        query_rows = part_heads(query_rows)
    rows_of_key = qkv[:, :, width_q : width_q + width_k].reshape(length, -1)
    rows_of_value = qkv[:, :, width_q + width_k :].reshape(length, -1)
    heads_of_key = rows_of_key.reshape(length, KEY_VALUE_HEADS, HEAD_SIZE)
    heads_of_value = rows_of_value.reshape(length, KEY_VALUE_HEADS, HEAD_SIZE)

    scores, heads_of_query = masked_scores(query_rows, heads_of_key, segments, head_scale)
    row_max = jnp.max(scores, axis=-1, keepdims=True)
    expo_rows = jnp.exp(scores - row_max)
    totals = jnp.sum(expo_rows, axis=-1, keepdims=True)
    soft_probs = expo_rows / totals
    probs_low = soft_probs.astype(jnp.bfloat16)
    attended = (
        jnp.einsum("kgqs,skd->qkgd", probs_low, heads_of_value, preferred_element_type=jnp.float32)
        .reshape(length, -1)
        .astype(jnp.bfloat16)
    )
    hidden = rows_f + dot(attended, full_out)
    factor_two = rms_factor(hidden)
    normed_two = (hidden * factor_two * gain_two).astype(jnp.bfloat16)
    logits = dot(normed_two, full_router)

    named = expert_ids[:, :, None] == jnp.arange(experts, dtype=jnp.int32)[None, None, :]
    chosen = jnp.sum(jnp.where(named, logits[:, None, :], 0.0), axis=2)
    gate_probs = jax.nn.softmax(chosen, axis=1)
    gate_table = jnp.sum(jnp.where(named, gate_probs[:, :, None], 0.0), axis=1)
    gate_table = jnp.where(jnp.any(named, axis=1), gate_table, -1.0)
    plane_normed, plane_gate = spread(normed_two, gate_table.T)
    mine = lax.dynamic_index_in_dim(plane_gate, lax.axis_index("row"), axis=1, keepdims=False)
    routed = mine >= 0.0
    place = jnp.cumsum(routed.astype(jnp.int32), axis=1) - 1
    any_named = jnp.any(named, axis=1)
    before = jnp.cumsum(any_named.astype(jnp.int32), axis=0) - 1
    slot_of = jnp.sum(
        jnp.where(named, before[:, None, :] + jnp.arange(experts, dtype=jnp.int32) * capacity, 0),
        axis=2,
    )
    if on_small_slice():
        in_grad, produced, slot_gate_grad, grad_gu_local, grad_down, back_far = run_expert(
            jnp.where(routed, place, -1), mine, plane_normed, plane_upstream, full_gu, own_down
        )
        grad_gu = lax.psum_scatter(grad_gu_local, "col", scatter_dimension=0, tiled=True)
        lse = (row_max + jnp.log(totals)).reshape(KEY_VALUE_HEADS, 1, QUERY_PER_KEY * length)
        output, d_tokens, sum_q, sum_k, sum_v, sum_out, sum_s = run_backward(
            slot_of, gate_probs, expert_ids, full_router, gains, lse, segments,
            slot_gate_grad, in_grad, back_far, produced, hidden, tokens, cotangent, normed, attended.T, normed_two,
            flat_qkv, full_a, full_out,
        )
        output, d_tokens, sum_q, sum_k, sum_v, sum_out, grad_down, grad_gate, grad_up, own_router, gain_a, gain_e = finish(
            (output, d_tokens, sum_q, sum_k, sum_v, sum_out, grad_down), grad_gu, sum_s, block, piece, router_cols
        )
        return (
            output,
            d_tokens,
            gain_a.reshape(piece),
            sum_q,
            sum_k,
            sum_v,
            sum_out,
            gain_e.reshape(piece),
            own_router.T,
            grad_gate[None],
            grad_up[None],
            grad_down[None],
        )
    else:
        in_grad, produced, slot_gate_grad, grad_gu_local, grad_down = expert_elsewhere(
            place, routed, mine, plane_normed, plane_upstream, full_gu, own_down
        )
    grad_gu = lax.psum_scatter(grad_gu_local, "col", scatter_dimension=0, tiled=True)
    back_grad = lax.all_to_all(
        in_grad.reshape(rows, capacity, model), "row", split_axis=0, concat_axis=0, tiled=True
    ).reshape(experts * capacity, model)
    back_gate_grad = lax.all_to_all(
        slot_gate_grad.reshape(rows, 1, capacity), "row", split_axis=0, concat_axis=0, tiled=True
    ).reshape(experts * capacity)
    produced, back_grad = lax.optimization_barrier((produced, back_grad))
    back_rows = lax.all_to_all(
        produced.reshape(rows, capacity, model), "row", split_axis=0, concat_axis=0, tiled=True
    ).reshape(experts * capacity, model)

    all_slots = jnp.arange(experts * capacity, dtype=jnp.int32)
    is_slot = slot_of.T[:, :, None] == all_slots[None, None, :]
    from_slot = is_slot.astype(jnp.bfloat16)
    gate_grad = jnp.sum(jnp.where(is_slot, back_gate_grad[None, None, :], 0.0), axis=2).T
    returned = [dot(from_slot[k], back_rows) for k in range(TOP)]
    upstream = cotangent.astype(jnp.float32)
    output = (
        hidden + sum(returned[k] * gate_probs[:, k : k + 1] for k in range(TOP))
    ).astype(jnp.bfloat16)
    normed_two_grad = dot(from_slot[0] + from_slot[1], back_grad)
    pair_mean = jnp.sum(gate_probs * gate_grad, axis=1, keepdims=True)
    pair_logit = gate_probs * (gate_grad - pair_mean)
    logit_grad = jnp.sum(jnp.where(named, pair_logit[:, :, None], 0.0), axis=1).astype(jnp.bfloat16)
    grad_router = t_dot(normed_two, logit_grad)
    normed_two_grad = normed_two_grad + dot_t(logit_grad, full_router)
    grad_expert_gain = jnp.sum(normed_two_grad * hidden * factor_two, axis=0)
    scaled_two = normed_two_grad * gain_two
    hidden_grad = (
        upstream
        + factor_two * scaled_two
        - hidden * factor_two**3 * jnp.mean(scaled_two * hidden, axis=1, keepdims=True)
    )
    branch_grad = hidden_grad.astype(jnp.bfloat16)
    grad_out_full = t_dot(attended, branch_grad).astype(jnp.bfloat16)
    attended_grad = dot_t(branch_grad, full_out).astype(jnp.bfloat16)

    gradient_heads = attended_grad.reshape(length, KEY_VALUE_HEADS, QUERY_PER_KEY, HEAD_SIZE)
    value_grad = jnp.einsum(
        "kgqs,qkgd->skd", probs_low, gradient_heads, preferred_element_type=jnp.float32
    )
    prob_grad = jnp.einsum(
        "qkgd,skd->kgqs", gradient_heads, heads_of_value, preferred_element_type=jnp.float32
    )
    delta_sum = jnp.sum(soft_probs * prob_grad, axis=-1, keepdims=True)
    score_grad = (soft_probs * (prob_grad - delta_sum)).astype(jnp.bfloat16)
    query_grad = (
        jnp.einsum("kgqs,skd->qkgd", score_grad, heads_of_key, preferred_element_type=jnp.float32)
        * head_scale
    )
    key_grad = (
        jnp.einsum("kgqs,qkgd->skd", score_grad, heads_of_query, preferred_element_type=jnp.float32)
        * head_scale
    )
    qkv_grad = jnp.concatenate(
        [
            query_grad.astype(jnp.bfloat16).reshape(length, cols, width_q),
            key_grad.astype(jnp.bfloat16).reshape(length, cols, width_k),
            value_grad.astype(jnp.bfloat16).reshape(length, cols, width_k),
        ],
        axis=2,
    ).reshape(length, cols * width_a)
    grad_a_full = t_dot(normed, qkv_grad).astype(jnp.bfloat16)
    normed_grad = dot_t(qkv_grad, full_a)
    grad_attn_gain = jnp.sum(normed_grad * rows_f * factor_one, axis=0)
    scaled_one = normed_grad * gain_one
    d_tokens = (
        hidden_grad
        + factor_one * scaled_one
        - rows_f * factor_one**3 * jnp.mean(scaled_one * rows_f, axis=1, keepdims=True)
    )
    grad_s = jnp.concatenate(
        [
            jnp.pad(
                grad_router.reshape(rows, block, cols, router_cols).transpose(0, 2, 3, 1),
                ((0, 0), (0, 0), (0, 0), (0, lane - block)),
            ),
            jnp.pad(
                jnp.stack([grad_attn_gain, grad_expert_gain])
                .reshape(2, rows, cols, piece)
                .transpose(1, 2, 0, 3),
                ((0, 0), (0, 0), (0, 6 - router_cols), (0, lane - piece)),
            ),
        ],
        axis=2,
    )
    grad_a_full, d_tokens, output = lax.optimization_barrier((grad_a_full, d_tokens, output))
    sum_a, sum_out, sum_s = reduce_all(grad_a_full, grad_out_full, grad_s)
    return (
        output,
        d_tokens,
        sum_s[router_cols, :piece],
        sum_a[:, :width_q],
        sum_a[:, width_q : width_q + width_k],
        sum_a[:, width_q + width_k :],
        sum_out,
        sum_s[router_cols + 1, :piece],
        sum_s[:router_cols, :block].T,
        grad_gu[:, :hidden_units].astype(jnp.float32)[None],
        grad_gu[:, hidden_units:].astype(jnp.float32)[None],
        grad_down[None],
    )


def solution(mesh):
    in_specs = (
        P(("row", "col"), None),
        P(("row", "col")),
        P("row", "col"),
        P("row", "col"),
        P("row", "col"),
        P("row", "col"),
        P(("row", "col")),
        P("row", "col"),
        P("row", "col", None),
        P("row", "col", None),
        P("row", "col", None),
        P(("row", "col"), None),
        P(("row", "col"), None),
        P(("row", "col"), None),
    )
    out_specs = (
        P(("row", "col"), None),
        P(("row", "col"), None),
        P(("row", "col")),
        P("row", "col"),
        P("row", "col"),
        P("row", "col"),
        P("row", "col"),
        P(("row", "col")),
        P("row", "col"),
        P("row", "col", None),
        P("row", "col", None),
        P("row", "col", None),
    )
    return jax.shard_map(
        per_device, mesh=mesh, in_specs=in_specs, out_specs=out_specs, check_vma=False
    )
```

```python
import functools

import jax
import jax.numpy as jnp
from jax import lax
from jax.experimental import pallas as pl
from jax.experimental.pallas import tpu as pltpu
from jax.sharding import PartitionSpec as P

KEY_VALUE_HEADS = 8
HEAD_SIZE = 64
TOP = 2
QUERY_PER_KEY = 3


EPSILON = 1e-05
NEGATIVE = -1e30


MESH = pl.DeviceIdType.MESH
ANY = pl.BlockSpec(memory_space=pl.ANY)


def row_at(row, flip):
    y, x, core = row // 4, (row // 2) % 2, row % 2
    return (
        (y + flip // 4) % 2 * 4 + (x + (flip // 2) % 2) % 2 * 2 + (core + flip % 2) % 2
    )


def remote(source, target, send, receive, device):
    return pltpu.make_async_remote_copy(
        source, target, send, receive, device_id=device, device_id_type=MESH
    )


def greet(row_flips, col_steps):
    row, col = lax.axis_index("row"), lax.axis_index("col")
    sem = pltpu.get_barrier_semaphore()
    for flip in row_flips:
        pl.semaphore_signal(
            sem, inc=1, device_id={"row": row_at(row, flip)}, device_id_type=MESH
        )
    for step in col_steps:
        pl.semaphore_signal(
            sem, inc=1, device_id={"col": (col + step) % 4}, device_id_type=MESH
        )
    pl.semaphore_wait(sem, len(row_flips) + len(col_steps))


def unit_order(col, k):
    table = ((0, 1, 2, 3), (1, 0, 2, 3), (2, 3, 1, 0), (3, 2, 1, 0))
    out = table[3][k]
    for c in (2, 1, 0):
        out = jnp.where(col == c, table[c][k], out)
    return out


def unit_at(col, k):
    end = (col == 0) | (col == 3)
    ends = jnp.where(col == 0, k, 3 - k)
    middle = jnp.where(k == 0, col, jnp.where(k == 3, jnp.where(col == 1, 3, 0), jnp.where(col == 1, 2 * k - 2, 5 - 2 * k)))
    return jnp.where(end, ends, middle)


X, Y, SIB = 2, 4, 1


def plane_send(view, row, ss, rs, source=None):
    source = view(row) if source is None else source
    for i, flip in enumerate((X, Y, SIB)):
        remote(source, view(row), ss(i), rs(i), {"row": row_at(row, flip)}).start()


def plane_forward(view, halves, row, ss, rs):
    first, second = halves
    from_x, from_y = row_at(row, X), row_at(row, Y)
    sib = {"row": row_at(row, SIB)}
    remote(view(from_x), view(from_x), ss(0), rs(0), sib).wait_recv()
    remote(first(from_x), first(from_x), ss(3), rs(3), {"row": from_y}).start()
    remote(view(from_x), view(from_x), ss(5), rs(5), sib).start()
    remote(view(from_y), view(from_y), ss(1), rs(1), sib).wait_recv()
    remote(second(from_y), second(from_y), ss(4), rs(4), {"row": from_x}).start()
    remote(view(from_y), view(from_y), ss(6), rs(6), sib).start()


def plane_last(view, halves, row, ss, rs):
    first, second = halves
    diag = row_at(row, X + Y)
    sib = {"row": row_at(row, SIB)}
    remote(first(diag), first(diag), ss(3), rs(3), sib).wait_recv()
    remote(first(diag), first(diag), ss(7), rs(7), sib).start()
    remote(second(diag), second(diag), ss(4), rs(4), sib).wait_recv()
    remote(second(diag), second(diag), ss(8), rs(8), sib).start()


def plane_finish(view, halves, row, ss, rs):
    first, second = halves
    sib_row = row_at(row, SIB)
    sib = {"row": sib_row}
    whole = view(sib_row)
    remote(whole, whole, ss(2), rs(2), sib).wait_recv()
    for i, flip in ((5, X), (6, Y)):
        block = view(row_at(sib_row, flip))
        remote(block, block, ss(i), rs(i), sib).wait_recv()
    far = row_at(sib_row, X + Y)
    remote(first(far), first(far), ss(7), rs(7), sib).wait_recv()
    remote(second(far), second(far), ss(8), rs(8), sib).wait_recv()
    for i in range(9):
        block = view(row) if i in (0, 1, 2, 5, 6) else (first(row) if i in (3, 7) else second(row))
        remote(block, block, ss(i), rs(i), sib).wait_send()


def pick(ref, cols, halves_rows):
    block, cut = halves_rows

    def at(start, size):
        def view(r):
            rows = pl.ds(pl.multiple_of(r * block + start, 16), size)
            if cols is None:
                return ref.at[rows, :]
            return ref.at[rows, pl.ds(pl.multiple_of(cols[0], 128), cols[1])]

        return view

    return at(0, block), (at(0, cut), at(cut, block - cut))


def through(source, middle, target, sem):
    return pltpu.make_async_copy(source, middle, sem), pltpu.make_async_copy(middle, target, sem)


def through(source, middle, target, sem):
    return pltpu.make_async_copy(source, middle, sem), pltpu.make_async_copy(middle, target, sem)


def line_kernel(own_a, own_b, own_s, own_c, w_gate, w_up, line_a, line_b, full_s, full_c, own_gu, mid_a, mid_b, mid_c, mid_gu,
                zss, zrs, css, crs, s_zs, s_zr, s_ps, s_pr, loc):
    row, col = lax.axis_index("row"), lax.axis_index("col")
    width_a, width_b = own_a.shape[1], own_b.shape[1]
    rows_c = own_c.shape[0]
    vc, hc = pick(full_c, None, (rows_c, rows_c // 2))
    csv, crv = (lambda i: css.at[i]), (lambda i: crs.at[i])

    def of_a(c):
        return line_a.at[:, pl.ds(pl.multiple_of(c * width_a, 128), width_a)]

    def of_b(c):
        return line_b.at[:, pl.ds(pl.multiple_of(c * width_b, 128), width_b)]

    copies = [
        through(own_a, mid_a, of_a(col), loc.at[0]),
        through(own_b, mid_b, of_b(col), loc.at[1]),
        through(own_c, mid_c, vc(row), loc.at[2]),
    ]
    for copy, _ in copies:
        copy.start()
    small_copy = pltpu.make_async_copy(own_s, full_s.at[col, row], loc.at[3])
    small_copy.start()
    units = w_gate.shape[1]
    to_gu = [
        pltpu.make_async_copy(w, mid_gu.at[:, pl.ds(i * units, units)], loc.at[4 + i])
        for i, w in enumerate((w_gate, w_up))
    ]
    from_gu = pltpu.make_async_copy(mid_gu, own_gu, loc.at[6])
    greet(range(1, 8), (1, 2, 3))

    def along(i, c, source, target, right, left):
        for d, (cond, step) in enumerate(((right, 1), (left, 3))):
            @pl.when(cond)
            def _():
                remote(source, target, zss.at[i, c, d], zrs.at[i, c], {"col": (col + step) % 4}).start()

    def arrived(k):
        c = unit_order(col, k)
        for i, view in enumerate((of_a(c), of_b(c))):
            remote(view, view, zss.at[i, c, 0], zrs.at[i, c], {"col": (col + 1) % 4}).wait_recv()
            along(i, c, view, view, (c < col) & (col < 3), (c > col) & (col > 0))

    along(0, col, own_a, of_a(col), col < 3, col > 0)
    along(1, col, own_b, of_b(col), col < 3, col > 0)
    for i, step in enumerate((1, 2, 3)):
        remote(own_s, full_s.at[col, row], s_zs.at[i], s_zr.at[i], {"col": (col + step) % 4}).start()
    plane_send(vc, row, csv, crv, own_c)
    for copy in to_gu:
        copy.start()
    for first, second in copies:
        first.wait()
        second.start()
    small_copy.wait()
    for copy in to_gu:
        copy.wait()
    from_gu.start()
    arrived(1)
    for i, step in enumerate((3, 2, 1)):
        remote(own_s, full_s.at[(col + step) % 4, row], s_zs.at[i], s_zr.at[i], {"col": (col + 1) % 4}).wait()
    for i in range(1, 8):
        remote(full_s.at[:, row], full_s.at[:, row], s_ps.at[i - 1], s_pr.at[i - 1], {"row": row_at(row, i)}).start()
    arrived(2)
    plane_forward(vc, hc, row, csv, crv)
    arrived(3)
    plane_last(vc, hc, row, csv, crv)
    for _, second in copies:
        second.wait()
    from_gu.wait()
    plane_finish(vc, hc, row, csv, crv)
    for i in range(1, 8):
        there = row_at(row, i)
        remote(full_s.at[:, there], full_s.at[:, there], s_ps.at[i - 1], s_pr.at[i - 1], {"row": there}).wait()
    for k in range(4):
        c = unit_order(col, k)
        right = (c <= col) & (col < 3)
        left = (c >= col) & (col > 0)
        for d, cond in enumerate((right, left)):
            @pl.when(cond)
            def _():
                there = {"col": (col + 1) % 4}
                remote(of_a(c), of_a(c), zss.at[0, c, d], zrs.at[0, c], there).wait_send()
                remote(of_b(c), of_b(c), zss.at[1, c, d], zrs.at[1, c], there).wait_send()


def gather_line(own_a, own_b, own_s, own_c, w_gate, w_up):
    sems = pltpu.SemaphoreType.DMA
    rows_c = own_c.shape[0]
    return pl.pallas_call(
        line_kernel,
        out_shape=(
            jax.ShapeDtypeStruct((own_a.shape[0], own_a.shape[1] * 4), own_a.dtype),
            jax.ShapeDtypeStruct((own_b.shape[0], own_b.shape[1] * 4), own_b.dtype),
            jax.ShapeDtypeStruct((4, 8) + own_s.shape, own_s.dtype),
            jax.ShapeDtypeStruct((8 * rows_c, own_c.shape[1]), own_c.dtype),
            jax.ShapeDtypeStruct((w_gate.shape[0], 2 * w_gate.shape[1]), w_gate.dtype),
        ),
        in_specs=[ANY] * 6,
        out_specs=(ANY,) * 5,
        scratch_shapes=[
            pltpu.VMEM(own_a.shape, own_a.dtype),
            pltpu.VMEM(own_b.shape, own_b.dtype),
            pltpu.VMEM(own_c.shape, own_c.dtype),
            pltpu.VMEM((w_gate.shape[0], 2 * w_gate.shape[1]), w_gate.dtype),
            sems((2, 4, 2)), sems((2, 4)),
            sems((9,)), sems((9,)),
            sems((3,)), sems((3,)), sems((7,)), sems((7,)), sems((7,)),
        ],
        compiler_params=pltpu.CompilerParams(collective_id=0, has_side_effects=True),
        cost_estimate=pl.CostEstimate(flops=0, bytes_accessed=1_000_000, transcendentals=0),
    )(own_a, own_b, own_s, own_c, w_gate, w_up)


def plane_kernel(count, *refs):
    row = lax.axis_index("row")
    owns, fulls, mids = refs[:count], refs[count : 2 * count], refs[2 * count : 3 * count]
    ss, rs, loc = refs[3 * count :]
    views, copies = [], []
    for i in range(count):
        block = owns[i].shape[0]
        views.append(pick(fulls[i], None, (block, block // 2)))
        copies.append(through(owns[i], mids[i], views[i][0](row), loc.at[i]))
        copies[i][0].start()
    greet(range(1, 8), ())

    def sems_of(i):
        return (lambda j: ss.at[i, j]), (lambda j: rs.at[i, j])

    for i in range(count):
        plane_send(views[i][0], row, *sems_of(i), owns[i])
    for first, second in copies:
        first.wait()
        second.start()
    for i in range(count):
        plane_forward(*views[i], row, *sems_of(i))
    for i in range(count):
        plane_last(*views[i], row, *sems_of(i))
    for _, second in copies:
        second.wait()
    for i in range(count):
        plane_finish(*views[i], row, *sems_of(i))


def gather_plane(collective, owns):
    sems = pltpu.SemaphoreType.DMA
    count = len(owns)
    return pl.pallas_call(
        functools.partial(plane_kernel, count),
        out_shape=tuple(
            jax.ShapeDtypeStruct((8 * own.shape[0], own.shape[1]), own.dtype) for own in owns
        ),
        in_specs=[ANY] * count,
        out_specs=(ANY,) * count,
        scratch_shapes=[pltpu.VMEM(own.shape, own.dtype) for own in owns]
        + [sems((count, 9)), sems((count, 9)), sems((count,))],
        compiler_params=pltpu.CompilerParams(collective_id=collective, has_side_effects=True),
        cost_estimate=pl.CostEstimate(flops=0, bytes_accessed=1_000_000, transcendentals=0),
    )(*owns)


def spread_kernel(own_c, own_g, full_c, full_g, mid_c, css, crs, gss, grs, loc):
    row = lax.axis_index("row")
    rows_c = own_c.shape[0]
    vc, hc = pick(full_c, None, (rows_c, rows_c // 2))
    csv, crv = (lambda i: css.at[i]), (lambda i: crs.at[i])
    first, second = through(own_c, mid_c, vc(row), loc.at[0])
    first.start()
    own_copy = pltpu.make_async_copy(own_g, full_g.at[row], loc.at[1])
    own_copy.start()
    greet(range(1, 8), ())
    plane_send(vc, row, csv, crv, own_c)
    for i in range(1, 8):
        remote(own_g, full_g.at[row], gss.at[i - 1], grs.at[i - 1], {"row": row_at(row, i)}).start()
    first.wait()
    second.start()
    plane_forward(vc, hc, row, csv, crv)
    plane_last(vc, hc, row, csv, crv)
    second.wait()
    own_copy.wait()
    plane_finish(vc, hc, row, csv, crv)
    for i in range(1, 8):
        there = row_at(row, i)
        remote(own_g, full_g.at[there], gss.at[i - 1], grs.at[i - 1], {"row": there}).wait()


def spread_tokens(own_c, own_g):
    sems = pltpu.SemaphoreType.DMA
    return pl.pallas_call(
        spread_kernel,
        out_shape=(
            jax.ShapeDtypeStruct((8 * own_c.shape[0], own_c.shape[1]), own_c.dtype),
            jax.ShapeDtypeStruct((8,) + own_g.shape, own_g.dtype),
        ),
        in_specs=[ANY] * 2,
        out_specs=(ANY,) * 2,
        scratch_shapes=[
            pltpu.VMEM(own_c.shape, own_c.dtype),
            sems((9,)), sems((9,)), sems((7,)), sems((7,)), sems((2,)),
        ],
        compiler_params=pltpu.CompilerParams(collective_id=1, has_side_effects=True),
        cost_estimate=pl.CostEstimate(flops=0, bytes_accessed=1_000_000, transcendentals=0),
    )(own_c, own_g)


def add_into(target, term):
    def body(i, carry):
        rows = pl.ds(pl.multiple_of(i * 32, 32), 32)
        total = target[rows, :].astype(jnp.float32) + term[rows, :].astype(jnp.float32)
        target[rows, :] = total.astype(target.dtype)
        return carry
    lax.fori_loop(0, target.shape[0] // 32, body, 0)


def finish_kernel(count, experts, block, piece, *refs):
    for source, target in zip(refs[:count], refs[count + 2 : 2 * count + 2]):
        target[...] = source[...]
    gu, sums = refs[count : count + 2]
    gate, up, router, gain_a, gain_e, turned = refs[2 * count + 2 :]
    gate[...] = gu[:, : gate.shape[1]].astype(gate.dtype)
    up[...] = gu[:, gate.shape[1] :].astype(up.dtype)

    @pl.when(pl.program_id(0) == 0)
    def _():
        core, col = lax.axis_index("row") % 2, lax.axis_index("col")
        turned[...] = sums[...].T
        mine = turned[pl.ds(pl.multiple_of(core * block, 8), block), :].T
        rows = lax.broadcasted_iota(jnp.int32, mine.shape, 0)
        for j in range(router.shape[0]):
            at = col * router.shape[0] + j
            router[j : j + 1, :] = jnp.sum(jnp.where(rows == at, mine, 0.0), axis=0, keepdims=True)
        own = turned[pl.ds(pl.multiple_of(core * block + col * piece, 8), piece), :].T
        gain_a[...] = own[experts : experts + 1, :]
        gain_e[...] = own[experts + 1 : experts + 2, :]


def finish(arrays, grad_gu, sums, block, piece, router_cols):
    steps = 2
    experts = router_cols * 4

    def spec(a):
        return pl.BlockSpec((a.shape[0] // steps, a.shape[1]), lambda i: (i, 0))

    def once(a):
        return pl.BlockSpec(a.shape, lambda i: (0, 0))

    f32 = jnp.float32
    half = jax.ShapeDtypeStruct((grad_gu.shape[0], grad_gu.shape[1] // 2), f32)
    small = [jax.ShapeDtypeStruct(shape, f32) for shape in ((router_cols, block), (1, piece), (1, piece))]
    return pl.pallas_call(
        functools.partial(finish_kernel, len(arrays), experts, block, piece),
        grid=(steps,),
        out_shape=(*(jax.ShapeDtypeStruct(a.shape, a.dtype) for a in arrays), half, half, *small),
        in_specs=[*(spec(a) for a in arrays), spec(grad_gu), once(sums)],
        out_specs=(*(spec(a) for a in arrays), spec(half), spec(half), *(once(a) for a in small)),
        scratch_shapes=[pltpu.VMEM((sums.shape[1], sums.shape[0]), f32)],
    )(*arrays, grad_gu, sums)


def expert_kernel(key, mine, normed_hbm, upstream_hbm, gu_hbm, own_down,
                  in_out, prod_out, gate_grad_out, grad_gu, sum_down, back_far,
                  in_ref, prod_ref, gate_grad_ref, x_t, ups, gu, down, act, silu, slope, both, gd, rec_right, rec_left, stage, gate,
                  load_sem, src_sem, stage_sem, zss, zrs, rss, rrs, fss, frs, in_sem, prod_sem):
    row, col = lax.axis_index("row"), lax.axis_index("col")
    sources, _, length = key.shape
    slots = in_ref.shape[0]
    capacity = slots // sources
    units = gu.shape[1] // 2
    width = units // 4
    chunk = 512
    x = in_ref
    right_dev, left_dev = {"col": (col + 1) % 4}, {"col": (col + 3) % 4}

    load_gu = pltpu.make_async_copy(gu_hbm, gu, load_sem.at[0])
    load_gu.start()
    load_down = pltpu.make_async_copy(own_down, down.at[col], load_sem.at[1])
    load_down.start()

    def fetch(s, slot):
        rows = pl.ds(pl.multiple_of(s * length, 16), length)
        for i, hbm in enumerate((normed_hbm, upstream_hbm)):
            to = prod_ref.at[pl.ds(pl.multiple_of((slot * 2 + i) * length, 16), length), :]
            yield pltpu.make_async_copy(hbm.at[rows, :], to, src_sem.at[slot, i])

    for copy in fetch(0, 0):
        copy.start()
    greet((X + Y, X + Y + SIB), (1, 2, 3))

    def pass_on(c, source, right, left):
        for d, (cond, there) in enumerate(((right, right_dev), (left, left_dev))):
            @pl.when(cond)
            def _():
                remote(source, down.at[c], zss.at[c, d], zrs.at[c], there).start()

    pass_on(col, own_down, col < 3, col > 0)

    def ag_step(s):
        @pl.when(col >= s)
        def _():
            c = col - s
            remote(down.at[c], down.at[c], zss.at[c, 0], zrs.at[c], right_dev).wait_recv()
            @pl.when(col < 3)
            def _():
                remote(down.at[c], down.at[c], zss.at[c, 0], zrs.at[c], right_dev).start()
        @pl.when(col + s < 4)
        def _():
            c = col + s
            remote(down.at[c], down.at[c], zss.at[c, 1], zrs.at[c], left_dev).wait_recv()
            @pl.when(col > 0)
            def _():
                remote(down.at[c], down.at[c], zss.at[c, 1], zrs.at[c], left_dev).start()

    def to_right(d):
        target = rec_right.at[d - 1]
        return remote(target, target, rss.at[0, d - 1], rrs.at[0, d - 1], right_dev)

    def to_left(d):
        target = rec_left.at[d]
        return remote(target, target, rss.at[1, d], rrs.at[1, d], left_dev)

    def from_end(d):
        @pl.when((col == 0) & (d > 0))
        def _():
            remote(gd.at[d], rec_right.at[d - 1], rss.at[0, d - 1], rrs.at[0, d - 1], right_dev).start()
        @pl.when((col == 3) & (d < 3))
        def _():
            remote(gd.at[d], rec_left.at[d], rss.at[1, d], rrs.at[1, d], left_dev).start()

    def add_rows(target, term):
        def body(i, carry):
            rows = pl.ds(pl.multiple_of(i * 64, 64), 64)
            total = target[rows, :].astype(jnp.float32) + term[rows, :].astype(jnp.float32)
            target[rows, :] = total.astype(target.dtype)
            return carry
        lax.fori_loop(0, width // 64, body, 0)

    def hop_right(d):
        to_right(d).wait_recv()
        add_rows(rec_right.at[d - 1], gd.at[d])
        to_right(d).start()

    def hop_left(d):
        to_left(d).wait_recv()
        add_rows(rec_left.at[d], gd.at[d])
        to_left(d).start()

    def select(s, carry):
        slot = s % 2
        @pl.when(s + 1 < sources)
        def _():
            for copy in fetch(s + 1, 1 - slot):
                copy.start()
        for copy in fetch(s, slot):
            copy.wait()
        chosen = key[s] == lax.broadcasted_iota(jnp.int32, (capacity, length), 0)
        value = jnp.sum(jnp.where(chosen, mine[s], 0.0), axis=1, keepdims=True)
        rows = pl.ds(pl.multiple_of(s * capacity, 16), capacity)
        gate[rows, :] = jnp.broadcast_to(value, (capacity, gate.shape[1]))
        one_hot = jnp.where(chosen, 1.0, 0.0).astype(x.dtype)
        for i, target in enumerate((x, ups)):
            block = prod_ref[pl.ds(pl.multiple_of((slot * 2 + i) * length, 16), length), :]
            target[rows, :] = dot(one_hot, block).astype(target.dtype)
        return carry
    lax.fori_loop(0, sources, select, 0)

    load_gu.wait()

    def forward(c):
        first = pl.ds(pl.multiple_of(c * width, width), width)
        second = pl.ds(pl.multiple_of(units + c * width, width), width)
        def body(m, carry):
            rows = pl.ds(pl.multiple_of(m * chunk, chunk), chunk)
            gate_pre = dot(x[rows, :], gu[:, first])
            up_pre = dot(x[rows, :], gu[:, second])
            sigma = jax.nn.sigmoid(gate_pre)
            silu_gate = gate_pre * sigma
            silu[rows, first] = silu_gate
            slope[rows, first] = up_pre * sigma * (1.0 + gate_pre * (1.0 - sigma))
            low = (silu_gate * up_pre).astype(act.dtype)
            act[rows, first] = low
            both[rows, first] = (low.astype(jnp.float32) * gate[rows, 0:1]).astype(both.dtype)
            return carry
        lax.fori_loop(0, slots // chunk, body, 0)
        gd[c] = t_dot(both[:, first], ups[...]).astype(gd.dtype)

    def forward_step(i, carry):
        c = jnp.where(i < 2, 3 - 3 * i, 4 - i)
        forward(c)
        pl.when((i < 2) | (col == 0))(lambda: from_end(c))
        pl.when(i == 1)(lambda: ag_step(1))
        @pl.when((i == 3) & (col == 3))
        def _():
            from_end(1)
            from_end(2)
        return carry
    lax.fori_loop(0, 4, forward_step, 0)
    load_down.wait()

    def turn(m, carry):
        rows = pl.ds(pl.multiple_of(m * chunk, chunk), chunk)
        x_t[:, rows] = x[rows, :].T
        return carry
    lax.fori_loop(0, slots // chunk, turn, 0)
    gate_grad_ref[...] = jnp.zeros_like(gate_grad_ref)

    def out_stage(c, slot):
        for i in range(2):
            yield pltpu.make_async_copy(
                stage.at[slot, :, pl.ds(i * width, width)],
                grad_gu.at[:, pl.ds(pl.multiple_of(i * units + c * width, width), width)],
                stage_sem.at[slot, i],
            )

    def far(j):
        there = row_at(row, X + Y + j)
        rows = pl.ds(pl.multiple_of(there * capacity, 16), capacity)
        return remote(in_ref.at[rows, :], back_far.at[j], fss.at[j], frs.at[j], {"row": there})

    def of_chip(i):
        chip = row_at(row, 2 * (3 - i)) // 2
        rows = pl.ds(pl.multiple_of(chip * 2 * capacity, 16), 2 * capacity)
        return rows, pltpu.make_async_copy(in_ref.at[rows, :], in_out.at[rows, :], in_sem.at[i])

    def inputs(i, carry):
        rows, copy = of_chip(i)
        in_ref[rows, :] = dot_t(both[rows, :], gu[...]).astype(in_ref.dtype)
        copy.start()
        return carry

    def backward(k):
        c = unit_at(col, k)
        first = pl.ds(pl.multiple_of(c * width, width), width)
        second = pl.ds(pl.multiple_of(units + c * width, width), width)
        def body(m, carry):
            rows = pl.ds(pl.multiple_of(m * chunk, chunk), chunk)
            plain = dot_t(ups[rows, :], down[c])
            term = jnp.sum(act[rows, first].astype(jnp.float32) * plain, axis=1, keepdims=True)
            gate_grad_ref[rows, :] += jnp.broadcast_to(term, (chunk, gate_grad_ref.shape[1]))
            act_grad = plain * gate[rows, 0:1]
            both[rows, first] = (act_grad * slope[rows, first]).astype(both.dtype)
            both[rows, second] = (act_grad * silu[rows, first]).astype(both.dtype)
            return carry
        lax.fori_loop(0, slots // chunk, body, 0)
        @pl.when(k == 3)
        def _():
            inputs(0, 0)
            far(0).start()
            far(1).start()
        slot = k % 2
        @pl.when(k >= 2)
        def _():
            for copy in out_stage(unit_at(col, k - 2), slot):
                copy.wait()
        def grads(i, carry):
            rows = pl.ds(pl.multiple_of(i * chunk, chunk), chunk)
            stage[slot, rows, 0:width] = dot(x_t[rows, :], both[:, first]).astype(stage.dtype)
            stage[slot, rows, width : 2 * width] = dot(x_t[rows, :], both[:, second]).astype(stage.dtype)
            return carry
        lax.fori_loop(0, x_t.shape[0] // chunk, grads, 0)
        for copy in out_stage(c, slot):
            copy.start()

    def backward_step(k, carry):
        backward(k)
        pl.when(k == 0)(lambda: ag_step(2))
        pl.when((k == 0) & (col == 1))(lambda: hop_right(3))
        pl.when((k == 0) & (col == 2))(lambda: hop_left(0))
        pl.when(k == 2)(lambda: ag_step(3))
        @pl.when((k == 2) & (col == 1))
        def _():
            hop_right(2)
            hop_left(0)
        @pl.when((k == 2) & (col == 2))
        def _():
            hop_right(3)
            hop_left(1)
        return carry
    lax.fori_loop(0, 4, backward_step, 0)

    lax.fori_loop(1, sources // 2, inputs, 0)

    def outputs(m, carry):
        rows = pl.ds(pl.multiple_of(m * chunk, chunk), chunk)
        total = dot(act[rows, 0:width], down[0])
        for c in range(1, 4):
            total = total + dot(act[rows, c * width : (c + 1) * width], down[c])
        prod_ref[rows, :] = total.astype(prod_ref.dtype)
        pltpu.make_async_copy(prod_ref.at[rows, :], prod_out.at[rows, :], prod_sem.at[m]).start()
        return carry
    lax.fori_loop(0, slots // chunk, outputs, 0)

    turned = gate_grad_ref[...].T
    for s in range(sources):
        gate_grad_out[s] = turned[0:1, s * capacity : (s + 1) * capacity]
    for k in (2, 3):
        for copy in out_stage(unit_at(col, k), k % 2):
            copy.wait()
    pl.when(col > 0)(lambda: to_right(col).wait_recv())
    pl.when(col < 3)(lambda: to_left(col).wait_recv())

    def to_sum(i, carry):
        rows = pl.ds(pl.multiple_of(i * 64, 64), 64)
        sum_down[rows, :] = gd[col, rows, :].astype(jnp.float32)
        @pl.when(col > 0)
        def _():
            sum_down[rows, :] += rec_right[jnp.maximum(col - 1, 0), rows, :].astype(jnp.float32)
        @pl.when(col < 3)
        def _():
            sum_down[rows, :] += rec_left[jnp.minimum(col, 2), rows, :].astype(jnp.float32)
        return carry
    lax.fori_loop(0, width // 64, to_sum, 0)

    def sent(e, carry):
        pl.when(e > col)(lambda: to_right(e).wait_send())
        pl.when(e < col)(lambda: to_left(e).wait_send())
        @pl.when((col < 3) & (e <= col))
        def _():
            remote(down.at[e], down.at[e], zss.at[e, 0], zrs.at[e], right_dev).wait_send()
        @pl.when((col > 0) & (e >= col))
        def _():
            remote(down.at[e], down.at[e], zss.at[e, 1], zrs.at[e], left_dev).wait_send()
        return carry
    lax.fori_loop(0, 4, sent, 0)
    for j in range(2):
        far(j).wait()

    def written(i, carry):
        of_chip(i)[1].wait()
        return carry
    lax.fori_loop(0, 4, written, 0)

    def produced(m, carry):
        rows = pl.ds(pl.multiple_of(m * chunk, chunk), chunk)
        pltpu.make_async_copy(prod_ref.at[rows, :], prod_out.at[rows, :], prod_sem.at[m]).wait()
        return carry
    lax.fori_loop(0, slots // chunk, produced, 0)


def run_expert(key, mine, normed, upstream, full_gu, own_down):
    sources, length = key.shape
    model, units = full_gu.shape[0], full_gu.shape[1] // 2
    width = own_down.shape[0]
    slots = sources * length // 2
    low, f32 = normed.dtype, jnp.float32
    sems = pltpu.SemaphoreType.DMA
    vm = pl.BlockSpec(memory_space=pltpu.VMEM)
    return pl.pallas_call(
        expert_kernel,
        out_shape=(
            jax.ShapeDtypeStruct((slots, model), low),
            jax.ShapeDtypeStruct((slots, model), low),
            jax.ShapeDtypeStruct((sources, 1, slots // sources), f32),
            jax.ShapeDtypeStruct((model, 2 * units), low),
            jax.ShapeDtypeStruct((width, model), f32),
            jax.ShapeDtypeStruct((2, slots // sources, model), low),
        ),
        in_specs=[vm, vm, ANY, ANY, ANY, ANY],
        out_specs=(ANY, ANY, vm, ANY, vm, ANY),
        scratch_shapes=[
            pltpu.VMEM((slots, model), low),
            pltpu.VMEM((slots, model), low),
            pltpu.VMEM((slots, 128), f32),
            pltpu.VMEM((model, slots), low),
            pltpu.VMEM((slots, model), low),
            pltpu.VMEM((model, 2 * units), low),
            pltpu.VMEM((4, width, model), low),
            pltpu.VMEM((slots, units), low),
            pltpu.VMEM((slots, units), f32),
            pltpu.VMEM((slots, units), f32),
            pltpu.VMEM((slots, 2 * units), low),
            pltpu.VMEM((4, width, model), low),
            pltpu.VMEM((3, width, model), low),
            pltpu.VMEM((3, width, model), low),
            pltpu.VMEM((2, model, 2 * width), low),
            pltpu.VMEM((slots, 128), f32),
            sems((2,)), sems((2, 2)), sems((2, 2)),
            sems((4, 2)), sems((4,)), sems((2, 3)), sems((2, 3)), sems((2,)), sems((2,)), sems((4,)), sems((4,)),
        ],
        compiler_params=pltpu.CompilerParams(
            collective_id=4, has_side_effects=True, vmem_limit_bytes=60 * 2**20
        ),
        cost_estimate=pl.CostEstimate(flops=0, bytes_accessed=1_000_000, transcendentals=0),
    )(key.reshape(sources, 1, length), mine.reshape(sources, 1, length), normed, upstream, full_gu, own_down)


def backward_kernel(table, router_p, gains, lse,
                    gate_grad, in_grad, back_far, produced, hidden_hbm, tokens_hbm, cot_hbm, normed_hbm, attended_hbm,
                    two_hbm, qkv_hbm, full_a_hbm, full_out_hbm,
                    out_hbm, d_hbm, sum_q, sum_k, sum_v, sum_b, sum_s,
                    out_ref, d_tokens, cols, rec_in, rec_gate, rec_prod, hidden, tokens, cot, two, qkv, full_a, full_out,
                    n_t, a_t, branch, bias, out_rows, grad_c, qg, lgs, small,
                    own, sib_out, rec_sib, rec_one, rec_two, rec_z, s_rec, s_mid, s_zrec,
                    load, in_ss, in_rs, g_ss, g_rs, pr_ss, pr_rs, loc, far_sem, write,
                    ss1, rs1, ss2, rs2, zss, zrs, s_ss, s_rs, sz_ss, sz_rs):
    row, col = lax.axis_index("row"), lax.axis_index("col")
    core = row % 2
    chip = row // 2
    cy, cx = chip // 2, chip % 2
    length, model = hidden.shape
    capacity = rec_in.shape[0] // 8
    block = own.shape[2]
    width_b = sum_b.shape[1]
    width_a = own.shape[3] - width_b
    cut = block // 2
    half = length
    f32, low = jnp.float32, branch.dtype
    sib = {"row": row_at(row, SIB)}
    to_x, to_y = {"row": row_at(row, X)}, {"row": row_at(row, Y)}

    def each_flip(function):
        def body(i, carry):
            function(7 - i)
            return carry
        lax.fori_loop(0, 7, body, 0)

    def block_of(r):
        return pl.ds(pl.multiple_of(r * capacity, 16), capacity)

    own_in = pltpu.make_async_copy(in_grad.at[block_of(row), :], rec_in.at[block_of(row), :], loc.at[0])
    own_gate = pltpu.make_async_copy(gate_grad.at[row], rec_gate.at[row], loc.at[1])
    own_prod = pltpu.make_async_copy(produced.at[block_of(row), :], rec_prod.at[block_of(row), :], loc.at[2])
    loads = [
        pltpu.make_async_copy(source, target, load.at[i])
        for i, (source, target) in enumerate((
            (normed_hbm, branch), (attended_hbm, a_t), (hidden_hbm, hidden), (cot_hbm, cot), (two_hbm, two),
            (qkv_hbm, qkv), (tokens_hbm, tokens), (full_out_hbm, full_out), (full_a_hbm, full_a),
        ))
    ]
    greet(range(1, 8), (1, 2, 3))

    far_in = [
        pltpu.make_async_copy(back_far.at[j], rec_in.at[block_of(row_at(row, X + Y + j)), :], far_sem.at[j])
        for j in range(2)
    ]

    def back(flip):
        there = row_at(row, flip)
        return remote(in_grad.at[block_of(there), :], rec_in.at[block_of(row), :],
                      in_ss.at[flip - 1], in_rs.at[flip - 1], {"row": there})

    def back_gate(flip):
        there = row_at(row, flip)
        return remote(gate_grad.at[there], rec_gate.at[row], g_ss.at[flip - 1], g_rs.at[flip - 1], {"row": there})

    def each_near(function):
        def body(i, carry):
            function(5 - i)
            return carry
        lax.fori_loop(0, 5, body, 0)

    def back_prod(flip):
        there = row_at(row, flip)
        return remote(produced.at[block_of(there), :], rec_prod.at[block_of(row), :],
                      pr_ss.at[flip - 1], pr_rs.at[flip - 1], {"row": there})

    each_near(lambda flip: back(flip).start())
    each_flip(lambda flip: back_gate(flip).start())
    for copy in (own_in, own_gate, own_prod, *far_in):
        copy.start()
    cols[...] = table[...].T
    for copy in loads:
        copy.start()
    loads[0].wait()
    n_t[...] = branch[...].T
    key_pos = lax.broadcasted_iota(jnp.int32, (length, length), 0)
    query_pos = lax.broadcasted_iota(jnp.int32, (length, length), 1)
    allowed = (key_pos <= query_pos) & (cols[:, 6:7] == table[6:7, :])
    bias[...] = jnp.where(allowed, 0.0, NEGATIVE)
    small[...] = jnp.zeros_like(small)
    for copy in loads[1:]:
        copy.wait()
    for copy in (own_in, own_gate, *far_in):
        copy.wait()
    each_flip(lambda flip: back_gate(flip).wait_recv())
    each_near(lambda flip: back(flip).wait_recv())

    all_gate = jnp.concatenate([rec_gate[e] for e in range(8)], axis=1)
    wide = rec_in.shape[0]
    lanes = lgs.shape[1]

    def at_slot(rows, k):
        return cols[rows, k : k + 1] == lax.broadcasted_iota(jnp.int32, (half, wide), 1).astype(f32)

    def to_hidden(m, carry):
        rows = pl.ds(pl.multiple_of(m * half, half), half)
        first, second = at_slot(rows, 0), at_slot(rows, 1)
        picked = jnp.where(first | second, 1.0, 0.0).astype(low)
        two_grad = dot(picked, rec_in[...])
        grad_0 = jnp.sum(jnp.where(first, all_gate, 0.0), axis=1, keepdims=True)
        grad_1 = jnp.sum(jnp.where(second, all_gate, 0.0), axis=1, keepdims=True)
        gate_0, gate_1 = cols[rows, 4:5], cols[rows, 5:6]
        mean = gate_0 * grad_0 + gate_1 * grad_1
        lane = lax.broadcasted_iota(jnp.int32, (half, lanes), 1).astype(f32)
        logit_grad = jnp.where(lane == cols[rows, 2:3], gate_0 * (grad_0 - mean), 0.0)
        logit_grad = logit_grad + jnp.where(lane == cols[rows, 3:4], gate_1 * (grad_1 - mean), 0.0)
        logit_grad = logit_grad.astype(low)
        lgs[rows, :] = logit_grad
        two_grad = two_grad + dot_t(logit_grad, router_p[...])
        h = hidden[rows, :]
        factor = lax.rsqrt(jnp.mean(h * h, axis=1, keepdims=True) + EPSILON)
        small[9:10, :] += jnp.sum(two_grad * h * factor, axis=0, keepdims=True)
        scaled = two_grad * gains[1:2, :]
        inner = jnp.mean(scaled * h, axis=1, keepdims=True)
        grad = cot[rows, :].astype(f32) + factor * scaled - h * (factor * factor * factor * inner)
        d_tokens[rows, :] = grad
        branch[rows, :] = grad.astype(low)
        return carry
    lax.fori_loop(0, 1, to_hidden, 0)
    small[0:8, :] = t_dot(lgs[...], two[...])[0:8, :]

    def nth(k):
        return (col + 1 + k) % 4

    lanes_of = {"a": pl.ds(0, width_a), "b": pl.ds(width_a, width_b)}
    part_at = {"a": 0, "b": 1}

    def to_sibling(part, c, q):
        view = lanes_of[part]
        i = part_at[part]
        return remote(sib_out.at[c, q, :, view], rec_sib.at[c, q, :, view], ss1.at[c, q, i], rs1.at[c, q, i], sib)

    def weight_grads(part, c, left, right):
        view = lanes_of[part]
        def body(q, carry):
            theirs = pl.ds(pl.multiple_of((q * 2 + 1 - core) * block, 16), block)
            sib_out[c, q, :, view] = dot(left[theirs, :], right()).astype(low)
            to_sibling(part, c, q).start()
            mine = pl.ds(pl.multiple_of((q * 2 + core) * block, 16), block)
            own[c, q, :, view] = dot(left[mine, :], right()).astype(low)
            return carry
        lax.fori_loop(0, 4, body, 0)

    def cols_b(c):
        return pl.ds(pl.multiple_of(c * width_b, 128), width_b)

    def attend_back(c):
        span_c = width_b // QUERY_PER_KEY
        for i in range(QUERY_PER_KEY):
            for u in range(2):
                rows = pl.ds(pl.multiple_of(c * width_b + (u * QUERY_PER_KEY + i) * HEAD_SIZE, HEAD_SIZE), HEAD_SIZE)
                out_rows[(2 * i + u) * HEAD_SIZE : (2 * i + u + 1) * HEAD_SIZE, :] = full_out[rows, :]
        grad_c[...] = dot_t(branch[...], out_rows[...]).astype(low)
        at_c = pl.multiple_of(c * width_a, 128)
        key = qkv[:, pl.ds(at_c + width_b, span_c)]
        value = qkv[:, pl.ds(at_c + width_b + span_c, span_c)]
        first = lax.broadcasted_iota(jnp.int32, (length, span_c), 1) < HEAD_SIZE
        none = jnp.zeros_like(key)
        keys = (jnp.where(first, key, none), jnp.where(first, none, key))
        values = (jnp.where(first, value, none), jnp.where(first, none, value))
        scale = HEAD_SIZE ** (-0.5)
        key_grads = [jnp.zeros((length, span_c), f32) for _ in range(2)]
        value_grads = [jnp.zeros((length, span_c), f32) for _ in range(2)]
        for i in range(QUERY_PER_KEY):
            q_i = qkv[:, pl.ds(at_c + i * span_c, span_c)]
            g_i = grad_c[:, i * span_c : (i + 1) * span_c]
            q_grad = jnp.zeros((length, span_c), f32)
            for u in range(2):
                log_total = lse[c * 2 + u, :, i * length : (i + 1) * length]
                probs = jnp.exp(dot_t(keys[u], q_i) * scale + bias[...] - log_total)
                prob_grad = dot_t(values[u], g_i)
                delta = jnp.sum(probs * prob_grad, axis=0, keepdims=True)
                score_grad = (probs * (prob_grad - delta)).astype(low)
                value_grads[u] += dot(probs.astype(low), g_i)
                key_grads[u] += dot(score_grad, q_i)
                q_grad += t_dot(score_grad, keys[u])
            qg[c, :, i * span_c : (i + 1) * span_c] = (q_grad * scale).astype(low)
        key_grad = jnp.where(first, key_grads[0], key_grads[1]) * scale
        qg[c, :, width_b : width_b + span_c] = key_grad.astype(low)
        qg[c, :, width_b + span_c : width_a] = jnp.where(first, value_grads[0], value_grads[1]).astype(low)

    top, bottom = pl.ds(0, cut), pl.ds(cut, block - cut)

    def one(part, c):
        view, i = lanes_of[part], part_at[part]
        for j in range(2):
            yield remote(own.at[c, j * 2 + 1 - cx, top, view], rec_one.at[c, 0, j, :, view],
                         ss2.at[c, i, 0, j], rs2.at[c, i, 0, j], to_x)
            yield remote(own.at[c, (1 - cy) * 2 + j, bottom, view], rec_one.at[c, 1, j, :, view],
                         ss2.at[c, i, 1, j], rs2.at[c, i, 1, j], to_y)

    def two_step(part, c):
        view, i = lanes_of[part], part_at[part]
        yield remote(own.at[c, (1 - cy) * 2 + cx, top, view], rec_two.at[c, 0, :, view],
                     ss2.at[c, i, 0, 2], rs2.at[c, i, 0, 2], to_y)
        yield remote(own.at[c, cy * 2 + 1 - cx, bottom, view], rec_two.at[c, 1, :, view],
                     ss2.at[c, i, 1, 2], rs2.at[c, i, 1, 2], to_x)

    def column(part, step):
        there = (col + step) % 4
        view, i = lanes_of[part], part_at[part]
        return remote(own.at[there, chip, :, view], rec_z.at[step - 1, :, view],
                      zss.at[i, step - 1], zrs.at[i, step - 1], {"col": there})

    def stage_one(part, k):
        c, view = nth(k), lanes_of[part]
        def body(q, carry):
            to_sibling(part, c, q).wait_recv()
            add_into(own.at[c, q, :, view], rec_sib.at[c, q, :, view])
            return carry
        lax.fori_loop(0, 4, body, 0)
        for copy in one(part, c):
            copy.start()

    def stage_two(part, k):
        c, view = nth(k), lanes_of[part]
        for copy in one(part, c):
            copy.wait_recv()
        for j in range(2):
            add_into(own.at[c, j * 2 + cx, top, view], rec_one.at[c, 0, j, :, view])
            add_into(own.at[c, cy * 2 + j, bottom, view], rec_one.at[c, 1, j, :, view])
        for copy in two_step(part, c):
            copy.start()

    def stage_three(part, k):
        c, view = nth(k), lanes_of[part]
        for copy in two_step(part, c):
            copy.wait_recv()
        add_into(own.at[c, chip, top, view], rec_two.at[c, 0, :, view])
        add_into(own.at[c, chip, bottom, view], rec_two.at[c, 1, :, view])
        pl.when(k < 3)(lambda: column(part, k + 1).start())

    def out_grads(k, carry):
        c = nth(k)
        weight_grads("b", c, a_t, lambda: branch[:, cols_b(c)])
        pl.when(k >= 1)(lambda: stage_one("b", k - 1))
        pl.when(k >= 2)(lambda: stage_two("b", k - 2))
        pl.when(k >= 3)(lambda: stage_three("b", k - 3))
        return carry
    lax.fori_loop(0, 4, out_grads, 0)

    def input_grads(k, carry):
        c = nth(k)
        attend_back(c)
        weight_grads("a", c, n_t, lambda: qg[c])
        pl.when(k == 0)(lambda: stage_one("b", k + 3))
        pl.when(k >= 1)(lambda: stage_one("a", k - 1))
        pl.when(k <= 1)(lambda: stage_two("b", k + 2))
        pl.when(k >= 2)(lambda: stage_two("a", k - 2))
        pl.when(k <= 2)(lambda: stage_three("b", k + 1))
        pl.when(k >= 3)(lambda: stage_three("a", k - 3))
        return carry
    lax.fori_loop(0, 4, input_grads, 0)
    stage_one("a", 3)
    each_flip(lambda flip: back_prod(flip).start())
    stage_two("a", 2)
    stage_three("a", 1)

    def to_tokens(m, carry):
        rows = pl.ds(pl.multiple_of(m * half, half), half)
        grad = dot_t(qg[0, rows, :], full_a[:, 0:width_a])
        for c in range(1, 4):
            grad = grad + dot_t(qg[c, rows, :], full_a[:, c * width_a : (c + 1) * width_a])
        x = tokens[rows, :].astype(f32)
        factor = lax.rsqrt(jnp.mean(x * x, axis=1, keepdims=True) + EPSILON)
        small[8:9, :] += jnp.sum(grad * x * factor, axis=0, keepdims=True)
        scaled = grad * gains[0:1, :]
        inner = jnp.mean(scaled * x, axis=1, keepdims=True)
        d_tokens[rows, :] += factor * scaled - x * (factor * factor * factor * inner)
        return carry
    lax.fori_loop(0, 1, to_tokens, 0)
    write_tokens = pltpu.make_async_copy(d_tokens, d_hbm, write.at[0])
    write_tokens.start()

    span = s_mid.shape[1]

    def small_plane(flip):
        there = row_at(row, flip)
        view = small.at[:, pl.ds(pl.multiple_of((there // 2) * span, 128), span)]
        return remote(view, s_rec.at[flip - 1], s_ss.at[flip - 1], s_rs.at[flip - 1], {"row": there})

    def small_column(step):
        return remote(s_mid, s_zrec.at[step - 1], sz_ss.at[step - 1], sz_rs.at[step - 1], {"col": (col + step) % 4})

    each_flip(lambda flip: small_plane(flip).start())
    stage_two("a", 3)
    stage_three("a", 2)
    s_mid[...] = small[:, pl.ds(pl.multiple_of(chip * span, 128), span)]

    def add_small(flip):
        small_plane(flip).wait_recv()
        s_mid[...] += s_rec[flip - 1]

    each_flip(add_small)
    for step in (1, 2, 3):
        small_column(step).start()
    stage_three("a", 3)

    own_prod.wait()
    each_flip(lambda flip: back_prod(flip).wait_recv())

    def to_output(m, carry):
        rows = pl.ds(pl.multiple_of(m * half, half), half)
        total = hidden[rows, :]
        for k in range(2):
            picked = jnp.where(at_slot(rows, k), 1.0, 0.0).astype(low)
            total = total + dot(picked, rec_prod[...]) * cols[rows, 4 + k : 5 + k]
        out_ref[rows, :] = total.astype(low)
        return carry
    lax.fori_loop(0, 1, to_output, 0)
    write_output = pltpu.make_async_copy(out_ref, out_hbm, write.at[1])
    write_output.start()

    total = s_mid[...]
    for step in (1, 2, 3):
        small_column(step).wait_recv()
        total = total + s_zrec[step - 1]
    sum_s[...] = total
    for part in ("b", "a"):
        for step in (1, 2, 3):
            column(part, step).wait_recv()

    def to_sums(i, carry):
        rows = pl.ds(pl.multiple_of(i * 32, 32), 32)
        total = own[col, chip, rows, :].astype(f32)
        for step in range(3):
            total = total + rec_z[step, rows, :].astype(f32)
        span_c = width_b // QUERY_PER_KEY
        zero, one_, two_ = (total[:, i * span_c : (i + 1) * span_c] for i in range(QUERY_PER_KEY))
        turned = pltpu.roll(one_, HEAD_SIZE, 1)
        first = lax.broadcasted_iota(jnp.int32, zero.shape, 1) < HEAD_SIZE
        sum_q[rows, 0:span_c] = jnp.where(first, zero, turned)
        sum_q[rows, span_c : 2 * span_c] = jnp.where(first, two_, zero)
        sum_q[rows, 2 * span_c : width_b] = jnp.where(first, turned, two_)
        sum_k[rows, :] = total[:, width_b : width_b + span_c]
        sum_v[rows, :] = total[:, width_b + span_c : width_a]
        sum_b[rows, :] = total[:, width_a:]
        return carry
    lax.fori_loop(0, block // 32, to_sums, 0)

    write_tokens.wait()
    write_output.wait()

    each_near(lambda flip: back(flip).wait_send())

    def all_sent(flip):
        back_gate(flip).wait_send()
        back_prod(flip).wait_send()
        small_plane(flip).wait_send()

    each_flip(all_sent)
    for step in (1, 2, 3):
        small_column(step).wait_send()
        column("a", step).wait_send()
        column("b", step).wait_send()

    def sent(c, carry):
        for part in ("a", "b"):
            def body(q, carry):
                to_sibling(part, c, q).wait_send()
                return carry
            lax.fori_loop(0, 4, body, 0)
            for copy in one(part, c):
                copy.wait_send()
            for copy in two_step(part, c):
                copy.wait_send()
        return carry
    lax.fori_loop(0, 4, sent, 0)


def run_backward(slot_of, gates, ids, router, gains, lse, segments, gate_grad, in_grad, back_far, produced,
                 hidden, tokens, cotangent, normed, attended, normed_two, qkv, full_a, full_out):
    table = jnp.concatenate(
        [slot_of.T.astype(jnp.float32), ids.T.astype(jnp.float32), gates.T, segments[None].astype(jnp.float32),
         jnp.zeros((1, segments.shape[0]), jnp.float32)], axis=0)
    sems = pltpu.SemaphoreType.DMA
    length, model = tokens.shape
    block = full_a.shape[0] // 8
    width_a, width_b = full_a.shape[1] // 4, full_out.shape[1] // 4
    width = width_a + width_b
    cut = block // 2
    low, f32 = tokens.dtype, jnp.float32
    vm = pl.BlockSpec(memory_space=pltpu.VMEM)
    slots = in_grad.shape[0]
    capacity = slots // 8
    span = model // 4
    router_p = jnp.pad(router, ((0, 0), (0, 128 - router.shape[1])))
    v = pltpu.VMEM
    rows_low = v((length, model), low)
    return pl.pallas_call(
        backward_kernel,
        out_shape=(
            jax.ShapeDtypeStruct((length, model), low),
            jax.ShapeDtypeStruct((length, model), f32),
            jax.ShapeDtypeStruct((block, width_b), f32),
            jax.ShapeDtypeStruct((block, (width_a - width_b) // 2), f32),
            jax.ShapeDtypeStruct((block, (width_a - width_b) // 2), f32),
            jax.ShapeDtypeStruct((block, width_b), f32),
            jax.ShapeDtypeStruct((16, span), f32),
        ),
        in_specs=[vm] * 4 + [ANY] * 13,
        out_specs=(ANY, ANY) + (vm,) * 5,
        scratch_shapes=[
            rows_low, v((length, model), f32), v((length, 8), f32), v((slots, model), low), v((8, 1, capacity), f32), v((slots, model), low),
            v((length, model), f32), rows_low, rows_low, rows_low,
            v(qkv.shape, low), v(full_a.shape, low), v(full_out.shape, low),
            v((model, length), low), v((model, length), low), rows_low,
            v((length, length), f32), v((width_b, model), low), v((length, width_b), low), v((4, length, width_a), low),
            v((length, 128), low), v((16, model), f32),
            v((4, 4, block, width), low), v((4, 4, block, width), low), v((4, 4, block, width), low),
            v((4, 2, 2, cut, width), low), v((4, 2, cut, width), low), v((3, block, width), low),
            v((7, 16, span), f32), v((16, span), f32), v((3, 16, span), f32),
            sems((9,)), sems((7,)), sems((7,)), sems((7,)), sems((7,)), sems((7,)), sems((7,)), sems((3,)), sems((2,)), sems((2,)),
            sems((4, 4, 2)), sems((4, 4, 2)), sems((4, 2, 2, 3)), sems((4, 2, 2, 3)),
            sems((2, 3)), sems((2, 3)), sems((7,)), sems((7,)), sems((3,)), sems((3,)),
        ],
        compiler_params=pltpu.CompilerParams(
            collective_id=2, has_side_effects=True, vmem_limit_bytes=60 * 2**20
        ),
        cost_estimate=pl.CostEstimate(flops=0, bytes_accessed=1_000_000, transcendentals=0),
    )(table, router_p, gains, lse, gate_grad, in_grad, back_far, produced, hidden, tokens,
      cotangent, normed, attended, normed_two, qkv, full_a, full_out)


def rms_factor(rows_in):
    return lax.rsqrt(jnp.mean(rows_in * rows_in, axis=1, keepdims=True) + EPSILON)


def dot(a, b):
    return jnp.dot(a, b, preferred_element_type=jnp.float32)


def dot_t(a, b):
    return lax.dot_general(a, b, (((1,), (1,)), ((), ())), preferred_element_type=jnp.float32)


def t_dot(a, b):
    return lax.dot_general(a, b, (((0,), (0,)), ((), ())), preferred_element_type=jnp.float32)


def on_small_slice():
    return lax.axis_size("row") == 8 and lax.axis_size("col") == 4


def pair_heads(a):
    if not on_small_slice():
        return [a]
    heads = [a[:, i * HEAD_SIZE : (i + 1) * HEAD_SIZE] for i in range(a.shape[1] // HEAD_SIZE)]
    return [heads[u * QUERY_PER_KEY + i] for i in range(QUERY_PER_KEY) for u in range(2)]


def part_heads(a):
    a = a.reshape(a.shape[0], -1, QUERY_PER_KEY, 2, HEAD_SIZE)
    return a.transpose(0, 1, 3, 2, 4).reshape(a.shape[0], -1)


def gather_all(own_a, own_b, own_s, own_c):
    col_a = lax.all_gather(own_a, "col", axis=1, tiled=True)
    col_b = lax.all_gather(own_b, "col", axis=1, tiled=True)
    small = lax.all_gather(lax.all_gather(own_s, "col", axis=0), "row", axis=1)
    return (
        lax.all_gather(col_a, "row", axis=0, tiled=True),
        lax.all_gather(col_b, "row", axis=0, tiled=True),
        small,
        lax.all_gather(own_c, "row", axis=0, tiled=True),
    )


def spread(own_c, own_g):
    if on_small_slice():
        return spread_tokens(own_c, own_g)
    return (
        lax.all_gather(own_c, "row", axis=0, tiled=True),
        lax.all_gather(own_g, "row", axis=0),
    )


def reduce_all(grad_a, grad_b, grad_s):
    def both(g):
        plane = lax.psum_scatter(g, "row", scatter_dimension=0, tiled=True).astype(jnp.float32)
        return lax.psum_scatter(plane, "col", scatter_dimension=1, tiled=True)

    small = lax.psum_scatter(grad_s, "row", scatter_dimension=0, tiled=False)
    return both(grad_a), both(grad_b), lax.psum_scatter(small, "col", scatter_dimension=0, tiled=False)


def expert_elsewhere(place, routed, mine, plane_normed, plane_upstream, full_gu, own_down):
    rows, length = place.shape
    model = plane_normed.shape[1]
    hidden_units = full_gu.shape[1] // 2
    capacity = 2 * length * TOP // rows
    full_down = lax.all_gather(own_down, "col", axis=0, tiled=True)
    chosen_rows = (
        (place[:, None, :] == jnp.arange(capacity, dtype=jnp.int32)[None, :, None]) & routed[:, None, :]
    ).astype(jnp.bfloat16)

    def of_slots(plane):
        return jnp.einsum(
            "rct,rtd->rcd",
            chosen_rows,
            plane.reshape(rows, length, model),
            preferred_element_type=jnp.float32,
        ).astype(jnp.bfloat16).reshape(rows * capacity, model)

    grouped, grouped_up = of_slots(plane_normed), of_slots(plane_upstream)
    slot_gate = jnp.sum(jnp.where(chosen_rows > 0, mine[:, None, :], 0.0), axis=2)
    slot_gate = slot_gate.reshape(rows * capacity, 1)
    grouped_grad = (grouped_up.astype(jnp.float32) * slot_gate).astype(jnp.bfloat16)
    both_pre = dot(grouped, full_gu)
    gate_pre, up_pre = both_pre[:, :hidden_units], both_pre[:, hidden_units:]
    sigma = jax.nn.sigmoid(gate_pre)
    silu_gate = gate_pre * sigma
    activation = (silu_gate * up_pre).astype(jnp.bfloat16)
    grad_down_local = t_dot(activation, grouped_grad).astype(jnp.bfloat16)
    grad_down = lax.psum_scatter(grad_down_local, "col", scatter_dimension=0, tiled=True)
    act_grad = dot_t(grouped_grad, full_down)
    both_grad = jnp.concatenate(
        [
            (act_grad * up_pre * sigma * (1.0 + gate_pre * (1.0 - sigma))).astype(jnp.bfloat16),
            (act_grad * silu_gate).astype(jnp.bfloat16),
        ],
        axis=1,
    )
    in_grad = dot_t(both_grad, full_gu).astype(jnp.bfloat16)
    produced = dot(activation, full_down).astype(jnp.bfloat16)
    slot_gate_grad = jnp.sum(produced.astype(jnp.float32) * grouped_up.astype(jnp.float32), axis=1)
    grad_gu_local = t_dot(grouped, both_grad).astype(jnp.bfloat16)
    return in_grad, produced, slot_gate_grad, grad_gu_local, grad_down.astype(jnp.float32)


def masked_scores(queries, heads_of_key, segments, head_scale):
    length = queries.shape[0]
    heads_of_query = queries.reshape(length, KEY_VALUE_HEADS, QUERY_PER_KEY, HEAD_SIZE)
    scores = (
        jnp.einsum("qkgd,skd->kgqs", heads_of_query, heads_of_key, preferred_element_type=jnp.float32)
        * head_scale
    )
    pos = jnp.arange(length, dtype=jnp.int32)
    allowed = (pos[None, :] <= pos[:, None]) & (segments[None, :] == segments[:, None])
    return jnp.where(allowed, scores, NEGATIVE), heads_of_query


def per_device(
    tokens,
    attn_gain,
    w_query,
    w_key,
    w_value,
    w_out,
    expert_gain,
    router,
    w_gate,
    w_up,
    w_down,
    segment_ids,
    expert_ids,
    cotangent,
):
    length, model = tokens.shape
    rows, cols = lax.axis_size("row"), lax.axis_size("col")
    experts = w_gate.shape[0] * rows
    capacity = 2 * length * TOP // experts
    head_scale = HEAD_SIZE ** (-0.5)
    segments = segment_ids.reshape(-1)
    block, width_q = w_query.shape
    width_k = w_key.shape[1]
    width_a = width_q + 2 * width_k
    piece = attn_gain.shape[0]
    router_cols = router.shape[1]

    hidden_units = w_gate.shape[2]
    own_down = w_down[0]

    lane = 256

    def at_row(v, row):
        return jnp.pad(v, ((row, 16 - row - v.shape[0]), (0, lane - v.shape[1])))

    own_s = (
        at_row(router.T, 0)
        + at_row(attn_gain[None], router_cols)
        + at_row(expert_gain[None], router_cols + 1)
    )
    own_a = jnp.concatenate([*pair_heads(w_query), w_key, w_value], axis=1)
    if on_small_slice():
        line_a, line_out, small, plane_upstream, own_gu = gather_line(
            own_a, w_out, own_s, cotangent, w_gate[0], w_up[0]
        )
        full_a, full_out = gather_plane(3, (line_a, line_out))
    else:
        own_gu = jnp.concatenate([w_gate[0], w_up[0]], axis=1)
        full_a, full_out, small, plane_upstream = gather_all(own_a, w_out, own_s, cotangent)
    full_gu = lax.all_gather(own_gu, "col", axis=0, tiled=True)
    full_router = small[:, :, :router_cols, :block].transpose(1, 3, 0, 2).reshape(model, experts)
    gains = (
        small[:, :, router_cols : router_cols + 2, :piece].transpose(2, 1, 0, 3).reshape(2, model).astype(jnp.float32)
    )
    gain_one, gain_two = gains[0:1], gains[1:2]

    rows_f = tokens.astype(jnp.float32)
    factor_one = rms_factor(rows_f)
    normed = (rows_f * factor_one * gain_one).astype(jnp.bfloat16)
    flat_qkv = dot(normed, full_a).astype(jnp.bfloat16)
    qkv = flat_qkv.reshape(length, cols, width_a)
    query_rows = qkv[:, :, :width_q].reshape(length, -1)
    if on_small_slice():
        query_rows = part_heads(query_rows)
    rows_of_key = qkv[:, :, width_q : width_q + width_k].reshape(length, -1)
    rows_of_value = qkv[:, :, width_q + width_k :].reshape(length, -1)
    heads_of_key = rows_of_key.reshape(length, KEY_VALUE_HEADS, HEAD_SIZE)
    heads_of_value = rows_of_value.reshape(length, KEY_VALUE_HEADS, HEAD_SIZE)

    scores, heads_of_query = masked_scores(query_rows, heads_of_key, segments, head_scale)
    row_max = jnp.max(scores, axis=-1, keepdims=True)
    expo_rows = jnp.exp(scores - row_max)
    totals = jnp.sum(expo_rows, axis=-1, keepdims=True)
    soft_probs = expo_rows / totals
    probs_low = soft_probs.astype(jnp.bfloat16)
    attended = (
        jnp.einsum("kgqs,skd->qkgd", probs_low, heads_of_value, preferred_element_type=jnp.float32)
        .reshape(length, -1)
        .astype(jnp.bfloat16)
    )
    hidden = rows_f + dot(attended, full_out)
    factor_two = rms_factor(hidden)
    normed_two = (hidden * factor_two * gain_two).astype(jnp.bfloat16)
    logits = dot(normed_two, full_router)

    named = expert_ids[:, :, None] == jnp.arange(experts, dtype=jnp.int32)[None, None, :]
    chosen = jnp.sum(jnp.where(named, logits[:, None, :], 0.0), axis=2)
    gate_probs = jax.nn.softmax(chosen, axis=1)
    gate_table = jnp.sum(jnp.where(named, gate_probs[:, :, None], 0.0), axis=1)
    gate_table = jnp.where(jnp.any(named, axis=1), gate_table, -1.0)
    plane_normed, plane_gate = spread(normed_two, gate_table.T)
    mine = lax.dynamic_index_in_dim(plane_gate, lax.axis_index("row"), axis=1, keepdims=False)
    routed = mine >= 0.0
    place = jnp.cumsum(routed.astype(jnp.int32), axis=1) - 1
    any_named = jnp.any(named, axis=1)
    before = jnp.cumsum(any_named.astype(jnp.int32), axis=0) - 1
    slot_of = jnp.sum(
        jnp.where(named, before[:, None, :] + jnp.arange(experts, dtype=jnp.int32) * capacity, 0),
        axis=2,
    )
    if on_small_slice():
        in_grad, produced, slot_gate_grad, grad_gu_local, grad_down, back_far = run_expert(
            jnp.where(routed, place, -1), mine, plane_normed, plane_upstream, full_gu, own_down
        )
        grad_gu = lax.psum_scatter(grad_gu_local, "col", scatter_dimension=0, tiled=True)
        lse = (row_max + jnp.log(totals)).reshape(KEY_VALUE_HEADS, 1, QUERY_PER_KEY * length)
        output, d_tokens, sum_q, sum_k, sum_v, sum_out, sum_s = run_backward(
            slot_of, gate_probs, expert_ids, full_router, gains, lse, segments,
            slot_gate_grad, in_grad, back_far, produced, hidden, tokens, cotangent, normed, attended.T, normed_two,
            flat_qkv, full_a, full_out,
        )
        output, d_tokens, sum_q, sum_k, sum_v, sum_out, grad_down, grad_gate, grad_up, own_router, gain_a, gain_e = finish(
            (output, d_tokens, sum_q, sum_k, sum_v, sum_out, grad_down), grad_gu, sum_s, block, piece, router_cols
        )
        return (
            output,
            d_tokens,
            gain_a.reshape(piece),
            sum_q,
            sum_k,
            sum_v,
            sum_out,
            gain_e.reshape(piece),
            own_router.T,
            grad_gate[None],
            grad_up[None],
            grad_down[None],
        )
    else:
        in_grad, produced, slot_gate_grad, grad_gu_local, grad_down = expert_elsewhere(
            place, routed, mine, plane_normed, plane_upstream, full_gu, own_down
        )
    grad_gu = lax.psum_scatter(grad_gu_local, "col", scatter_dimension=0, tiled=True)
    back_grad = lax.all_to_all(
        in_grad.reshape(rows, capacity, model), "row", split_axis=0, concat_axis=0, tiled=True
    ).reshape(experts * capacity, model)
    back_gate_grad = lax.all_to_all(
        slot_gate_grad.reshape(rows, 1, capacity), "row", split_axis=0, concat_axis=0, tiled=True
    ).reshape(experts * capacity)
    produced, back_grad = lax.optimization_barrier((produced, back_grad))
    back_rows = lax.all_to_all(
        produced.reshape(rows, capacity, model), "row", split_axis=0, concat_axis=0, tiled=True
    ).reshape(experts * capacity, model)

    all_slots = jnp.arange(experts * capacity, dtype=jnp.int32)
    is_slot = slot_of.T[:, :, None] == all_slots[None, None, :]
    from_slot = is_slot.astype(jnp.bfloat16)
    gate_grad = jnp.sum(jnp.where(is_slot, back_gate_grad[None, None, :], 0.0), axis=2).T
    returned = [dot(from_slot[k], back_rows) for k in range(TOP)]
    upstream = cotangent.astype(jnp.float32)
    output = (
        hidden + sum(returned[k] * gate_probs[:, k : k + 1] for k in range(TOP))
    ).astype(jnp.bfloat16)
    normed_two_grad = dot(from_slot[0] + from_slot[1], back_grad)
    pair_mean = jnp.sum(gate_probs * gate_grad, axis=1, keepdims=True)
    pair_logit = gate_probs * (gate_grad - pair_mean)
    logit_grad = jnp.sum(jnp.where(named, pair_logit[:, :, None], 0.0), axis=1).astype(jnp.bfloat16)
    grad_router = t_dot(normed_two, logit_grad)
    normed_two_grad = normed_two_grad + dot_t(logit_grad, full_router)
    grad_expert_gain = jnp.sum(normed_two_grad * hidden * factor_two, axis=0)
    scaled_two = normed_two_grad * gain_two
    hidden_grad = (
        upstream
        + factor_two * scaled_two
        - hidden * factor_two**3 * jnp.mean(scaled_two * hidden, axis=1, keepdims=True)
    )
    branch_grad = hidden_grad.astype(jnp.bfloat16)
    grad_out_full = t_dot(attended, branch_grad).astype(jnp.bfloat16)
    attended_grad = dot_t(branch_grad, full_out).astype(jnp.bfloat16)

    gradient_heads = attended_grad.reshape(length, KEY_VALUE_HEADS, QUERY_PER_KEY, HEAD_SIZE)
    value_grad = jnp.einsum(
        "kgqs,qkgd->skd", probs_low, gradient_heads, preferred_element_type=jnp.float32
    )
    prob_grad = jnp.einsum(
        "qkgd,skd->kgqs", gradient_heads, heads_of_value, preferred_element_type=jnp.float32
    )
    delta_sum = jnp.sum(soft_probs * prob_grad, axis=-1, keepdims=True)
    score_grad = (soft_probs * (prob_grad - delta_sum)).astype(jnp.bfloat16)
    query_grad = (
        jnp.einsum("kgqs,skd->qkgd", score_grad, heads_of_key, preferred_element_type=jnp.float32)
        * head_scale
    )
    key_grad = (
        jnp.einsum("kgqs,qkgd->skd", score_grad, heads_of_query, preferred_element_type=jnp.float32)
        * head_scale
    )
    qkv_grad = jnp.concatenate(
        [
            query_grad.astype(jnp.bfloat16).reshape(length, cols, width_q),
            key_grad.astype(jnp.bfloat16).reshape(length, cols, width_k),
            value_grad.astype(jnp.bfloat16).reshape(length, cols, width_k),
        ],
        axis=2,
    ).reshape(length, cols * width_a)
    grad_a_full = t_dot(normed, qkv_grad).astype(jnp.bfloat16)
    normed_grad = dot_t(qkv_grad, full_a)
    grad_attn_gain = jnp.sum(normed_grad * rows_f * factor_one, axis=0)
    scaled_one = normed_grad * gain_one
    d_tokens = (
        hidden_grad
        + factor_one * scaled_one
        - rows_f * factor_one**3 * jnp.mean(scaled_one * rows_f, axis=1, keepdims=True)
    )
    grad_s = jnp.concatenate(
        [
            jnp.pad(
                grad_router.reshape(rows, block, cols, router_cols).transpose(0, 2, 3, 1),
                ((0, 0), (0, 0), (0, 0), (0, lane - block)),
            ),
            jnp.pad(
                jnp.stack([grad_attn_gain, grad_expert_gain])
                .reshape(2, rows, cols, piece)
                .transpose(1, 2, 0, 3),
                ((0, 0), (0, 0), (0, 6 - router_cols), (0, lane - piece)),
            ),
        ],
        axis=2,
    )
    grad_a_full, d_tokens, output = lax.optimization_barrier((grad_a_full, d_tokens, output))
    sum_a, sum_out, sum_s = reduce_all(grad_a_full, grad_out_full, grad_s)
    return (
        output,
        d_tokens,
        sum_s[router_cols, :piece],
        sum_a[:, :width_q],
        sum_a[:, width_q : width_q + width_k],
        sum_a[:, width_q + width_k :],
        sum_out,
        sum_s[router_cols + 1, :piece],
        sum_s[:router_cols, :block].T,
        grad_gu[:, :hidden_units].astype(jnp.float32)[None],
        grad_gu[:, hidden_units:].astype(jnp.float32)[None],
        grad_down[None],
    )


def solution(mesh):
    in_specs = (
        P(("row", "col"), None),
        P(("row", "col")),
        P("row", "col"),
        P("row", "col"),
        P("row", "col"),
        P("row", "col"),
        P(("row", "col")),
        P("row", "col"),
        P("row", "col", None),
        P("row", "col", None),
        P("row", "col", None),
        P(("row", "col"), None),
        P(("row", "col"), None),
        P(("row", "col"), None),
    )
    out_specs = (
        P(("row", "col"), None),
        P(("row", "col"), None),
        P(("row", "col")),
        P("row", "col"),
        P("row", "col"),
        P("row", "col"),
        P("row", "col"),
        P(("row", "col")),
        P("row", "col"),
        P("row", "col", None),
        P("row", "col", None),
        P("row", "col", None),
    )
    return jax.shard_map(
        per_device, mesh=mesh, in_specs=in_specs, out_specs=out_specs, check_vma=False
    )
```
